32 devices in a mesh: dp: 2 (over core), seq: 4 (over y, x), tensor: 4 (over z).
Axes of the slice: x: 2, y: 2, z: 4, core: 2. Of those that a mesh axis runs over, the one named last changes fastest.
Arguments:
- pool: bfloat16 [512, 16, 1792], P(('dp', 'seq'), 'tensor')
- page_table: int32 [8, 64], replicated, may hold values from 0 to 511, as said below
- reassign: int32 [8], replicated, may hold values from 0 to 7, as said below
- lengths: int32 [8], replicated, may hold values from 1 to 1024, as said below
- gain_one: float32 [1792], replicated, may hold values from 0.1 to 1.9
- w_featmap: bfloat16 [1792, 2, 256], P(None, None, 'tensor'), may hold values from -0.25 to 0.25
- w_value: bfloat16 [1792, 1792], P(None, 'tensor'), may hold values from -0.125 to 0.125
- w_out_one: bfloat16 [1792, 1792], P('tensor'), may hold values from -0.5 to 0.5
- gain_two: float32 [1792], replicated, may hold values from 0.1 to 1.9
- w_window: bfloat16 [1792, 3, 1792], P(None, None, 'tensor')
- conv_window: float32 [3, 3, 1792], P(None, None, 'tensor')
- w_out_two: bfloat16 [1792, 1792], P('tensor'), may hold values from -0.125 to 0.125
Outputs:
- out: bfloat16 [8, 64, 16, 1792], P('dp', 'seq', 'tensor')
The draws below stay inside these ranges and needn't reach their ends.
Inputs may be any that keep to these rules, and one draw needn't show every extreme that they name: A permutation: output slot i holds request reassign[i]; requests are dealt by falling length to the 2 groups of 4 slots in alternating order, so the first slot of every group holds a request of length 1024. page_table[r, p] is the pool page that holds positions p * 16 to p * 16 + 15 of request r, and every pool page is named once. Take the pool in aligned blocks of 64 pages, and the pages that the output needs in blocks: block g * 4 + b holds positions b * 256 to b * 256 + 255 of slots g * 4 to g * 4 + 3. No pool block holds more than 8 pages of one such block, and 8 is reached. `lengths`: at least 2 requests have length 1024.
All inputs are finite; a program needn't handle non-finite values.
Results may differ from the reference program's by a relative error of at most 0.039.
Values may be sent and summed in bfloat16 or wider, within the bound.
No kernel may reach another device: no remote copies, remote signals or barrier semaphores. Data moves between devices by JAX's collectives and lax.ppermute only.
A program may use at most 256 MiB of HBM per device.

```python
import jax
import jax.numpy as jnp
from jax import lax

D = 1792
HEADS = 16
HEAD = 112
FEAT = 16
WINDOW = 64
KERNEL = 3
PAGE = 16
REQ_DEV = 4
BLOCK = 256
FEATS = 256
LEN = 1024
PAGES = 64
PAGES_DEV = 64
REQUESTS = 8
POOL_PAGES = 512
N_DP = 2
N_SEQ = 4
N_TENSOR = 4


def routing_tables(key):
    base_key = jax.random.fold_in(key, 11)
    group_key, slot_key, length_key, long_key, tie_key = jax.random.split(base_key, 5)
    devices_all = N_DP * N_SEQ
    block_pages = BLOCK // PAGE
    raw_lengths = jax.random.randint(length_key, (REQUESTS,), 1, LEN + 1, jnp.int32)
    long_pick = jax.random.permutation(long_key, REQUESTS) < N_DP
    lengths = jnp.where(long_pick, LEN, raw_lengths).astype(jnp.int32)
    ties = jax.random.permutation(tie_key, REQUESTS).astype(jnp.int32)
    score = lengths * REQUESTS + ties
    order = jnp.argsort(-score).astype(jnp.int32)
    rank = jnp.arange(REQUESTS, dtype=jnp.int32)
    rounds = rank // N_DP
    within = rank % N_DP
    group = jnp.where(rounds % 2 == 0, within, N_DP - 1 - within)
    slot = group * REQ_DEV + rounds
    reassign = jnp.zeros((REQUESTS,), jnp.int32).at[slot].set(order)
    device_order = jax.random.permutation(group_key, devices_all).astype(jnp.int32)
    slot_keys = jax.random.split(slot_key, devices_all)
    slot_orders = jax.vmap(lambda one_key: jax.random.permutation(one_key, PAGES_DEV))(slot_keys).astype(jnp.int32)
    target = jnp.arange(devices_all, dtype=jnp.int32)[:, None]
    local_page = jnp.arange(PAGES_DEV, dtype=jnp.int32)[None, :]
    source = device_order[(target + local_page) % devices_all]
    pool_index = source * PAGES_DEV + slot_orders[source, jnp.broadcast_to(local_page, source.shape)]
    inverse = jnp.argsort(reassign).astype(jnp.int32)
    request_ids = jnp.arange(REQUESTS, dtype=jnp.int32)[:, None]
    page_ids = jnp.arange(PAGES, dtype=jnp.int32)[None, :]
    slot_ids = inverse[request_ids]
    target_ids = slot_ids // REQ_DEV * N_SEQ + page_ids // block_pages
    local_ids = slot_ids % REQ_DEV * block_pages + page_ids % block_pages
    page_table = pool_index[target_ids, local_ids]
    return (reassign, page_table.astype(jnp.int32), lengths)


def draw_reassign(key, part):
    return routing_tables(key)[0]


def draw_page_table(key, part):
    return routing_tables(key)[1]


def draw_lengths(key, part):
    return routing_tables(key)[2]


def draw_pool(key, part):
    first_key = jax.random.fold_in(key, 0)
    draws = jax.random.normal(first_key, (POOL_PAGES, PAGE, D), jnp.float32)
    return draws.astype(jnp.bfloat16)


def draw_w_window(key, part):
    first_key = jax.random.fold_in(key, 0)
    spread = D ** (-0.5)
    draws = jax.random.normal(first_key, (D, 3, D), jnp.float32) * spread
    return draws.astype(jnp.bfloat16)


def draw_conv_window(key, part):
    first_key, second_key = jax.random.split(key, 2)
    leading = jax.random.uniform(first_key, (1, 3, D), jnp.float32, 0.6, 1.4)
    others = 0.3 * jax.random.normal(second_key, (KERNEL - 1, 3, D), jnp.float32)
    return jnp.concatenate([leading, others], axis=0)


def steps_of(own_key, shape, pieces, low, high):
    def one(axis_at, blocks):
        heights = jax.random.uniform(jax.random.fold_in(jax.random.fold_in(own_key, 6), axis_at), (blocks,), jnp.float32, low / len(pieces), high / len(pieces))
        return jnp.repeat(jnp.exp(heights), shape[axis_at] // blocks).reshape((-1,) + (1,) * (len(shape) - axis_at - 1))

    gain = one(*pieces[0])
    for cut in pieces[1:]:
        gain = gain * one(*cut)
    return gain


def gaussian(key, extent, width, bound, shards=(), kind=jnp.bfloat16):
    array = width * jax.random.normal(key, extent, jnp.float32)
    if shards:
        array = array * steps_of(key, extent, shards, -0.22, 0.18)
    return jnp.clip(array, -bound, bound).astype(kind)


def setup_inputs(seed: int = 0) -> dict:
    splits = jax.random.split(jax.random.key(seed), 13)
    pool = draw_pool(jax.random.fold_in(splits[12], 71), 0)
    page_table = draw_page_table(jax.random.fold_in(splits[12], 71), 0)
    reassign = draw_reassign(jax.random.fold_in(splits[12], 71), 0)
    lengths = draw_lengths(jax.random.fold_in(splits[12], 71), 0)
    gain_one = jnp.clip(1.0 + 0.18 * jax.random.normal(splits[4], (D,), jnp.float32), 0.1, 1.9)
    w_featmap = gaussian(splits[5], (D, 2, FEATS), (D // 4) ** -0.5, 0.25, ((2, 4),))
    w_value = gaussian(splits[6], (D, D), D ** -0.5, 0.125, ((1, 4),))
    w_out_one = gaussian(splits[7], (D, D), (D // 16) ** -0.5, 0.5, ((0, 4),))
    gain_two = jnp.clip(1.0 + 0.18 * jax.random.normal(splits[8], (D,), jnp.float32), 0.1, 1.9)
    w_window = draw_w_window(jax.random.fold_in(splits[12], 71), 0)
    conv_window = draw_conv_window(jax.random.fold_in(splits[12], 71), 0)
    w_out_two = gaussian(splits[11], (D, D), D ** -0.5, 0.125, ((0, 4),))
    return {"pool": pool, "page_table": page_table, "reassign": reassign, "lengths": lengths, "gain_one": gain_one, "w_featmap": w_featmap, "w_value": w_value, "w_out_one": w_out_one, "gain_two": gain_two, "w_window": w_window, "conv_window": conv_window, "w_out_two": w_out_two}


norm_eps = 1e-05

def rounded(values):
    return lax.optimization_barrier(values.astype(jnp.bfloat16)).astype(jnp.float32)

def rms_normed(row_block, gain_vector):
    values = row_block.astype(jnp.float32)
    scale = lax.rsqrt(lax.optimization_barrier(jnp.mean(values * values, axis=-1, keepdims=True)) + norm_eps)
    return (values * scale * gain_vector).astype(jnp.bfloat16)

def causal_conv(projected, tap_table):
    seq_rows = projected.shape[0]
    padded = jnp.pad(projected, ((KERNEL - 1, 0), (0, 0)))
    total = tap_table[0] * padded[KERNEL - 1:KERNEL - 1 + seq_rows]
    for offset in range(1, KERNEL):
        total = total + tap_table[offset] * padded[KERNEL - 1 - offset:KERNEL - 1 - offset + seq_rows]
    return total

def grouped_sum(mixed, weight):
    group_cols = D // N_TENSOR
    total = jnp.zeros((mixed.shape[0], D), jnp.float32)
    for group in range(N_TENSOR):
        partial_value = jnp.dot(mixed[:, group * group_cols:(group + 1) * group_cols], weight[group * group_cols:(group + 1) * group_cols], preferred_element_type=jnp.float32)
        total = total + rounded(partial_value)
    return total

def reference(pool, page_table, reassign, lengths, gain_one, w_featmap, w_value, w_out_one, gain_two, w_window, conv_window, w_out_two):
    highest = lax.Precision.HIGHEST

    def one_request(carried):
        tokens, prompt_length = carried
        normed_one = rms_normed(tokens, gain_one)
        featured = jnp.dot(normed_one, w_featmap.reshape(D, 2 * FEATS), preferred_element_type=jnp.float32)
        queries = rounded(featured[:, :FEATS]).reshape(LEN, HEADS, FEAT)
        key_rows = rounded(featured[:, FEATS:]).reshape(LEN, HEADS, FEAT)
        values = rounded(jnp.dot(normed_one, w_value, preferred_element_type=jnp.float32)).reshape(LEN, HEADS, HEAD)
        scores = jnp.einsum('thf,uhf->htu', queries, key_rows, precision=highest) * FEAT ** (-0.5)
        causal = jnp.arange(LEN)[None, :] <= jnp.arange(LEN)[:, None]
        kernel = jnp.where(causal[None], 1.0 + scores + 0.5 * scores * scores, 0.0)
        numerator = jnp.einsum('htu,uhd->thd', kernel, values, precision=highest)
        denominator = lax.optimization_barrier(jnp.sum(kernel, axis=2)).T
        mixed_one = (numerator / denominator[..., None]).reshape(LEN, D).astype(jnp.bfloat16)
        residual_one = (tokens.astype(jnp.float32) + grouped_sum(mixed_one, w_out_one)).astype(jnp.bfloat16)
        normed_two = rms_normed(residual_one, gain_two)
        projected = jnp.dot(normed_two, w_window.reshape(D, 3 * D), preferred_element_type=jnp.float32)
        convolved = rounded(causal_conv(projected, conv_window.reshape(KERNEL, 3 * D)))
        queries_two = convolved[:, :D].reshape(LEN, HEADS, HEAD)
        keys_two = convolved[:, D:2 * D].reshape(LEN, HEADS, HEAD)
        values_two = convolved[:, 2 * D:].reshape(LEN, HEADS, HEAD)
        logits = jnp.einsum('thd,uhd->htu', queries_two, keys_two, precision=highest) * HEAD ** (-0.5)
        query_pos = jnp.arange(LEN)[:, None]
        key_pos = jnp.arange(LEN)[None, :]
        allowed = (key_pos <= query_pos) & (key_pos > query_pos - WINDOW)
        logits = jnp.where(allowed[None], logits, -jnp.inf)
        row_top = lax.optimization_barrier(jnp.max(logits, axis=2, keepdims=True))
        weights = jnp.exp(logits - row_top)
        attention = rounded(weights / lax.optimization_barrier(jnp.sum(weights, axis=2, keepdims=True)))
        mixed_two = jnp.einsum('htu,uhd->thd', attention, values_two, precision=highest).reshape(LEN, D).astype(jnp.bfloat16)
        result = (residual_one.astype(jnp.float32) + grouped_sum(mixed_two, w_out_two)).astype(jnp.bfloat16)
        positions = jnp.arange(LEN)
        result = jnp.where((positions < prompt_length)[:, None], result, jnp.zeros_like(result))
        return result.reshape(PAGES, PAGE, D)
    tokens = pool[page_table[reassign]].reshape(REQUESTS, LEN, D)
    prompt_length = lengths[reassign]
    return lax.map(one_request, (tokens, prompt_length))
```

```python
import functools

import jax
import jax.numpy as jnp
import numpy as np
from jax import lax
from jax.experimental import pallas as pl
from jax.experimental.pallas import tpu as pltpu
from jax.sharding import PartitionSpec as P

HEAD = 112
WINDOW = 64
EPS = 1e-05
SLOT = 128
FEAT_SLOT = 256
HALO = 80
VMEM = 60 * 1024 * 1024
F32 = jnp.float32
BF16 = jnp.bfloat16


def dot(a, b, dims=((1,), (0,))):
    return lax.dot_general(a, b, (dims, ((), ())), preferred_element_type=F32)


def normed_rows(rows, gain):
    scale = lax.rsqrt(jnp.mean(rows * rows, axis=-1, keepdims=True) + EPS)
    return (rows * scale * gain).astype(BF16)


def feature_tables(heads, feature_dim):
    pairs = [(i, j) for i in range(feature_dim) for j in range(i, feature_dim)]
    pairs += [(i, -1) for i in range(feature_dim)] + [(-1, -1)]
    first = np.zeros((heads * feature_dim, heads * FEAT_SLOT), np.float32)
    second = np.zeros_like(first)
    ones = np.zeros((2, heads * FEAT_SLOT), np.float32)
    scale = np.zeros((1, heads * FEAT_SLOT), np.float32)
    for h in range(heads):
        for n, (i, j) in enumerate(pairs):
            at = h * FEAT_SLOT + n
            if i >= 0:
                first[h * feature_dim + i, at] = 1
            else:
                ones[0, at] = 1
            if j >= 0:
                second[h * feature_dim + j, at] = 1
            else:
                ones[1, at] = 1
            if i < 0:
                scale[0, at] = 1
            elif j < 0:
                scale[0, at] = feature_dim**-0.5
            else:
                scale[0, at] = (0.5 if i == j else 1.0) / feature_dim
    return first, second, ones, scale, -(-len(pairs) // 16) * 16


def spread_table(heads):
    spread = np.zeros((heads * HEAD, heads * SLOT), np.float32)
    ones = np.zeros((1, heads * SLOT), np.float32)
    for h in range(heads):
        spread[h * HEAD : (h + 1) * HEAD, h * SLOT : h * SLOT + HEAD] = np.eye(HEAD)
        ones[0, h * SLOT + HEAD] = 1
    return spread, ones


def features(rows, first, second, ones):
    return (dot(rows, first) + ones[0:1]) * (dot(rows, second) + ones[1:2])


def linear_kernel(
    heads,
    feature_dim,
    kept,
    x_ref,
    gain_ref,
    w_ref,
    first_ref,
    second_ref,
    ones_ref,
    spread_ref,
    column_ref,
    num_ref,
    q_ref,
    state_ref,
    normed_ref,
):
    @pl.when(pl.program_id(0) == 0)
    def _():
        normed_ref[...] = normed_rows(x_ref[...].astype(F32), gain_ref[...])

    rows = x_ref.shape[0]
    width = heads * feature_dim
    projected = dot(normed_ref[...], w_ref[0]).astype(BF16)
    queries = projected[:, :width]
    keys = projected[:, width : 2 * width]
    values = dot(projected[:, 2 * width :], spread_ref[...]) + column_ref[...]
    values = values.astype(BF16)
    q_ref[0] = queries
    lane_head = lax.broadcasted_iota(jnp.int32, (rows, width), 1) // feature_dim
    causal = lax.broadcasted_iota(jnp.int32, (rows, rows), 1) <= lax.broadcasted_iota(
        jnp.int32, (rows, rows), 0
    )
    key_features = features(keys, first_ref[...], second_ref[...], ones_ref[...]).astype(BF16)
    for h in range(heads):
        own = jnp.where(lane_head == h, queries, jnp.zeros_like(queries))
        scores = dot(own, keys, ((1,), (1,))) * feature_dim**-0.5
        kernel = jnp.where(causal, 1.0 + scores + 0.5 * scores * scores, 0.0).astype(BF16)
        value = values[:, h * SLOT : (h + 1) * SLOT]
        num_ref[0, :, h * SLOT : (h + 1) * SLOT] = dot(kernel, value)
        state = dot(key_features[:, h * FEAT_SLOT : h * FEAT_SLOT + kept], value, ((0,), (0,)))
        state_ref[0, h * kept : (h + 1) * kept, :] = state.astype(BF16)


def padded_heads(heads, w, padded_ref):
    cols = w.shape[1]
    for h in range(heads):
        padded_ref[h * SLOT : h * SLOT + HEAD, :] = w[h * HEAD : (h + 1) * HEAD, :]
        padded_ref[h * SLOT + HEAD : (h + 1) * SLOT, :] = jnp.zeros((SLOT - HEAD, cols), BF16)


def add_branch(heads, mixed, w_ref, padded_ref, total_ref):
    parts, cols = w_ref.shape[1], w_ref.shape[3]
    for part in range(parts):
        padded_heads(heads, w_ref[0, part], padded_ref)
        share = dot(mixed, padded_ref[...]).astype(BF16).astype(F32)
        total_ref[:, part * cols : (part + 1) * cols] += share


def out_one_kernel(
    heads,
    kept,
    priors,
    *refs,
):
    num_ref, q_ref, first_ref, second_ref, ones_ref, scale_ref = refs[:6]
    prior_refs = refs[6 : 6 + priors]
    w_ref, x_ref, gain_ref, residual_ref, normed_ref, total_ref, padded_ref, mixed_ref = refs[
        6 + priors :
    ]
    step = pl.program_id(0)

    @pl.when(step == 0)
    def _():
        total_ref[...] = jnp.zeros_like(total_ref)

    query_features = features(q_ref[0], first_ref[...], second_ref[...], ones_ref[...])
    query_features = (query_features * scale_ref[...]).astype(BF16)
    for h in range(heads):
        at = slice(h * kept, (h + 1) * kept)
        prior = prior_refs[0][0, at, :].astype(F32)
        for ref in prior_refs[1:]:
            prior = prior + ref[0, at, :].astype(F32)
        lanes = slice(h * SLOT, (h + 1) * SLOT)
        total = num_ref[0, :, lanes] + dot(
            query_features[:, h * FEAT_SLOT : h * FEAT_SLOT + kept], prior.astype(BF16)
        )
        mixed_ref[:, lanes] = (total / total[:, HEAD : HEAD + 1]).astype(BF16)
    add_branch(heads, mixed_ref[...], w_ref, padded_ref, total_ref)

    @pl.when(step == pl.num_programs(0) - 1)
    def _():
        residual = (x_ref[...].astype(F32) + total_ref[...]).astype(BF16)
        residual_ref[...] = residual
        normed_ref[...] = normed_rows(residual.astype(F32), gain_ref[...])


def window_kernel(heads, first_ref, x_ref, halo_ref, w_ref, tap_ref, mixed_ref, rows_ref):
    @pl.when(pl.program_id(0) == 0)
    def _():
        rows_ref[:HALO] = halo_ref[...]
        rows_ref[HALO:] = x_ref[...]

    rows = x_ref.shape[0]
    lead = HALO - WINDOW
    cols = heads * HEAD
    projected = dot(rows_ref[...], w_ref[0])
    taps = tap_ref[0]
    convolved = taps[0:1] * projected
    for offset in range(1, taps.shape[0]):
        convolved = convolved + taps[offset : offset + 1] * pltpu.roll(projected, offset, 0)
    convolved = convolved[lead:].astype(BF16)
    tile = 128
    span = tile + WINDOW
    row = lax.broadcasted_iota(jnp.int32, (tile, span), 0)
    col = lax.broadcasted_iota(jnp.int32, (tile, span), 1)
    band = (col > row) & (col <= row + WINDOW)
    for h in range(heads):
        queries = convolved[WINDOW:, h * HEAD : (h + 1) * HEAD]
        keys = convolved[:, cols + h * HEAD : cols + (h + 1) * HEAD]
        values = convolved[:, 2 * cols + h * HEAD : 2 * cols + (h + 1) * HEAD]
        for start in range(0, rows, tile):
            logits = dot(queries[start : start + tile], keys[start : start + span], ((1,), (1,)))
            allowed = band
            if start < WINDOW:
                allowed = band & (col >= WINDOW - start - first_ref[0])
            logits = jnp.where(allowed, logits * HEAD**-0.5, -jnp.inf)
            weights = jnp.exp(logits - jnp.max(logits, axis=1, keepdims=True))
            weights = weights / jnp.sum(weights, axis=1, keepdims=True)
            mixed = dot(weights.astype(BF16), values[start : start + span])
            mixed_ref[0, start : start + tile, h * SLOT : h * SLOT + HEAD] = mixed.astype(BF16)
    for h in range(heads):
        mixed_ref[0, :, h * SLOT + HEAD : (h + 1) * SLOT] = jnp.zeros((rows, SLOT - HEAD), BF16)


def out_two_kernel(heads, live_ref, mixed_ref, w_ref, residual_ref, out_ref, total_ref, padded_ref):
    step = pl.program_id(0)

    @pl.when(step == 0)
    def _():
        total_ref[...] = jnp.zeros_like(total_ref)

    add_branch(heads, mixed_ref[0], w_ref, padded_ref, total_ref)

    @pl.when(step == pl.num_programs(0) - 1)
    def _():
        result = (residual_ref[...].astype(F32) + total_ref[...]).astype(BF16)
        row = lax.broadcasted_iota(jnp.int32, result.shape, 0)
        out_ref[...] = jnp.where(row < live_ref[0], result, jnp.zeros_like(result))


def whole(shape):
    return pl.BlockSpec(shape, lambda g: (0,) * len(shape))


def each(shape):
    return pl.BlockSpec((1,) + shape, lambda g: (g,) + (0,) * len(shape))


SMEM = pl.BlockSpec(memory_space=pltpu.SMEM)


def call(kernel, groups, in_specs, out_specs, out_shape, scratch, flops, moved, name):
    return pl.pallas_call(
        kernel,
        grid=(groups,),
        in_specs=in_specs,
        out_specs=out_specs,
        out_shape=out_shape,
        scratch_shapes=scratch,
        compiler_params=pltpu.CompilerParams(
            dimension_semantics=("arbitrary",), vmem_limit_bytes=VMEM
        ),
        cost_estimate=pl.CostEstimate(flops=flops, bytes_accessed=moved, transcendentals=0),
        name=name,
    )


def from_all_planes(piece):
    names = ("tensor", "dp", "seq")
    gathered = lax.all_gather(piece, names)
    return gathered.reshape(tuple(lax.axis_size(n) for n in names) + piece.shape)


def earlier_blocks(state, axis):
    peers = lax.axis_size(axis)
    if peers <= 4:
        return [
            lax.ppermute(state, axis, [(i, i + by) for i in range(peers - by)])
            for by in range(1, peers)
        ]
    everything = lax.all_gather(state, axis).astype(F32)
    reached = jnp.arange(peers) < lax.axis_index(axis)
    return [jnp.sum(jnp.where(reached[:, None, None, None], everything, 0.0), axis=0)]


def on_device(
    pool,
    page_table,
    reassign,
    lengths,
    gain_one,
    w_featmap,
    w_value,
    w_out_one,
    gain_two,
    w_window,
    conv_window,
    w_out_two,
):
    dp_count, seq_count, group_count = (lax.axis_size(n) for n in ("dp", "seq", "tensor"))
    groups = dp_count * seq_count
    device_place = lax.axis_index(("dp", "seq"))
    dp_place, seq_place, tensor_place = (lax.axis_index(n) for n in ("dp", "seq", "tensor"))
    pages_dev, page_share, width = pool.shape
    slots_total, pages_total = page_table.shape
    req_dev = slots_total // dp_count
    page_span = pages_total // seq_count
    page_rows = page_share * group_count
    rows = page_span * page_rows
    assert req_dev == group_count
    heads = w_value.shape[1] // HEAD
    head_cols = heads * HEAD
    feat_cols = w_featmap.shape[2]
    feature_dim = feat_cols // heads
    tap_count = conv_window.shape[0]

    plane_rows = width // groups
    row_at = device_place * plane_rows
    out_rows, out_cols = head_cols // seq_count, width // dp_count

    def row_piece(w):
        return lax.dynamic_slice_in_dim(w, row_at, plane_rows).reshape(plane_rows, -1)

    def out_piece(w):
        return lax.dynamic_slice(w, (seq_place * out_rows, dp_place * out_cols), (out_rows, out_cols))

    piece_one = jnp.concatenate([row_piece(w_featmap), row_piece(w_value)], axis=1)
    all_one = from_all_planes(piece_one).reshape(group_count, width, -1)
    all_out_one = from_all_planes(out_piece(w_out_one)).reshape(
        group_count, dp_count, head_cols, out_cols
    )
    all_window = from_all_planes(row_piece(w_window)).reshape(group_count, width, -1)
    all_out_two = from_all_planes(out_piece(w_out_two)).reshape(
        group_count, dp_count, head_cols, out_cols
    )
    all_taps = lax.all_gather(conv_window.reshape(tap_count, 3 * head_cols), "tensor")

    placed = reassign[:, None] == jnp.arange(slots_total, dtype=jnp.int32)[None, :]
    table = jnp.sum(jnp.where(placed[:, :, None], page_table[None], 0), axis=1)
    slot_lengths = jnp.sum(jnp.where(placed, lengths[None, :], 0), axis=1)
    source_page = (
        table.reshape(dp_count, req_dev, seq_count, page_span)
        .transpose(0, 2, 1, 3)
        .reshape(groups, req_dev * page_span)
    )
    capacity = (pages_dev + groups - 1) // groups
    page_owner = source_page // pages_dev
    pool_slot = source_page % pages_dev
    before = jnp.arange(pages_dev)[None, :] < jnp.arange(pages_dev)[:, None]
    pair_rank = jnp.sum((page_owner[:, :, None] == page_owner[:, None, :]) & before[None], axis=2)
    send_hit = (page_owner == device_place)[:, None, :] & (
        pair_rank[:, None, :] == jnp.arange(capacity)[None, :, None]
    )
    send_slot = jnp.sum(jnp.where(send_hit, pool_slot[:, None, :], 0), axis=2)
    outgoing = pool.at[send_slot.reshape(-1)].get(mode="promise_in_bounds")
    outgoing = outgoing.reshape(groups, capacity, page_share, width)
    arrived = lax.all_to_all(outgoing, ("dp", "seq"), split_axis=0, concat_axis=0, tiled=True)
    own_row = jnp.arange(groups)[:, None] == device_place
    pick_rows = jnp.sum(jnp.where(own_row, page_owner * capacity + pair_rank, 0), axis=0)
    picked = arrived.reshape(groups * capacity, page_share, width)
    picked = picked.at[pick_rows].get(mode="promise_in_bounds")

    picked = picked.reshape(req_dev, page_span, page_share, width)
    swapped = lax.all_to_all(picked, "tensor", split_axis=0, concat_axis=0, tiled=True)
    tokens = swapped.transpose(1, 0, 2, 3).reshape(rows, width)
    slot = dp_place * req_dev + tensor_place
    length = jnp.sum(jnp.where(jnp.arange(slots_total) == slot, slot_lengths, 0))

    first, second, ones, scale, kept = feature_tables(heads, feature_dim)
    first, second = jnp.asarray(first, BF16), jnp.asarray(second, BF16)
    spread, column = spread_table(heads)
    spread = jnp.asarray(spread, BF16)
    one_cols = 2 * feat_cols + head_cols
    slots = heads * SLOT
    num, queries, state = call(
        functools.partial(linear_kernel, heads, feature_dim, kept),
        group_count,
        [
            whole((rows, width)),
            whole((1, width)),
            each((width, one_cols)),
            whole(first.shape),
            whole(second.shape),
            whole(ones.shape),
            whole(spread.shape),
            whole(column.shape),
        ],
        [each((rows, slots)), each((rows, feat_cols)), each((heads * kept, SLOT))],
        [
            jax.ShapeDtypeStruct((group_count, rows, slots), F32),
            jax.ShapeDtypeStruct((group_count, rows, feat_cols), BF16),
            jax.ShapeDtypeStruct((group_count, heads * kept, SLOT), BF16),
        ],
        [pltpu.VMEM((rows, width), BF16)],
        3 * group_count * rows * width * one_cols,
        group_count * width * one_cols * 2,
        "linear_rows",
    )(tokens, gain_one[None], all_one, first, second, ones, spread, column)
    priors = earlier_blocks(state, "seq")
    residual, normed_two = call(
        functools.partial(out_one_kernel, heads, kept, len(priors)),
        group_count,
        [
            each((rows, slots)),
            each((rows, feat_cols)),
            whole(first.shape),
            whole(second.shape),
            whole(ones.shape),
            whole(scale.shape),
        ]
        + [each((heads * kept, SLOT))] * len(priors)
        + [
            each((dp_count, head_cols, out_cols)),
            whole((rows, width)),
            whole((1, width)),
        ],
        [whole((rows, width)), whole((rows, width))],
        [jax.ShapeDtypeStruct((rows, width), BF16)] * 2,
        [
            pltpu.VMEM((rows, width), F32),
            pltpu.VMEM((slots, out_cols), BF16),
            pltpu.VMEM((rows, slots), BF16),
        ],
        3 * group_count * rows * width * head_cols,
        group_count * width * head_cols * 2,
        "linear_out",
    )(num, queries, first, second, ones, scale, *priors, all_out_one, tokens, gain_two[None])

    halo = lax.ppermute(
        normed_two[rows - HALO :], "seq", [(i, i + 1) for i in range(seq_count - 1)]
    )
    block_start = (seq_place * rows).astype(jnp.int32)[None]
    mixed_two = call(
        functools.partial(window_kernel, heads),
        group_count,
        [
            SMEM,
            whole((rows, width)),
            whole((HALO, width)),
            each((width, 3 * head_cols)),
            each((tap_count, 3 * head_cols)),
        ],
        each((rows, slots)),
        jax.ShapeDtypeStruct((group_count, rows, slots), BF16),
        [pltpu.VMEM((HALO + rows, width), BF16)],
        3 * group_count * rows * width * 3 * head_cols,
        group_count * width * 3 * head_cols * 2,
        "window_rows",
    )(block_start, normed_two, halo, all_window, all_taps)
    live = (length - seq_place * rows).astype(jnp.int32)[None]
    result = call(
        functools.partial(out_two_kernel, heads),
        group_count,
        [
            SMEM,
            each((rows, slots)),
            each((dp_count, head_cols, out_cols)),
            whole((rows, width)),
        ],
        whole((rows, width)),
        jax.ShapeDtypeStruct((rows, width), BF16),
        [pltpu.VMEM((rows, width), F32), pltpu.VMEM((slots, out_cols), BF16)],
        2 * group_count * rows * width * head_cols,
        group_count * width * head_cols * 2,
        "window_out",
    )(live, mixed_two, all_out_two, residual)

    result = result.reshape(page_span, group_count, page_share, width).transpose(1, 0, 2, 3)
    return lax.all_to_all(result, "tensor", split_axis=0, concat_axis=0, tiled=True)


def solution(mesh):
    return jax.shard_map(
        on_device,
        mesh=mesh,
        in_specs=(
            P(("dp", "seq"), "tensor", None),
            P(),
            P(),
            P(),
            P(),
            P(None, None, "tensor"),
            P(None, "tensor"),
            P("tensor", None),
            P(),
            P(None, None, "tensor"),
            P(None, None, "tensor"),
            P("tensor", None),
        ),
        out_specs=P("dp", "seq", "tensor", None),
        check_vma=False,
    )
```

```python
import functools

import jax
import jax.numpy as jnp
import numpy as np
from jax import lax
from jax.experimental import pallas as pl
from jax.experimental.pallas import tpu as pltpu
from jax.sharding import PartitionSpec as P

HEAD = 112
WINDOW = 64
EPS = 1e-05
SLOT = 128
FEAT_SLOT = 256
HALO = 80
NEAR = 4
VMEM = 60 * 1024 * 1024
F32 = jnp.float32
BF16 = jnp.bfloat16


def dot(a, b, dims=((1,), (0,))):
    return lax.dot_general(a, b, (dims, ((), ())), preferred_element_type=F32)


def normed_rows(rows, gain):
    scale = lax.rsqrt(jnp.mean(rows * rows, axis=-1, keepdims=True) + EPS)
    return (rows * scale * gain).astype(BF16)


def feature_tables(heads, feature_dim):
    pairs = [(i, j) for i in range(feature_dim) for j in range(i, feature_dim)]
    pairs += [(i, -1) for i in range(feature_dim)] + [(-1, -1)]
    first = np.zeros((2 * heads * feature_dim, heads * FEAT_SLOT), np.float32)
    second = np.zeros_like(first)
    ones = np.zeros((2, heads * FEAT_SLOT), np.float32)
    scale = np.zeros((1, heads * FEAT_SLOT), np.float32)
    for h in range(heads):
        for n, (i, j) in enumerate(pairs):
            at = h * FEAT_SLOT + n
            if i >= 0:
                first[2 * h * feature_dim + i, at] = 1
            else:
                ones[0, at] = 1
            if j >= 0:
                second[2 * h * feature_dim + j, at] = 1
            else:
                ones[1, at] = 1
            if i < 0:
                scale[0, at] = 1
            elif j < 0:
                scale[0, at] = feature_dim**-0.5
            else:
                scale[0, at] = (0.5 if i == j else 1.0) / feature_dim
    return first, second, ones, scale, -(-len(pairs) // 16) * 16


def features(rows, first, second, ones):
    return (dot(rows, first) + ones[0:1]) * (dot(rows, second) + ones[1:2])


def run_copies(copies_of, groups, meanwhile=None):
    step = pl.program_id(0)

    @pl.when(step == 0)
    def _():
        for group in range(groups):
            for copy in copies_of(group):
                copy.start()
        if meanwhile is not None:
            meanwhile()

    for group in range(groups):

        @pl.when(step == group)
        def _(group=group):
            for copy in copies_of(group):
                copy.wait()


def weight_copies(place_ref, near_ref, far_ref, targets, sems, group):
    near = near_ref.shape[0]
    cols = near_ref.shape[3]
    found = []
    for n in range(2 * near):
        at = 0
        for own_ref, kind, rows, w_ref, off in targets:
            if group == 0:
                part, head = n // near, n % near
                src = own_ref.at[
                    kind, head * rows : (head + 1) * rows, part * cols : (part + 1) * cols
                ]
            else:
                part, head = place_ref[near], place_ref[n % near]
                if n >= near:
                    part = 1 - part
                src = (near_ref if n < near else far_ref).at[
                    n % near, group - 1, at : at + rows, :
                ]
            dst = w_ref.at[group, part, head, off : off + rows, :]
            found.append(pltpu.make_async_copy(src, dst, sems.at[group, len(found)]))
            at += rows
    return found


def zero_between_heads(w_ref):
    groups, parts, heads, rows, cols = w_ref.shape
    for at in range(HEAD, rows, SLOT):
        w_ref[:, :, :, at : at + SLOT - HEAD, :] = jnp.zeros(
            (groups, parts, heads, SLOT - HEAD, cols), BF16
        )


def group_weights(w_ref, step, part):
    heads, rows, cols = w_ref.shape[2:]
    return w_ref[step, part].reshape(heads * rows, cols)


def project(rows_ref, w_ref, step):
    parts, cols = w_ref.shape[1], w_ref.shape[4]
    total = None
    for part in range(parts):
        rows = rows_ref[:, part * cols : (part + 1) * cols]
        share = dot(rows, group_weights(w_ref, step, part), ((1,), (1,)))
        total = share if total is None else total + share
    return total


def linear_kernel(
    heads,
    feature_dim,
    kept,
    place_ref,
    x_ref,
    gain_ref,
    value_ref,
    featmap_ref,
    near_ref,
    far_ref,
    first_ref,
    second_ref,
    ones_ref,
    column_ref,
    num_ref,
    q_ref,
    state_ref,
    normed_ref,
    value_w_ref,
    feat_w_ref,
    sems,
):
    step = pl.program_id(0)
    targets = [
        (value_ref, 0, HEAD, value_w_ref, 0),
        (featmap_ref, 0, feature_dim, feat_w_ref, 0),
        (featmap_ref, 1, feature_dim, feat_w_ref, feature_dim),
    ]

    @pl.when(step == 0)
    def _():
        zero_between_heads(value_w_ref)

    run_copies(
        functools.partial(weight_copies, place_ref, near_ref, far_ref, targets, sems),
        value_w_ref.shape[0],
        lambda: normed_ref.__setitem__(
            ..., normed_rows(x_ref[...].astype(F32), gain_ref[...])
        ),
    )
    rows = x_ref.shape[0]
    width = 2 * heads * feature_dim
    queries = project(normed_ref, feat_w_ref, step).astype(BF16)
    keys = pltpu.roll(queries.astype(F32), width - feature_dim, 1).astype(BF16)
    values = (project(normed_ref, value_w_ref, step) + column_ref[...]).astype(BF16)
    q_ref[0] = queries
    lane = lax.broadcasted_iota(jnp.int32, (rows, width), 1)
    causal = lax.broadcasted_iota(jnp.int32, (rows, rows), 1) <= lax.broadcasted_iota(
        jnp.int32, (rows, rows), 0
    )
    key_features = features(keys, first_ref[...], second_ref[...], ones_ref[...]).astype(BF16)
    for h in range(heads):
        at = 2 * h * feature_dim
        own = jnp.where((lane >= at) & (lane < at + feature_dim), queries, jnp.zeros_like(queries))
        scores = dot(own, keys, ((1,), (1,))) * feature_dim**-0.5
        kernel = jnp.where(causal, 1.0 + scores + 0.5 * scores * scores, 0.0).astype(BF16)
        value = values[:, h * SLOT : (h + 1) * SLOT]
        num_ref[0, :, h * SLOT : (h + 1) * SLOT] = dot(kernel, value)
        state = dot(key_features[:, h * FEAT_SLOT : h * FEAT_SLOT + kept], value, ((0,), (0,)))
        state_ref[0, h * kept : (h + 1) * kept, :] = state.astype(BF16)


def add_branch(mixed, w_ref, total_ref):
    step = pl.program_id(0)
    parts, cols = w_ref.shape[1], w_ref.shape[4]
    for part in range(parts):
        share = dot(mixed, group_weights(w_ref, step, part)).astype(BF16).astype(F32)
        total_ref[:, part * cols : (part + 1) * cols] += share


def out_one_kernel(
    heads,
    kept,
    priors,
    *refs,
):
    place_ref, num_ref, q_ref, first_ref, second_ref, ones_ref, scale_ref = refs[:7]
    prior_refs = refs[7 : 7 + priors]
    own_ref, near_ref, far_ref, x_ref, gain_ref = refs[7 + priors : 12 + priors]
    residual_ref, normed_ref, total_ref, mixed_ref, w_ref, sems = refs[12 + priors :]
    step = pl.program_id(0)

    @pl.when(step == 0)
    def _():
        total_ref[...] = jnp.zeros_like(total_ref)
        zero_between_heads(w_ref)

    run_copies(
        functools.partial(
            weight_copies, place_ref, near_ref, far_ref, [(own_ref, 0, HEAD, w_ref, 0)], sems
        ),
        w_ref.shape[0],
    )

    query_features = features(q_ref[0], first_ref[...], second_ref[...], ones_ref[...])
    query_features = (query_features * scale_ref[...]).astype(BF16)
    for h in range(heads):
        at = slice(h * kept, (h + 1) * kept)
        prior = prior_refs[0][0, at, :].astype(F32)
        for ref in prior_refs[1:]:
            prior = prior + ref[0, at, :].astype(F32)
        lanes = slice(h * SLOT, (h + 1) * SLOT)
        total = num_ref[0, :, lanes] + dot(
            query_features[:, h * FEAT_SLOT : h * FEAT_SLOT + kept], prior.astype(BF16)
        )
        mixed_ref[:, lanes] = (total / total[:, HEAD : HEAD + 1]).astype(BF16)
    add_branch(mixed_ref[...], w_ref, total_ref)

    @pl.when(step == pl.num_programs(0) - 1)
    def _():
        residual = (x_ref[...].astype(F32) + total_ref[...]).astype(BF16)
        residual_ref[...] = residual
        normed_ref[...] = normed_rows(residual.astype(F32), gain_ref[...])


def window_kernel(
    heads,
    place_ref,
    first_ref,
    x_ref,
    halo_ref,
    own_ref,
    near_ref,
    far_ref,
    tap_ref,
    mixed_ref,
    rows_ref,
    w_ref,
    sems,
):
    step = pl.program_id(0)
    targets = [(own_ref, kind, HEAD, w_ref, kind * SLOT) for kind in range(3)]

    def place_rows():
        rows_ref[:HALO] = halo_ref[...]
        rows_ref[HALO:] = x_ref[...]

    @pl.when(step == 0)
    def _():
        zero_between_heads(w_ref)

    run_copies(
        functools.partial(weight_copies, place_ref, near_ref, far_ref, targets, sems),
        w_ref.shape[0],
        place_rows,
    )
    rows = x_ref.shape[0]
    lead = HALO - WINDOW
    projected = project(rows_ref, w_ref, step)
    taps = tap_ref[0]
    convolved = taps[0:1] * projected
    for offset in range(1, taps.shape[0]):
        convolved = convolved + taps[offset : offset + 1] * pltpu.roll(projected, offset, 0)
    convolved = convolved[lead:].astype(BF16)
    tile = 128
    span = tile + WINDOW
    row = lax.broadcasted_iota(jnp.int32, (tile, span), 0)
    col = lax.broadcasted_iota(jnp.int32, (tile, span), 1)
    band = (col > row) & (col <= row + WINDOW)
    for h in range(heads):
        at = 3 * h * SLOT
        queries = convolved[WINDOW:, at : at + SLOT]
        keys = convolved[:, at + SLOT : at + 2 * SLOT]
        values = convolved[:, at + 2 * SLOT : at + 3 * SLOT]
        for start in range(0, rows, tile):
            logits = dot(queries[start : start + tile], keys[start : start + span], ((1,), (1,)))
            allowed = band
            if start < WINDOW:
                allowed = band & (col >= WINDOW - start - first_ref[0])
            logits = jnp.where(allowed, logits * HEAD**-0.5, -jnp.inf)
            weights = jnp.exp(logits - jnp.max(logits, axis=1, keepdims=True))
            weights = weights / jnp.sum(weights, axis=1, keepdims=True)
            mixed = dot(weights.astype(BF16), values[start : start + span])
            mixed_ref[0, start : start + tile, h * SLOT : (h + 1) * SLOT] = mixed.astype(BF16)


def out_two_kernel(
    place_ref,
    live_ref,
    mixed_ref,
    own_ref,
    near_ref,
    far_ref,
    residual_ref,
    out_ref,
    total_ref,
    w_ref,
    sems,
):
    step = pl.program_id(0)

    @pl.when(step == 0)
    def _():
        total_ref[...] = jnp.zeros_like(total_ref)
        zero_between_heads(w_ref)

    run_copies(
        functools.partial(
            weight_copies, place_ref, near_ref, far_ref, [(own_ref, 0, HEAD, w_ref, 0)], sems
        ),
        w_ref.shape[0],
    )
    add_branch(mixed_ref[0], w_ref, total_ref)

    @pl.when(step == pl.num_programs(0) - 1)
    def _():
        result = (residual_ref[...].astype(F32) + total_ref[...]).astype(BF16)
        row = lax.broadcasted_iota(jnp.int32, result.shape, 0)
        out_ref[...] = jnp.where(row < live_ref[0], result, jnp.zeros_like(result))


def whole(shape):
    return pl.BlockSpec(shape, lambda g: (0,) * len(shape))


def each(shape):
    return pl.BlockSpec((1,) + shape, lambda g: (g,) + (0,) * len(shape))


SMEM = pl.BlockSpec(memory_space=pltpu.SMEM)
HBM = pl.BlockSpec(memory_space=pl.ANY)


def call(kernel, groups, in_specs, out_specs, out_shape, scratch, flops, moved, name):
    return pl.pallas_call(
        kernel,
        grid=(groups,),
        in_specs=in_specs,
        out_specs=out_specs,
        out_shape=out_shape,
        scratch_shapes=scratch,
        compiler_params=pltpu.CompilerParams(
            dimension_semantics=("arbitrary",), vmem_limit_bytes=VMEM
        ),
        cost_estimate=pl.CostEstimate(flops=flops, bytes_accessed=moved, transcendentals=0),
        name=name,
    )


def own_piece(whole_weights):
    head, part = lax.axis_index("seq") % NEAR, lax.axis_index("dp")
    found = []
    for weights in whole_weights:
        kinds, rows, cols = weights.shape
        rows, cols = rows // NEAR, cols // lax.axis_size("dp")
        piece = lax.dynamic_slice(weights, (0, head * rows, part * cols), (kinds, rows, cols))
        found.append(piece.reshape(kinds * rows, cols))
    return jnp.concatenate(found, axis=0)


def from_other_groups(piece, after):
    groups, mine = lax.axis_size("tensor"), lax.axis_index("tensor")
    order = (mine + 1 + after + jnp.arange(groups - 1)) % groups
    held = lax.all_gather(piece, "tensor").at[order].get(mode="promise_in_bounds")

    def across(array, bit):
        return lax.ppermute(array, "seq", [(i, i ^ bit) for i in range(lax.axis_size("seq"))])

    half = -(-piece.shape[0] // 32) * 16
    beside, above = across(held, 1), across(held, 2)
    opposite = jnp.concatenate([across(above[:, :half], 1), across(beside[:, half:], 2)], axis=1)
    near = jnp.stack([held, beside, above, opposite])
    return near, lax.ppermute(near, "dp", [(0, 1), (1, 0)])


def nothing_of(array):
    return (array.reshape(-1)[0].astype(F32) * 0.0).astype(jnp.int32)


def earlier_blocks(state, axis):
    peers = lax.axis_size(axis)
    if peers <= 4:
        return [
            lax.ppermute(state, axis, [(i, i + by) for i in range(peers - by)])
            for by in range(1, peers)
        ]
    everything = lax.all_gather(state, axis).astype(F32)
    reached = jnp.arange(peers) < lax.axis_index(axis)
    return [jnp.sum(jnp.where(reached[:, None, None, None], everything, 0.0), axis=0)]


def on_device(
    pool,
    page_table,
    reassign,
    lengths,
    gain_one,
    w_featmap,
    w_value,
    w_out_one,
    gain_two,
    w_window,
    conv_window,
    w_out_two,
):
    dp_count, seq_count, group_count = (lax.axis_size(n) for n in ("dp", "seq", "tensor"))
    groups = dp_count * seq_count
    device_place = lax.axis_index(("dp", "seq"))
    dp_place, seq_place, tensor_place = (lax.axis_index(n) for n in ("dp", "seq", "tensor"))
    pages_dev, page_share, width = pool.shape
    slots_total, pages_total = page_table.shape
    req_dev = slots_total // dp_count
    page_span = pages_total // seq_count
    page_rows = page_share * group_count
    rows = page_span * page_rows
    assert req_dev == group_count
    heads = w_value.shape[1] // HEAD
    head_cols = heads * HEAD
    feat_cols = w_featmap.shape[2]
    feature_dim = feat_cols // heads
    tap_count = conv_window.shape[0]

    placed = reassign[:, None] == jnp.arange(slots_total, dtype=jnp.int32)[None, :]
    table = jnp.sum(jnp.where(placed[:, :, None], page_table[None], 0), axis=1)
    slot_lengths = jnp.sum(jnp.where(placed, lengths[None, :], 0), axis=1)
    source_page = (
        table.reshape(dp_count, req_dev, seq_count, page_span)
        .transpose(0, 2, 1, 3)
        .reshape(groups, req_dev * page_span)
    )
    capacity = (pages_dev + groups - 1) // groups
    page_owner = source_page // pages_dev
    pool_slot = source_page % pages_dev
    before = jnp.arange(pages_dev)[None, :] < jnp.arange(pages_dev)[:, None]
    pair_rank = jnp.sum((page_owner[:, :, None] == page_owner[:, None, :]) & before[None], axis=2)
    send_hit = (page_owner == device_place)[:, None, :] & (
        pair_rank[:, None, :] == jnp.arange(capacity)[None, :, None]
    )
    send_slot = jnp.sum(jnp.where(send_hit, pool_slot[:, None, :], 0), axis=2)
    outgoing = pool.at[send_slot.reshape(-1)].get(mode="promise_in_bounds")
    outgoing = outgoing.reshape(groups, capacity, page_share, width)
    arrived = lax.all_to_all(outgoing, ("dp", "seq"), split_axis=0, concat_axis=0, tiled=True)
    own_row = jnp.arange(groups)[:, None] == device_place
    pick_rows = jnp.sum(jnp.where(own_row, page_owner * capacity + pair_rank, 0), axis=0)
    picked = arrived.reshape(groups * capacity, page_share, width)
    picked = picked.at[pick_rows].get(mode="promise_in_bounds")

    picked = picked.reshape(req_dev, page_span, page_share, width)
    swapped = lax.all_to_all(picked, "tensor", split_axis=0, concat_axis=0, tiled=True)
    tokens = swapped.transpose(1, 0, 2, 3).reshape(rows, width)
    slot = dp_place * req_dev + tensor_place
    length = jnp.sum(jnp.where(jnp.arange(slots_total) == slot, slot_lengths, 0))

    assert heads == NEAR and dp_count == 2
    values_t = w_value.T[None]
    featmap_t = w_featmap.transpose(1, 2, 0)
    window_t = w_window.transpose(1, 2, 0)
    out_one, out_two = w_out_one[None], w_out_two[None]
    near_one = from_other_groups(own_piece([values_t, featmap_t]), 0)
    near_out_one = from_other_groups(own_piece([out_one]), 0)
    near_window = from_other_groups(own_piece([window_t]), nothing_of(picked))
    near_out_two = from_other_groups(own_piece([out_two]), nothing_of(swapped))
    places = jnp.concatenate([(seq_place % NEAR) ^ jnp.arange(NEAR), dp_place[None]])
    places = places.astype(jnp.int32)
    group_order = (tensor_place + jnp.arange(group_count)) % group_count
    taps = conv_window.reshape(tap_count, 3, heads, HEAD).transpose(0, 2, 1, 3)
    taps = jnp.pad(taps, ((0, 0), (0, 0), (0, 0), (0, SLOT - HEAD)))
    taps = lax.all_gather(taps.reshape(tap_count, 3 * heads * SLOT), "tensor")
    taps = taps.at[group_order].get(mode="promise_in_bounds")

    first, second, ones, scale, kept = feature_tables(heads, feature_dim)
    first, second = jnp.asarray(first, BF16), jnp.asarray(second, BF16)
    column = np.zeros((1, heads * SLOT), np.float32)
    column[0, HEAD::SLOT] = 1
    one_cols = 2 * feat_cols + head_cols

    def copy_sems(kinds):
        return pltpu.SemaphoreType.DMA((group_count, dp_count * NEAR * kinds))

    def weights_of(rows_of_head):
        return pltpu.VMEM((group_count, dp_count, heads, rows_of_head, width // dp_count), BF16)

    slots = heads * SLOT
    num, queries, state = call(
        functools.partial(linear_kernel, heads, feature_dim, kept),
        group_count,
        [
            SMEM,
            whole((rows, width)),
            whole((1, width)),
            *[HBM] * 4,
            whole(first.shape),
            whole(second.shape),
            whole(ones.shape),
            whole(column.shape),
        ],
        [each((rows, slots)), each((rows, 2 * feat_cols)), each((heads * kept, SLOT))],
        [
            jax.ShapeDtypeStruct((group_count, rows, slots), F32),
            jax.ShapeDtypeStruct((group_count, rows, 2 * feat_cols), BF16),
            jax.ShapeDtypeStruct((group_count, heads * kept, SLOT), BF16),
        ],
        [
            pltpu.VMEM((rows, width), BF16),
            weights_of(SLOT),
            weights_of(2 * feature_dim),
            copy_sems(3),
        ],
        3 * group_count * rows * width * one_cols,
        group_count * width * one_cols * 2,
        "linear_rows",
    )(
        places, tokens, gain_one[None], values_t, featmap_t, *near_one, first, second, ones, column
    )
    priors = earlier_blocks(state, "seq")
    residual, normed_two = call(
        functools.partial(out_one_kernel, heads, kept, len(priors)),
        group_count,
        [
            SMEM,
            each((rows, slots)),
            each((rows, 2 * feat_cols)),
            whole(first.shape),
            whole(second.shape),
            whole(ones.shape),
            whole(scale.shape),
        ]
        + [each((heads * kept, SLOT))] * len(priors)
        + [HBM] * 3
        + [
            whole((rows, width)),
            whole((1, width)),
        ],
        [whole((rows, width)), whole((rows, width))],
        [jax.ShapeDtypeStruct((rows, width), BF16)] * 2,
        [
            pltpu.VMEM((rows, width), F32),
            pltpu.VMEM((rows, slots), BF16),
            weights_of(SLOT),
            copy_sems(1),
        ],
        3 * group_count * rows * width * head_cols,
        group_count * width * head_cols * 2,
        "linear_out",
    )(
        places, num, queries, first, second, ones, scale, *priors, out_one, *near_out_one, tokens,
        gain_two[None],
    )

    halo = lax.ppermute(
        normed_two[rows - HALO :], "seq", [(i, i + 1) for i in range(seq_count - 1)]
    )
    block_start = (seq_place * rows).astype(jnp.int32)[None]
    mixed_two = call(
        functools.partial(window_kernel, heads),
        group_count,
        [
            SMEM,
            SMEM,
            whole((rows, width)),
            whole((HALO, width)),
            *[HBM] * 3,
            each((tap_count, 3 * slots)),
        ],
        each((rows, slots)),
        jax.ShapeDtypeStruct((group_count, rows, slots), BF16),
        [
            pltpu.VMEM((HALO + rows, width), BF16),
            weights_of(3 * SLOT),
            copy_sems(3),
        ],
        3 * group_count * rows * width * 3 * head_cols,
        group_count * width * 3 * head_cols * 2,
        "window_rows",
    )(places, block_start, normed_two, halo, window_t, *near_window, taps)
    live = (length - seq_place * rows).astype(jnp.int32)[None]
    result = call(
        out_two_kernel,
        group_count,
        [
            SMEM,
            SMEM,
            each((rows, slots)),
            *[HBM] * 3,
            whole((rows, width)),
        ],
        whole((rows, width)),
        jax.ShapeDtypeStruct((rows, width), BF16),
        [
            pltpu.VMEM((rows, width), F32),
            weights_of(SLOT),
            copy_sems(1),
        ],
        2 * group_count * rows * width * head_cols,
        group_count * width * head_cols * 2,
        "window_out",
    )(places, live, mixed_two, out_two, *near_out_two, residual)

    result = result.reshape(page_span, group_count, page_share, width).transpose(1, 0, 2, 3)
    return lax.all_to_all(result, "tensor", split_axis=0, concat_axis=0, tiled=True)


def solution(mesh):
    return jax.shard_map(
        on_device,
        mesh=mesh,
        in_specs=(
            P(("dp", "seq"), "tensor", None),
            P(),
            P(),
            P(),
            P(),
            P(None, None, "tensor"),
            P(None, "tensor"),
            P("tensor", None),
            P(),
            P(None, None, "tensor"),
            P(None, None, "tensor"),
            P("tensor", None),
        ),
        out_specs=P("dp", "seq", "tensor", None),
        check_vma=False,
    )
```

```python
import functools

import jax
import jax.numpy as jnp
import numpy as np
from jax import lax
from jax.experimental import pallas as pl
from jax.experimental.pallas import tpu as pltpu
from jax.sharding import PartitionSpec as P

HEAD = 112
WINDOW = 64
EPS = 1e-05
SLOT = 128
FEAT_SLOT = 256
HALO = 80
NEAR = 4
VMEM = 60 * 1024 * 1024
F32 = jnp.float32
BF16 = jnp.bfloat16


def dot(a, b, dims=((1,), (0,))):
    return lax.dot_general(a, b, (dims, ((), ())), preferred_element_type=F32)


def normed_rows(rows, gain):
    scale = lax.rsqrt(jnp.mean(rows * rows, axis=-1, keepdims=True) + EPS)
    return (rows * scale * gain).astype(BF16)


def feature_tables(heads, feature_dim):
    pairs = [(i, j) for i in range(feature_dim) for j in range(i, feature_dim)]
    pairs += [(i, -1) for i in range(feature_dim)] + [(-1, -1)]
    first = np.zeros((2 * heads * feature_dim, heads * FEAT_SLOT), np.float32)
    second = np.zeros_like(first)
    ones = np.zeros((2, heads * FEAT_SLOT), np.float32)
    scale = np.zeros((1, heads * FEAT_SLOT), np.float32)
    for h in range(heads):
        for n, (i, j) in enumerate(pairs):
            at = h * FEAT_SLOT + n
            if i >= 0:
                first[2 * h * feature_dim + i, at] = 1
            else:
                ones[0, at] = 1
            if j >= 0:
                second[2 * h * feature_dim + j, at] = 1
            else:
                ones[1, at] = 1
            if i < 0:
                scale[0, at] = 1
            elif j < 0:
                scale[0, at] = feature_dim**-0.5
            else:
                scale[0, at] = (0.5 if i == j else 1.0) / feature_dim
    return first, second, ones, scale, -(-len(pairs) // 16) * 16


def features(rows, first, second, ones):
    return (dot(rows, first) + ones[0:1]) * (dot(rows, second) + ones[1:2])


def run_copies(copies_of, groups, meanwhile=None):
    step = pl.program_id(0)

    @pl.when(step == 0)
    def _():
        for group in range(groups):
            for copy in copies_of(group):
                copy.start()
        if meanwhile is not None:
            meanwhile()

    for group in range(groups):

        @pl.when(step == group)
        def _(group=group):
            for copy in copies_of(group):
                copy.wait()


def weight_copies(place_ref, near_ref, far_ref, targets, sems, group):
    near = near_ref.shape[0]
    cols = near_ref.shape[3]
    found = []
    for n in range(2 * near):
        at = 0
        for own_ref, kind, rows, w_ref, off in targets:
            if group == 0:
                part, head = n // near, n % near
                src = own_ref.at[
                    kind, head * rows : (head + 1) * rows, part * cols : (part + 1) * cols
                ]
            else:
                part, head = place_ref[near], place_ref[n % near]
                if n >= near:
                    part = 1 - part
                src = (near_ref if n < near else far_ref).at[
                    n % near, group - 1, at : at + rows, :
                ]
            dst = w_ref.at[group, part, head, off : off + rows, :]
            found.append(pltpu.make_async_copy(src, dst, sems.at[group, len(found)]))
            at += rows
    return found


def zero_between_heads(w_ref):
    groups, parts, heads, rows, cols = w_ref.shape
    for at in range(HEAD, rows, SLOT):
        w_ref[:, :, :, at : at + SLOT - HEAD, :] = jnp.zeros(
            (groups, parts, heads, SLOT - HEAD, cols), BF16
        )


def group_weights(w_ref, step, part):
    heads, rows, cols = w_ref.shape[2:]
    return w_ref[step, part].reshape(heads * rows, cols)


def project(rows_ref, w_ref, step):
    parts, cols = w_ref.shape[1], w_ref.shape[4]
    total = None
    for part in range(parts):
        rows = rows_ref[:, part * cols : (part + 1) * cols]
        share = dot(rows, group_weights(w_ref, step, part), ((1,), (1,)))
        total = share if total is None else total + share
    return total


def linear_kernel(
    heads,
    feature_dim,
    kept,
    place_ref,
    x_ref,
    gain_ref,
    value_ref,
    featmap_ref,
    near_ref,
    far_ref,
    first_ref,
    second_ref,
    ones_ref,
    column_ref,
    num_ref,
    q_ref,
    state_ref,
    normed_ref,
    value_w_ref,
    feat_w_ref,
    sems,
):
    step = pl.program_id(0)
    targets = [
        (value_ref, 0, HEAD, value_w_ref, 0),
        (featmap_ref, 0, feature_dim, feat_w_ref, 0),
        (featmap_ref, 1, feature_dim, feat_w_ref, feature_dim),
    ]

    @pl.when(step == 0)
    def _():
        zero_between_heads(value_w_ref)

    run_copies(
        functools.partial(weight_copies, place_ref, near_ref, far_ref, targets, sems),
        value_w_ref.shape[0],
        lambda: normed_ref.__setitem__(
            ..., normed_rows(x_ref[...].astype(F32), gain_ref[...])
        ),
    )
    rows = x_ref.shape[0]
    width = 2 * heads * feature_dim
    queries = project(normed_ref, feat_w_ref, step).astype(BF16)
    keys = pltpu.roll(queries.astype(F32), width - feature_dim, 1).astype(BF16)
    values = (project(normed_ref, value_w_ref, step) + column_ref[...]).astype(BF16)
    q_ref[0] = queries
    lane = lax.broadcasted_iota(jnp.int32, (rows, width), 1)
    causal = lax.broadcasted_iota(jnp.int32, (rows, rows), 1) <= lax.broadcasted_iota(
        jnp.int32, (rows, rows), 0
    )
    key_features = features(keys, first_ref[...], second_ref[...], ones_ref[...]).astype(BF16)
    for h in range(heads):
        at = 2 * h * feature_dim
        own = jnp.where((lane >= at) & (lane < at + feature_dim), queries, jnp.zeros_like(queries))
        scores = dot(own, keys, ((1,), (1,))) * feature_dim**-0.5
        kernel = jnp.where(causal, 1.0 + scores + 0.5 * scores * scores, 0.0).astype(BF16)
        value = values[:, h * SLOT : (h + 1) * SLOT]
        num_ref[0, :, h * SLOT : (h + 1) * SLOT] = dot(kernel, value)
        state = dot(key_features[:, h * FEAT_SLOT : h * FEAT_SLOT + kept], value, ((0,), (0,)))
        state_ref[0, h * kept : (h + 1) * kept, :] = state.astype(BF16)


def add_branch(mixed, w_ref, total_ref):
    step = pl.program_id(0)
    parts, cols = w_ref.shape[1], w_ref.shape[4]
    for part in range(parts):
        share = dot(mixed, group_weights(w_ref, step, part)).astype(BF16).astype(F32)
        total_ref[:, part * cols : (part + 1) * cols] += share


def out_one_kernel(
    heads,
    kept,
    priors,
    *refs,
):
    place_ref, num_ref, q_ref, first_ref, second_ref, ones_ref, scale_ref = refs[:7]
    prior_refs = refs[7 : 7 + priors]
    own_ref, near_ref, far_ref, x_ref, gain_ref = refs[7 + priors : 12 + priors]
    residual_ref, normed_ref, total_ref, mixed_ref, w_ref, sems = refs[12 + priors :]
    step = pl.program_id(0)

    @pl.when(step == 0)
    def _():
        total_ref[...] = jnp.zeros_like(total_ref)
        zero_between_heads(w_ref)

    run_copies(
        functools.partial(
            weight_copies, place_ref, near_ref, far_ref, [(own_ref, 0, HEAD, w_ref, 0)], sems
        ),
        w_ref.shape[0],
    )

    query_features = features(q_ref[0], first_ref[...], second_ref[...], ones_ref[...])
    query_features = (query_features * scale_ref[...]).astype(BF16)
    for h in range(heads):
        at = slice(h * kept, (h + 1) * kept)
        prior = prior_refs[0][0, at, :].astype(F32)
        for ref in prior_refs[1:]:
            prior = prior + ref[0, at, :].astype(F32)
        lanes = slice(h * SLOT, (h + 1) * SLOT)
        total = num_ref[0, :, lanes] + dot(
            query_features[:, h * FEAT_SLOT : h * FEAT_SLOT + kept], prior.astype(BF16)
        )
        mixed_ref[:, lanes] = (total / total[:, HEAD : HEAD + 1]).astype(BF16)
    add_branch(mixed_ref[...], w_ref, total_ref)

    @pl.when(step == pl.num_programs(0) - 1)
    def _():
        residual = (x_ref[...].astype(F32) + total_ref[...]).astype(BF16)
        residual_ref[...] = residual
        normed_ref[...] = normed_rows(residual.astype(F32), gain_ref[...])


def window_kernel(
    heads,
    place_ref,
    first_ref,
    low_ref,
    high_ref,
    halo_ref,
    own_ref,
    near_ref,
    far_ref,
    tap_ref,
    mixed_ref,
    rows_ref,
    w_ref,
    sems,
):
    step = pl.program_id(0)
    targets = [(own_ref, kind, HEAD, w_ref, kind * SLOT) for kind in range(3)]

    mid = low_ref.shape[0]

    def place_rows():
        rows_ref[:HALO] = halo_ref[...]
        rows_ref[HALO : HALO + mid] = low_ref[...]
        rows_ref[HALO + mid :] = high_ref[...]

    @pl.when(step == 0)
    def _():
        zero_between_heads(w_ref)

    run_copies(
        functools.partial(weight_copies, place_ref, near_ref, far_ref, targets, sems),
        w_ref.shape[0],
        place_rows,
    )
    rows = 2 * mid
    lead = HALO - WINDOW
    projected = project(rows_ref, w_ref, step)
    taps = tap_ref[0]
    convolved = taps[0:1] * projected
    for offset in range(1, taps.shape[0]):
        convolved = convolved + taps[offset : offset + 1] * pltpu.roll(projected, offset, 0)
    convolved = convolved[lead:].astype(BF16)
    tile = 128
    span = tile + WINDOW
    row = lax.broadcasted_iota(jnp.int32, (tile, span), 0)
    col = lax.broadcasted_iota(jnp.int32, (tile, span), 1)
    band = (col > row) & (col <= row + WINDOW)
    for h in range(heads):
        at = 3 * h * SLOT
        queries = convolved[WINDOW:, at : at + SLOT]
        keys = convolved[:, at + SLOT : at + 2 * SLOT]
        values = convolved[:, at + 2 * SLOT : at + 3 * SLOT]
        for start in range(0, rows, tile):
            logits = dot(queries[start : start + tile], keys[start : start + span], ((1,), (1,)))
            allowed = band
            if start < WINDOW:
                allowed = band & (col >= WINDOW - start - first_ref[0])
            logits = jnp.where(allowed, logits * HEAD**-0.5, -jnp.inf)
            weights = jnp.exp(logits - jnp.max(logits, axis=1, keepdims=True))
            weights = weights / jnp.sum(weights, axis=1, keepdims=True)
            mixed = dot(weights.astype(BF16), values[start : start + span])
            mixed_ref[0, start : start + tile, h * SLOT : (h + 1) * SLOT] = mixed.astype(BF16)


def out_two_kernel(
    place_ref,
    live_ref,
    mixed_ref,
    pair_ref,
    own_ref,
    near_ref,
    far_ref,
    residual_ref,
    out_ref,
    total_ref,
    w_ref,
    sems,
):
    step = pl.program_id(0)

    @pl.when(step == 0)
    def _():
        total_ref[...] = jnp.zeros_like(total_ref)
        zero_between_heads(w_ref)

    run_copies(
        functools.partial(
            weight_copies, place_ref, near_ref, far_ref, [(own_ref, 0, HEAD, w_ref, 0)], sems
        ),
        w_ref.shape[0],
    )
    mixed = jnp.where(step < 2, mixed_ref[step % 2], pair_ref[step % 2])
    add_branch(mixed, w_ref, total_ref)

    @pl.when(step == pl.num_programs(0) - 1)
    def _():
        result = (residual_ref[...].astype(F32) + total_ref[...]).astype(BF16)
        row = lax.broadcasted_iota(jnp.int32, result.shape, 0)
        out_ref[...] = jnp.where(row < live_ref[0], result, jnp.zeros_like(result))


def whole(shape):
    return pl.BlockSpec(shape, lambda g: (0,) * len(shape))


def each(shape):
    return pl.BlockSpec((1,) + shape, lambda g: (g,) + (0,) * len(shape))


SMEM = pl.BlockSpec(memory_space=pltpu.SMEM)
HBM = pl.BlockSpec(memory_space=pl.ANY)


def call(kernel, groups, in_specs, out_specs, out_shape, scratch, flops, moved, name):
    return pl.pallas_call(
        kernel,
        grid=(groups,),
        in_specs=in_specs,
        out_specs=out_specs,
        out_shape=out_shape,
        scratch_shapes=scratch,
        compiler_params=pltpu.CompilerParams(
            dimension_semantics=("arbitrary",), vmem_limit_bytes=VMEM
        ),
        cost_estimate=pl.CostEstimate(flops=flops, bytes_accessed=moved, transcendentals=0),
        name=name,
    )


def own_piece(whole_weights):
    head, part = lax.axis_index("seq") % NEAR, lax.axis_index("dp")
    found = []
    for weights in whole_weights:
        kinds, rows, cols = weights.shape
        rows, cols = rows // NEAR, cols // lax.axis_size("dp")
        piece = lax.dynamic_slice(weights, (0, head * rows, part * cols), (kinds, rows, cols))
        found.append(piece.reshape(kinds * rows, cols))
    return jnp.concatenate(found, axis=0)


def across(array, axis, bit):
    return lax.ppermute(array, axis, [(i, i ^ bit) for i in range(lax.axis_size(axis))])


def after(array, others):
    if not others:
        return array
    zero = sum(other.reshape(-1)[0].astype(F32) * 0.0 for other in others)
    return jnp.where(zero == 0.0, array, jnp.zeros_like(array))


def from_groups(piece, offsets, over_z):
    piece = after(piece, over_z)
    return jnp.stack([across(piece, "tensor", offset) for offset in offsets])


def from_plane(held, over_xy, diagonal, over_cores):
    held = after(held, over_xy)
    half = -(-held.shape[1] // 32) * 16
    beside, above = across(held, "seq", 1), across(held, "seq", 2)
    opposite = jnp.concatenate(
        [
            across(after(above[:, :half], diagonal), "seq", 1),
            across(after(beside[:, half:], diagonal), "seq", 2),
        ],
        axis=1,
    )
    near = after(jnp.stack([held, beside, above, opposite]), over_cores)
    return near, across(near, "dp", 1)


def earlier_blocks(state, axis):
    peers = lax.axis_size(axis)
    if peers <= 4:
        return [
            lax.ppermute(state, axis, [(i, i + by) for i in range(peers - by)])
            for by in range(1, peers)
        ]
    everything = lax.all_gather(state, axis).astype(F32)
    reached = jnp.arange(peers) < lax.axis_index(axis)
    return [jnp.sum(jnp.where(reached[:, None, None, None], everything, 0.0), axis=0)]


def on_device(
    pool,
    page_table,
    reassign,
    lengths,
    gain_one,
    w_featmap,
    w_value,
    w_out_one,
    gain_two,
    w_window,
    conv_window,
    w_out_two,
):
    dp_count, seq_count, group_count = (lax.axis_size(n) for n in ("dp", "seq", "tensor"))
    groups = dp_count * seq_count
    device_place = lax.axis_index(("dp", "seq"))
    dp_place, seq_place, tensor_place = (lax.axis_index(n) for n in ("dp", "seq", "tensor"))
    pages_dev, page_share, width = pool.shape
    slots_total, pages_total = page_table.shape
    req_dev = slots_total // dp_count
    page_span = pages_total // seq_count
    page_rows = page_share * group_count
    rows = page_span * page_rows
    assert req_dev == group_count
    heads = w_value.shape[1] // HEAD
    head_cols = heads * HEAD
    feat_cols = w_featmap.shape[2]
    feature_dim = feat_cols // heads
    tap_count = conv_window.shape[0]

    placed = reassign[:, None] == jnp.arange(slots_total, dtype=jnp.int32)[None, :]
    table = jnp.sum(jnp.where(placed[:, :, None], page_table[None], 0), axis=1)
    slot_lengths = jnp.sum(jnp.where(placed, lengths[None, :], 0), axis=1)
    source_page = (
        table.reshape(dp_count, req_dev, seq_count, page_span)
        .transpose(0, 2, 1, 3)
        .reshape(groups, req_dev * page_span)
    )
    capacity = (pages_dev + groups - 1) // groups
    page_owner = source_page // pages_dev
    pool_slot = source_page % pages_dev
    before = jnp.arange(pages_dev)[None, :] < jnp.arange(pages_dev)[:, None]
    pair_rank = jnp.sum((page_owner[:, :, None] == page_owner[:, None, :]) & before[None], axis=2)
    send_hit = (page_owner == device_place)[:, None, :] & (
        pair_rank[:, None, :] == jnp.arange(capacity)[None, :, None]
    )
    send_slot = jnp.sum(jnp.where(send_hit, pool_slot[:, None, :], 0), axis=2)
    outgoing = pool.at[send_slot.reshape(-1)].get(mode="promise_in_bounds")
    outgoing = outgoing.reshape(groups, capacity, page_share, width)
    arrived = lax.all_to_all(outgoing, ("dp", "seq"), split_axis=0, concat_axis=0, tiled=True)
    own_row = jnp.arange(groups)[:, None] == device_place
    pick_rows = jnp.sum(jnp.where(own_row, page_owner * capacity + pair_rank, 0), axis=0)
    picked = arrived.reshape(groups * capacity, page_share, width)
    picked = picked.at[pick_rows].get(mode="promise_in_bounds")

    picked = picked.reshape(req_dev, page_span, page_share, width)
    swapped = lax.all_to_all(picked, "tensor", split_axis=0, concat_axis=0, tiled=True)
    tokens = swapped.transpose(1, 0, 2, 3).reshape(rows, width)
    slot = dp_place * req_dev + tensor_place
    length = jnp.sum(jnp.where(jnp.arange(slots_total) == slot, slot_lengths, 0))

    assert heads == NEAR and dp_count == 2
    values_t = w_value.T[None]
    featmap_t = w_featmap.transpose(1, 2, 0)
    window_t = w_window.transpose(1, 2, 0)
    out_one, out_two = w_out_one[None], w_out_two[None]
    held_one = from_groups(own_piece([values_t, featmap_t]), (1, 2, 3), ())
    held_out_one = from_groups(own_piece([out_one]), (1, 2, 3), (picked,))
    near_one = from_plane(held_one, (picked,), (swapped,), (held_out_one,))
    held_window = from_groups(own_piece([window_t]), (2,), (swapped,))
    held_out_two = from_groups(own_piece([out_two]), (2, 1, 3), (swapped,))
    places = jnp.concatenate([(seq_place % NEAR) ^ jnp.arange(NEAR), dp_place[None]])
    places = places.astype(jnp.int32)
    taps = conv_window.reshape(tap_count, 3, heads, HEAD).transpose(0, 2, 1, 3)
    taps = jnp.pad(taps, ((0, 0), (0, 0), (0, 0), (0, SLOT - HEAD)))
    taps = taps.reshape(tap_count, 3 * heads * SLOT)
    taps = jnp.stack([taps, across(taps, "tensor", 2)])

    first, second, ones, scale, kept = feature_tables(heads, feature_dim)
    first, second = jnp.asarray(first, BF16), jnp.asarray(second, BF16)
    column = np.zeros((1, heads * SLOT), np.float32)
    column[0, HEAD::SLOT] = 1
    one_cols = 2 * feat_cols + head_cols

    def copy_sems(kinds):
        return pltpu.SemaphoreType.DMA((group_count, dp_count * NEAR * kinds))

    def weights_of(rows_of_head):
        return pltpu.VMEM((group_count, dp_count, heads, rows_of_head, width // dp_count), BF16)

    slots = heads * SLOT
    num, queries, state = call(
        functools.partial(linear_kernel, heads, feature_dim, kept),
        group_count,
        [
            SMEM,
            whole((rows, width)),
            whole((1, width)),
            *[HBM] * 4,
            whole(first.shape),
            whole(second.shape),
            whole(ones.shape),
            whole(column.shape),
        ],
        [each((rows, slots)), each((rows, 2 * feat_cols)), each((heads * kept, SLOT))],
        [
            jax.ShapeDtypeStruct((group_count, rows, slots), F32),
            jax.ShapeDtypeStruct((group_count, rows, 2 * feat_cols), BF16),
            jax.ShapeDtypeStruct((group_count, heads * kept, SLOT), BF16),
        ],
        [
            pltpu.VMEM((rows, width), BF16),
            weights_of(SLOT),
            weights_of(2 * feature_dim),
            copy_sems(3),
        ],
        3 * group_count * rows * width * one_cols,
        group_count * width * one_cols * 2,
        "linear_rows",
    )(
        places, tokens, gain_one[None], values_t, featmap_t, *near_one, first, second, ones, column
    )
    priors = earlier_blocks(state, "seq")
    held_window, held_out_two = after(held_window, (state,)), after(held_out_two, (state,))
    near_out_one = from_plane(held_out_one, (swapped,), (held_window,), [*priors, held_out_two])
    residual, normed_two = call(
        functools.partial(out_one_kernel, heads, kept, len(priors)),
        group_count,
        [
            SMEM,
            each((rows, slots)),
            each((rows, 2 * feat_cols)),
            whole(first.shape),
            whole(second.shape),
            whole(ones.shape),
            whole(scale.shape),
        ]
        + [each((heads * kept, SLOT))] * len(priors)
        + [HBM] * 3
        + [
            whole((rows, width)),
            whole((1, width)),
        ],
        [whole((rows, width)), whole((rows, width))],
        [jax.ShapeDtypeStruct((rows, width), BF16)] * 2,
        [
            pltpu.VMEM((rows, width), F32),
            pltpu.VMEM((rows, slots), BF16),
            weights_of(SLOT),
            copy_sems(1),
        ],
        3 * group_count * rows * width * head_cols,
        group_count * width * head_cols * 2,
        "linear_out",
    )(
        places, num, queries, first, second, ones, scale, *priors, out_one, *near_out_one, tokens,
        gain_two[None],
    )

    tail = normed_two[rows - HALO :]
    halo = lax.ppermute(tail, "seq", [(i, i + 1) for i in range(seq_count - 1)])
    mid = rows // 2
    pair_rows = [across(normed_two[at : at + mid], "tensor", 1) for at in (0, mid)]
    pair_halo = lax.ppermute(
        tail,
        ("seq", "tensor"),
        [
            (i * group_count + j, (i + 1) * group_count + (j ^ 1))
            for i in range(seq_count - 1)
            for j in range(group_count)
        ],
    )
    near_window = from_plane(held_window, (priors[0],), (residual,), (pair_rows[0],))
    block_start = (seq_place * rows).astype(jnp.int32)[None]

    def window_rows(low, high, at, slot_halo):
        return call(
            functools.partial(window_kernel, heads),
            2,
            [
                SMEM,
                SMEM,
                whole((mid, width)),
                pl.BlockSpec((mid, width), lambda g: (at, 0)),
                whole((HALO, width)),
                *[HBM] * 3,
                each((tap_count, 3 * slots)),
            ],
            each((rows, slots)),
            jax.ShapeDtypeStruct((2, rows, slots), BF16),
            [
                pltpu.VMEM((HALO + rows, width), BF16),
                pltpu.VMEM((2, dp_count, heads, 3 * SLOT, width // dp_count), BF16),
                copy_sems(3),
            ],
            6 * rows * width * 3 * head_cols,
            2 * width * 3 * head_cols * 2,
            "window_rows",
        )(places, block_start, low, high, slot_halo, window_t, *near_window, taps)

    mixed_pair = window_rows(*pair_rows, 0, pair_halo)
    near_out_two = from_plane(held_out_two, (pair_rows[0],), (pair_rows[1],), (mixed_pair,))
    mixed_pair = across(mixed_pair, "tensor", 1)
    mixed_own = window_rows(normed_two, normed_two, 1, halo)
    live = (length - seq_place * rows).astype(jnp.int32)[None]
    result = call(
        out_two_kernel,
        group_count,
        [
            SMEM,
            SMEM,
            whole((2, rows, slots)),
            whole((2, rows, slots)),
            *[HBM] * 3,
            whole((rows, width)),
        ],
        whole((rows, width)),
        jax.ShapeDtypeStruct((rows, width), BF16),
        [
            pltpu.VMEM((rows, width), F32),
            weights_of(SLOT),
            copy_sems(1),
        ],
        2 * group_count * rows * width * head_cols,
        group_count * width * head_cols * 2,
        "window_out",
    )(places, live, mixed_own, mixed_pair, out_two, *near_out_two, residual)

    result = result.reshape(page_span, group_count, page_share, width).transpose(1, 0, 2, 3)
    return lax.all_to_all(result, "tensor", split_axis=0, concat_axis=0, tiled=True)


def solution(mesh):
    return jax.shard_map(
        on_device,
        mesh=mesh,
        in_specs=(
            P(("dp", "seq"), "tensor", None),
            P(),
            P(),
            P(),
            P(),
            P(None, None, "tensor"),
            P(None, "tensor"),
            P("tensor", None),
            P(),
            P(None, None, "tensor"),
            P(None, None, "tensor"),
            P("tensor", None),
        ),
        out_specs=P("dp", "seq", "tensor", None),
        check_vma=False,
    )
```

```python
import functools

import jax
import jax.numpy as jnp
import numpy as np
from jax import lax
from jax.experimental import pallas as pl
from jax.experimental.pallas import tpu as pltpu
from jax.sharding import PartitionSpec as P

HEAD = 112
WINDOW = 64
EPS = 1e-05
SLOT = 128
FEAT_SLOT = 256
HALO = 80
NEAR = 4
VMEM = 60 * 1024 * 1024
F32 = jnp.float32
BF16 = jnp.bfloat16


def dot(a, b, dims=((1,), (0,))):
    return lax.dot_general(a, b, (dims, ((), ())), preferred_element_type=F32)


def normed_rows(rows, gain):
    scale = lax.rsqrt(jnp.mean(rows * rows, axis=-1, keepdims=True) + EPS)
    return (rows * scale * gain).astype(BF16)


def feature_tables(heads, feature_dim):
    pairs = [(i, j) for i in range(feature_dim) for j in range(i, feature_dim)]
    pairs += [(i, -1) for i in range(feature_dim)] + [(-1, -1)]
    first = np.zeros((2 * heads * feature_dim, heads * FEAT_SLOT), np.float32)
    second = np.zeros_like(first)
    ones = np.zeros((2, heads * FEAT_SLOT), np.float32)
    scale = np.zeros((1, heads * FEAT_SLOT), np.float32)
    for h in range(heads):
        for n, (i, j) in enumerate(pairs):
            at = h * FEAT_SLOT + n
            if i >= 0:
                first[2 * h * feature_dim + i, at] = 1
            else:
                ones[0, at] = 1
            if j >= 0:
                second[2 * h * feature_dim + j, at] = 1
            else:
                ones[1, at] = 1
            if i < 0:
                scale[0, at] = 1
            elif j < 0:
                scale[0, at] = feature_dim**-0.5
            else:
                scale[0, at] = (0.5 if i == j else 1.0) / feature_dim
    return first, second, ones, scale, -(-len(pairs) // 16) * 16


def features(rows, first, second, ones):
    return (dot(rows, first) + ones[0:1]) * (dot(rows, second) + ones[1:2])


def run_copies(copies_of, groups, meanwhile=None):
    step = pl.program_id(0)

    @pl.when(step == 0)
    def _():
        for group in range(groups):
            for copy in copies_of(group):
                copy.start()
        if meanwhile is not None:
            meanwhile()

    for group in range(groups):

        @pl.when(step == group)
        def _(group=group):
            for copy in copies_of(group):
                copy.wait()


def weight_copies(place_ref, near_ref, far_ref, targets, sems, group):
    near = near_ref.shape[0]
    cols = near_ref.shape[3]
    found = []
    for n in range(2 * near):
        at = 0
        for own_ref, kind, rows, w_ref, off in targets:
            if group == 0:
                part, head = n // near, n % near
                src = own_ref.at[
                    kind, head * rows : (head + 1) * rows, part * cols : (part + 1) * cols
                ]
            else:
                part, head = place_ref[near], place_ref[n % near]
                if n >= near:
                    part = 1 - part
                src = (near_ref if n < near else far_ref).at[
                    n % near, group - 1, at : at + rows, :
                ]
            dst = w_ref.at[group, part, head, off : off + rows, :]
            found.append(pltpu.make_async_copy(src, dst, sems.at[group, len(found)]))
            at += rows
    return found


def zero_between_heads(w_ref):
    groups, parts, heads, rows, cols = w_ref.shape
    for at in range(HEAD, rows, SLOT):
        w_ref[:, :, :, at : at + SLOT - HEAD, :] = jnp.zeros(
            (groups, parts, heads, SLOT - HEAD, cols), BF16
        )


def group_weights(w_ref, step, part):
    heads, rows, cols = w_ref.shape[2:]
    return w_ref[step, part].reshape(heads * rows, cols)


def project(rows_ref, w_ref, step):
    parts, cols = w_ref.shape[1], w_ref.shape[4]
    total = None
    for part in range(parts):
        rows = rows_ref[:, part * cols : (part + 1) * cols]
        share = dot(rows, group_weights(w_ref, step, part), ((1,), (1,)))
        total = share if total is None else total + share
    return total


def linear_kernel(
    heads,
    feature_dim,
    kept,
    place_ref,
    x_ref,
    gain_ref,
    value_ref,
    featmap_ref,
    near_ref,
    far_ref,
    first_ref,
    second_ref,
    ones_ref,
    column_ref,
    num_ref,
    q_ref,
    state_ref,
    normed_ref,
    value_w_ref,
    feat_w_ref,
    sems,
):
    step = pl.program_id(0)
    targets = [
        (value_ref, 0, HEAD, value_w_ref, 0),
        (featmap_ref, 0, feature_dim, feat_w_ref, 0),
        (featmap_ref, 1, feature_dim, feat_w_ref, feature_dim),
    ]

    @pl.when(step == 0)
    def _():
        zero_between_heads(value_w_ref)

    run_copies(
        functools.partial(weight_copies, place_ref, near_ref, far_ref, targets, sems),
        value_w_ref.shape[0],
        lambda: normed_ref.__setitem__(
            ..., normed_rows(x_ref[...].astype(F32), gain_ref[...])
        ),
    )
    rows = x_ref.shape[0]
    width = 2 * heads * feature_dim
    queries = project(normed_ref, feat_w_ref, step).astype(BF16)
    keys = pltpu.roll(queries.astype(F32), width - feature_dim, 1).astype(BF16)
    values = (project(normed_ref, value_w_ref, step) + column_ref[...]).astype(BF16)
    q_ref[0] = queries
    lane = lax.broadcasted_iota(jnp.int32, (rows, width), 1)
    causal = lax.broadcasted_iota(jnp.int32, (rows, rows), 1) <= lax.broadcasted_iota(
        jnp.int32, (rows, rows), 0
    )
    key_features = features(keys, first_ref[...], second_ref[...], ones_ref[...]).astype(BF16)
    for h in range(heads):
        at = 2 * h * feature_dim
        own = jnp.where((lane >= at) & (lane < at + feature_dim), queries, jnp.zeros_like(queries))
        scores = dot(own, keys, ((1,), (1,))) * feature_dim**-0.5
        kernel = jnp.where(causal, 1.0 + scores + 0.5 * scores * scores, 0.0).astype(BF16)
        value = values[:, h * SLOT : (h + 1) * SLOT]
        num_ref[0, :, h * SLOT : (h + 1) * SLOT] = dot(kernel, value)
        state = dot(key_features[:, h * FEAT_SLOT : h * FEAT_SLOT + kept], value, ((0,), (0,)))
        state_ref[0, h * kept : (h + 1) * kept, :] = state.astype(BF16)


def add_branch(mixed, w_ref, total_ref):
    step = pl.program_id(0)
    parts, cols = w_ref.shape[1], w_ref.shape[4]
    for part in range(parts):
        share = dot(mixed, group_weights(w_ref, step, part)).astype(BF16).astype(F32)
        total_ref[:, part * cols : (part + 1) * cols] += share


def out_one_kernel(
    heads,
    kept,
    priors,
    *refs,
):
    place_ref, num_ref, q_ref, first_ref, second_ref, ones_ref, scale_ref = refs[:7]
    prior_refs = refs[7 : 7 + priors]
    own_ref, near_ref, far_ref, x_ref, gain_ref = refs[7 + priors : 12 + priors]
    residual_ref, normed_ref, total_ref, mixed_ref, w_ref, sems = refs[12 + priors :]
    step = pl.program_id(0)

    @pl.when(step == 0)
    def _():
        total_ref[...] = jnp.zeros_like(total_ref)
        zero_between_heads(w_ref)

    run_copies(
        functools.partial(
            weight_copies, place_ref, near_ref, far_ref, [(own_ref, 0, HEAD, w_ref, 0)], sems
        ),
        w_ref.shape[0],
    )

    query_features = features(q_ref[0], first_ref[...], second_ref[...], ones_ref[...])
    query_features = (query_features * scale_ref[...]).astype(BF16)
    for h in range(heads):
        at = slice(h * kept, (h + 1) * kept)
        prior = prior_refs[0][0, at, :].astype(F32)
        for ref in prior_refs[1:]:
            prior = prior + ref[0, at, :].astype(F32)
        lanes = slice(h * SLOT, (h + 1) * SLOT)
        total = num_ref[0, :, lanes] + dot(
            query_features[:, h * FEAT_SLOT : h * FEAT_SLOT + kept], prior.astype(BF16)
        )
        mixed_ref[:, lanes] = (total / total[:, HEAD : HEAD + 1]).astype(BF16)
    add_branch(mixed_ref[...], w_ref, total_ref)

    @pl.when(step == pl.num_programs(0) - 1)
    def _():
        residual = (x_ref[...].astype(F32) + total_ref[...]).astype(BF16)
        residual_ref[...] = residual
        normed_ref[...] = normed_rows(residual.astype(F32), gain_ref[...])


def window_kernel(
    heads,
    place_ref,
    first_ref,
    low_ref,
    high_ref,
    halo_ref,
    own_ref,
    near_ref,
    far_ref,
    tap_ref,
    mixed_ref,
    rows_ref,
    w_ref,
    sems,
):
    step = pl.program_id(0)
    targets = [(own_ref, kind, HEAD, w_ref, kind * SLOT) for kind in range(3)]

    mid = low_ref.shape[0]

    def place_rows():
        rows_ref[:HALO] = halo_ref[...]
        rows_ref[HALO : HALO + mid] = low_ref[...]
        rows_ref[HALO + mid :] = high_ref[...]

    @pl.when(step == 0)
    def _():
        zero_between_heads(w_ref)

    run_copies(
        functools.partial(weight_copies, place_ref, near_ref, far_ref, targets, sems),
        w_ref.shape[0],
        place_rows,
    )
    rows = 2 * mid
    lead = HALO - WINDOW
    projected = project(rows_ref, w_ref, step)
    taps = tap_ref[0]
    convolved = taps[0:1] * projected
    for offset in range(1, taps.shape[0]):
        convolved = convolved + taps[offset : offset + 1] * pltpu.roll(projected, offset, 0)
    convolved = convolved[lead:].astype(BF16)
    tile = 128
    span = tile + WINDOW
    row = lax.broadcasted_iota(jnp.int32, (tile, span), 0)
    col = lax.broadcasted_iota(jnp.int32, (tile, span), 1)
    band = (col > row) & (col <= row + WINDOW)
    for h in range(heads):
        at = 3 * h * SLOT
        queries = convolved[WINDOW:, at : at + SLOT]
        keys = convolved[:, at + SLOT : at + 2 * SLOT]
        values = convolved[:, at + 2 * SLOT : at + 3 * SLOT]
        for start in range(0, rows, tile):
            logits = dot(queries[start : start + tile], keys[start : start + span], ((1,), (1,)))
            allowed = band
            if start < WINDOW:
                allowed = band & (col >= WINDOW - start - first_ref[0])
            logits = jnp.where(allowed, logits * HEAD**-0.5, -jnp.inf)
            weights = jnp.exp(logits - jnp.max(logits, axis=1, keepdims=True))
            weights = weights / jnp.sum(weights, axis=1, keepdims=True)
            mixed = dot(weights.astype(BF16), values[start : start + span])
            mixed_ref[0, start : start + tile, h * SLOT : (h + 1) * SLOT] = mixed.astype(BF16)


def out_two_kernel(
    place_ref,
    live_ref,
    mixed_ref,
    pair_ref,
    own_ref,
    near_ref,
    far_ref,
    residual_ref,
    out_ref,
    total_ref,
    w_ref,
    sems,
):
    step = pl.program_id(0)

    @pl.when(step == 0)
    def _():
        total_ref[...] = jnp.zeros_like(total_ref)
        zero_between_heads(w_ref)

    run_copies(
        functools.partial(
            weight_copies, place_ref, near_ref, far_ref, [(own_ref, 0, HEAD, w_ref, 0)], sems
        ),
        w_ref.shape[0],
    )
    mixed = jnp.where(step < 2, mixed_ref[step % 2], pair_ref[step % 2])
    add_branch(mixed, w_ref, total_ref)

    @pl.when(step == pl.num_programs(0) - 1)
    def _():
        result = (residual_ref[...].astype(F32) + total_ref[...]).astype(BF16)
        row = lax.broadcasted_iota(jnp.int32, result.shape, 0)
        out_ref[...] = jnp.where(row < live_ref[0], result, jnp.zeros_like(result))


def whole(shape):
    return pl.BlockSpec(shape, lambda g: (0,) * len(shape))


def each(shape):
    return pl.BlockSpec((1,) + shape, lambda g: (g,) + (0,) * len(shape))


SMEM = pl.BlockSpec(memory_space=pltpu.SMEM)
HBM = pl.BlockSpec(memory_space=pl.ANY)


def call(kernel, groups, in_specs, out_specs, out_shape, scratch, name):
    return pl.pallas_call(
        kernel,
        grid=(groups,),
        in_specs=in_specs,
        out_specs=out_specs,
        out_shape=out_shape,
        scratch_shapes=scratch,
        compiler_params=pltpu.CompilerParams(
            dimension_semantics=("arbitrary",), vmem_limit_bytes=VMEM
        ),
        cost_estimate=pl.CostEstimate(flops=0, bytes_accessed=0, transcendentals=0),
        name=name,
    )


def own_piece(whole_weights):
    head, part = lax.axis_index("seq") % NEAR, lax.axis_index("dp")
    found = []
    for weights in whole_weights:
        kinds, rows, cols = weights.shape
        rows, cols = rows // NEAR, cols // lax.axis_size("dp")
        piece = lax.dynamic_slice(weights, (0, head * rows, part * cols), (kinds, rows, cols))
        found.append(piece.reshape(kinds * rows, cols))
    return jnp.concatenate(found, axis=0)


def across(array, axis, bit):
    return lax.ppermute(array, axis, [(i, i ^ bit) for i in range(lax.axis_size(axis))])


def after(array, others):
    if not others:
        return array
    first = [lax.slice(other, (0,) * other.ndim, (1,) * other.ndim) for other in others]
    zero = sum(one.reshape(()).astype(F32) * 0.0 for one in first)
    return jnp.where(zero == 0.0, array, jnp.zeros_like(array))


def from_groups(piece, offsets, over_z):
    piece = after(piece, over_z)
    return jnp.stack([across(piece, "tensor", offset) for offset in offsets])


def from_plane(held, over_xy, diagonal, over_cores):
    held = after(held, over_xy)
    half = -(-held.shape[1] // 32) * 16
    beside, above = across(held, "seq", 1), across(held, "seq", 2)
    opposite = jnp.concatenate(
        [
            across(after(above[:, :half], diagonal), "seq", 1),
            across(after(beside[:, half:], diagonal), "seq", 2),
        ],
        axis=1,
    )
    near = after(jnp.stack([held, beside, above, opposite]), over_cores)
    return near, across(near, "dp", 1)


def earlier_blocks(state, axis):
    peers = lax.axis_size(axis)
    if peers <= 4:
        return [
            lax.ppermute(state, axis, [(i, i + by) for i in range(peers - by)])
            for by in range(1, peers)
        ]
    everything = lax.all_gather(state, axis).astype(F32)
    reached = jnp.arange(peers) < lax.axis_index(axis)
    return [jnp.sum(jnp.where(reached[:, None, None, None], everything, 0.0), axis=0)]


def on_device(
    pool,
    page_table,
    reassign,
    lengths,
    gain_one,
    w_featmap,
    w_value,
    w_out_one,
    gain_two,
    w_window,
    conv_window,
    w_out_two,
):
    dp_count, seq_count, group_count = (lax.axis_size(n) for n in ("dp", "seq", "tensor"))
    groups = dp_count * seq_count
    device_place = lax.axis_index(("dp", "seq"))
    dp_place, seq_place, tensor_place = (lax.axis_index(n) for n in ("dp", "seq", "tensor"))
    pages_dev, page_share, width = pool.shape
    slots_total, pages_total = page_table.shape
    req_dev = slots_total // dp_count
    page_span = pages_total // seq_count
    page_rows = page_share * group_count
    rows = page_span * page_rows
    assert req_dev == group_count
    heads = w_value.shape[1] // HEAD
    head_cols = heads * HEAD
    feat_cols = w_featmap.shape[2]
    feature_dim = feat_cols // heads
    tap_count = conv_window.shape[0]

    assert heads == NEAR and dp_count == 2
    values_t = w_value.T[None]
    featmap_t = w_featmap.transpose(1, 2, 0)
    window_t = w_window.transpose(1, 2, 0)
    out_one, out_two = w_out_one[None], w_out_two[None]
    held_one = from_groups(own_piece([values_t, featmap_t]), (1, 2, 3), ())

    placed = reassign[:, None] == jnp.arange(slots_total, dtype=jnp.int32)[None, :]
    table = jnp.sum(jnp.where(placed[:, :, None], page_table[None], 0), axis=1)
    slot_lengths = jnp.sum(jnp.where(placed, lengths[None, :], 0), axis=1)
    source_page = (
        table.reshape(dp_count, req_dev, seq_count, page_span)
        .transpose(0, 2, 1, 3)
        .reshape(groups, req_dev * page_span)
    )
    capacity = (pages_dev + groups - 1) // groups
    page_owner = source_page // pages_dev
    pool_slot = source_page % pages_dev
    before = jnp.arange(pages_dev)[None, :] < jnp.arange(pages_dev)[:, None]
    pair_rank = jnp.sum((page_owner[:, :, None] == page_owner[:, None, :]) & before[None], axis=2)
    send_hit = (page_owner == device_place)[:, None, :] & (
        pair_rank[:, None, :] == jnp.arange(capacity)[None, :, None]
    )
    send_slot = jnp.sum(jnp.where(send_hit, pool_slot[:, None, :], 0), axis=2)
    outgoing = pool.at[send_slot.reshape(-1)].get(mode="promise_in_bounds")
    outgoing = outgoing.reshape(groups, capacity, page_share, width)
    arrived = lax.all_to_all(outgoing, ("dp", "seq"), split_axis=0, concat_axis=0, tiled=True)
    own_row = jnp.arange(groups)[:, None] == device_place
    pick_rows = jnp.sum(jnp.where(own_row, page_owner * capacity + pair_rank, 0), axis=0)
    picked = arrived.reshape(groups * capacity, page_share, width)
    picked = picked.at[pick_rows].get(mode="promise_in_bounds")

    picked = after(picked.reshape(req_dev, page_span, page_share, width), (held_one,))
    swapped = lax.all_to_all(picked, "tensor", split_axis=0, concat_axis=0, tiled=True)
    tokens = swapped.transpose(1, 0, 2, 3).reshape(rows, width)
    slot = dp_place * req_dev + tensor_place
    length = jnp.sum(jnp.where(jnp.arange(slots_total) == slot, slot_lengths, 0))

    held_out_one = from_groups(own_piece([out_one]), (1, 2, 3), (picked,))
    near_one = from_plane(held_one, (picked,), (swapped,), ())
    held_window = from_groups(own_piece([window_t]), (2,), (swapped,))
    held_out_two = from_groups(own_piece([out_two]), (2, 1, 3), (swapped,))
    places = jnp.concatenate([(seq_place % NEAR) ^ jnp.arange(NEAR), dp_place[None]])
    places = places.astype(jnp.int32)
    taps = conv_window.reshape(tap_count, 3, heads, HEAD).transpose(0, 2, 1, 3)
    taps = jnp.pad(taps, ((0, 0), (0, 0), (0, 0), (0, SLOT - HEAD)))
    taps = taps.reshape(tap_count, 3 * heads * SLOT)
    taps = jnp.stack([taps, across(taps, "tensor", 2)])

    first, second, ones, scale, kept = feature_tables(heads, feature_dim)
    first, second = jnp.asarray(first, BF16), jnp.asarray(second, BF16)
    column = np.zeros((1, heads * SLOT), np.float32)
    column[0, HEAD::SLOT] = 1

    def copy_sems(kinds):
        return pltpu.SemaphoreType.DMA((group_count, dp_count * NEAR * kinds))

    def weights_of(rows_of_head):
        return pltpu.VMEM((group_count, dp_count, heads, rows_of_head, width // dp_count), BF16)

    slots = heads * SLOT
    num, queries, state = call(
        functools.partial(linear_kernel, heads, feature_dim, kept),
        group_count,
        [
            SMEM,
            whole((rows, width)),
            whole((1, width)),
            *[HBM] * 4,
            whole(first.shape),
            whole(second.shape),
            whole(ones.shape),
            whole(column.shape),
        ],
        [each((rows, slots)), each((rows, 2 * feat_cols)), each((heads * kept, SLOT))],
        [
            jax.ShapeDtypeStruct((group_count, rows, slots), F32),
            jax.ShapeDtypeStruct((group_count, rows, 2 * feat_cols), BF16),
            jax.ShapeDtypeStruct((group_count, heads * kept, SLOT), BF16),
        ],
        [
            pltpu.VMEM((rows, width), BF16),
            weights_of(SLOT),
            weights_of(2 * feature_dim),
            copy_sems(3),
        ],
        "linear_rows",
    )(
        places, tokens, gain_one[None], values_t, featmap_t, *near_one, first, second, ones, column
    )
    priors = earlier_blocks(state, "seq")
    held_window, held_out_two = after(held_window, (state,)), after(held_out_two, (state,))
    near_out_one = from_plane(held_out_one, (swapped,), (state,), [*priors, held_window, held_out_two])
    residual, normed_two = call(
        functools.partial(out_one_kernel, heads, kept, len(priors)),
        group_count,
        [
            SMEM,
            each((rows, slots)),
            each((rows, 2 * feat_cols)),
            whole(first.shape),
            whole(second.shape),
            whole(ones.shape),
            whole(scale.shape),
        ]
        + [each((heads * kept, SLOT))] * len(priors)
        + [HBM] * 3
        + [
            whole((rows, width)),
            whole((1, width)),
        ],
        [whole((rows, width)), whole((rows, width))],
        [jax.ShapeDtypeStruct((rows, width), BF16)] * 2,
        [
            pltpu.VMEM((rows, width), F32),
            pltpu.VMEM((rows, slots), BF16),
            weights_of(SLOT),
            copy_sems(1),
        ],
        "linear_out",
    )(
        places, num, queries, first, second, ones, scale, *priors, out_one, *near_out_one, tokens,
        gain_two[None],
    )

    tail = normed_two[rows - HALO :]
    halo = lax.ppermute(tail, "seq", [(i, i + 1) for i in range(seq_count - 1)])
    mid = rows // 2
    pair_rows = [across(normed_two[at : at + mid], "tensor", 1) for at in (0, mid)]
    pair_halo = lax.ppermute(
        tail,
        ("seq", "tensor"),
        [
            (i * group_count + j, (i + 1) * group_count + (j ^ 1))
            for i in range(seq_count - 1)
            for j in range(group_count)
        ],
    )
    near_window = from_plane(held_window, priors, (residual,), (pair_rows[0],))
    block_start = (seq_place * rows).astype(jnp.int32)[None]

    def window_rows(low, high, at, slot_halo):
        return call(
            functools.partial(window_kernel, heads),
            2,
            [
                SMEM,
                SMEM,
                whole((mid, width)),
                pl.BlockSpec((mid, width), lambda g: (at, 0)),
                whole((HALO, width)),
                *[HBM] * 3,
                each((tap_count, 3 * slots)),
            ],
            each((rows, slots)),
            jax.ShapeDtypeStruct((2, rows, slots), BF16),
            [
                pltpu.VMEM((HALO + rows, width), BF16),
                pltpu.VMEM((2, dp_count, heads, 3 * SLOT, width // dp_count), BF16),
                copy_sems(3),
            ],
            "window_rows",
        )(places, block_start, low, high, slot_halo, window_t, *near_window, taps)

    mixed_pair = window_rows(*pair_rows, 0, pair_halo)
    near_out_two = from_plane(held_out_two, (pair_rows[0],), (pair_rows[1],), (mixed_pair,))
    mixed_pair = across(mixed_pair, "tensor", 1)
    mixed_own = window_rows(normed_two, normed_two, 1, halo)
    live = (length - seq_place * rows).astype(jnp.int32)[None]
    result = call(
        out_two_kernel,
        group_count,
        [
            SMEM,
            SMEM,
            whole((2, rows, slots)),
            whole((2, rows, slots)),
            *[HBM] * 3,
            whole((rows, width)),
        ],
        whole((rows, width)),
        jax.ShapeDtypeStruct((rows, width), BF16),
        [
            pltpu.VMEM((rows, width), F32),
            weights_of(SLOT),
            copy_sems(1),
        ],
        "window_out",
    )(places, live, mixed_own, mixed_pair, out_two, *near_out_two, residual)

    result = result.reshape(page_span, group_count, page_share, width).transpose(1, 0, 2, 3)
    return lax.all_to_all(result, "tensor", split_axis=0, concat_axis=0, tiled=True)


def solution(mesh):
    return jax.shard_map(
        on_device,
        mesh=mesh,
        in_specs=(
            P(("dp", "seq"), "tensor", None),
            P(),
            P(),
            P(),
            P(),
            P(None, None, "tensor"),
            P(None, "tensor"),
            P("tensor", None),
            P(),
            P(None, None, "tensor"),
            P(None, None, "tensor"),
            P("tensor", None),
        ),
        out_specs=P("dp", "seq", "tensor", None),
        check_vma=False,
    )
```

```python
import functools

import jax
import jax.numpy as jnp
import numpy as np
from jax import lax
from jax.experimental import pallas as pl
from jax.experimental.pallas import tpu as pltpu
from jax.sharding import PartitionSpec as P

HEAD = 112
WINDOW = 64
EPS = 1e-05
SLOT = 128
FEAT_SLOT = 256
HALO = 80
NEAR = 4
VMEM = 32 * 1024 * 1024
F32 = jnp.float32
BF16 = jnp.bfloat16


def dot(a, b, dims=((1,), (0,))):
    return lax.dot_general(a, b, (dims, ((), ())), preferred_element_type=F32)


def normed_rows(rows, gain):
    scale = lax.rsqrt(jnp.mean(rows * rows, axis=-1, keepdims=True) + EPS)
    return (rows * scale * gain).astype(BF16)


def feature_tables(heads, feature_dim):
    pairs = [(i, j) for i in range(feature_dim) for j in range(i, feature_dim)]
    pairs += [(i, -1) for i in range(feature_dim)] + [(-1, -1)]
    first = np.zeros((2 * heads * feature_dim, heads * FEAT_SLOT), np.float32)
    second = np.zeros_like(first)
    ones = np.zeros((2, heads * FEAT_SLOT), np.float32)
    scale = np.zeros((1, heads * FEAT_SLOT), np.float32)
    for h in range(heads):
        for n, (i, j) in enumerate(pairs):
            at = h * FEAT_SLOT + n
            if i >= 0:
                first[2 * h * feature_dim + i, at] = 1
            else:
                ones[0, at] = 1
            if j >= 0:
                second[2 * h * feature_dim + j, at] = 1
            else:
                ones[1, at] = 1
            if i < 0:
                scale[0, at] = 1
            elif j < 0:
                scale[0, at] = feature_dim**-0.5
            else:
                scale[0, at] = (0.5 if i == j else 1.0) / feature_dim
    return first, second, ones, scale, -(-len(pairs) // 16) * 16


def features(rows, first, second, ones):
    return (dot(rows, first) + ones[0:1]) * (dot(rows, second) + ones[1:2])


def run_copies(copies_of, groups, meanwhile=None):
    step = pl.program_id(0)

    @pl.when(step == 0)
    def _():
        for group in range(groups):
            for copy in copies_of(group):
                copy.start()
        if meanwhile is not None:
            meanwhile()

    for group in range(groups):

        @pl.when(step == group)
        def _(group=group):
            for copy in copies_of(group):
                copy.wait()


def weight_copies(place_ref, near_ref, far_ref, targets, sems, group):
    near = near_ref.shape[0]
    cols = near_ref.shape[3]
    found = []
    for n in range(2 * near):
        at = 0
        for own_ref, kind, rows, w_ref, off in targets:
            if group == 0:
                part, head = n // near, n % near
                src = own_ref.at[
                    kind, head * rows : (head + 1) * rows, part * cols : (part + 1) * cols
                ]
            else:
                part, head = place_ref[near], place_ref[n % near]
                if n >= near:
                    part = 1 - part
                src = (near_ref if n < near else far_ref).at[
                    n % near, group - 1, at : at + rows, :
                ]
            dst = w_ref.at[group, part, head, off : off + rows, :]
            found.append(pltpu.make_async_copy(src, dst, sems.at[group, len(found)]))
            at += rows
    return found


def zero_between_heads(w_ref):
    groups, parts, heads, rows, cols = w_ref.shape
    for at in range(HEAD, rows, SLOT):
        w_ref[:, :, :, at : at + SLOT - HEAD, :] = jnp.zeros(
            (groups, parts, heads, SLOT - HEAD, cols), BF16
        )


def group_weights(w_ref, step, part):
    heads, rows, cols = w_ref.shape[2:]
    return w_ref[step, part].reshape(heads * rows, cols)


def project(rows_ref, w_ref, step):
    parts, cols = w_ref.shape[1], w_ref.shape[4]
    total = None
    for part in range(parts):
        rows = rows_ref[:, part * cols : (part + 1) * cols]
        share = dot(rows, group_weights(w_ref, step, part), ((1,), (1,)))
        total = share if total is None else total + share
    return total


def linear_kernel(
    heads,
    feature_dim,
    kept,
    place_ref,
    x_ref,
    gain_ref,
    value_ref,
    featmap_ref,
    near_ref,
    far_ref,
    first_ref,
    second_ref,
    ones_ref,
    column_ref,
    num_ref,
    q_ref,
    state_ref,
    normed_ref,
    value_w_ref,
    feat_w_ref,
    sems,
):
    step = pl.program_id(0)
    targets = [
        (value_ref, 0, HEAD, value_w_ref, 0),
        (featmap_ref, 0, feature_dim, feat_w_ref, 0),
        (featmap_ref, 1, feature_dim, feat_w_ref, feature_dim),
    ]

    @pl.when(step == 0)
    def _():
        zero_between_heads(value_w_ref)

    run_copies(
        functools.partial(weight_copies, place_ref, near_ref, far_ref, targets, sems),
        value_w_ref.shape[0],
        lambda: normed_ref.__setitem__(
            ..., normed_rows(x_ref[...].astype(F32), gain_ref[...])
        ),
    )
    rows = x_ref.shape[0]
    width = 2 * heads * feature_dim
    queries = project(normed_ref, feat_w_ref, step).astype(BF16)
    keys = pltpu.roll(queries.astype(F32), width - feature_dim, 1).astype(BF16)
    values = (project(normed_ref, value_w_ref, step) + column_ref[...]).astype(BF16)
    q_ref[0] = queries
    lane = lax.broadcasted_iota(jnp.int32, (rows, width), 1)
    causal = lax.broadcasted_iota(jnp.int32, (rows, rows), 1) <= lax.broadcasted_iota(
        jnp.int32, (rows, rows), 0
    )
    key_features = features(keys, first_ref[...], second_ref[...], ones_ref[...]).astype(BF16)
    for h in range(heads):
        at = 2 * h * feature_dim
        own = jnp.where((lane >= at) & (lane < at + feature_dim), queries, jnp.zeros_like(queries))
        scores = dot(own, keys, ((1,), (1,))) * feature_dim**-0.5
        kernel = jnp.where(causal, 1.0 + scores + 0.5 * scores * scores, 0.0).astype(BF16)
        value = values[:, h * SLOT : (h + 1) * SLOT]
        num_ref[0, :, h * SLOT : (h + 1) * SLOT] = dot(kernel, value)
        state = dot(key_features[:, h * FEAT_SLOT : h * FEAT_SLOT + kept], value, ((0,), (0,)))
        state_ref[0, h * kept : (h + 1) * kept, :] = state.astype(BF16)


def add_branch(mixed, w_ref, total_ref):
    step = pl.program_id(0)
    parts, cols = w_ref.shape[1], w_ref.shape[4]
    for part in range(parts):
        share = dot(mixed, group_weights(w_ref, step, part)).astype(BF16).astype(F32)
        total_ref[:, part * cols : (part + 1) * cols] += share


def out_one_kernel(
    heads,
    kept,
    place_ref,
    num_ref,
    q_ref,
    first_ref,
    second_ref,
    ones_ref,
    scale_ref,
    prior_ref,
    own_ref,
    near_ref,
    far_ref,
    x_ref,
    gain_ref,
    residual_ref,
    normed_ref,
    tail_ref,
    total_ref,
    mixed_ref,
    w_ref,
    sems,
):
    step = pl.program_id(0)

    @pl.when(step == 0)
    def _():
        total_ref[...] = jnp.zeros_like(total_ref)
        zero_between_heads(w_ref)

    run_copies(
        functools.partial(
            weight_copies, place_ref, near_ref, far_ref, [(own_ref, 0, HEAD, w_ref, 0)], sems
        ),
        w_ref.shape[0],
    )

    query_features = features(q_ref[0], first_ref[...], second_ref[...], ones_ref[...])
    query_features = (query_features * scale_ref[...]).astype(BF16)
    for h in range(heads):
        at = slice(h * kept, (h + 1) * kept)
        prior = prior_ref[0, at, :]
        lanes = slice(h * SLOT, (h + 1) * SLOT)
        total = num_ref[0, :, lanes] + dot(
            query_features[:, h * FEAT_SLOT : h * FEAT_SLOT + kept], prior.astype(BF16)
        )
        mixed_ref[:, lanes] = (total / total[:, HEAD : HEAD + 1]).astype(BF16)
    add_branch(mixed_ref[...], w_ref, total_ref)

    @pl.when(step == pl.num_programs(0) - 1)
    def _():
        residual = (x_ref[...].astype(F32) + total_ref[...]).astype(BF16)
        residual_ref[...] = residual
        normed = normed_rows(residual.astype(F32), gain_ref[...])
        normed_ref[...] = normed
        tail_ref[...] = normed[-HALO:]


def window_kernel(
    heads,
    place_ref,
    first_ref,
    x_ref,
    halo_ref,
    own_ref,
    near_ref,
    far_ref,
    tap_ref,
    mixed_ref,
    rows_ref,
    w_ref,
    sems,
):
    step = pl.program_id(0)
    targets = [(own_ref, kind, HEAD, w_ref, kind * SLOT) for kind in range(3)]

    def place_rows():
        rows_ref[:HALO] = halo_ref[...]
        rows_ref[HALO:] = x_ref[...]

    @pl.when(step == 0)
    def _():
        zero_between_heads(w_ref)

    run_copies(
        functools.partial(weight_copies, place_ref, near_ref, far_ref, targets, sems),
        w_ref.shape[0],
        place_rows,
    )
    rows = x_ref.shape[0]
    lead = HALO - WINDOW
    projected = project(rows_ref, w_ref, step)
    taps = tap_ref[0]
    convolved = taps[0:1] * projected
    for offset in range(1, taps.shape[0]):
        convolved = convolved + taps[offset : offset + 1] * pltpu.roll(projected, offset, 0)
    convolved = convolved[lead:].astype(BF16)
    tile = 128
    span = tile + WINDOW
    row = lax.broadcasted_iota(jnp.int32, (tile, span), 0)
    col = lax.broadcasted_iota(jnp.int32, (tile, span), 1)
    band = (col > row) & (col <= row + WINDOW)
    for h in range(heads):
        at = 3 * h * SLOT
        queries = convolved[WINDOW:, at : at + SLOT]
        keys = convolved[:, at + SLOT : at + 2 * SLOT]
        values = convolved[:, at + 2 * SLOT : at + 3 * SLOT]
        for start in range(0, rows, tile):
            logits = dot(queries[start : start + tile], keys[start : start + span], ((1,), (1,)))
            allowed = band
            if start < WINDOW:
                allowed = band & (col >= WINDOW - start - first_ref[0])
            logits = jnp.where(allowed, logits * HEAD**-0.5, -jnp.inf)
            weights = jnp.exp(logits - jnp.max(logits, axis=1, keepdims=True))
            weights = weights / jnp.sum(weights, axis=1, keepdims=True)
            mixed = dot(weights.astype(BF16), values[start : start + span])
            mixed_ref[0, start : start + tile, h * SLOT : (h + 1) * SLOT] = mixed.astype(BF16)


def out_two_kernel(
    place_ref,
    live_ref,
    mixed_ref,
    pair_ref,
    own_ref,
    near_ref,
    far_ref,
    residual_ref,
    out_ref,
    total_ref,
    w_ref,
    sems,
):
    step = pl.program_id(0)

    @pl.when(step == 0)
    def _():
        total_ref[...] = jnp.zeros_like(total_ref)
        zero_between_heads(w_ref)

    run_copies(
        functools.partial(
            weight_copies, place_ref, near_ref, far_ref, [(own_ref, 0, HEAD, w_ref, 0)], sems
        ),
        w_ref.shape[0],
    )
    mixed = jnp.where(step < 2, mixed_ref[step % 2], pair_ref[step % 2])
    add_branch(mixed, w_ref, total_ref)

    @pl.when(step == pl.num_programs(0) - 1)
    def _():
        result = (residual_ref[...].astype(F32) + total_ref[...]).astype(BF16)
        row = lax.broadcasted_iota(jnp.int32, result.shape, 0)
        out_ref[...] = jnp.where(row < live_ref[0], result, jnp.zeros_like(result))


def whole(shape):
    return pl.BlockSpec(shape, lambda g: (0,) * len(shape))


def each(shape):
    return pl.BlockSpec((1,) + shape, lambda g: (g,) + (0,) * len(shape))


SMEM = pl.BlockSpec(memory_space=pltpu.SMEM)
HBM = pl.BlockSpec(memory_space=pl.ANY)


def call(kernel, groups, in_specs, out_specs, out_shape, scratch, name):
    return pl.pallas_call(
        kernel,
        grid=(groups,),
        in_specs=in_specs,
        out_specs=out_specs,
        out_shape=out_shape,
        scratch_shapes=scratch,
        compiler_params=pltpu.CompilerParams(
            dimension_semantics=("arbitrary",), vmem_limit_bytes=VMEM
        ),
        cost_estimate=pl.CostEstimate(flops=0, bytes_accessed=0, transcendentals=0),
        name=name,
    )


def own_piece(whole_weights):
    head, part = lax.axis_index("seq") % NEAR, lax.axis_index("dp")
    found = []
    for weights in whole_weights:
        kinds, rows, cols = weights.shape
        rows, cols = rows // NEAR, cols // lax.axis_size("dp")
        piece = lax.dynamic_slice(weights, (0, head * rows, part * cols), (kinds, rows, cols))
        found.append(piece.reshape(kinds * rows, cols))
    return jnp.concatenate(found, axis=0)


def across(array, axis, bit):
    return lax.ppermute(array, axis, [(i, i ^ bit) for i in range(lax.axis_size(axis))])


def after(array, others):
    if not others:
        return array
    first = [lax.slice(other, (0,) * other.ndim, (1,) * other.ndim) for other in others]
    zero = sum(one.reshape(()).astype(F32) * 0.0 for one in first)
    return jnp.where(zero == 0.0, array, jnp.zeros_like(array))


def settled(array, others=()):
    return lax.optimization_barrier(after(array, others))


def from_group(piece, over_z):
    return across(after(piece, over_z), "tensor", 2)[None]


def from_groups(piece, over_z, order=(0, 1, 2)):
    piece = after(piece, over_z)
    beside, beyond = across(piece, "tensor", 1), across(piece, "tensor", 2)
    found = (beside, beyond, across(beyond, "tensor", 1))
    return [found[n] for n in order]


def neighbours(held):
    return across(held, "seq", 1), across(held, "seq", 2)


def from_plane(held, near_by, diagonal, over_cores):
    half = -(-held.shape[1] // 32) * 16
    beside, above = near_by
    opposite = [
        across(after(above[:, :half], diagonal), "seq", 1),
        across(after(beside[:, half:], diagonal), "seq", 2),
    ]
    opposite = after(jnp.concatenate(opposite, axis=1), over_cores)
    near = after(jnp.stack([held, beside, above, opposite]), over_cores)
    return near, across(near, "dp", 1)


def earlier_blocks(state, axis):
    peers = lax.axis_size(axis)
    if peers <= 4:
        found = [
            lax.ppermute(state, axis, [(i, i + by) for i in range(peers - by)])
            for by in range(1, peers)
        ]
        return sum(one.astype(F32) for one in found)
    everything = lax.all_gather(state, axis).astype(F32)
    reached = jnp.arange(peers) < lax.axis_index(axis)
    return jnp.sum(jnp.where(reached[:, None, None, None], everything, 0.0), axis=0)


def on_device(
    pool,
    page_table,
    reassign,
    lengths,
    gain_one,
    w_featmap,
    w_value,
    w_out_one,
    gain_two,
    w_window,
    conv_window,
    w_out_two,
):
    dp_count, seq_count, group_count = (lax.axis_size(n) for n in ("dp", "seq", "tensor"))
    groups = dp_count * seq_count
    device_place = lax.axis_index(("dp", "seq"))
    dp_place, seq_place, tensor_place = (lax.axis_index(n) for n in ("dp", "seq", "tensor"))
    pages_dev, page_share, width = pool.shape
    slots_total, pages_total = page_table.shape
    req_dev = slots_total // dp_count
    page_span = pages_total // seq_count
    page_rows = page_share * group_count
    rows = page_span * page_rows
    assert req_dev == group_count
    heads = w_value.shape[1] // HEAD
    head_cols = heads * HEAD
    feat_cols = w_featmap.shape[2]
    feature_dim = feat_cols // heads
    tap_count = conv_window.shape[0]

    assert heads == NEAR and dp_count == 2
    values_t = w_value.T[None]
    featmap_t = w_featmap.transpose(1, 2, 0)
    window_t = w_window.transpose(1, 2, 0)
    out_one, out_two = w_out_one[None], w_out_two[None]
    held_one = settled(jnp.stack(from_groups(own_piece([values_t, featmap_t]), ())))

    placed = reassign[:, None] == jnp.arange(slots_total, dtype=jnp.int32)[None, :]
    table = jnp.sum(jnp.where(placed[:, :, None], page_table[None], 0), axis=1)
    slot_lengths = jnp.sum(jnp.where(placed, lengths[None, :], 0), axis=1)
    source_page = (
        table.reshape(dp_count, req_dev, seq_count, page_span)
        .transpose(0, 2, 1, 3)
        .reshape(groups, req_dev * page_span)
    )
    capacity = (pages_dev + groups - 1) // groups
    page_owner = source_page // pages_dev
    pool_slot = source_page % pages_dev
    before = jnp.arange(pages_dev)[None, :] < jnp.arange(pages_dev)[:, None]
    pair_rank = jnp.sum((page_owner[:, :, None] == page_owner[:, None, :]) & before[None], axis=2)
    send_hit = (page_owner == device_place)[:, None, :] & (
        pair_rank[:, None, :] == jnp.arange(capacity)[None, :, None]
    )
    send_slot = jnp.sum(jnp.where(send_hit, pool_slot[:, None, :], 0), axis=2)
    outgoing = pool.at[send_slot.reshape(-1)].get(mode="promise_in_bounds")
    outgoing = outgoing.reshape(groups, capacity, page_share, width)
    arrived = lax.all_to_all(outgoing, ("dp", "seq"), split_axis=0, concat_axis=0, tiled=True)
    own_row = jnp.arange(groups)[:, None] == device_place
    pick_rows = jnp.sum(jnp.where(own_row, page_owner * capacity + pair_rank, 0), axis=0)
    picked = arrived.reshape(groups * capacity, page_share, width)
    picked = picked.at[pick_rows].get(mode="promise_in_bounds")

    picked = after(picked.reshape(req_dev, page_span, page_share, width), (held_one,))
    swapped = lax.all_to_all(picked, "tensor", split_axis=0, concat_axis=0, tiled=True)
    tokens = swapped.transpose(1, 0, 2, 3).reshape(rows, width)
    slot = dp_place * req_dev + tensor_place
    length = jnp.sum(jnp.where(jnp.arange(slots_total) == slot, slot_lengths, 0))

    held_out_one = settled(jnp.stack(from_groups(own_piece([out_one]), (picked,))))
    near_one = from_plane(held_one, neighbours(held_one), (), (held_out_one,))
    held_window = from_group(own_piece([window_t]), (swapped,))
    held_out_two = from_groups(own_piece([out_two]), (swapped,), (1, 0, 2))
    places = jnp.concatenate([(seq_place % NEAR) ^ jnp.arange(NEAR), dp_place[None]])
    places = places.astype(jnp.int32)
    taps = conv_window.reshape(tap_count, 3, heads, HEAD).transpose(0, 2, 1, 3)
    taps = jnp.pad(taps, ((0, 0), (0, 0), (0, 0), (0, SLOT - HEAD)))
    taps = taps.reshape(tap_count, 3 * heads * SLOT)
    taps = jnp.stack([taps, across(taps, "tensor", 2)])

    first, second, ones, scale, kept = feature_tables(heads, feature_dim)
    first, second = jnp.asarray(first, BF16), jnp.asarray(second, BF16)
    column = np.zeros((1, heads * SLOT), np.float32)
    column[0, HEAD::SLOT] = 1

    def copy_sems(kinds):
        return pltpu.SemaphoreType.DMA((group_count, dp_count * NEAR * kinds))

    def weights_of(rows_of_head):
        return pltpu.VMEM((group_count, dp_count, heads, rows_of_head, width // dp_count), BF16)

    slots = heads * SLOT
    num, queries, state = call(
        functools.partial(linear_kernel, heads, feature_dim, kept),
        group_count,
        [
            SMEM,
            whole((rows, width)),
            whole((1, width)),
            *[HBM] * 4,
            whole(first.shape),
            whole(second.shape),
            whole(ones.shape),
            whole(column.shape),
        ],
        [each((rows, slots)), each((rows, 2 * feat_cols)), each((heads * kept, SLOT))],
        [
            jax.ShapeDtypeStruct((group_count, rows, slots), F32),
            jax.ShapeDtypeStruct((group_count, rows, 2 * feat_cols), BF16),
            jax.ShapeDtypeStruct((group_count, heads * kept, SLOT), BF16),
        ],
        [
            pltpu.VMEM((rows, width), BF16),
            weights_of(SLOT),
            weights_of(2 * feature_dim),
            copy_sems(3),
        ],
        "linear_rows",
    )(
        places, tokens, gain_one[None], values_t, featmap_t, *near_one, first, second, ones, column
    )
    prior = settled(earlier_blocks(state, "seq"))
    held_out_one = after(held_out_one, (swapped,))
    near_out_one = from_plane(
        held_out_one, neighbours(held_out_one), (state,), (prior, held_window)
    )
    held_out_two = settled(jnp.stack(held_out_two), (state,))
    residual, normed_two, tail = call(
        functools.partial(out_one_kernel, heads, kept),
        group_count,
        [
            SMEM,
            each((rows, slots)),
            each((rows, 2 * feat_cols)),
            whole(first.shape),
            whole(second.shape),
            whole(ones.shape),
            whole(scale.shape),
        ]
        + [each((heads * kept, SLOT))]
        + [HBM] * 3
        + [
            whole((rows, width)),
            whole((1, width)),
        ],
        [whole((rows, width)), whole((rows, width)), whole((HALO, width))],
        [jax.ShapeDtypeStruct((n, width), BF16) for n in (rows, rows, HALO)],
        [
            pltpu.VMEM((rows, width), F32),
            pltpu.VMEM((rows, slots), BF16),
            weights_of(SLOT),
            copy_sems(1),
        ],
        "linear_out",
    )(
        places, num, queries, first, second, ones, scale, prior, out_one, *near_out_one, tokens,
        gain_two[None],
    )

    halo = lax.ppermute(tail, "seq", [(i, i + 1) for i in range(seq_count - 1)])
    pair_rows = across(normed_two, "tensor", 1)
    pair_halo = lax.ppermute(
        tail,
        ("seq", "tensor"),
        [
            (i * group_count + j, (i + 1) * group_count + (j ^ 1))
            for i in range(seq_count - 1)
            for j in range(group_count)
        ],
    )
    held_window, held_out_two = after(held_window, (prior,)), after(held_out_two, (residual,))
    near_by = neighbours(held_out_two)
    near_window = from_plane(
        held_window,
        neighbours(held_window),
        (residual, held_out_two),
        (pair_rows, halo, pair_halo, *near_by),
    )
    block_start = (seq_place * rows).astype(jnp.int32)[None]

    def window_rows(slot_rows, slot_halo):
        return call(
            functools.partial(window_kernel, heads),
            2,
            [
                SMEM,
                SMEM,
                whole((rows, width)),
                whole((HALO, width)),
                *[HBM] * 3,
                each((tap_count, 3 * slots)),
            ],
            each((rows, slots)),
            jax.ShapeDtypeStruct((2, rows, slots), BF16),
            [
                pltpu.VMEM((HALO + rows, width), BF16),
                pltpu.VMEM((2, dp_count, heads, 3 * SLOT, width // dp_count), BF16),
                copy_sems(3),
            ],
            "window_rows",
        )(places, block_start, slot_rows, slot_halo, window_t, *near_window, taps)

    mixed_pair = window_rows(pair_rows, pair_halo)
    near_out_two = from_plane(held_out_two, near_by, (pair_rows,), (mixed_pair,))
    mixed_pair = across(mixed_pair, "tensor", 1)
    mixed_own = window_rows(normed_two, halo)
    live = (length - seq_place * rows).astype(jnp.int32)[None]
    result = call(
        out_two_kernel,
        group_count,
        [
            SMEM,
            SMEM,
            whole((2, rows, slots)),
            whole((2, rows, slots)),
            *[HBM] * 3,
            whole((rows, width)),
        ],
        whole((rows, width)),
        jax.ShapeDtypeStruct((rows, width), BF16),
        [
            pltpu.VMEM((rows, width), F32),
            weights_of(SLOT),
            copy_sems(1),
        ],
        "window_out",
    )(places, live, mixed_own, mixed_pair, out_two, *near_out_two, residual)

    result = result.reshape(page_span, group_count, page_share, width).transpose(1, 0, 2, 3)
    return lax.all_to_all(result, "tensor", split_axis=0, concat_axis=0, tiled=True)


def solution(mesh):
    return jax.shard_map(
        on_device,
        mesh=mesh,
        in_specs=(
            P(("dp", "seq"), "tensor", None),
            P(),
            P(),
            P(),
            P(),
            P(None, None, "tensor"),
            P(None, "tensor"),
            P("tensor", None),
            P(),
            P(None, None, "tensor"),
            P(None, None, "tensor"),
            P("tensor", None),
        ),
        out_specs=P("dp", "seq", "tensor", None),
        check_vma=False,
    )
```

```python
import functools

import jax
import jax.numpy as jnp
import numpy as np
from jax import lax
from jax.experimental import pallas as pl
from jax.experimental.pallas import tpu as pltpu
from jax.sharding import PartitionSpec as P

HEAD = 112
WINDOW = 64
EPS = 1e-05
SLOT = 128
FEAT_SLOT = 256
HALO = 80
NEAR = 4
VMEM = 32 * 1024 * 1024
F32 = jnp.float32
BF16 = jnp.bfloat16


def dot(a, b, dims=((1,), (0,))):
    return lax.dot_general(a, b, (dims, ((), ())), preferred_element_type=F32)


def normed_rows(rows, gain):
    scale = lax.rsqrt(jnp.mean(rows * rows, axis=-1, keepdims=True) + EPS)
    return (rows * scale * gain).astype(BF16)


def feature_tables(heads, feature_dim):
    pairs = [(i, j) for i in range(feature_dim) for j in range(i, feature_dim)]
    pairs += [(i, -1) for i in range(feature_dim)] + [(-1, -1)]
    first = np.zeros((2 * heads * feature_dim, heads * FEAT_SLOT), np.float32)
    second = np.zeros_like(first)
    ones = np.zeros((2, heads * FEAT_SLOT), np.float32)
    scale = np.zeros((1, heads * FEAT_SLOT), np.float32)
    for h in range(heads):
        for n, (i, j) in enumerate(pairs):
            at = h * FEAT_SLOT + n
            if i >= 0:
                first[2 * h * feature_dim + i, at] = 1
            else:
                ones[0, at] = 1
            if j >= 0:
                second[2 * h * feature_dim + j, at] = 1
            else:
                ones[1, at] = 1
            if i < 0:
                scale[0, at] = 1
            elif j < 0:
                scale[0, at] = feature_dim**-0.5
            else:
                scale[0, at] = (0.5 if i == j else 1.0) / feature_dim
    return first, second, ones, scale, -(-len(pairs) // 16) * 16


def features(rows, first, second, ones):
    return (dot(rows, first) + ones[0:1]) * (dot(rows, second) + ones[1:2])


def run_copies(copies_of, groups, meanwhile=None):
    step = pl.program_id(0)

    @pl.when(step == 0)
    def _():
        for group in range(groups):
            for copy in copies_of(group):
                copy.start()
        if meanwhile is not None:
            meanwhile()

    for group in range(groups):

        @pl.when(step == group)
        def _(group=group):
            for copy in copies_of(group):
                copy.wait()


def weight_copies(place_ref, piece_refs, targets, sems, group):
    found = []
    for n, piece_ref in enumerate(piece_refs):
        cols = piece_ref.shape[2]
        at = 0
        for own_ref, kind, rows, w_ref, off in targets:
            if group == 0:
                part, head = n // NEAR, n % NEAR
                src = own_ref.at[
                    kind, head * rows : (head + 1) * rows, part * cols : (part + 1) * cols
                ]
            else:
                part, head = place_ref[NEAR], place_ref[n % NEAR]
                if n >= NEAR:
                    part = 1 - part
                src = piece_ref.at[group - 1, at : at + rows, :]
            dst = w_ref.at[group, part, head, off : off + rows, :]
            found.append(pltpu.make_async_copy(src, dst, sems.at[group, len(found)]))
            at += rows
    return found


def zero_between_heads(w_ref):
    groups, parts, heads, rows, cols = w_ref.shape
    for at in range(HEAD, rows, SLOT):
        w_ref[:, :, :, at : at + SLOT - HEAD, :] = jnp.zeros(
            (groups, parts, heads, SLOT - HEAD, cols), BF16
        )


def group_weights(w_ref, step, part):
    heads, rows, cols = w_ref.shape[2:]
    return w_ref[step, part].reshape(heads * rows, cols)


def project(rows_ref, w_ref, step):
    parts, cols = w_ref.shape[1], w_ref.shape[4]
    total = None
    for part in range(parts):
        rows = rows_ref[:, part * cols : (part + 1) * cols]
        share = dot(rows, group_weights(w_ref, step, part), ((1,), (1,)))
        total = share if total is None else total + share
    return total


def linear_kernel(heads, feature_dim, kept, *refs):
    place_ref, x_ref, gain_ref, value_ref, featmap_ref = refs[:5]
    piece_refs = refs[5 : 5 + 2 * NEAR]
    (
        first_ref,
        second_ref,
        ones_ref,
        column_ref,
        num_ref,
        q_ref,
        state_ref,
        state_two_ref,
        normed_ref,
        value_w_ref,
        feat_w_ref,
        sems,
    ) = refs[5 + 2 * NEAR :]
    step = pl.program_id(0)
    targets = [
        (value_ref, 0, HEAD, value_w_ref, 0),
        (featmap_ref, 0, feature_dim, feat_w_ref, 0),
        (featmap_ref, 1, feature_dim, feat_w_ref, feature_dim),
    ]

    @pl.when(step == 0)
    def _():
        zero_between_heads(value_w_ref)

    run_copies(
        functools.partial(weight_copies, place_ref, piece_refs, targets, sems),
        value_w_ref.shape[0],
        lambda: normed_ref.__setitem__(
            ..., normed_rows(x_ref[...].astype(F32), gain_ref[...])
        ),
    )
    rows = x_ref.shape[0]
    width = 2 * heads * feature_dim
    queries = project(normed_ref, feat_w_ref, step).astype(BF16)
    keys = pltpu.roll(queries.astype(F32), width - feature_dim, 1).astype(BF16)
    values = (project(normed_ref, value_w_ref, step) + column_ref[...]).astype(BF16)
    q_ref[0] = queries
    lane = lax.broadcasted_iota(jnp.int32, (rows, width), 1)
    causal = lax.broadcasted_iota(jnp.int32, (rows, rows), 1) <= lax.broadcasted_iota(
        jnp.int32, (rows, rows), 0
    )
    states = []
    key_features = features(keys, first_ref[...], second_ref[...], ones_ref[...]).astype(BF16)
    for h in range(heads):
        at = 2 * h * feature_dim
        own = jnp.where((lane >= at) & (lane < at + feature_dim), queries, jnp.zeros_like(queries))
        scores = dot(own, keys, ((1,), (1,))) * feature_dim**-0.5
        kernel = jnp.where(causal, 1.0 + scores + 0.5 * scores * scores, 0.0).astype(BF16)
        value = values[:, h * SLOT : (h + 1) * SLOT]
        num_ref[0, :, h * SLOT : (h + 1) * SLOT] = dot(kernel, value)
        state = dot(key_features[:, h * FEAT_SLOT : h * FEAT_SLOT + kept], value, ((0,), (0,)))
        states.append(state.astype(BF16))

    @pl.when(step < pl.num_programs(0) // 2)
    def _():
        state_ref[0] = jnp.concatenate(states, axis=0)

    @pl.when(step >= pl.num_programs(0) // 2)
    def _():
        state_two_ref[0] = jnp.concatenate(states, axis=0)


def add_branch(mixed, w_ref, total_ref):
    step = pl.program_id(0)
    parts, cols = w_ref.shape[1], w_ref.shape[4]
    for part in range(parts):
        share = dot(mixed, group_weights(w_ref, step, part)).astype(BF16).astype(F32)
        total_ref[:, part * cols : (part + 1) * cols] += share


def out_one_kernel(heads, kept, *refs):
    place_ref, num_ref, q_ref, first_ref, second_ref, ones_ref, scale_ref, *prior_refs = refs[:9]
    own_ref = refs[9]
    piece_refs = refs[10 : 10 + 2 * NEAR]
    (
        x_ref,
        gain_ref,
        residual_ref,
        normed_ref,
        tail_ref,
        total_ref,
        mixed_ref,
        w_ref,
        sems,
    ) = refs[10 + 2 * NEAR :]
    step = pl.program_id(0)

    @pl.when(step == 0)
    def _():
        total_ref[...] = jnp.zeros_like(total_ref)
        zero_between_heads(w_ref)

    run_copies(
        functools.partial(
            weight_copies, place_ref, piece_refs, [(own_ref, 0, HEAD, w_ref, 0)], sems
        ),
        w_ref.shape[0],
    )

    query_features = features(q_ref[0], first_ref[...], second_ref[...], ones_ref[...])
    query_features = (query_features * scale_ref[...]).astype(BF16)
    for h in range(heads):
        at = slice(h * kept, (h + 1) * kept)
        prior = jnp.where(step < pl.num_programs(0) // 2, *(ref[0, at, :] for ref in prior_refs))
        lanes = slice(h * SLOT, (h + 1) * SLOT)
        total = num_ref[0, :, lanes] + dot(
            query_features[:, h * FEAT_SLOT : h * FEAT_SLOT + kept], prior.astype(BF16)
        )
        mixed_ref[:, lanes] = (total / total[:, HEAD : HEAD + 1]).astype(BF16)
    add_branch(mixed_ref[...], w_ref, total_ref)

    @pl.when(step == pl.num_programs(0) - 1)
    def _():
        residual = (x_ref[...].astype(F32) + total_ref[...]).astype(BF16)
        residual_ref[...] = residual
        normed = normed_rows(residual.astype(F32), gain_ref[...])
        normed_ref[...] = normed
        tail_ref[...] = normed[-HALO:]


def window_kernel(heads, *refs):
    place_ref, first_ref, x_ref, halo_ref, own_ref = refs[:5]
    piece_refs = refs[5 : 5 + 2 * NEAR]
    (
        tap_ref,
        mixed_ref,
        rows_ref,
        w_ref,
        sems,
    ) = refs[5 + 2 * NEAR :]
    step = pl.program_id(0)
    targets = [(own_ref, kind, HEAD, w_ref, kind * SLOT) for kind in range(3)]

    def place_rows():
        rows_ref[:HALO] = halo_ref[...]
        rows_ref[HALO:] = x_ref[...]

    @pl.when(step == 0)
    def _():
        zero_between_heads(w_ref)

    run_copies(
        functools.partial(weight_copies, place_ref, piece_refs, targets, sems),
        w_ref.shape[0],
        place_rows,
    )
    rows = x_ref.shape[0]
    lead = HALO - WINDOW
    projected = project(rows_ref, w_ref, step)
    taps = tap_ref[0]
    convolved = taps[0:1] * projected
    for offset in range(1, taps.shape[0]):
        convolved = convolved + taps[offset : offset + 1] * pltpu.roll(projected, offset, 0)
    convolved = convolved[lead:].astype(BF16)
    tile = 128
    span = tile + WINDOW
    row = lax.broadcasted_iota(jnp.int32, (tile, span), 0)
    col = lax.broadcasted_iota(jnp.int32, (tile, span), 1)
    band = (col > row) & (col <= row + WINDOW)
    for h in range(heads):
        at = 3 * h * SLOT
        queries = convolved[WINDOW:, at : at + SLOT]
        keys = convolved[:, at + SLOT : at + 2 * SLOT]
        values = convolved[:, at + 2 * SLOT : at + 3 * SLOT]
        for start in range(0, rows, tile):
            logits = dot(queries[start : start + tile], keys[start : start + span], ((1,), (1,)))
            allowed = band
            if start < WINDOW:
                allowed = band & (col >= WINDOW - start - first_ref[0])
            logits = jnp.where(allowed, logits * HEAD**-0.5, -jnp.inf)
            weights = jnp.exp(logits - jnp.max(logits, axis=1, keepdims=True))
            weights = weights / jnp.sum(weights, axis=1, keepdims=True)
            mixed = dot(weights.astype(BF16), values[start : start + span])
            mixed_ref[0, start : start + tile, h * SLOT : (h + 1) * SLOT] = mixed.astype(BF16)


def out_two_kernel(*refs):
    place_ref, live_ref, mixed_ref, pair_ref, own_ref = refs[:5]
    piece_refs = refs[5 : 5 + 2 * NEAR]
    (
        residual_ref,
        out_ref,
        total_ref,
        w_ref,
        sems,
    ) = refs[5 + 2 * NEAR :]
    step = pl.program_id(0)

    @pl.when(step == 0)
    def _():
        total_ref[...] = jnp.zeros_like(total_ref)
        zero_between_heads(w_ref)

    run_copies(
        functools.partial(
            weight_copies, place_ref, piece_refs, [(own_ref, 0, HEAD, w_ref, 0)], sems
        ),
        w_ref.shape[0],
    )
    mixed = jnp.where(step < 2, mixed_ref[step % 2], pair_ref[step % 2])
    add_branch(mixed, w_ref, total_ref)

    @pl.when(step == pl.num_programs(0) - 1)
    def _():
        result = (residual_ref[...].astype(F32) + total_ref[...]).astype(BF16)
        row = lax.broadcasted_iota(jnp.int32, result.shape, 0)
        out_ref[...] = jnp.where(row < live_ref[0], result, jnp.zeros_like(result))


def whole(shape):
    return pl.BlockSpec(shape, lambda g: (0,) * len(shape))


def each(shape):
    return pl.BlockSpec((1,) + shape, lambda g: (g,) + (0,) * len(shape))


SMEM = pl.BlockSpec(memory_space=pltpu.SMEM)
HBM = pl.BlockSpec(memory_space=pl.ANY)


def call(kernel, groups, in_specs, out_specs, out_shape, scratch, flops, name):
    return pl.pallas_call(
        kernel,
        grid=(groups,),
        in_specs=in_specs,
        out_specs=out_specs,
        out_shape=out_shape,
        scratch_shapes=scratch,
        compiler_params=pltpu.CompilerParams(
            dimension_semantics=("arbitrary",), vmem_limit_bytes=VMEM
        ),
        cost_estimate=pl.CostEstimate(flops=flops, bytes_accessed=0, transcendentals=0),
        name=name,
    )


def own_piece(whole_weights):
    head, part = lax.axis_index("seq") % NEAR, lax.axis_index("dp")
    found = []
    for weights in whole_weights:
        kinds, rows, cols = weights.shape
        rows, cols = rows // NEAR, cols // lax.axis_size("dp")
        piece = lax.dynamic_slice(weights, (0, head * rows, part * cols), (kinds, rows, cols))
        found.append(piece.reshape(kinds * rows, cols))
    return jnp.concatenate(found, axis=0)


def across(array, axis, bit):
    return lax.ppermute(array, axis, [(i, i ^ bit) for i in range(lax.axis_size(axis))])


def after(array, others):
    if not others:
        return array
    first = [lax.slice(other, (0,) * other.ndim, (1,) * other.ndim) for other in others]
    zero = sum(one.reshape(()).astype(F32) * 0.0 for one in first)
    return jnp.where(zero == 0.0, array, jnp.zeros_like(array))


def settled(array, others=()):
    return lax.optimization_barrier(after(array, others))


def from_group(piece, over_z):
    return across(after(piece, over_z), "tensor", 2)[None]


def from_groups(piece, over_z, order=(0, 1, 2)):
    piece = after(piece, over_z)
    beside, beyond = across(piece, "tensor", 1), across(piece, "tensor", 2)
    found = (beside, beyond, across(beyond, "tensor", 1))
    return [found[n] for n in order]


def neighbours(held):
    return across(held, "seq", 1), across(held, "seq", 2)


def from_plane(held, near_by, diagonal, last):
    beside, above = near_by
    if diagonal is None:
        near = [held, beside, above, across(held, "seq", 3)]
        return near + [across(piece, "dp", 1) for piece in near]
    half = -(-held.shape[1] // 32) * 16
    opposite = [
        across(after(above[:, :half], diagonal), "seq", 1),
        across(after(beside[:, half:], diagonal), "seq", 2),
    ]
    near = [held, beside, above, after(jnp.concatenate(opposite, axis=1), last)]
    return near + [across(piece, "dp", 1) for piece in near]


def earlier_blocks(one, two, axis):
    peers, mine = lax.axis_size(axis), lax.axis_index(axis)
    if peers != 4:
        both = lax.all_gather(jnp.concatenate([one, two]), axis).astype(F32)
        reached = (jnp.arange(peers) < mine)[:, None, None, None]
        total = jnp.sum(jnp.where(reached, both, 0.0), axis=0)
        return total[: one.shape[0]], total[one.shape[0] :]
    upward = [(0, 2), (1, 3)]
    one_beside, two_below = across(one, axis, 1), lax.ppermute(two, axis, upward)
    pair = (one.astype(F32) + one_beside.astype(F32)).astype(one.dtype)
    pair = after(pair, (two_below,))
    two_sent = jnp.where(mine == 2, two.astype(F32), 0.0) + two_below.astype(F32)
    two_sent = jnp.where(mine < 2, two, two_sent.astype(two.dtype))
    one_below, two_beside = lax.ppermute(pair, axis, upward), across(two_sent, axis, 1)
    one_total = jnp.where(mine % 2 == 1, one_beside.astype(F32), 0.0) + one_below.astype(F32)
    two_total = jnp.where(mine > 0, two_beside.astype(F32), 0.0) + two_below.astype(F32)
    return one_total, two_total


def on_device(
    pool,
    page_table,
    reassign,
    lengths,
    gain_one,
    w_featmap,
    w_value,
    w_out_one,
    gain_two,
    w_window,
    conv_window,
    w_out_two,
):
    dp_count, seq_count, group_count = (lax.axis_size(n) for n in ("dp", "seq", "tensor"))
    groups = dp_count * seq_count
    device_place = lax.axis_index(("dp", "seq"))
    dp_place, seq_place, tensor_place = (lax.axis_index(n) for n in ("dp", "seq", "tensor"))
    pages_dev, page_share, width = pool.shape
    slots_total, pages_total = page_table.shape
    req_dev = slots_total // dp_count
    page_span = pages_total // seq_count
    page_rows = page_share * group_count
    rows = page_span * page_rows
    assert req_dev == group_count
    heads = w_value.shape[1] // HEAD
    head_cols = heads * HEAD
    feat_cols = w_featmap.shape[2]
    feature_dim = feat_cols // heads
    tap_count = conv_window.shape[0]

    assert heads == NEAR and dp_count == 2
    values_t = w_value.T[None]
    featmap_t = w_featmap.transpose(1, 2, 0)
    window_t = w_window.transpose(1, 2, 0)
    out_one, out_two = w_out_one[None], w_out_two[None]
    held_one = settled(jnp.stack(from_groups(own_piece([values_t, featmap_t]), ())))

    placed = reassign[:, None] == jnp.arange(slots_total, dtype=jnp.int32)[None, :]
    table = jnp.sum(jnp.where(placed[:, :, None], page_table[None], 0), axis=1)
    slot_lengths = jnp.sum(jnp.where(placed, lengths[None, :], 0), axis=1)
    source_page = (
        table.reshape(dp_count, req_dev, seq_count, page_span)
        .transpose(0, 2, 1, 3)
        .reshape(groups, req_dev * page_span)
    )
    capacity = (pages_dev + groups - 1) // groups
    page_owner = source_page // pages_dev
    pool_slot = source_page % pages_dev
    before = jnp.arange(pages_dev)[None, :] < jnp.arange(pages_dev)[:, None]
    pair_rank = jnp.sum((page_owner[:, :, None] == page_owner[:, None, :]) & before[None], axis=2)
    send_hit = (page_owner == device_place)[:, None, :] & (
        pair_rank[:, None, :] == jnp.arange(capacity)[None, :, None]
    )
    send_slot = jnp.sum(jnp.where(send_hit, pool_slot[:, None, :], 0), axis=2)
    outgoing = pool.at[send_slot.reshape(-1)].get(mode="promise_in_bounds")
    outgoing = outgoing.reshape(groups, capacity, page_share, width)
    arrived = lax.all_to_all(outgoing, ("dp", "seq"), split_axis=0, concat_axis=0, tiled=True)
    own_row = jnp.arange(groups)[:, None] == device_place
    pick_rows = jnp.sum(jnp.where(own_row, page_owner * capacity + pair_rank, 0), axis=0)
    picked = arrived.reshape(groups * capacity, page_share, width)
    picked = picked.at[pick_rows].get(mode="promise_in_bounds")

    picked = after(picked.reshape(req_dev, page_span, page_share, width), (held_one,))
    swapped = lax.all_to_all(picked, "tensor", split_axis=0, concat_axis=0, tiled=True)
    tokens = swapped.transpose(1, 0, 2, 3).reshape(rows, width)
    slot = dp_place * req_dev + tensor_place
    length = jnp.sum(jnp.where(jnp.arange(slots_total) == slot, slot_lengths, 0))

    held_out_one = settled(jnp.stack(from_groups(own_piece([out_one]), (swapped,))))
    near_one = from_plane(held_one, neighbours(held_one), (swapped,), ())
    held_window = from_group(own_piece([window_t]), (held_out_one,))
    held_out_two = from_groups(own_piece([out_two]), (swapped,), (1, 0, 2))
    places = jnp.concatenate([(seq_place % NEAR) ^ jnp.arange(NEAR), dp_place[None]])
    places = places.astype(jnp.int32)
    taps = conv_window.reshape(tap_count, 3, heads, HEAD).transpose(0, 2, 1, 3)
    taps = jnp.pad(taps, ((0, 0), (0, 0), (0, 0), (0, SLOT - HEAD)))
    taps = taps.reshape(tap_count, 3 * heads * SLOT)
    taps = jnp.stack([taps, across(taps, "tensor", 2)])

    first, second, ones, scale, kept = feature_tables(heads, feature_dim)
    first, second = jnp.asarray(first, BF16), jnp.asarray(second, BF16)
    column = np.zeros((1, heads * SLOT), np.float32)
    column[0, HEAD::SLOT] = 1

    def copy_sems(kinds):
        return pltpu.SemaphoreType.DMA((group_count, dp_count * NEAR * kinds))

    def weights_of(rows_of_head):
        return pltpu.VMEM((group_count, dp_count, heads, rows_of_head, width // dp_count), BF16)

    slots = heads * SLOT
    half = group_count // 2
    halves = [
        pl.BlockSpec((1, heads * kept, SLOT), lambda g: (jnp.minimum(g, half - 1), 0, 0)),
        pl.BlockSpec((1, heads * kept, SLOT), lambda g: (jnp.maximum(g - half, 0), 0, 0)),
    ]
    num, queries, state, state_two = call(
        functools.partial(linear_kernel, heads, feature_dim, kept),
        group_count,
        [
            SMEM,
            whole((rows, width)),
            whole((1, width)),
            *[HBM] * (2 + 2 * NEAR),
            whole(first.shape),
            whole(second.shape),
            whole(ones.shape),
            whole(column.shape),
        ],
        [each((rows, slots)), each((rows, 2 * feat_cols)), *halves],
        [
            jax.ShapeDtypeStruct((group_count, rows, slots), F32),
            jax.ShapeDtypeStruct((group_count, rows, 2 * feat_cols), BF16),
            *[jax.ShapeDtypeStruct((group_count // 2, heads * kept, SLOT), BF16)] * 2,
        ],
        [
            pltpu.VMEM((rows, width), BF16),
            weights_of(SLOT),
            weights_of(2 * feature_dim),
            copy_sems(3),
        ],
        2 * group_count * rows * width * 640,
        "linear_rows",
    )(
        places, tokens, gain_one[None], values_t, featmap_t, *near_one, first, second, ones, column
    )
    prior_one, prior_two = earlier_blocks(state, state_two, "seq")
    held_window = after(held_window, (state,))
    near_out_one = from_plane(
        held_out_one, neighbours(held_out_one), (state,), (held_window,)
    )
    residual, normed_two, tail = call(
        functools.partial(out_one_kernel, heads, kept),
        group_count,
        [
            SMEM,
            each((rows, slots)),
            each((rows, 2 * feat_cols)),
            whole(first.shape),
            whole(second.shape),
            whole(ones.shape),
            whole(scale.shape),
        ]
        + halves
        + [HBM] * (1 + 2 * NEAR)
        + [
            whole((rows, width)),
            whole((1, width)),
        ],
        [whole((rows, width)), whole((rows, width)), whole((HALO, width))],
        [jax.ShapeDtypeStruct((n, width), BF16) for n in (rows, rows, HALO)],
        [
            pltpu.VMEM((rows, width), F32),
            pltpu.VMEM((rows, slots), BF16),
            weights_of(SLOT),
            copy_sems(1),
        ],
        2 * group_count * rows * width * 640,
        "linear_out",
    )(
        places, num, queries, first, second, ones, scale, prior_one, prior_two, out_one, *near_out_one, tokens,
        gain_two[None],
    )

    halo = lax.ppermute(tail, "seq", [(i, i + 1) for i in range(seq_count - 1)])
    pair_rows = across(normed_two, "tensor", 1)
    pair_halo = across(halo, "tensor", 1)
    held_window = after(held_window, (prior_one,))
    held_out_two = settled(jnp.stack(held_out_two), (residual,))
    near_window = from_plane(held_window, neighbours(held_window), None, ())
    block_start = (seq_place * rows).astype(jnp.int32)[None]

    def window_rows(slot_rows, slot_halo):
        return call(
            functools.partial(window_kernel, heads),
            2,
            [
                SMEM,
                SMEM,
                whole((rows, width)),
                whole((HALO, width)),
                *[HBM] * (1 + 2 * NEAR),
                each((tap_count, 3 * slots)),
            ],
            each((rows, slots)),
            jax.ShapeDtypeStruct((2, rows, slots), BF16),
            [
                pltpu.VMEM((HALO + rows, width), BF16),
                pltpu.VMEM((2, dp_count, heads, 3 * SLOT, width // dp_count), BF16),
                copy_sems(3),
            ],
            6 * rows * width * 3 * head_cols,
        "window_rows",
        )(places, block_start, slot_rows, slot_halo, window_t, *near_window, taps)

    mixed_pair = window_rows(pair_rows, pair_halo)
    back = across(mixed_pair, "tensor", 1)
    mixed_own = window_rows(normed_two, halo)
    near_out_two = from_plane(
        held_out_two, neighbours(held_out_two), (mixed_pair,), (back, mixed_own)
    )
    live = (length - seq_place * rows).astype(jnp.int32)[None]
    result = call(
        out_two_kernel,
        group_count,
        [
            SMEM,
            SMEM,
            whole((2, rows, slots)),
            whole((2, rows, slots)),
            *[HBM] * (1 + 2 * NEAR),
            whole((rows, width)),
        ],
        whole((rows, width)),
        jax.ShapeDtypeStruct((rows, width), BF16),
        [
            pltpu.VMEM((rows, width), F32),
            weights_of(SLOT),
            copy_sems(1),
        ],
        2 * group_count * rows * width * head_cols,
        "window_out",
    )(places, live, mixed_own, back, out_two, *near_out_two, residual)

    result = result.reshape(page_span, group_count, page_share, width).transpose(1, 0, 2, 3)
    return lax.all_to_all(result, "tensor", split_axis=0, concat_axis=0, tiled=True)


def solution(mesh):
    return jax.shard_map(
        on_device,
        mesh=mesh,
        in_specs=(
            P(("dp", "seq"), "tensor", None),
            P(),
            P(),
            P(),
            P(),
            P(None, None, "tensor"),
            P(None, "tensor"),
            P("tensor", None),
            P(),
            P(None, None, "tensor"),
            P(None, None, "tensor"),
            P("tensor", None),
        ),
        out_specs=P("dp", "seq", "tensor", None),
        check_vma=False,
    )
```

```python
import functools

import jax
import jax.numpy as jnp
import numpy as np
from jax import lax
from jax.experimental import pallas as pl
from jax.experimental.pallas import tpu as pltpu
from jax.sharding import PartitionSpec as P

HEAD = 112
WINDOW = 64
EPS = 1e-05
SLOT = 128
FEAT_SLOT = 256
HALO = 80
NEAR = 4
VMEM = 32 * 1024 * 1024
F32 = jnp.float32
BF16 = jnp.bfloat16


def dot(a, b, dims=((1,), (0,))):
    return lax.dot_general(a, b, (dims, ((), ())), preferred_element_type=F32)


def normed_rows(rows, gain):
    scale = lax.rsqrt(jnp.mean(rows * rows, axis=-1, keepdims=True) + EPS)
    return (rows * scale * gain).astype(BF16)


def feature_tables(heads, feature_dim):
    pairs = [(i, j) for i in range(feature_dim) for j in range(i, feature_dim)]
    pairs += [(i, -1) for i in range(feature_dim)] + [(-1, -1)]
    first = np.zeros((2 * heads * feature_dim, heads * FEAT_SLOT), np.float32)
    second = np.zeros_like(first)
    ones = np.zeros((2, heads * FEAT_SLOT), np.float32)
    scale = np.zeros((1, heads * FEAT_SLOT), np.float32)
    for h in range(heads):
        for n, (i, j) in enumerate(pairs):
            at = h * FEAT_SLOT + n
            if i >= 0:
                first[2 * h * feature_dim + i, at] = 1
            else:
                ones[0, at] = 1
            if j >= 0:
                second[2 * h * feature_dim + j, at] = 1
            else:
                ones[1, at] = 1
            if i < 0:
                scale[0, at] = 1
            elif j < 0:
                scale[0, at] = feature_dim**-0.5
            else:
                scale[0, at] = (0.5 if i == j else 1.0) / feature_dim
    return first, second, ones, scale, -(-len(pairs) // 16) * 16


def features(rows, first, second, ones):
    return (dot(rows, first) + ones[0:1]) * (dot(rows, second) + ones[1:2])


def run_copies(copies_of, groups, meanwhile=None):
    step = pl.program_id(0)

    @pl.when(step == 0)
    def _():
        for group in range(groups):
            for copy in copies_of(group):
                copy.start()
        if meanwhile is not None:
            meanwhile()

    for group in range(groups):

        @pl.when(step == group)
        def _(group=group):
            for copy in copies_of(group):
                copy.wait()


def weight_copies(place_ref, near_ref, far_ref, targets, sems, group):
    near = near_ref.shape[0]
    cols = near_ref.shape[3]
    found = []
    for n in range(2 * near):
        at = 0
        for own_ref, kind, rows, w_ref, off in targets:
            if group == 0:
                part, head = n // near, n % near
                src = own_ref.at[
                    kind, head * rows : (head + 1) * rows, part * cols : (part + 1) * cols
                ]
            else:
                part, head = place_ref[near], place_ref[n % near]
                if n >= near:
                    part = 1 - part
                src = (near_ref if n < near else far_ref).at[
                    n % near, group - 1, at : at + rows, :
                ]
            dst = w_ref.at[group, part, head, off : off + rows, :]
            found.append(pltpu.make_async_copy(src, dst, sems.at[group, len(found)]))
            at += rows
    return found


def zero_between_heads(w_ref):
    groups, parts, heads, rows, cols = w_ref.shape
    for at in range(HEAD, rows, SLOT):
        w_ref[:, :, :, at : at + SLOT - HEAD, :] = jnp.zeros(
            (groups, parts, heads, SLOT - HEAD, cols), BF16
        )


def group_weights(w_ref, step, part):
    heads, rows, cols = w_ref.shape[2:]
    return w_ref[step, part].reshape(heads * rows, cols)


def project(rows_ref, w_ref, step):
    parts, cols = w_ref.shape[1], w_ref.shape[4]
    total = None
    for part in range(parts):
        rows = rows_ref[:, part * cols : (part + 1) * cols]
        share = dot(rows, group_weights(w_ref, step, part), ((1,), (1,)))
        total = share if total is None else total + share
    return total


def linear_kernel(
    heads,
    feature_dim,
    kept,
    place_ref,
    x_ref,
    gain_ref,
    value_ref,
    featmap_ref,
    near_ref,
    far_ref,
    first_ref,
    second_ref,
    ones_ref,
    column_ref,
    num_ref,
    q_ref,
    state_ref,
    normed_ref,
    value_w_ref,
    feat_w_ref,
    sems,
):
    step = pl.program_id(0)
    targets = [
        (value_ref, 0, HEAD, value_w_ref, 0),
        (featmap_ref, 0, feature_dim, feat_w_ref, 0),
        (featmap_ref, 1, feature_dim, feat_w_ref, feature_dim),
    ]

    @pl.when(step == 0)
    def _():
        zero_between_heads(value_w_ref)

    run_copies(
        functools.partial(weight_copies, place_ref, near_ref, far_ref, targets, sems),
        value_w_ref.shape[0],
        lambda: normed_ref.__setitem__(
            ..., normed_rows(x_ref[...].astype(F32), gain_ref[...])
        ),
    )
    rows = x_ref.shape[0]
    width = 2 * heads * feature_dim
    queries = project(normed_ref, feat_w_ref, step).astype(BF16)
    keys = pltpu.roll(queries.astype(F32), width - feature_dim, 1).astype(BF16)
    values = (project(normed_ref, value_w_ref, step) + column_ref[...]).astype(BF16)
    q_ref[0] = queries
    lane = lax.broadcasted_iota(jnp.int32, (rows, width), 1)
    causal = lax.broadcasted_iota(jnp.int32, (rows, rows), 1) <= lax.broadcasted_iota(
        jnp.int32, (rows, rows), 0
    )
    key_features = features(keys, first_ref[...], second_ref[...], ones_ref[...]).astype(BF16)
    for h in range(heads):
        at = 2 * h * feature_dim
        own = jnp.where((lane >= at) & (lane < at + feature_dim), queries, jnp.zeros_like(queries))
        scores = dot(own, keys, ((1,), (1,))) * feature_dim**-0.5
        kernel = jnp.where(causal, 1.0 + scores + 0.5 * scores * scores, 0.0).astype(BF16)
        value = values[:, h * SLOT : (h + 1) * SLOT]
        num_ref[0, :, h * SLOT : (h + 1) * SLOT] = dot(kernel, value)
        state = dot(key_features[:, h * FEAT_SLOT : h * FEAT_SLOT + kept], value, ((0,), (0,)))
        state_ref[0, h * kept : (h + 1) * kept, :] = state.astype(BF16)


def add_branch(mixed, w_ref, total_ref):
    step = pl.program_id(0)
    parts, cols = w_ref.shape[1], w_ref.shape[4]
    for part in range(parts):
        share = dot(mixed, group_weights(w_ref, step, part)).astype(BF16).astype(F32)
        total_ref[:, part * cols : (part + 1) * cols] += share


def out_one_kernel(
    heads,
    kept,
    place_ref,
    num_ref,
    q_ref,
    first_ref,
    second_ref,
    ones_ref,
    scale_ref,
    prior_ref,
    own_ref,
    near_ref,
    far_ref,
    x_ref,
    gain_ref,
    residual_ref,
    normed_ref,
    tail_ref,
    total_ref,
    mixed_ref,
    w_ref,
    sems,
):
    step = pl.program_id(0)

    @pl.when(step == 0)
    def _():
        total_ref[...] = jnp.zeros_like(total_ref)
        zero_between_heads(w_ref)

    run_copies(
        functools.partial(
            weight_copies, place_ref, near_ref, far_ref, [(own_ref, 0, HEAD, w_ref, 0)], sems
        ),
        w_ref.shape[0],
    )

    query_features = features(q_ref[0], first_ref[...], second_ref[...], ones_ref[...])
    query_features = (query_features * scale_ref[...]).astype(BF16)
    for h in range(heads):
        at = slice(h * kept, (h + 1) * kept)
        prior = prior_ref[0, at, :]
        lanes = slice(h * SLOT, (h + 1) * SLOT)
        total = num_ref[0, :, lanes] + dot(
            query_features[:, h * FEAT_SLOT : h * FEAT_SLOT + kept], prior.astype(BF16)
        )
        mixed_ref[:, lanes] = (total / total[:, HEAD : HEAD + 1]).astype(BF16)
    add_branch(mixed_ref[...], w_ref, total_ref)

    @pl.when(step == pl.num_programs(0) - 1)
    def _():
        residual = (x_ref[...].astype(F32) + total_ref[...]).astype(BF16)
        residual_ref[...] = residual
        normed = normed_rows(residual.astype(F32), gain_ref[...])
        normed_ref[...] = normed
        tail_ref[...] = normed[-HALO:]


def window_kernel(
    heads,
    place_ref,
    first_ref,
    x_ref,
    halo_ref,
    own_ref,
    near_ref,
    far_ref,
    tap_ref,
    _,
    mixed_ref,
    rows_ref,
    w_ref,
    sems,
):
    step = pl.program_id(0)
    targets = [(own_ref, kind, HEAD, w_ref, kind * SLOT) for kind in range(3)]

    def place_rows():
        rows_ref[:HALO] = halo_ref[...]
        rows_ref[HALO:] = x_ref[...]

    @pl.when(step == 0)
    def _():
        zero_between_heads(w_ref)

    run_copies(
        functools.partial(weight_copies, place_ref, near_ref, far_ref, targets, sems),
        w_ref.shape[0],
        place_rows,
    )
    rows = x_ref.shape[0]
    lead = HALO - WINDOW
    projected = project(rows_ref, w_ref, step)
    taps = tap_ref[0]
    convolved = taps[0:1] * projected
    for offset in range(1, taps.shape[0]):
        convolved = convolved + taps[offset : offset + 1] * pltpu.roll(projected, offset, 0)
    convolved = convolved[lead:].astype(BF16)
    tile = 128
    span = tile + WINDOW
    row = lax.broadcasted_iota(jnp.int32, (tile, span), 0)
    col = lax.broadcasted_iota(jnp.int32, (tile, span), 1)
    band = (col > row) & (col <= row + WINDOW)
    for h in range(heads):
        at = 3 * h * SLOT
        queries = convolved[WINDOW:, at : at + SLOT]
        keys = convolved[:, at + SLOT : at + 2 * SLOT]
        values = convolved[:, at + 2 * SLOT : at + 3 * SLOT]
        for start in range(0, rows, tile):
            logits = dot(queries[start : start + tile], keys[start : start + span], ((1,), (1,)))
            allowed = band
            if start < WINDOW:
                allowed = band & (col >= WINDOW - start - first_ref[0])
            logits = jnp.where(allowed, logits * HEAD**-0.5, -jnp.inf)
            weights = jnp.exp(logits - jnp.max(logits, axis=1, keepdims=True))
            weights = weights / jnp.sum(weights, axis=1, keepdims=True)
            mixed = dot(weights.astype(BF16), values[start : start + span])
            mixed_ref[0, start : start + tile, h * SLOT : (h + 1) * SLOT] = mixed.astype(BF16)


def out_two_kernel(
    place_ref,
    live_ref,
    mixed_ref,
    pair_ref,
    own_ref,
    near_ref,
    far_ref,
    residual_ref,
    out_ref,
    total_ref,
    w_ref,
    sems,
):
    step = pl.program_id(0)

    @pl.when(step == 0)
    def _():
        total_ref[...] = jnp.zeros_like(total_ref)
        zero_between_heads(w_ref)

    run_copies(
        functools.partial(
            weight_copies, place_ref, near_ref, far_ref, [(own_ref, 0, HEAD, w_ref, 0)], sems
        ),
        w_ref.shape[0],
    )
    mixed = jnp.where(step < 2, mixed_ref[step % 2], pair_ref[step % 2])
    add_branch(mixed, w_ref, total_ref)

    @pl.when(step == pl.num_programs(0) - 1)
    def _():
        result = (residual_ref[...].astype(F32) + total_ref[...]).astype(BF16)
        row = lax.broadcasted_iota(jnp.int32, result.shape, 0)
        out_ref[...] = jnp.where(row < live_ref[0], result, jnp.zeros_like(result))


def whole(shape):
    return pl.BlockSpec(shape, lambda g: (0,) * len(shape))


def each(shape):
    return pl.BlockSpec((1,) + shape, lambda g: (g,) + (0,) * len(shape))


SMEM = pl.BlockSpec(memory_space=pltpu.SMEM)
HBM = pl.BlockSpec(memory_space=pl.ANY)


def call(kernel, groups, in_specs, out_specs, out_shape, scratch, name, flops=0):
    return pl.pallas_call(
        kernel,
        grid=(groups,),
        in_specs=in_specs,
        out_specs=out_specs,
        out_shape=out_shape,
        scratch_shapes=scratch,
        compiler_params=pltpu.CompilerParams(
            dimension_semantics=("arbitrary",), vmem_limit_bytes=VMEM
        ),
        cost_estimate=pl.CostEstimate(flops=flops, bytes_accessed=0, transcendentals=0),
        name=name,
    )


def own_piece(whole_weights):
    head, part = lax.axis_index("seq") % NEAR, lax.axis_index("dp")
    found = []
    for weights in whole_weights:
        kinds, rows, cols = weights.shape
        rows, cols = rows // NEAR, cols // lax.axis_size("dp")
        piece = lax.dynamic_slice(weights, (0, head * rows, part * cols), (kinds, rows, cols))
        found.append(piece.reshape(kinds * rows, cols))
    return jnp.concatenate(found, axis=0)


def across(array, axis, bit):
    return lax.ppermute(array, axis, [(i, i ^ bit) for i in range(lax.axis_size(axis))])


def after(array, others):
    if not others:
        return array
    first = [lax.slice(other, (0,) * other.ndim, (1,) * other.ndim) for other in others]
    zero = sum(one.reshape(()).astype(F32) * 0.0 for one in first)
    return jnp.where(zero == 0.0, array, jnp.zeros_like(array))


def settled(array, others=()):
    return lax.optimization_barrier(after(array, others))


def from_group(piece, over_z):
    return across(after(piece, over_z), "tensor", 2)[None]


def from_groups(piece, over_z, order=(0, 1, 2)):
    piece = after(piece, over_z)
    beside, beyond = across(piece, "tensor", 1), across(piece, "tensor", 2)
    found = (beside, beyond, across(beyond, "tensor", 1))
    return [found[n] for n in order]


def neighbours(held):
    return across(held, "seq", 1), across(held, "seq", 2)


def from_plane(held, near_by, diagonal, over_cores):
    beside, above = near_by
    if diagonal is None:
        opposite = across(held, "seq", 3)
    else:
        half = -(-held.shape[1] // 32) * 16
        opposite = [
            across(after(above[:, :half], diagonal), "seq", 1),
            across(after(beside[:, half:], diagonal), "seq", 2),
        ]
        opposite = after(jnp.concatenate(opposite, axis=1), over_cores)
    near = after(jnp.stack([held, beside, above, opposite]), over_cores)
    return near, across(near, "dp", 1)


def earlier_blocks(state, axis):
    peers = lax.axis_size(axis)
    if peers <= 4:
        found = [
            lax.ppermute(state, axis, [(i, i + by) for i in range(peers - by)])
            for by in range(1, peers)
        ]
        return sum(one.astype(F32) for one in found)
    everything = lax.all_gather(state, axis).astype(F32)
    reached = jnp.arange(peers) < lax.axis_index(axis)
    return jnp.sum(jnp.where(reached[:, None, None, None], everything, 0.0), axis=0)


def on_device(
    pool,
    page_table,
    reassign,
    lengths,
    gain_one,
    w_featmap,
    w_value,
    w_out_one,
    gain_two,
    w_window,
    conv_window,
    w_out_two,
):
    dp_count, seq_count, group_count = (lax.axis_size(n) for n in ("dp", "seq", "tensor"))
    groups = dp_count * seq_count
    device_place = lax.axis_index(("dp", "seq"))
    dp_place, seq_place, tensor_place = (lax.axis_index(n) for n in ("dp", "seq", "tensor"))
    pages_dev, page_share, width = pool.shape
    slots_total, pages_total = page_table.shape
    req_dev = slots_total // dp_count
    page_span = pages_total // seq_count
    page_rows = page_share * group_count
    rows = page_span * page_rows
    assert req_dev == group_count
    heads = w_value.shape[1] // HEAD
    head_cols = heads * HEAD
    feat_cols = w_featmap.shape[2]
    feature_dim = feat_cols // heads
    tap_count = conv_window.shape[0]

    assert heads == NEAR and dp_count == 2
    values_t = w_value.T[None]
    featmap_t = w_featmap.transpose(1, 2, 0)
    window_t = w_window.transpose(1, 2, 0)
    out_one, out_two = w_out_one[None], w_out_two[None]
    held_one = settled(jnp.stack(from_groups(own_piece([values_t, featmap_t]), ())))

    placed = reassign[:, None] == jnp.arange(slots_total, dtype=jnp.int32)[None, :]
    table = jnp.sum(jnp.where(placed[:, :, None], page_table[None], 0), axis=1)
    slot_lengths = jnp.sum(jnp.where(placed, lengths[None, :], 0), axis=1)
    source_page = (
        table.reshape(dp_count, req_dev, seq_count, page_span)
        .transpose(0, 2, 1, 3)
        .reshape(groups, req_dev * page_span)
    )
    capacity = (pages_dev + groups - 1) // groups
    page_owner = source_page // pages_dev
    pool_slot = source_page % pages_dev
    before = jnp.arange(pages_dev)[None, :] < jnp.arange(pages_dev)[:, None]
    pair_rank = jnp.sum((page_owner[:, :, None] == page_owner[:, None, :]) & before[None], axis=2)
    send_hit = (page_owner == device_place)[:, None, :] & (
        pair_rank[:, None, :] == jnp.arange(capacity)[None, :, None]
    )
    send_slot = jnp.sum(jnp.where(send_hit, pool_slot[:, None, :], 0), axis=2)
    outgoing = pool.at[send_slot.reshape(-1)].get(mode="promise_in_bounds")
    outgoing = outgoing.reshape(groups, capacity, page_share, width)
    arrived = lax.all_to_all(outgoing, ("dp", "seq"), split_axis=0, concat_axis=0, tiled=True)
    own_row = jnp.arange(groups)[:, None] == device_place
    pick_rows = jnp.sum(jnp.where(own_row, page_owner * capacity + pair_rank, 0), axis=0)
    picked = arrived.reshape(groups * capacity, page_share, width)
    picked = picked.at[pick_rows].get(mode="promise_in_bounds")

    picked = after(picked.reshape(req_dev, page_span, page_share, width), (held_one,))
    swapped = lax.all_to_all(picked, "tensor", split_axis=0, concat_axis=0, tiled=True)
    tokens = swapped.transpose(1, 0, 2, 3).reshape(rows, width)
    slot = dp_place * req_dev + tensor_place
    length = jnp.sum(jnp.where(jnp.arange(slots_total) == slot, slot_lengths, 0))

    held_out_one = settled(jnp.stack(from_groups(own_piece([out_one]), (picked,))))
    near_one = from_plane(held_one, neighbours(held_one), (swapped,), (held_out_one,))
    out_piece = after(own_piece([out_two]), (swapped,))
    beyond = from_group(own_piece([window_t, out_two]), (swapped,))
    places = jnp.concatenate([(seq_place % NEAR) ^ jnp.arange(NEAR), dp_place[None]])
    places = places.astype(jnp.int32)
    taps = conv_window.reshape(tap_count, 3, heads, HEAD).transpose(0, 2, 1, 3)
    taps = jnp.pad(taps, ((0, 0), (0, 0), (0, 0), (0, SLOT - HEAD)))
    taps = taps.reshape(tap_count, 3 * heads * SLOT)
    taps = jnp.stack([taps, across(taps, "tensor", 2)])

    first, second, ones, scale, kept = feature_tables(heads, feature_dim)
    first, second = jnp.asarray(first, BF16), jnp.asarray(second, BF16)
    column = np.zeros((1, heads * SLOT), np.float32)
    column[0, HEAD::SLOT] = 1

    def copy_sems(kinds):
        return pltpu.SemaphoreType.DMA((group_count, dp_count * NEAR * kinds))

    def weights_of(rows_of_head):
        return pltpu.VMEM((group_count, dp_count, heads, rows_of_head, width // dp_count), BF16)

    slots = heads * SLOT
    num, queries, state = call(
        functools.partial(linear_kernel, heads, feature_dim, kept),
        group_count,
        [
            SMEM,
            whole((rows, width)),
            whole((1, width)),
            *[HBM] * 4,
            whole(first.shape),
            whole(second.shape),
            whole(ones.shape),
            whole(column.shape),
        ],
        [each((rows, slots)), each((rows, 2 * feat_cols)), each((heads * kept, SLOT))],
        [
            jax.ShapeDtypeStruct((group_count, rows, slots), F32),
            jax.ShapeDtypeStruct((group_count, rows, 2 * feat_cols), BF16),
            jax.ShapeDtypeStruct((group_count, heads * kept, SLOT), BF16),
        ],
        [
            pltpu.VMEM((rows, width), BF16),
            weights_of(SLOT),
            weights_of(2 * feature_dim),
            copy_sems(3),
        ],
        "linear_rows",
    )(
        places, tokens, gain_one[None], values_t, featmap_t, *near_one, first, second, ones, column
    )
    prior = settled(earlier_blocks(state, "seq"))
    beyond = after(beyond, (state,))
    held_window, out_beyond = beyond[:, : 3 * HEAD], beyond[0, 3 * HEAD :]
    held_out_two = [out_beyond, across(out_piece, "tensor", 1), across(out_beyond, "tensor", 1)]
    held_out_two = settled(jnp.stack(held_out_two), (prior,))
    near_out_one = from_plane(
        held_out_one, neighbours(held_out_one), (state,), (beyond, held_out_two)
    )
    held_window = after(held_window, (prior,))
    near_by_window = neighbours(held_window)
    residual, normed_two, tail = call(
        functools.partial(out_one_kernel, heads, kept),
        group_count,
        [
            SMEM,
            each((rows, slots)),
            each((rows, 2 * feat_cols)),
            whole(first.shape),
            whole(second.shape),
            whole(ones.shape),
            whole(scale.shape),
        ]
        + [each((heads * kept, SLOT))]
        + [HBM] * 3
        + [
            whole((rows, width)),
            whole((1, width)),
        ],
        [whole((rows, width)), whole((rows, width)), whole((HALO, width))],
        [jax.ShapeDtypeStruct((n, width), BF16) for n in (rows, rows, HALO)],
        [
            pltpu.VMEM((rows, width), F32),
            pltpu.VMEM((rows, slots), BF16),
            weights_of(SLOT),
            copy_sems(1),
        ],
        "linear_out",
    )(
        places, num, queries, first, second, ones, scale, prior, out_one, *near_out_one, tokens,
        gain_two[None],
    )

    halo = lax.ppermute(tail, "seq", [(i, i + 1) for i in range(seq_count - 1)])
    pair_rows = across(normed_two, "tensor", 1)
    pair_halo = lax.ppermute(
        tail,
        ("seq", "tensor"),
        [
            (i * group_count + j, (i + 1) * group_count + (j ^ 1))
            for i in range(seq_count - 1)
            for j in range(group_count)
        ],
    )
    near_window = from_plane(held_window, near_by_window, None, (residual,))
    held_out_two = after(held_out_two, (residual,))
    block_start = (seq_place * rows).astype(jnp.int32)[None]

    def window_rows(slot_rows, slot_halo, earlier):
        return call(
            functools.partial(window_kernel, heads),
            2,
            [
                SMEM,
                SMEM,
                whole((rows, width)),
                whole((HALO, width)),
                *[HBM] * 3,
                each((tap_count, 3 * slots)),
                HBM,
            ],
            each((rows, slots)),
            jax.ShapeDtypeStruct((2, rows, slots), BF16),
            [
                pltpu.VMEM((HALO + rows, width), BF16),
                pltpu.VMEM((2, dp_count, heads, 3 * SLOT, width // dp_count), BF16),
                copy_sems(3),
            ],
            "window_rows",
            6 * rows * width * 3 * head_cols,
        )(places, block_start, slot_rows, slot_halo, window_t, *near_window, taps, earlier)

    mixed_own = window_rows(normed_two, halo, normed_two)
    mixed_pair = window_rows(pair_rows, pair_halo, mixed_own)
    near_out_two = from_plane(held_out_two, neighbours(held_out_two), None, (mixed_pair,))
    mixed_pair = across(mixed_pair, "tensor", 1)
    live = (length - seq_place * rows).astype(jnp.int32)[None]
    result = call(
        out_two_kernel,
        group_count,
        [
            SMEM,
            SMEM,
            whole((2, rows, slots)),
            whole((2, rows, slots)),
            *[HBM] * 3,
            whole((rows, width)),
        ],
        whole((rows, width)),
        jax.ShapeDtypeStruct((rows, width), BF16),
        [
            pltpu.VMEM((rows, width), F32),
            weights_of(SLOT),
            copy_sems(1),
        ],
        "window_out",
    )(places, live, mixed_own, mixed_pair, out_two, *near_out_two, residual)

    result = result.reshape(page_span, group_count, page_share, width).transpose(1, 0, 2, 3)
    return lax.all_to_all(result, "tensor", split_axis=0, concat_axis=0, tiled=True)


def solution(mesh):
    return jax.shard_map(
        on_device,
        mesh=mesh,
        in_specs=(
            P(("dp", "seq"), "tensor", None),
            P(),
            P(),
            P(),
            P(),
            P(None, None, "tensor"),
            P(None, "tensor"),
            P("tensor", None),
            P(),
            P(None, None, "tensor"),
            P(None, None, "tensor"),
            P("tensor", None),
        ),
        out_specs=P("dp", "seq", "tensor", None),
        check_vma=False,
    )
```

```python
import functools

import jax
import jax.numpy as jnp
import numpy as np
from jax import lax
from jax.experimental import pallas as pl
from jax.experimental.pallas import tpu as pltpu
from jax.sharding import PartitionSpec as P

HEAD = 112
WINDOW = 64
EPS = 1e-05
SLOT = 128
FEAT_SLOT = 256
HALO = 80
NEAR = 4
VMEM = 60 * 1024 * 1024
F32 = jnp.float32
BF16 = jnp.bfloat16


def dot(a, b, dims=((1,), (0,))):
    return lax.dot_general(a, b, (dims, ((), ())), preferred_element_type=F32)


def normed_rows(rows, gain):
    scale = lax.rsqrt(jnp.mean(rows * rows, axis=-1, keepdims=True) + EPS)
    return (rows * scale * gain).astype(BF16)


def feature_tables(heads, feature_dim):
    pairs = [(i, j) for i in range(feature_dim) for j in range(i, feature_dim)]
    pairs += [(i, -1) for i in range(feature_dim)] + [(-1, -1)]
    first = np.zeros((2 * heads * feature_dim, heads * FEAT_SLOT), np.float32)
    second = np.zeros_like(first)
    ones = np.zeros((2, heads * FEAT_SLOT), np.float32)
    scale = np.zeros((1, heads * FEAT_SLOT), np.float32)
    for h in range(heads):
        for n, (i, j) in enumerate(pairs):
            at = h * FEAT_SLOT + n
            if i >= 0:
                first[2 * h * feature_dim + i, at] = 1
            else:
                ones[0, at] = 1
            if j >= 0:
                second[2 * h * feature_dim + j, at] = 1
            else:
                ones[1, at] = 1
            if i < 0:
                scale[0, at] = 1
            elif j < 0:
                scale[0, at] = feature_dim**-0.5
            else:
                scale[0, at] = (0.5 if i == j else 1.0) / feature_dim
    return first, second, ones, scale, -(-len(pairs) // 16) * 16


def features(rows, first, second, ones):
    return (dot(rows, first) + ones[0:1]) * (dot(rows, second) + ones[1:2])


def run_copies(copies_of, groups, meanwhile=None):
    step = pl.program_id(0)

    @pl.when(step == 0)
    def _():
        for group in range(groups):
            for copy in copies_of(group):
                copy.start()
        if meanwhile is not None:
            meanwhile()

    for group in range(groups):

        @pl.when(step == group)
        def _(group=group):
            for copy in copies_of(group):
                copy.wait()


def weight_copies(place_ref, near_ref, far_ref, targets, pieces, sems, group):
    found = []

    def copy(src, dst):
        found.append(pltpu.make_async_copy(src, dst, sems.at[group, len(found)]))

    if group == 0:
        for own_ref, kind, w_ref, off in targets:
            rows = own_ref.shape[2]
            for n in range(NEAR):
                copy(own_ref.at[kind, place_ref[n]], w_ref.at[0, n, off : off + rows, :])
        return found
    cols = near_ref.shape[3]
    for ref, part in ((near_ref, place_ref[NEAR]), (far_ref, 1 - place_ref[NEAR])):
        at = 0
        lanes = pl.ds(pl.multiple_of(part * cols, SLOT), cols)
        for rows, w_ref, off in pieces:
            copy(ref.at[:, group - 1, at : at + rows, :], w_ref.at[group, :, off : off + rows, lanes])
            at += rows
    return found


def zero_between_heads(w_ref):
    groups, heads, rows, width = w_ref.shape
    for at in range(HEAD, rows, SLOT):
        w_ref[:, :, at : at + SLOT - HEAD, :] = jnp.zeros(
            (groups, heads, SLOT - HEAD, width), BF16
        )


def group_weights(w_ref, step):
    heads, rows, width = w_ref.shape[1:]
    return w_ref[step].reshape(heads * rows, width)


def project(rows_ref, w_ref, step):
    return dot(rows_ref[...], group_weights(w_ref, step), ((1,), (1,)))


def linear_kernel(
    heads,
    feature_dim,
    kept,
    place_ref,
    x_ref,
    gain_ref,
    value_ref,
    featmap_ref,
    near_ref,
    far_ref,
    first_ref,
    second_ref,
    ones_ref,
    column_ref,
    num_ref,
    q_ref,
    state_ref,
    normed_ref,
    value_w_ref,
    feat_w_ref,
    sems,
):
    step = pl.program_id(0)
    targets = [
        (value_ref, 0, value_w_ref, 0),
        (featmap_ref, 0, feat_w_ref, 0),
        (featmap_ref, 1, feat_w_ref, feature_dim),
    ]
    pieces = [(HEAD, value_w_ref, 0), (2 * feature_dim, feat_w_ref, 0)]

    @pl.when(step == 0)
    def _():
        zero_between_heads(value_w_ref)

    run_copies(
        functools.partial(weight_copies, place_ref, near_ref, far_ref, targets, pieces, sems),
        value_w_ref.shape[0],
        lambda: normed_ref.__setitem__(
            ..., normed_rows(x_ref[...].astype(F32), gain_ref[...])
        ),
    )
    rows = x_ref.shape[0]
    width = 2 * heads * feature_dim
    queries = project(normed_ref, feat_w_ref, step).astype(BF16)
    keys = pltpu.roll(queries.astype(F32), width - feature_dim, 1).astype(BF16)
    values = (project(normed_ref, value_w_ref, step) + column_ref[...]).astype(BF16)
    q_ref[0] = queries
    lane = lax.broadcasted_iota(jnp.int32, (rows, width), 1)
    causal = lax.broadcasted_iota(jnp.int32, (rows, rows), 1) <= lax.broadcasted_iota(
        jnp.int32, (rows, rows), 0
    )
    key_features = features(keys, first_ref[...], second_ref[...], ones_ref[...]).astype(BF16)
    for h in range(heads):
        at = 2 * h * feature_dim
        own = jnp.where((lane >= at) & (lane < at + feature_dim), queries, jnp.zeros_like(queries))
        scores = dot(own, keys, ((1,), (1,))) * feature_dim**-0.5
        kernel = jnp.where(causal, 1.0 + scores + 0.5 * scores * scores, 0.0).astype(BF16)
        value = values[:, h * SLOT : (h + 1) * SLOT]
        num_ref[0, :, h * SLOT : (h + 1) * SLOT] = dot(kernel, value)
        state = dot(key_features[:, h * FEAT_SLOT : h * FEAT_SLOT + kept], value, ((0,), (0,)))
        head = pl.multiple_of(place_ref[h] * kept, 16)
        state_ref[0, pl.ds(head, kept), :] = state.astype(BF16)


def add_branch(mixed, w_ref, total_ref):
    step = pl.program_id(0)
    total_ref[...] += dot(mixed, group_weights(w_ref, step)).astype(BF16).astype(F32)


def out_one_kernel(
    heads,
    kept,
    place_ref,
    num_ref,
    q_ref,
    first_ref,
    second_ref,
    ones_ref,
    scale_ref,
    prior_ref,
    own_ref,
    near_ref,
    far_ref,
    x_ref,
    gain_ref,
    residual_ref,
    low_ref,
    high_ref,
    tail_ref,
    total_ref,
    mixed_ref,
    w_ref,
    sems,
):
    step = pl.program_id(0)

    @pl.when(step == 0)
    def _():
        total_ref[...] = jnp.zeros_like(total_ref)
        zero_between_heads(w_ref)

    run_copies(
        functools.partial(
            weight_copies,
            place_ref,
            near_ref,
            far_ref,
            [(own_ref, 0, w_ref, 0)],
            [(HEAD, w_ref, 0)],
            sems,
        ),
        w_ref.shape[0],
    )

    query_features = features(q_ref[0], first_ref[...], second_ref[...], ones_ref[...])
    query_features = (query_features * scale_ref[...]).astype(BF16)
    for h in range(heads):
        prior = prior_ref[0, pl.ds(pl.multiple_of(place_ref[h] * kept, 16), kept), :]
        lanes = slice(h * SLOT, (h + 1) * SLOT)
        total = num_ref[0, :, lanes] + dot(
            query_features[:, h * FEAT_SLOT : h * FEAT_SLOT + kept], prior.astype(BF16)
        )
        mixed_ref[:, lanes] = (total * (1.0 / total[:, HEAD : HEAD + 1])).astype(BF16)
    add_branch(mixed_ref[...], w_ref, total_ref)

    @pl.when(step == pl.num_programs(0) - 1)
    def _():
        residual = (x_ref[...].astype(F32) + total_ref[...]).astype(BF16)
        residual_ref[...] = residual
        normed = normed_rows(residual.astype(F32), gain_ref[...])
        mid = low_ref.shape[0]
        low_ref[...] = normed[:mid]
        high_ref[...] = normed[mid:]
        tail_ref[...] = normed[normed.shape[0] - HALO :]


def window_kernel(
    heads,
    place_ref,
    first_ref,
    low_ref,
    high_ref,
    halo_ref,
    own_ref,
    near_ref,
    far_ref,
    tap_ref,
    _,
    mixed_ref,
    rows_ref,
    w_ref,
    sems,
):
    step = pl.program_id(0)
    targets = [(own_ref, kind, w_ref, kind * SLOT) for kind in range(3)]
    pieces = [(HEAD, w_ref, kind * SLOT) for kind in range(3)]
    mid = low_ref.shape[0]

    def place_rows():
        rows_ref[:HALO] = halo_ref[...]
        rows_ref[HALO : HALO + mid] = low_ref[...]
        rows_ref[HALO + mid :] = high_ref[...]

    @pl.when(step == 0)
    def _():
        zero_between_heads(w_ref)

    run_copies(
        functools.partial(weight_copies, place_ref, near_ref, far_ref, targets, pieces, sems),
        w_ref.shape[0],
        place_rows,
    )
    rows = mid + high_ref.shape[0]
    lead = HALO - WINDOW
    projected = project(rows_ref, w_ref, step)
    taps = tap_ref[0]
    convolved = taps[0:1] * projected
    for offset in range(1, taps.shape[0]):
        convolved = convolved + taps[offset : offset + 1] * pltpu.roll(projected, offset, 0)
    convolved = convolved[lead:].astype(BF16)
    tile = 128
    span = tile + WINDOW
    row = lax.broadcasted_iota(jnp.int32, (tile, span), 0)
    col = lax.broadcasted_iota(jnp.int32, (tile, span), 1)
    band = (col > row) & (col <= row + WINDOW)
    for h in range(heads):
        at = 3 * h * SLOT
        queries = convolved[WINDOW:, at : at + SLOT]
        keys = convolved[:, at + SLOT : at + 2 * SLOT]
        values = convolved[:, at + 2 * SLOT : at + 3 * SLOT]
        for start in range(0, rows, tile):
            logits = dot(queries[start : start + tile], keys[start : start + span], ((1,), (1,)))
            allowed = band
            if start < WINDOW:
                allowed = band & (col >= WINDOW - start - first_ref[0])
            logits = jnp.where(allowed, logits * HEAD**-0.5, -jnp.inf)
            weights = jnp.exp(logits - jnp.max(logits, axis=1, keepdims=True))
            weights = weights * (1.0 / jnp.sum(weights, axis=1, keepdims=True))
            mixed = dot(weights.astype(BF16), values[start : start + span])
            mixed_ref[0, start : start + tile, h * SLOT : (h + 1) * SLOT] = mixed.astype(BF16)


def out_two_kernel(
    place_ref,
    live_ref,
    mixed_ref,
    pair_ref,
    own_ref,
    near_ref,
    far_ref,
    residual_ref,
    out_ref,
    total_ref,
    w_ref,
    sems,
):
    step = pl.program_id(0)

    @pl.when(step == 0)
    def _():
        total_ref[...] = jnp.zeros_like(total_ref)
        zero_between_heads(w_ref)

    run_copies(
        functools.partial(
            weight_copies,
            place_ref,
            near_ref,
            far_ref,
            [(own_ref, 0, w_ref, 0)],
            [(HEAD, w_ref, 0)],
            sems,
        ),
        w_ref.shape[0],
    )
    mixed = jnp.where(step < 2, mixed_ref[step % 2], pair_ref[step % 2])
    add_branch(mixed, w_ref, total_ref)

    @pl.when(step == pl.num_programs(0) - 1)
    def _():
        result = (residual_ref[...].astype(F32) + total_ref[...]).astype(BF16)
        row = lax.broadcasted_iota(jnp.int32, result.shape, 0)
        out_ref[...] = jnp.where(row < live_ref[0], result, jnp.zeros_like(result))


def whole(shape):
    return pl.BlockSpec(shape, lambda g: (0,) * len(shape))


def each(shape):
    return pl.BlockSpec((1,) + shape, lambda g: (g,) + (0,) * len(shape))


SMEM = pl.BlockSpec(memory_space=pltpu.SMEM)
HBM = pl.BlockSpec(memory_space=pl.ANY)


def call(kernel, groups, in_specs, out_specs, out_shape, scratch, name, flops=0):
    return pl.pallas_call(
        kernel,
        grid=(groups,),
        in_specs=in_specs,
        out_specs=out_specs,
        out_shape=out_shape,
        scratch_shapes=scratch,
        compiler_params=pltpu.CompilerParams(
            dimension_semantics=("arbitrary",), vmem_limit_bytes=VMEM
        ),
        cost_estimate=pl.CostEstimate(flops=flops, bytes_accessed=0, transcendentals=0),
        name=name,
    )


def own_piece(whole_weights):
    head, part = lax.axis_index("seq") % NEAR, lax.axis_index("dp")
    found = []
    for weights in whole_weights:
        kinds, _, rows, cols = weights.shape
        cols = cols // lax.axis_size("dp")
        piece = lax.dynamic_slice(weights, (0, head, 0, part * cols), (kinds, 1, rows, cols))
        found.append(piece.reshape(kinds * rows, cols))
    return jnp.concatenate(found, axis=0)


def across(array, axis, bit):
    return lax.ppermute(array, axis, [(i, i ^ bit) for i in range(lax.axis_size(axis))])


def after(array, others):
    if not others:
        return array
    first = [lax.slice(other, (0,) * other.ndim, (1,) * other.ndim) for other in others]
    zero = sum(one.reshape(()).astype(F32) * 0.0 for one in first)
    return jnp.where(zero == 0.0, array, jnp.zeros_like(array))


def settled(array, others=()):
    return lax.optimization_barrier(after(array, others))


def from_group(piece, over_z):
    return across(after(piece, over_z), "tensor", 2)[None]


def from_groups(piece, over_z, order=(0, 1, 2)):
    piece = after(piece, over_z)
    beside, beyond = across(piece, "tensor", 1), across(piece, "tensor", 2)
    found = (beside, beyond, across(beyond, "tensor", 1))
    return [found[n] for n in order]


def neighbours(held):
    return across(held, "seq", 1), across(held, "seq", 2)


def from_plane(held, near_by, diagonal, over_cores):
    beside, above = near_by
    if diagonal is None:
        opposite = across(held, "seq", 3)
    else:
        half = -(-held.shape[1] // 32) * 16
        opposite = [
            across(after(above[:, :half], diagonal), "seq", 1),
            across(after(beside[:, half:], diagonal), "seq", 2),
        ]
        opposite = after(jnp.concatenate(opposite, axis=1), over_cores)
    near = after(jnp.stack([held, beside, above, opposite]), over_cores)
    return near, across(near, "dp", 1)


def earlier_blocks(state, axis):
    peers = lax.axis_size(axis)
    if peers <= 4:
        found = [
            lax.ppermute(state, axis, [(i, i + by) for i in range(peers - by)])
            for by in range(1, peers)
        ]
        return sum(one.astype(F32) for one in found), found[0]
    everything = lax.all_gather(state, axis).astype(F32)
    reached = jnp.arange(peers) < lax.axis_index(axis)
    return jnp.sum(jnp.where(reached[:, None, None, None], everything, 0.0), axis=0), state


def on_device(
    pool,
    page_table,
    reassign,
    lengths,
    gain_one,
    w_featmap,
    w_value,
    w_out_one,
    gain_two,
    w_window,
    conv_window,
    w_out_two,
):
    dp_count, seq_count, group_count = (lax.axis_size(n) for n in ("dp", "seq", "tensor"))
    groups = dp_count * seq_count
    device_place = lax.axis_index(("dp", "seq"))
    dp_place, seq_place, tensor_place = (lax.axis_index(n) for n in ("dp", "seq", "tensor"))
    pages_dev, page_share, width = pool.shape
    slots_total, pages_total = page_table.shape
    req_dev = slots_total // dp_count
    page_span = pages_total // seq_count
    page_rows = page_share * group_count
    rows = page_span * page_rows
    assert req_dev == group_count
    heads = w_value.shape[1] // HEAD
    head_cols = heads * HEAD
    feat_cols = w_featmap.shape[2]
    feature_dim = feat_cols // heads
    tap_count = conv_window.shape[0]

    assert heads == NEAR and dp_count == 2
    values_t = w_value.T.reshape(1, heads, HEAD, width)
    featmap_t = w_featmap.transpose(1, 2, 0).reshape(2, heads, feature_dim, width)
    window_t = w_window.transpose(1, 2, 0).reshape(3, heads, HEAD, width)
    out_one, out_two = (w.reshape(1, heads, HEAD, width) for w in (w_out_one, w_out_two))
    held_one = settled(jnp.stack(from_groups(own_piece([values_t, featmap_t]), ())))

    placed = reassign[:, None] == jnp.arange(slots_total, dtype=jnp.int32)[None, :]
    table = jnp.sum(jnp.where(placed[:, :, None], page_table[None], 0), axis=1)
    slot_lengths = jnp.sum(jnp.where(placed, lengths[None, :], 0), axis=1)
    source_page = (
        table.reshape(dp_count, req_dev, seq_count, page_span)
        .transpose(0, 2, 1, 3)
        .reshape(groups, req_dev * page_span)
    )
    capacity = (pages_dev + groups - 1) // groups
    page_owner = source_page // pages_dev
    pool_slot = source_page % pages_dev
    before = jnp.arange(pages_dev)[None, :] < jnp.arange(pages_dev)[:, None]
    pair_rank = jnp.sum((page_owner[:, :, None] == page_owner[:, None, :]) & before[None], axis=2)
    send_hit = (page_owner == device_place)[:, None, :] & (
        pair_rank[:, None, :] == jnp.arange(capacity)[None, :, None]
    )
    send_slot = jnp.sum(jnp.where(send_hit, pool_slot[:, None, :], 0), axis=2)
    outgoing = pool.at[send_slot.reshape(-1)].get(mode="promise_in_bounds")
    outgoing = outgoing.reshape(groups, capacity, page_share, width)
    arrived = lax.all_to_all(outgoing, ("dp", "seq"), split_axis=0, concat_axis=0, tiled=True)
    own_row = jnp.arange(groups)[:, None] == device_place
    pick_rows = jnp.sum(jnp.where(own_row, page_owner * capacity + pair_rank, 0), axis=0)
    picked = arrived.reshape(groups * capacity, page_share, width)
    picked = picked.at[pick_rows].get(mode="promise_in_bounds")

    picked = after(picked.reshape(req_dev, page_span, page_share, width), (held_one,))
    swapped = lax.all_to_all(picked, "tensor", split_axis=0, concat_axis=0, tiled=True)
    tokens = swapped.transpose(1, 0, 2, 3).reshape(rows, width)
    slot = dp_place * req_dev + tensor_place
    length = jnp.sum(jnp.where(jnp.arange(slots_total) == slot, slot_lengths, 0))

    held_out_one = settled(jnp.stack(from_groups(own_piece([out_one]), (picked,))))
    near_one = from_plane(held_one, neighbours(held_one), (swapped,), (held_out_one,))
    out_piece = after(own_piece([out_two]), (swapped,))
    beyond = from_group(own_piece([window_t, out_two]), (swapped,))
    places = jnp.concatenate([(seq_place % NEAR) ^ jnp.arange(NEAR), dp_place[None]])
    places = places.astype(jnp.int32)
    taps = conv_window.reshape(tap_count, 3, heads, HEAD).transpose(0, 2, 1, 3)
    taps = jnp.take(taps, places[:NEAR], axis=1, mode="clip")
    taps = jnp.pad(taps, ((0, 0), (0, 0), (0, 0), (0, SLOT - HEAD)))
    taps = taps.reshape(tap_count, 3 * heads * SLOT)
    taps = jnp.stack([taps, across(taps, "tensor", 2)])

    first, second, ones, scale, kept = feature_tables(heads, feature_dim)
    first, second = jnp.asarray(first, BF16), jnp.asarray(second, BF16)
    column = np.zeros((1, heads * SLOT), np.float32)
    column[0, HEAD::SLOT] = 1

    def copy_sems(kinds):
        return pltpu.SemaphoreType.DMA((group_count, NEAR * kinds))

    def weights_of(rows_of_head):
        return pltpu.VMEM((group_count, heads, rows_of_head, width), BF16)

    slots = heads * SLOT
    mid = 3 * rows // 4
    num, queries, state = call(
        functools.partial(linear_kernel, heads, feature_dim, kept),
        group_count,
        [
            SMEM,
            whole((rows, width)),
            whole((1, width)),
            *[HBM] * 4,
            whole(first.shape),
            whole(second.shape),
            whole(ones.shape),
            whole(column.shape),
        ],
        [each((rows, slots)), each((rows, 2 * feat_cols)), each((heads * kept, SLOT))],
        [
            jax.ShapeDtypeStruct((group_count, rows, slots), F32),
            jax.ShapeDtypeStruct((group_count, rows, 2 * feat_cols), BF16),
            jax.ShapeDtypeStruct((group_count, heads * kept, SLOT), BF16),
        ],
        [
            pltpu.VMEM((rows, width), BF16),
            weights_of(SLOT),
            weights_of(2 * feature_dim),
            copy_sems(3),
        ],
        "linear_rows",
    )(
        places, tokens, gain_one[None], values_t, featmap_t, *near_one, first, second, ones, column
    )
    prior, first_arrived = earlier_blocks(state, "seq")
    prior = settled(prior)
    beyond = after(beyond, (first_arrived,))
    held_window, out_beyond = beyond[:, : 3 * HEAD], beyond[0, 3 * HEAD :]
    held_out_two = [out_beyond, across(out_piece, "tensor", 1), across(out_beyond, "tensor", 1)]
    held_out_two = settled(jnp.stack(held_out_two))
    near_out_one = from_plane(held_out_one, neighbours(held_out_one), (state,), (prior, beyond))
    held_window = after(held_window, (prior,))
    near_by_window = neighbours(held_window)
    residual, low, high, tail = call(
        functools.partial(out_one_kernel, heads, kept),
        group_count,
        [
            SMEM,
            each((rows, slots)),
            each((rows, 2 * feat_cols)),
            whole(first.shape),
            whole(second.shape),
            whole(ones.shape),
            whole(scale.shape),
        ]
        + [each((heads * kept, SLOT))]
        + [HBM] * 3
        + [
            whole((rows, width)),
            whole((1, width)),
        ],
        [whole((n, width)) for n in (rows, mid, rows - mid, HALO)],
        [jax.ShapeDtypeStruct((n, width), BF16) for n in (rows, mid, rows - mid, HALO)],
        [
            pltpu.VMEM((rows, width), F32),
            pltpu.VMEM((rows, slots), BF16),
            weights_of(SLOT),
            copy_sems(1),
        ],
        "linear_out",
    )(
        places, num, queries, first, second, ones, scale, prior, out_one, *near_out_one, tokens,
        gain_two[None],
    )

    halo = lax.ppermute(tail, "seq", [(i, i + 1) for i in range(seq_count - 1)])
    pair_low, pair_high = across(low, "tensor", 1), across(high, "tensor", 1)
    pair_halo = lax.ppermute(
        tail,
        ("seq", "tensor"),
        [
            (i * group_count + j, (i + 1) * group_count + (j ^ 1))
            for i in range(seq_count - 1)
            for j in range(group_count)
        ],
    )
    near_window = from_plane(held_window, near_by_window, None, (pair_low, held_out_two))
    held_out_two = after(held_out_two, (residual,))
    block_start = (seq_place * rows).astype(jnp.int32)[None]

    def window_rows(slot_low, slot_high, slot_halo, earlier):
        return call(
            functools.partial(window_kernel, heads),
            2,
            [
                SMEM,
                SMEM,
                whole((mid, width)),
                whole((rows - mid, width)),
                whole((HALO, width)),
                *[HBM] * 3,
                each((tap_count, 3 * slots)),
                HBM,
            ],
            each((rows, slots)),
            jax.ShapeDtypeStruct((2, rows, slots), BF16),
            [
                pltpu.VMEM((HALO + rows, width), BF16),
                pltpu.VMEM((2, heads, 3 * SLOT, width), BF16),
                copy_sems(3),
            ],
            "window_rows",
            6 * rows * width * 3 * head_cols,
        )(places, block_start, slot_low, slot_high, slot_halo, window_t, *near_window, taps, earlier)

    mixed_pair = window_rows(pair_low, pair_high, pair_halo, halo)
    near_out_two = from_plane(held_out_two, neighbours(held_out_two), None, (mixed_pair,))
    mixed_own = window_rows(low, high, halo, mixed_pair)
    mixed_pair = across(mixed_pair, "tensor", 1)
    live = (length - seq_place * rows).astype(jnp.int32)[None]
    result = call(
        out_two_kernel,
        group_count,
        [
            SMEM,
            SMEM,
            whole((2, rows, slots)),
            whole((2, rows, slots)),
            *[HBM] * 3,
            whole((rows, width)),
        ],
        whole((rows, width)),
        jax.ShapeDtypeStruct((rows, width), BF16),
        [
            pltpu.VMEM((rows, width), F32),
            weights_of(SLOT),
            copy_sems(1),
        ],
        "window_out",
    )(places, live, mixed_own, mixed_pair, out_two, *near_out_two, residual)

    result = result.reshape(page_span, group_count, page_share, width).transpose(1, 0, 2, 3)
    return lax.all_to_all(result, "tensor", split_axis=0, concat_axis=0, tiled=True)


def solution(mesh):
    return jax.shard_map(
        on_device,
        mesh=mesh,
        in_specs=(
            P(("dp", "seq"), "tensor", None),
            P(),
            P(),
            P(),
            P(),
            P(None, None, "tensor"),
            P(None, "tensor"),
            P("tensor", None),
            P(),
            P(None, None, "tensor"),
            P(None, None, "tensor"),
            P("tensor", None),
        ),
        out_specs=P("dp", "seq", "tensor", None),
        check_vma=False,
    )
```

```python
import functools

import jax
import jax.numpy as jnp
import numpy as np
from jax import lax
from jax.experimental import pallas as pl
from jax.experimental.pallas import tpu as pltpu
from jax.sharding import PartitionSpec as P

HEAD = 112
WINDOW = 64
EPS = 1e-05
SLOT = 128
FEAT_SLOT = 256
HALO = 80
NEAR = 4
VMEM = 60 * 1024 * 1024
F32 = jnp.float32
BF16 = jnp.bfloat16


def dot(a, b, dims=((1,), (0,))):
    return lax.dot_general(a, b, (dims, ((), ())), preferred_element_type=F32)


def normed_rows(rows, gain):
    scale = lax.rsqrt(jnp.mean(rows * rows, axis=-1, keepdims=True) + EPS)
    return (rows * scale * gain).astype(BF16)


def feature_tables(heads, feature_dim):
    pairs = [(i, j) for i in range(feature_dim) for j in range(i, feature_dim)]
    pairs += [(i, -1) for i in range(feature_dim)] + [(-1, -1)]
    first = np.zeros((2 * heads * feature_dim, heads * FEAT_SLOT), np.float32)
    second = np.zeros_like(first)
    ones = np.zeros((2, heads * FEAT_SLOT), np.float32)
    scale = np.zeros((1, heads * FEAT_SLOT), np.float32)
    for h in range(heads):
        for n, (i, j) in enumerate(pairs):
            at = h * FEAT_SLOT + n
            if i >= 0:
                first[2 * h * feature_dim + i, at] = 1
            else:
                ones[0, at] = 1
            if j >= 0:
                second[2 * h * feature_dim + j, at] = 1
            else:
                ones[1, at] = 1
            if i < 0:
                scale[0, at] = 1
            elif j < 0:
                scale[0, at] = feature_dim**-0.5
            else:
                scale[0, at] = (0.5 if i == j else 1.0) / feature_dim
    return first, second, ones, scale, -(-len(pairs) // 16) * 16


def features(rows, first, second, ones):
    return (dot(rows, first) + ones[0:1]) * (dot(rows, second) + ones[1:2])


def run_copies(copies_of, groups, loads, meanwhile=None):
    step = pl.program_id(0)

    @pl.when(step == 0)
    def _():
        for copy, _ in loads:
            copy.start()
        for group in range(groups):
            for copy in copies_of(group):
                copy.start()

    for group in range(groups):

        @pl.when(step == group)
        def _(group=group):
            for copy, at in loads:
                if at == group:
                    copy.wait()
            if meanwhile is not None and group == 0:
                meanwhile()
            for copy in copies_of(group):
                copy.wait()


def weight_copies(place_ref, near_ref, far_ref, targets, pieces, sems, group):
    found = []

    def copy(src, dst):
        found.append(pltpu.make_async_copy(src, dst, sems.at[group, len(found)]))

    if group == 0:
        for own_ref, kind, w_ref, off in targets:
            rows = own_ref.shape[2]
            for n in range(NEAR):
                copy(own_ref.at[kind, place_ref[n]], w_ref.at[0, n, off : off + rows, :])
        return found
    cols = near_ref.shape[3]
    for ref, part in ((near_ref, place_ref[NEAR]), (far_ref, 1 - place_ref[NEAR])):
        at = 0
        lanes = pl.ds(pl.multiple_of(part * cols, SLOT), cols)
        for rows, w_ref, off in pieces:
            copy(ref.at[:, group - 1, at : at + rows, :], w_ref.at[group, :, off : off + rows, lanes])
            at += rows
    return found


def zero_between_heads(w_ref):
    groups, heads, rows, width = w_ref.shape
    for at in range(HEAD, rows, SLOT):
        w_ref[:, :, at : at + SLOT - HEAD, :] = jnp.zeros(
            (groups, heads, SLOT - HEAD, width), BF16
        )


def group_weights(w_ref, step):
    heads, rows, width = w_ref.shape[1:]
    return w_ref[step].reshape(heads * rows, width)


def project(rows_ref, w_ref, step):
    return dot(rows_ref[...], group_weights(w_ref, step), ((1,), (1,)))


def linear_kernel(
    heads,
    feature_dim,
    kept,
    place_ref,
    x_ref,
    gain_ref,
    value_ref,
    featmap_ref,
    near_ref,
    far_ref,
    first_ref,
    second_ref,
    ones_ref,
    column_ref,
    num_ref,
    q_ref,
    state_ref,
    tokens_ref,
    normed_ref,
    value_w_ref,
    feat_w_ref,
    sems,
):
    step = pl.program_id(0)
    targets = [
        (value_ref, 0, value_w_ref, 0),
        (featmap_ref, 0, feat_w_ref, 0),
        (featmap_ref, 1, feat_w_ref, feature_dim),
    ]
    pieces = [(HEAD, value_w_ref, 0), (2 * feature_dim, feat_w_ref, 0)]

    groups = value_w_ref.shape[0]

    @pl.when(step == 0)
    def _():
        zero_between_heads(value_w_ref)

    def normalize():
        normed_ref[...] = normed_rows(tokens_ref[...].astype(F32), gain_ref[...])

    run_copies(
        functools.partial(weight_copies, place_ref, near_ref, far_ref, targets, pieces, sems),
        groups,
        [(pltpu.make_async_copy(x_ref, tokens_ref, sems.at[groups, 0]), 0)],
        normalize,
    )
    rows = x_ref.shape[0]
    width = 2 * heads * feature_dim
    queries = project(normed_ref, feat_w_ref, step).astype(BF16)
    keys = pltpu.roll(queries.astype(F32), width - feature_dim, 1).astype(BF16)
    values = (project(normed_ref, value_w_ref, step) + column_ref[...]).astype(BF16)
    q_ref[0] = queries
    lane = lax.broadcasted_iota(jnp.int32, (rows, width), 1)
    causal = lax.broadcasted_iota(jnp.int32, (rows, rows), 1) <= lax.broadcasted_iota(
        jnp.int32, (rows, rows), 0
    )
    key_features = features(keys, first_ref[...], second_ref[...], ones_ref[...]).astype(BF16)
    for h in range(heads):
        at = 2 * h * feature_dim
        own = jnp.where((lane >= at) & (lane < at + feature_dim), queries, jnp.zeros_like(queries))
        scores = dot(own, keys, ((1,), (1,))) * feature_dim**-0.5
        kernel = jnp.where(causal, 1.0 + scores + 0.5 * scores * scores, 0.0).astype(BF16)
        value = values[:, h * SLOT : (h + 1) * SLOT]
        num_ref[0, :, h * SLOT : (h + 1) * SLOT] = dot(kernel, value)
        state = dot(key_features[:, h * FEAT_SLOT : h * FEAT_SLOT + kept], value, ((0,), (0,)))
        head = pl.multiple_of(place_ref[h] * kept, 16)
        state_ref[0, pl.ds(head, kept), :] = state.astype(BF16)


def add_branch(mixed, w_ref, total_ref):
    step = pl.program_id(0)
    total_ref[...] += dot(mixed, group_weights(w_ref, step)).astype(BF16).astype(F32)


def out_one_kernel(
    heads,
    kept,
    place_ref,
    num_ref,
    q_ref,
    first_ref,
    second_ref,
    ones_ref,
    scale_ref,
    prior_ref,
    own_ref,
    near_ref,
    far_ref,
    x_ref,
    gain_ref,
    residual_ref,
    low_ref,
    high_ref,
    tail_ref,
    tokens_ref,
    total_ref,
    mixed_ref,
    w_ref,
    sems,
):
    step = pl.program_id(0)
    groups = w_ref.shape[0]

    @pl.when(step == 0)
    def _():
        total_ref[...] = jnp.zeros_like(total_ref)
        zero_between_heads(w_ref)

    loads = [(pltpu.make_async_copy(x_ref, tokens_ref, sems.at[groups, 0]), groups - 1)]
    run_copies(
        functools.partial(
            weight_copies,
            place_ref,
            near_ref,
            far_ref,
            [(own_ref, 0, w_ref, 0)],
            [(HEAD, w_ref, 0)],
            sems,
        ),
        groups,
        loads,
    )

    query_features = features(q_ref[0], first_ref[...], second_ref[...], ones_ref[...])
    query_features = (query_features * scale_ref[...]).astype(BF16)
    for h in range(heads):
        prior = prior_ref[0, pl.ds(pl.multiple_of(place_ref[h] * kept, 16), kept), :]
        lanes = slice(h * SLOT, (h + 1) * SLOT)
        total = num_ref[0, :, lanes] + dot(
            query_features[:, h * FEAT_SLOT : h * FEAT_SLOT + kept], prior.astype(BF16)
        )
        mixed_ref[:, lanes] = (total * (1.0 / total[:, HEAD : HEAD + 1])).astype(BF16)
    add_branch(mixed_ref[...], w_ref, total_ref)

    @pl.when(step == pl.num_programs(0) - 1)
    def _():
        residual = (tokens_ref[...].astype(F32) + total_ref[...]).astype(BF16)
        residual_ref[...] = residual
        normed = normed_rows(residual.astype(F32), gain_ref[...])
        mid = low_ref.shape[0]
        low_ref[...] = normed[:mid]
        high_ref[...] = normed[mid:]
        tail_ref[...] = normed[normed.shape[0] - HALO :]


def window_kernel(
    heads,
    place_ref,
    first_ref,
    low_ref,
    high_ref,
    halo_ref,
    own_ref,
    near_ref,
    far_ref,
    tap_ref,
    _,
    mixed_ref,
    rows_ref,
    w_ref,
    sems,
):
    step = pl.program_id(0)
    targets = [(own_ref, kind, w_ref, kind * SLOT) for kind in range(3)]
    pieces = [(HEAD, w_ref, kind * SLOT) for kind in range(3)]
    mid = low_ref.shape[0]

    groups = w_ref.shape[0]
    loads = [
        (pltpu.make_async_copy(src, rows_ref.at[at : at + src.shape[0], :], sems.at[groups, n]), 0)
        for n, (src, at) in enumerate(((halo_ref, 0), (low_ref, HALO), (high_ref, HALO + mid)))
    ]

    @pl.when(step == 0)
    def _():
        zero_between_heads(w_ref)

    run_copies(
        functools.partial(weight_copies, place_ref, near_ref, far_ref, targets, pieces, sems),
        groups,
        loads,
    )
    rows = mid + high_ref.shape[0]
    lead = HALO - WINDOW
    projected = project(rows_ref, w_ref, step)
    taps = tap_ref[0]
    convolved = taps[0:1] * projected
    for offset in range(1, taps.shape[0]):
        convolved = convolved + taps[offset : offset + 1] * pltpu.roll(projected, offset, 0)
    convolved = convolved[lead:].astype(BF16)
    tile = 128
    span = tile + WINDOW
    row = lax.broadcasted_iota(jnp.int32, (tile, span), 0)
    col = lax.broadcasted_iota(jnp.int32, (tile, span), 1)
    band = (col > row) & (col <= row + WINDOW)
    for h in range(heads):
        at = 3 * h * SLOT
        queries = convolved[WINDOW:, at : at + SLOT]
        keys = convolved[:, at + SLOT : at + 2 * SLOT]
        values = convolved[:, at + 2 * SLOT : at + 3 * SLOT]
        for start in range(0, rows, tile):
            logits = dot(queries[start : start + tile], keys[start : start + span], ((1,), (1,)))
            allowed = band
            if start < WINDOW:
                allowed = band & (col >= WINDOW - start - first_ref[0])
            logits = jnp.where(allowed, logits * HEAD**-0.5, -jnp.inf)
            weights = jnp.exp(logits - jnp.max(logits, axis=1, keepdims=True))
            weights = weights * (1.0 / jnp.sum(weights, axis=1, keepdims=True))
            mixed = dot(weights.astype(BF16), values[start : start + span])
            mixed_ref[0, start : start + tile, h * SLOT : (h + 1) * SLOT] = mixed.astype(BF16)


def out_two_kernel(
    place_ref,
    live_ref,
    mixed_ref,
    pair_ref,
    own_ref,
    near_ref,
    far_ref,
    residual_ref,
    out_ref,
    mixed_all_ref,
    rows_ref,
    total_ref,
    w_ref,
    sems,
):
    step = pl.program_id(0)
    groups = w_ref.shape[0]
    loads = [
        (pltpu.make_async_copy(mixed_ref, mixed_all_ref.at[:2], sems.at[groups, 0]), 0),
        (pltpu.make_async_copy(pair_ref, mixed_all_ref.at[2:], sems.at[groups, 1]), 2),
        (pltpu.make_async_copy(residual_ref, rows_ref, sems.at[groups, 2]), groups - 1),
    ]

    @pl.when(step == 0)
    def _():
        total_ref[...] = jnp.zeros_like(total_ref)
        zero_between_heads(w_ref)

    run_copies(
        functools.partial(
            weight_copies,
            place_ref,
            near_ref,
            far_ref,
            [(own_ref, 0, w_ref, 0)],
            [(HEAD, w_ref, 0)],
            sems,
        ),
        groups,
        loads,
    )
    add_branch(mixed_all_ref[step], w_ref, total_ref)

    @pl.when(step == pl.num_programs(0) - 1)
    def _():
        result = (rows_ref[...].astype(F32) + total_ref[...]).astype(BF16)
        row = lax.broadcasted_iota(jnp.int32, result.shape, 0)
        out_ref[...] = jnp.where(row < live_ref[0], result, jnp.zeros_like(result))


def whole(shape):
    return pl.BlockSpec(shape, lambda g: (0,) * len(shape))


def each(shape):
    return pl.BlockSpec((1,) + shape, lambda g: (g,) + (0,) * len(shape))


SMEM = pl.BlockSpec(memory_space=pltpu.SMEM)
HBM = pl.BlockSpec(memory_space=pl.ANY)


def call(kernel, groups, in_specs, out_specs, out_shape, scratch, name):
    return pl.pallas_call(
        kernel,
        grid=(groups,),
        in_specs=in_specs,
        out_specs=out_specs,
        out_shape=out_shape,
        scratch_shapes=scratch,
        compiler_params=pltpu.CompilerParams(
            dimension_semantics=("arbitrary",), vmem_limit_bytes=VMEM
        ),
        cost_estimate=pl.CostEstimate(flops=0, bytes_accessed=0, transcendentals=0),
        name=name,
    )


def own_piece(whole_weights):
    head, part = lax.axis_index("seq") % NEAR, lax.axis_index("dp")
    found = []
    for weights in whole_weights:
        kinds, _, rows, cols = weights.shape
        cols = cols // lax.axis_size("dp")
        piece = lax.dynamic_slice(weights, (0, head, 0, part * cols), (kinds, 1, rows, cols))
        found.append(piece.reshape(kinds * rows, cols))
    return jnp.concatenate(found, axis=0)


def across(array, axis, bit):
    return lax.ppermute(array, axis, [(i, i ^ bit) for i in range(lax.axis_size(axis))])


def after(array, others):
    if not others:
        return array
    first = [lax.slice(other, (0,) * other.ndim, (1,) * other.ndim) for other in others]
    zero = sum(one.reshape(()).astype(F32) * 0.0 for one in first)
    return jnp.where(zero == 0.0, array, jnp.zeros_like(array))


def settled(array, others=()):
    return lax.optimization_barrier(after(array, others))


def from_group(piece, over_z):
    return across(after(piece, over_z), "tensor", 2)[None]


def from_groups(piece, over_z, order=(0, 1, 2)):
    piece = after(piece, over_z)
    beside, beyond = across(piece, "tensor", 1), across(piece, "tensor", 2)
    found = (beside, beyond, across(beyond, "tensor", 1))
    return [found[n] for n in order]


def neighbours(held):
    return across(held, "seq", 1), across(held, "seq", 2)


def from_plane(held, near_by, diagonal, over_cores):
    beside, above = near_by
    if diagonal is None:
        opposite = across(held, "seq", 3)
    else:
        half = -(-held.shape[1] // 32) * 16
        opposite = [
            across(after(above[:, :half], diagonal), "seq", 1),
            across(after(beside[:, half:], diagonal), "seq", 2),
        ]
        opposite = after(jnp.concatenate(opposite, axis=1), over_cores)
    near = after(jnp.stack([held, beside, above, opposite]), over_cores)
    return near, across(near, "dp", 1)


def earlier_blocks(state, axis):
    peers = lax.axis_size(axis)
    if peers <= 4:
        found = [
            lax.ppermute(state, axis, [(i, i + by) for i in range(peers - by)])
            for by in range(1, peers)
        ]
        return sum(one.astype(F32) for one in found)
    everything = lax.all_gather(state, axis).astype(F32)
    reached = jnp.arange(peers) < lax.axis_index(axis)
    return jnp.sum(jnp.where(reached[:, None, None, None], everything, 0.0), axis=0)


def on_device(
    pool,
    page_table,
    reassign,
    lengths,
    gain_one,
    w_featmap,
    w_value,
    w_out_one,
    gain_two,
    w_window,
    conv_window,
    w_out_two,
):
    dp_count, seq_count, group_count = (lax.axis_size(n) for n in ("dp", "seq", "tensor"))
    groups = dp_count * seq_count
    device_place = lax.axis_index(("dp", "seq"))
    dp_place, seq_place, tensor_place = (lax.axis_index(n) for n in ("dp", "seq", "tensor"))
    pages_dev, page_share, width = pool.shape
    slots_total, pages_total = page_table.shape
    req_dev = slots_total // dp_count
    page_span = pages_total // seq_count
    page_rows = page_share * group_count
    rows = page_span * page_rows
    assert req_dev == group_count
    heads = w_value.shape[1] // HEAD
    head_cols = heads * HEAD
    feat_cols = w_featmap.shape[2]
    feature_dim = feat_cols // heads
    tap_count = conv_window.shape[0]

    assert heads == NEAR and dp_count == 2
    values_t = w_value.T.reshape(1, heads, HEAD, width)
    featmap_t = w_featmap.transpose(1, 2, 0).reshape(2, heads, feature_dim, width)
    window_t = w_window.transpose(1, 2, 0).reshape(3, heads, HEAD, width)
    out_one, out_two = (w.reshape(1, heads, HEAD, width) for w in (w_out_one, w_out_two))
    held_one = settled(jnp.stack(from_groups(own_piece([values_t, featmap_t]), ())))

    placed = reassign[:, None] == jnp.arange(slots_total, dtype=jnp.int32)[None, :]
    table = jnp.sum(jnp.where(placed[:, :, None], page_table[None], 0), axis=1)
    slot_lengths = jnp.sum(jnp.where(placed, lengths[None, :], 0), axis=1)
    source_page = (
        table.reshape(dp_count, req_dev, seq_count, page_span)
        .transpose(0, 2, 1, 3)
        .reshape(groups, req_dev * page_span)
    )
    capacity = (pages_dev + groups - 1) // groups
    page_owner = source_page // pages_dev
    pool_slot = source_page % pages_dev
    before = jnp.arange(pages_dev)[None, :] < jnp.arange(pages_dev)[:, None]
    pair_rank = jnp.sum((page_owner[:, :, None] == page_owner[:, None, :]) & before[None], axis=2)
    send_hit = (page_owner == device_place)[:, None, :] & (
        pair_rank[:, None, :] == jnp.arange(capacity)[None, :, None]
    )
    send_slot = jnp.sum(jnp.where(send_hit, pool_slot[:, None, :], 0), axis=2)
    outgoing = pool.at[send_slot.reshape(-1)].get(mode="promise_in_bounds")
    outgoing = outgoing.reshape(groups, capacity, page_share, width)
    arrived = lax.all_to_all(outgoing, ("dp", "seq"), split_axis=0, concat_axis=0, tiled=True)
    own_row = jnp.arange(groups)[:, None] == device_place
    pick_rows = jnp.sum(jnp.where(own_row, page_owner * capacity + pair_rank, 0), axis=0)
    picked = arrived.reshape(groups * capacity, page_share, width)
    picked = picked.at[pick_rows].get(mode="promise_in_bounds")

    picked = after(picked.reshape(req_dev, page_span, page_share, width), (held_one,))
    swapped = lax.all_to_all(picked, "tensor", split_axis=0, concat_axis=0, tiled=True)
    tokens = swapped.transpose(1, 0, 2, 3).reshape(rows, width)
    slot = dp_place * req_dev + tensor_place
    length = jnp.sum(jnp.where(jnp.arange(slots_total) == slot, slot_lengths, 0))

    held_out_one = settled(jnp.stack(from_groups(own_piece([out_one]), (picked,))))
    near_one = from_plane(held_one, neighbours(held_one), (swapped,), (held_out_one,))
    out_piece = after(own_piece([out_two]), (swapped,))
    beyond = from_group(own_piece([window_t, out_two]), (swapped,))
    places = jnp.concatenate([(seq_place % NEAR) ^ jnp.arange(NEAR), dp_place[None]])
    places = places.astype(jnp.int32)
    taps = conv_window.reshape(tap_count, 3, heads, HEAD).transpose(0, 2, 1, 3)
    taps = jnp.take(taps, places[:NEAR], axis=1, mode="clip")
    taps = jnp.pad(taps, ((0, 0), (0, 0), (0, 0), (0, SLOT - HEAD)))
    taps = taps.reshape(tap_count, 3 * heads * SLOT)
    taps = jnp.stack([taps, across(taps, "tensor", 2)])

    first, second, ones, scale, kept = feature_tables(heads, feature_dim)
    first, second = jnp.asarray(first, BF16), jnp.asarray(second, BF16)
    column = np.zeros((1, heads * SLOT), np.float32)
    column[0, HEAD::SLOT] = 1

    def copy_sems(kinds):
        return pltpu.SemaphoreType.DMA((group_count + 1, NEAR * kinds))

    def weights_of(rows_of_head):
        return pltpu.VMEM((group_count, heads, rows_of_head, width), BF16)

    slots = heads * SLOT
    mid = 3 * rows // 4
    num, queries, state = call(
        functools.partial(linear_kernel, heads, feature_dim, kept),
        group_count,
        [
            SMEM,
            HBM,
            whole((1, width)),
            *[HBM] * 4,
            whole(first.shape),
            whole(second.shape),
            whole(ones.shape),
            whole(column.shape),
        ],
        [each((rows, slots)), each((rows, 2 * feat_cols)), each((heads * kept, SLOT))],
        [
            jax.ShapeDtypeStruct((group_count, rows, slots), F32),
            jax.ShapeDtypeStruct((group_count, rows, 2 * feat_cols), BF16),
            jax.ShapeDtypeStruct((group_count, heads * kept, SLOT), BF16),
        ],
        [
            pltpu.VMEM((rows, width), BF16),
            pltpu.VMEM((rows, width), BF16),
            weights_of(SLOT),
            weights_of(2 * feature_dim),
            copy_sems(3),
        ],
        "linear_rows",
    )(
        places, tokens, gain_one[None], values_t, featmap_t, *near_one, first, second, ones, column
    )
    prior = settled(earlier_blocks(state, "seq"))
    beyond = after(beyond, (state,))
    held_window, out_beyond = beyond[:, : 3 * HEAD], beyond[0, 3 * HEAD :]
    held_out_two = [out_beyond, across(out_piece, "tensor", 1), across(out_beyond, "tensor", 1)]
    held_out_two = settled(jnp.stack(held_out_two), (prior,))
    near_out_one = from_plane(
        held_out_one, neighbours(held_out_one), (state,), (beyond, held_out_two)
    )
    held_window = after(held_window, (prior,))
    near_by_window = neighbours(held_window)
    residual, low, high, tail = call(
        functools.partial(out_one_kernel, heads, kept),
        group_count,
        [
            SMEM,
            each((rows, slots)),
            each((rows, 2 * feat_cols)),
            whole(first.shape),
            whole(second.shape),
            whole(ones.shape),
            whole(scale.shape),
        ]
        + [each((heads * kept, SLOT))]
        + [HBM] * 4
        + [whole((1, width))],
        [whole((n, width)) for n in (rows, mid, rows - mid, HALO)],
        [jax.ShapeDtypeStruct((n, width), BF16) for n in (rows, mid, rows - mid, HALO)],
        [
            pltpu.VMEM((rows, width), BF16),
            pltpu.VMEM((rows, width), F32),
            pltpu.VMEM((rows, slots), BF16),
            weights_of(SLOT),
            copy_sems(1),
        ],
        "linear_out",
    )(
        places, num, queries, first, second, ones, scale, prior, out_one, *near_out_one, tokens,
        gain_two[None],
    )

    halo = lax.ppermute(tail, "seq", [(i, i + 1) for i in range(seq_count - 1)])
    pair_low, pair_high = across(low, "tensor", 1), across(high, "tensor", 1)
    pair_halo = lax.ppermute(
        tail,
        ("seq", "tensor"),
        [
            (i * group_count + j, (i + 1) * group_count + (j ^ 1))
            for i in range(seq_count - 1)
            for j in range(group_count)
        ],
    )
    near_window = from_plane(held_window, near_by_window, (residual,), (pair_low, pair_halo))
    held_out_two = after(held_out_two, (residual,))
    block_start = (seq_place * rows).astype(jnp.int32)[None]

    def window_rows(slot_low, slot_high, slot_halo, earlier):
        return call(
            functools.partial(window_kernel, heads),
            2,
            [
                SMEM,
                SMEM,
                *[HBM] * 6,
                each((tap_count, 3 * slots)),
                HBM,
            ],
            each((rows, slots)),
            jax.ShapeDtypeStruct((2, rows, slots), BF16),
            [
                pltpu.VMEM((HALO + rows, width), BF16),
                pltpu.VMEM((2, heads, 3 * SLOT, width), BF16),
                copy_sems(3),
            ],
            "window_rows",
        )(places, block_start, slot_low, slot_high, slot_halo, window_t, *near_window, taps, earlier)

    mixed_pair = window_rows(pair_low, pair_high, pair_halo, halo)
    near_out_two = from_plane(held_out_two, neighbours(held_out_two), None, (mixed_pair,))
    mixed_own = window_rows(low, high, halo, mixed_pair)
    mixed_pair = across(mixed_pair, "tensor", 1)
    live = (length - seq_place * rows).astype(jnp.int32)[None]
    result = call(
        out_two_kernel,
        group_count,
        [
            SMEM,
            SMEM,
            *[HBM] * 6,
        ],
        whole((rows, width)),
        jax.ShapeDtypeStruct((rows, width), BF16),
        [
            pltpu.VMEM((group_count, rows, slots), BF16),
            pltpu.VMEM((rows, width), BF16),
            pltpu.VMEM((rows, width), F32),
            weights_of(SLOT),
            copy_sems(1),
        ],
        "window_out",
    )(places, live, mixed_own, mixed_pair, out_two, *near_out_two, residual)

    result = result.reshape(page_span, group_count, page_share, width).transpose(1, 0, 2, 3)
    return lax.all_to_all(result, "tensor", split_axis=0, concat_axis=0, tiled=True)


def solution(mesh):
    return jax.shard_map(
        on_device,
        mesh=mesh,
        in_specs=(
            P(("dp", "seq"), "tensor", None),
            P(),
            P(),
            P(),
            P(),
            P(None, None, "tensor"),
            P(None, "tensor"),
            P("tensor", None),
            P(),
            P(None, None, "tensor"),
            P(None, None, "tensor"),
            P("tensor", None),
        ),
        out_specs=P("dp", "seq", "tensor", None),
        check_vma=False,
    )
```

```python
import functools

import jax
import jax.numpy as jnp
import numpy as np
from jax import lax
from jax.experimental import pallas as pl
from jax.experimental.pallas import tpu as pltpu
from jax.sharding import PartitionSpec as P

HEAD = 112
WINDOW = 64
EPS = 1e-05
SLOT = 128
FEAT_SLOT = 256
HALO = 80
NEAR = 4
VMEM = 60 * 1024 * 1024
F32 = jnp.float32
BF16 = jnp.bfloat16


def dot(a, b, dims=((1,), (0,))):
    return lax.dot_general(a, b, (dims, ((), ())), preferred_element_type=F32)


def normed_rows(rows, gain):
    scale = lax.rsqrt(jnp.mean(rows * rows, axis=-1, keepdims=True) + EPS)
    return (rows * scale * gain).astype(BF16)


def feature_tables(heads, feature_dim):
    pairs = [(i, j) for i in range(feature_dim) for j in range(i, feature_dim)]
    pairs += [(i, -1) for i in range(feature_dim)] + [(-1, -1)]
    first = np.zeros((2 * heads * feature_dim, heads * FEAT_SLOT), np.float32)
    second = np.zeros_like(first)
    ones = np.zeros((2, heads * FEAT_SLOT), np.float32)
    scale = np.zeros((1, heads * FEAT_SLOT), np.float32)
    for h in range(heads):
        for n, (i, j) in enumerate(pairs):
            at = h * FEAT_SLOT + n
            if i >= 0:
                first[2 * h * feature_dim + i, at] = 1
            else:
                ones[0, at] = 1
            if j >= 0:
                second[2 * h * feature_dim + j, at] = 1
            else:
                ones[1, at] = 1
            if i < 0:
                scale[0, at] = 1
            elif j < 0:
                scale[0, at] = feature_dim**-0.5
            else:
                scale[0, at] = (0.5 if i == j else 1.0) / feature_dim
    return first, second, ones, scale, -(-len(pairs) // 16) * 16


def features(rows, first, second, ones):
    return (dot(rows, first) + ones[0:1]) * (dot(rows, second) + ones[1:2])


def run_copies(copies_of, groups, loads, meanwhile=None):
    step = pl.program_id(0)

    @pl.when(step == 0)
    def _():
        for copy, _ in loads:
            copy.start()
        for group in range(groups):
            for copy in copies_of(group):
                copy.start()

    for group in range(groups):

        @pl.when(step == group)
        def _(group=group):
            for copy, at in loads:
                if at == group:
                    copy.wait()
            if meanwhile is not None and group == 0:
                meanwhile()
            for copy in copies_of(group):
                copy.wait()


def weight_copies(place_ref, near_ref, far_ref, targets, pieces, sems, group):
    found = []

    def copy(src, dst):
        found.append(pltpu.make_async_copy(src, dst, sems.at[group, len(found)]))

    if group == 0:
        for own_ref, kind, w_ref, off in targets:
            rows = own_ref.shape[2]
            for n in range(NEAR):
                copy(own_ref.at[kind, place_ref[n]], w_ref.at[0, n, off : off + rows, :])
        return found
    cols = near_ref.shape[3]
    for ref, part in ((near_ref, place_ref[NEAR]), (far_ref, 1 - place_ref[NEAR])):
        at = 0
        lanes = pl.ds(pl.multiple_of(part * cols, SLOT), cols)
        for rows, w_ref, off in pieces:
            copy(ref.at[:, group - 1, at : at + rows, :], w_ref.at[group, :, off : off + rows, lanes])
            at += rows
    return found


def zero_between_heads(w_ref):
    groups, heads, rows, width = w_ref.shape
    for at in range(HEAD, rows, SLOT):
        w_ref[:, :, at : at + SLOT - HEAD, :] = jnp.zeros(
            (groups, heads, SLOT - HEAD, width), BF16
        )


def group_weights(w_ref, step):
    heads, rows, width = w_ref.shape[1:]
    return w_ref[step].reshape(heads * rows, width)


def project(rows_ref, w_ref, step):
    return dot(rows_ref[...], group_weights(w_ref, step), ((1,), (1,)))


def linear_kernel(
    heads,
    feature_dim,
    kept,
    place_ref,
    x_ref,
    gain_ref,
    value_ref,
    featmap_ref,
    near_ref,
    far_ref,
    first_ref,
    second_ref,
    ones_ref,
    column_ref,
    num_ref,
    q_ref,
    state_ref,
    state_two_ref,
    tokens_ref,
    normed_ref,
    value_w_ref,
    feat_w_ref,
    sems,
):
    step = pl.program_id(0)
    targets = [
        (value_ref, 0, value_w_ref, 0),
        (featmap_ref, 0, feat_w_ref, 0),
        (featmap_ref, 1, feat_w_ref, feature_dim),
    ]
    pieces = [(HEAD, value_w_ref, 0), (2 * feature_dim, feat_w_ref, 0)]

    groups = value_w_ref.shape[0]

    @pl.when(step == 0)
    def _():
        zero_between_heads(value_w_ref)

    def normalize():
        normed_ref[...] = normed_rows(tokens_ref[...].astype(F32), gain_ref[...])

    run_copies(
        functools.partial(weight_copies, place_ref, near_ref, far_ref, targets, pieces, sems),
        groups,
        [(pltpu.make_async_copy(x_ref, tokens_ref, sems.at[groups, 0]), 0)],
        normalize,
    )
    rows = x_ref.shape[0]
    width = 2 * heads * feature_dim
    queries = project(normed_ref, feat_w_ref, step).astype(BF16)
    keys = pltpu.roll(queries.astype(F32), width - feature_dim, 1).astype(BF16)
    values = (project(normed_ref, value_w_ref, step) + column_ref[...]).astype(BF16)
    q_ref[0] = queries
    lane = lax.broadcasted_iota(jnp.int32, (rows, width), 1)
    causal = lax.broadcasted_iota(jnp.int32, (rows, rows), 1) <= lax.broadcasted_iota(
        jnp.int32, (rows, rows), 0
    )
    states = []
    key_features = features(keys, first_ref[...], second_ref[...], ones_ref[...]).astype(BF16)
    for h in range(heads):
        at = 2 * h * feature_dim
        own = jnp.where((lane >= at) & (lane < at + feature_dim), queries, jnp.zeros_like(queries))
        scores = dot(own, keys, ((1,), (1,))) * feature_dim**-0.5
        kernel = jnp.where(causal, 1.0 + scores + 0.5 * scores * scores, 0.0).astype(BF16)
        value = values[:, h * SLOT : (h + 1) * SLOT]
        num_ref[0, :, h * SLOT : (h + 1) * SLOT] = dot(kernel, value)
        state = dot(key_features[:, h * FEAT_SLOT : h * FEAT_SLOT + kept], value, ((0,), (0,)))
        states.append(state.astype(BF16))
    for first_step, ref in ((0, state_ref), (groups // 2, state_two_ref)):

        @pl.when((step >= first_step) & (step < first_step + groups // 2))
        def _(ref=ref):
            for h in range(heads):
                ref[0, pl.ds(pl.multiple_of(place_ref[h] * kept, 16), kept), :] = states[h]


def add_branch(mixed, w_ref, total_ref):
    step = pl.program_id(0)
    total_ref[...] += dot(mixed, group_weights(w_ref, step)).astype(BF16).astype(F32)


def out_one_kernel(
    heads,
    kept,
    place_ref,
    num_ref,
    q_ref,
    first_ref,
    second_ref,
    ones_ref,
    scale_ref,
    prior_ref,
    prior_two_ref,
    own_ref,
    near_ref,
    far_ref,
    x_ref,
    gain_ref,
    residual_ref,
    low_ref,
    high_ref,
    tail_ref,
    tokens_ref,
    total_ref,
    mixed_ref,
    w_ref,
    sems,
):
    step = pl.program_id(0)
    groups = w_ref.shape[0]

    @pl.when(step == 0)
    def _():
        total_ref[...] = jnp.zeros_like(total_ref)
        zero_between_heads(w_ref)

    loads = [(pltpu.make_async_copy(x_ref, tokens_ref, sems.at[groups, 0]), groups - 1)]
    run_copies(
        functools.partial(
            weight_copies,
            place_ref,
            near_ref,
            far_ref,
            [(own_ref, 0, w_ref, 0)],
            [(HEAD, w_ref, 0)],
            sems,
        ),
        groups,
        loads,
    )

    query_features = features(q_ref[0], first_ref[...], second_ref[...], ones_ref[...])
    query_features = (query_features * scale_ref[...]).astype(BF16)
    for h in range(heads):
        at = pl.ds(pl.multiple_of(place_ref[h] * kept, 16), kept)
        prior = jnp.where(step < groups // 2, prior_ref[0, at, :], prior_two_ref[0, at, :])
        lanes = slice(h * SLOT, (h + 1) * SLOT)
        total = num_ref[0, :, lanes] + dot(
            query_features[:, h * FEAT_SLOT : h * FEAT_SLOT + kept], prior.astype(BF16)
        )
        mixed_ref[:, lanes] = (total * (1.0 / total[:, HEAD : HEAD + 1])).astype(BF16)
    add_branch(mixed_ref[...], w_ref, total_ref)

    @pl.when(step == pl.num_programs(0) - 1)
    def _():
        residual = (tokens_ref[...].astype(F32) + total_ref[...]).astype(BF16)
        residual_ref[...] = residual
        normed = normed_rows(residual.astype(F32), gain_ref[...])
        mid = low_ref.shape[0]
        low_ref[...] = normed[:mid]
        high_ref[...] = normed[mid:]
        tail_ref[...] = normed[normed.shape[0] - HALO :]


def window_kernel(
    heads,
    place_ref,
    first_ref,
    low_ref,
    high_ref,
    halo_ref,
    own_ref,
    near_ref,
    far_ref,
    tap_ref,
    _,
    mixed_ref,
    rows_ref,
    w_ref,
    sems,
):
    step = pl.program_id(0)
    targets = [(own_ref, kind, w_ref, kind * SLOT) for kind in range(3)]
    pieces = [(HEAD, w_ref, kind * SLOT) for kind in range(3)]
    mid = low_ref.shape[0]

    groups = w_ref.shape[0]
    loads = [
        (pltpu.make_async_copy(src, rows_ref.at[at : at + src.shape[0], :], sems.at[groups, n]), 0)
        for n, (src, at) in enumerate(((halo_ref, 0), (low_ref, HALO), (high_ref, HALO + mid)))
    ]

    @pl.when(step == 0)
    def _():
        zero_between_heads(w_ref)

    run_copies(
        functools.partial(weight_copies, place_ref, near_ref, far_ref, targets, pieces, sems),
        groups,
        loads,
    )
    rows = mid + high_ref.shape[0]
    lead = HALO - WINDOW
    projected = project(rows_ref, w_ref, step)
    taps = tap_ref[0]
    convolved = taps[0:1] * projected
    for offset in range(1, taps.shape[0]):
        convolved = convolved + taps[offset : offset + 1] * pltpu.roll(projected, offset, 0)
    convolved = convolved[lead:].astype(BF16)
    tile = 128
    span = tile + WINDOW
    row = lax.broadcasted_iota(jnp.int32, (tile, span), 0)
    col = lax.broadcasted_iota(jnp.int32, (tile, span), 1)
    band = (col > row) & (col <= row + WINDOW)
    for h in range(heads):
        at = 3 * h * SLOT
        queries = convolved[WINDOW:, at : at + SLOT]
        keys = convolved[:, at + SLOT : at + 2 * SLOT]
        values = convolved[:, at + 2 * SLOT : at + 3 * SLOT]
        for start in range(0, rows, tile):
            logits = dot(queries[start : start + tile], keys[start : start + span], ((1,), (1,)))
            allowed = band
            if start < WINDOW:
                allowed = band & (col >= WINDOW - start - first_ref[0])
            logits = jnp.where(allowed, logits * HEAD**-0.5, -jnp.inf)
            weights = jnp.exp(logits - jnp.max(logits, axis=1, keepdims=True))
            weights = weights * (1.0 / jnp.sum(weights, axis=1, keepdims=True))
            mixed = dot(weights.astype(BF16), values[start : start + span])
            mixed_ref[0, start : start + tile, h * SLOT : (h + 1) * SLOT] = mixed.astype(BF16)


def out_two_kernel(
    place_ref,
    live_ref,
    mixed_ref,
    pair_ref,
    own_ref,
    near_ref,
    far_ref,
    residual_ref,
    out_ref,
    mixed_all_ref,
    rows_ref,
    total_ref,
    w_ref,
    sems,
):
    step = pl.program_id(0)
    groups = w_ref.shape[0]
    loads = [
        (pltpu.make_async_copy(mixed_ref, mixed_all_ref.at[:2], sems.at[groups, 0]), 0),
        (pltpu.make_async_copy(pair_ref, mixed_all_ref.at[2:], sems.at[groups, 1]), 2),
        (pltpu.make_async_copy(residual_ref, rows_ref, sems.at[groups, 2]), groups - 1),
    ]

    @pl.when(step == 0)
    def _():
        total_ref[...] = jnp.zeros_like(total_ref)
        zero_between_heads(w_ref)

    run_copies(
        functools.partial(
            weight_copies,
            place_ref,
            near_ref,
            far_ref,
            [(own_ref, 0, w_ref, 0)],
            [(HEAD, w_ref, 0)],
            sems,
        ),
        groups,
        loads,
    )
    add_branch(mixed_all_ref[step], w_ref, total_ref)

    @pl.when(step == pl.num_programs(0) - 1)
    def _():
        result = (rows_ref[...].astype(F32) + total_ref[...]).astype(BF16)
        row = lax.broadcasted_iota(jnp.int32, result.shape, 0)
        out_ref[...] = jnp.where(row < live_ref[0], result, jnp.zeros_like(result))


def whole(shape):
    return pl.BlockSpec(shape, lambda g: (0,) * len(shape))


def each(shape):
    return pl.BlockSpec((1,) + shape, lambda g: (g,) + (0,) * len(shape))


SMEM = pl.BlockSpec(memory_space=pltpu.SMEM)
HBM = pl.BlockSpec(memory_space=pl.ANY)


def call(kernel, groups, in_specs, out_specs, out_shape, scratch, name):
    return pl.pallas_call(
        kernel,
        grid=(groups,),
        in_specs=in_specs,
        out_specs=out_specs,
        out_shape=out_shape,
        scratch_shapes=scratch,
        compiler_params=pltpu.CompilerParams(
            dimension_semantics=("arbitrary",), vmem_limit_bytes=VMEM
        ),
        cost_estimate=pl.CostEstimate(flops=0, bytes_accessed=0, transcendentals=0),
        name=name,
    )


def own_piece(whole_weights):
    head, part = lax.axis_index("seq") % NEAR, lax.axis_index("dp")
    found = []
    for weights in whole_weights:
        kinds, _, rows, cols = weights.shape
        cols = cols // lax.axis_size("dp")
        piece = lax.dynamic_slice(weights, (0, head, 0, part * cols), (kinds, 1, rows, cols))
        found.append(piece.reshape(kinds * rows, cols))
    return jnp.concatenate(found, axis=0)


def across(array, axis, bit):
    return lax.ppermute(array, axis, [(i, i ^ bit) for i in range(lax.axis_size(axis))])


def after(array, others):
    if not others:
        return array
    first = [lax.slice(other, (0,) * other.ndim, (1,) * other.ndim) for other in others]
    zero = sum(one.reshape(()).astype(F32) * 0.0 for one in first)
    return jnp.where(zero == 0.0, array, jnp.zeros_like(array))


def settled(array, others=()):
    return lax.optimization_barrier(after(array, others))


def from_group(piece, over_z):
    return across(after(piece, over_z), "tensor", 2)[None]


def from_groups(piece, over_z, order=(0, 1, 2)):
    piece = after(piece, over_z)
    beside, beyond = across(piece, "tensor", 1), across(piece, "tensor", 2)
    found = (beside, beyond, across(beyond, "tensor", 1))
    return [found[n] for n in order]


def neighbours(held):
    return across(held, "seq", 1), across(held, "seq", 2)


def from_plane(held, near_by, diagonal, over_cores):
    beside, above = near_by
    if diagonal is None:
        opposite = across(held, "seq", 3)
    else:
        half = -(-held.shape[1] // 32) * 16
        opposite = [
            across(after(above[:, :half], diagonal), "seq", 1),
            across(after(beside[:, half:], diagonal), "seq", 2),
        ]
        opposite = after(jnp.concatenate(opposite, axis=1), over_cores)
    near = after(jnp.stack([held, beside, above, opposite]), over_cores)
    return near, across(near, "dp", 1)


def earlier_blocks(one, two, axis, second):
    peers, mine = lax.axis_size(axis), lax.axis_index(axis)
    if peers != 4:
        both = lax.all_gather(jnp.concatenate([one, two]), axis).astype(F32)
        reached = (jnp.arange(peers) < mine)[:, None, None, None]
        total = jnp.sum(jnp.where(reached, both, 0.0), axis=0)
        return total[: one.shape[0]], total[one.shape[0] :]
    upward = [(0, 2), (1, 3)]
    one_beside, two_below = across(one, axis, 1), lax.ppermute(two, axis, upward)
    pair = after((one.astype(F32) + one_beside.astype(F32)).astype(one.dtype), second)
    two_sent = jnp.where(mine == 2, two.astype(F32), 0.0) + two_below.astype(F32)
    two_sent = jnp.where(mine < 2, two, two_sent.astype(two.dtype))
    one_below, two_beside = lax.ppermute(pair, axis, upward), across(two_sent, axis, 1)
    one_total = jnp.where(mine % 2 == 1, one_beside.astype(F32), 0.0) + one_below.astype(F32)
    two_total = jnp.where(mine > 0, two_beside.astype(F32), 0.0) + two_below.astype(F32)
    return one_total, two_total


def on_device(
    pool,
    page_table,
    reassign,
    lengths,
    gain_one,
    w_featmap,
    w_value,
    w_out_one,
    gain_two,
    w_window,
    conv_window,
    w_out_two,
):
    dp_count, seq_count, group_count = (lax.axis_size(n) for n in ("dp", "seq", "tensor"))
    groups = dp_count * seq_count
    device_place = lax.axis_index(("dp", "seq"))
    dp_place, seq_place, tensor_place = (lax.axis_index(n) for n in ("dp", "seq", "tensor"))
    pages_dev, page_share, width = pool.shape
    slots_total, pages_total = page_table.shape
    req_dev = slots_total // dp_count
    page_span = pages_total // seq_count
    page_rows = page_share * group_count
    rows = page_span * page_rows
    assert req_dev == group_count
    heads = w_value.shape[1] // HEAD
    head_cols = heads * HEAD
    feat_cols = w_featmap.shape[2]
    feature_dim = feat_cols // heads
    tap_count = conv_window.shape[0]

    assert heads == NEAR and dp_count == 2
    values_t = w_value.T.reshape(1, heads, HEAD, width)
    featmap_t = w_featmap.transpose(1, 2, 0).reshape(2, heads, feature_dim, width)
    window_t = w_window.transpose(1, 2, 0).reshape(3, heads, HEAD, width)
    out_one, out_two = (w.reshape(1, heads, HEAD, width) for w in (w_out_one, w_out_two))
    held_one = settled(jnp.stack(from_groups(own_piece([values_t, featmap_t]), ())))

    placed = reassign[:, None] == jnp.arange(slots_total, dtype=jnp.int32)[None, :]
    table = jnp.sum(jnp.where(placed[:, :, None], page_table[None], 0), axis=1)
    slot_lengths = jnp.sum(jnp.where(placed, lengths[None, :], 0), axis=1)
    source_page = (
        table.reshape(dp_count, req_dev, seq_count, page_span)
        .transpose(0, 2, 1, 3)
        .reshape(groups, req_dev * page_span)
    )
    capacity = (pages_dev + groups - 1) // groups
    page_owner = source_page // pages_dev
    pool_slot = source_page % pages_dev
    before = jnp.arange(pages_dev)[None, :] < jnp.arange(pages_dev)[:, None]
    pair_rank = jnp.sum((page_owner[:, :, None] == page_owner[:, None, :]) & before[None], axis=2)
    send_hit = (page_owner == device_place)[:, None, :] & (
        pair_rank[:, None, :] == jnp.arange(capacity)[None, :, None]
    )
    send_slot = jnp.sum(jnp.where(send_hit, pool_slot[:, None, :], 0), axis=2)
    outgoing = pool.at[send_slot.reshape(-1)].get(mode="promise_in_bounds")
    outgoing = outgoing.reshape(groups, capacity, page_share, width)
    arrived = lax.all_to_all(outgoing, ("dp", "seq"), split_axis=0, concat_axis=0, tiled=True)
    own_row = jnp.arange(groups)[:, None] == device_place
    pick_rows = jnp.sum(jnp.where(own_row, page_owner * capacity + pair_rank, 0), axis=0)
    picked = arrived.reshape(groups * capacity, page_share, width)
    picked = picked.at[pick_rows].get(mode="promise_in_bounds")

    picked = after(picked.reshape(req_dev, page_span, page_share, width), (held_one,))
    swapped = lax.all_to_all(picked, "tensor", split_axis=0, concat_axis=0, tiled=True)
    tokens = swapped.transpose(1, 0, 2, 3).reshape(rows, width)
    slot = dp_place * req_dev + tensor_place
    length = jnp.sum(jnp.where(jnp.arange(slots_total) == slot, slot_lengths, 0))

    held_out_one = settled(jnp.stack(from_groups(own_piece([out_one]), (picked,))))
    near_one = from_plane(held_one, neighbours(held_one), (swapped,), (held_out_one,))
    beyond = from_group(own_piece([window_t, out_two]), (swapped,))
    places = jnp.concatenate([(seq_place % NEAR) ^ jnp.arange(NEAR), dp_place[None]])
    places = places.astype(jnp.int32)
    taps = conv_window.reshape(tap_count, 3, heads, HEAD).transpose(0, 2, 1, 3)
    taps = jnp.take(taps, places[:NEAR], axis=1, mode="clip")
    taps = jnp.pad(taps, ((0, 0), (0, 0), (0, 0), (0, SLOT - HEAD)))
    taps = taps.reshape(tap_count, 3 * heads * SLOT)
    taps = jnp.stack([taps, across(taps, "tensor", 2)])

    first, second, ones, scale, kept = feature_tables(heads, feature_dim)
    first, second = jnp.asarray(first, BF16), jnp.asarray(second, BF16)
    column = np.zeros((1, heads * SLOT), np.float32)
    column[0, HEAD::SLOT] = 1

    def copy_sems(kinds):
        return pltpu.SemaphoreType.DMA((group_count + 1, NEAR * kinds))

    def weights_of(rows_of_head):
        return pltpu.VMEM((group_count, heads, rows_of_head, width), BF16)

    slots = heads * SLOT
    mid = 3 * rows // 4
    half = group_count // 2
    halves = [
        pl.BlockSpec((1, heads * kept, SLOT), lambda g: (jnp.minimum(g, half - 1), 0, 0)),
        pl.BlockSpec((1, heads * kept, SLOT), lambda g: (jnp.maximum(g - half, 0), 0, 0)),
    ]
    num, queries, state, state_two = call(
        functools.partial(linear_kernel, heads, feature_dim, kept),
        group_count,
        [
            SMEM,
            HBM,
            whole((1, width)),
            *[HBM] * 4,
            whole(first.shape),
            whole(second.shape),
            whole(ones.shape),
            whole(column.shape),
        ],
        [each((rows, slots)), each((rows, 2 * feat_cols)), *halves],
        [
            jax.ShapeDtypeStruct((group_count, rows, slots), F32),
            jax.ShapeDtypeStruct((group_count, rows, 2 * feat_cols), BF16),
            *[jax.ShapeDtypeStruct((half, heads * kept, SLOT), BF16)] * 2,
        ],
        [
            pltpu.VMEM((rows, width), BF16),
            pltpu.VMEM((rows, width), BF16),
            weights_of(SLOT),
            weights_of(2 * feature_dim),
            copy_sems(3),
        ],
        "linear_rows",
    )(
        places, tokens, gain_one[None], values_t, featmap_t, *near_one, first, second, ones, column
    )
    prior_one, prior_two = earlier_blocks(state, state_two, "seq", (beyond,))
    prior_two = settled(prior_two, (prior_one,))
    beyond = after(beyond, (state,))
    out_piece = after(own_piece([out_two]), (state,))
    held_window, out_beyond = beyond[:, : 3 * HEAD], beyond[0, 3 * HEAD :]
    held_out_two = [out_beyond, across(out_piece, "tensor", 1), across(out_beyond, "tensor", 1)]
    held_out_two = settled(jnp.stack(held_out_two), (prior_two,))
    near_out_one = from_plane(
        held_out_one, neighbours(held_out_one), (state,), (held_out_two,)
    )
    held_window = after(held_window, (prior_two,))
    near_by_window = neighbours(held_window)
    residual, low, high, tail = call(
        functools.partial(out_one_kernel, heads, kept),
        group_count,
        [
            SMEM,
            each((rows, slots)),
            each((rows, 2 * feat_cols)),
            whole(first.shape),
            whole(second.shape),
            whole(ones.shape),
            whole(scale.shape),
        ]
        + halves
        + [HBM] * 4
        + [whole((1, width))],
        [whole((n, width)) for n in (rows, mid, rows - mid, HALO)],
        [jax.ShapeDtypeStruct((n, width), BF16) for n in (rows, mid, rows - mid, HALO)],
        [
            pltpu.VMEM((rows, width), BF16),
            pltpu.VMEM((rows, width), F32),
            pltpu.VMEM((rows, slots), BF16),
            weights_of(SLOT),
            copy_sems(1),
        ],
        "linear_out",
    )(
        places, num, queries, first, second, ones, scale, prior_one, prior_two, out_one, *near_out_one, tokens,
        gain_two[None],
    )

    halo = lax.ppermute(tail, "seq", [(i, i + 1) for i in range(seq_count - 1)])
    pair_low, pair_high = across(low, "tensor", 1), across(high, "tensor", 1)
    pair_halo = lax.ppermute(
        tail,
        ("seq", "tensor"),
        [
            (i * group_count + j, (i + 1) * group_count + (j ^ 1))
            for i in range(seq_count - 1)
            for j in range(group_count)
        ],
    )
    near_window = from_plane(held_window, near_by_window, (residual,), (pair_low, pair_halo, halo))
    held_out_two = after(held_out_two, (residual,))
    block_start = (seq_place * rows).astype(jnp.int32)[None]

    def window_rows(slot_low, slot_high, slot_halo, earlier):
        return call(
            functools.partial(window_kernel, heads),
            2,
            [
                SMEM,
                SMEM,
                *[HBM] * 6,
                each((tap_count, 3 * slots)),
                HBM,
            ],
            each((rows, slots)),
            jax.ShapeDtypeStruct((2, rows, slots), BF16),
            [
                pltpu.VMEM((HALO + rows, width), BF16),
                pltpu.VMEM((2, heads, 3 * SLOT, width), BF16),
                copy_sems(3),
            ],
            "window_rows",
        )(places, block_start, slot_low, slot_high, slot_halo, window_t, *near_window, taps, earlier)

    mixed_pair = window_rows(pair_low, pair_high, pair_halo, low)
    near_out_two = from_plane(held_out_two, neighbours(held_out_two), None, (mixed_pair,))
    mixed_own = window_rows(low, high, halo, mixed_pair)
    mixed_pair = across(mixed_pair, "tensor", 1)
    live = (length - seq_place * rows).astype(jnp.int32)[None]
    result = call(
        out_two_kernel,
        group_count,
        [
            SMEM,
            SMEM,
            *[HBM] * 6,
        ],
        whole((rows, width)),
        jax.ShapeDtypeStruct((rows, width), BF16),
        [
            pltpu.VMEM((group_count, rows, slots), BF16),
            pltpu.VMEM((rows, width), BF16),
            pltpu.VMEM((rows, width), F32),
            weights_of(SLOT),
            copy_sems(1),
        ],
        "window_out",
    )(places, live, mixed_own, mixed_pair, out_two, *near_out_two, residual)

    result = result.reshape(page_span, group_count, page_share, width).transpose(1, 0, 2, 3)
    return lax.all_to_all(result, "tensor", split_axis=0, concat_axis=0, tiled=True)


def solution(mesh):
    return jax.shard_map(
        on_device,
        mesh=mesh,
        in_specs=(
            P(("dp", "seq"), "tensor", None),
            P(),
            P(),
            P(),
            P(),
            P(None, None, "tensor"),
            P(None, "tensor"),
            P("tensor", None),
            P(),
            P(None, None, "tensor"),
            P(None, None, "tensor"),
            P("tensor", None),
        ),
        out_specs=P("dp", "seq", "tensor", None),
        check_vma=False,
    )
```

```python
import functools

import jax
import jax.numpy as jnp
import numpy as np
from jax import lax
from jax.experimental import pallas as pl
from jax.experimental.pallas import tpu as pltpu
from jax.sharding import PartitionSpec as P

HEAD = 112
WINDOW = 64
EPS = 1e-05
SLOT = 128
FEAT_SLOT = 256
HALO = 80
NEAR = 4
VMEM = 60 * 1024 * 1024
F32 = jnp.float32
BF16 = jnp.bfloat16


def dot(a, b, dims=((1,), (0,))):
    return lax.dot_general(a, b, (dims, ((), ())), preferred_element_type=F32)


def normed_rows(rows, gain):
    scale = lax.rsqrt(jnp.mean(rows * rows, axis=-1, keepdims=True) + EPS)
    return (rows * scale * gain).astype(BF16)


def feature_tables(heads, feature_dim):
    pairs = [(i, j) for i in range(feature_dim) for j in range(i, feature_dim)]
    pairs += [(i, -1) for i in range(feature_dim)] + [(-1, -1)]
    first = np.zeros((2 * heads * feature_dim, heads * FEAT_SLOT), np.float32)
    second = np.zeros_like(first)
    ones = np.zeros((2, heads * FEAT_SLOT), np.float32)
    scale = np.zeros((1, heads * FEAT_SLOT), np.float32)
    for h in range(heads):
        for n, (i, j) in enumerate(pairs):
            at = h * FEAT_SLOT + n
            if i >= 0:
                first[2 * h * feature_dim + i, at] = 1
            else:
                ones[0, at] = 1
            if j >= 0:
                second[2 * h * feature_dim + j, at] = 1
            else:
                ones[1, at] = 1
            if i < 0:
                scale[0, at] = 1
            elif j < 0:
                scale[0, at] = feature_dim**-0.5
            else:
                scale[0, at] = (0.5 if i == j else 1.0) / feature_dim
    return first, second, ones, scale, -(-len(pairs) // 16) * 16


def features(rows, first, second, ones):
    return (dot(rows, first) + ones[0:1]) * (dot(rows, second) + ones[1:2])


def run_copies(copies_of, groups, loads, meanwhile=None):
    step = pl.program_id(0)

    @pl.when(step == 0)
    def _():
        for copy, _ in loads:
            copy.start()
        for group in range(groups):
            for copy in copies_of(group):
                copy.start()

    for group in range(groups):

        @pl.when(step == group)
        def _(group=group):
            for copy, at in loads:
                if at == group:
                    copy.wait()
            if meanwhile is not None and group == 0:
                meanwhile()
            for copy in copies_of(group):
                copy.wait()


def weight_copies(place_ref, near_ref, far_ref, targets, pieces, sems, group):
    found = []

    def copy(src, dst):
        found.append(pltpu.make_async_copy(src, dst, sems.at[group, len(found)]))

    if group == 0:
        for own_ref, kind, w_ref, off in targets:
            rows = own_ref.shape[2]
            for n in range(NEAR):
                copy(own_ref.at[kind, place_ref[n]], w_ref.at[0, n, off : off + rows, :])
        return found
    cols = near_ref.shape[3]
    for ref, part in ((near_ref, place_ref[NEAR]), (far_ref, 1 - place_ref[NEAR])):
        at = 0
        lanes = pl.ds(pl.multiple_of(part * cols, SLOT), cols)
        for rows, w_ref, off in pieces:
            copy(ref.at[:, group - 1, at : at + rows, :], w_ref.at[group, :, off : off + rows, lanes])
            at += rows
    return found


def zero_between_heads(w_ref):
    groups, heads, rows, width = w_ref.shape
    for at in range(HEAD, rows, SLOT):
        w_ref[:, :, at : at + SLOT - HEAD, :] = jnp.zeros(
            (groups, heads, SLOT - HEAD, width), BF16
        )


def group_weights(w_ref, step):
    heads, rows, width = w_ref.shape[1:]
    return w_ref[step].reshape(heads * rows, width)


def project(rows_ref, w_ref, step):
    return dot(rows_ref[...], group_weights(w_ref, step), ((1,), (1,)))


def linear_kernel(
    heads,
    feature_dim,
    kept,
    place_ref,
    x_ref,
    gain_ref,
    value_ref,
    featmap_ref,
    near_ref,
    far_ref,
    first_ref,
    second_ref,
    ones_ref,
    column_ref,
    num_ref,
    q_ref,
    state_ref,
    tokens_ref,
    normed_ref,
    value_w_ref,
    feat_w_ref,
    sems,
):
    step = pl.program_id(0)
    targets = [
        (value_ref, 0, value_w_ref, 0),
        (featmap_ref, 0, feat_w_ref, 0),
        (featmap_ref, 1, feat_w_ref, feature_dim),
    ]
    pieces = [(HEAD, value_w_ref, 0), (2 * feature_dim, feat_w_ref, 0)]

    groups = value_w_ref.shape[0]

    @pl.when(step == 0)
    def _():
        zero_between_heads(value_w_ref)

    def normalize():
        normed_ref[...] = normed_rows(tokens_ref[...].astype(F32), gain_ref[...])

    run_copies(
        functools.partial(weight_copies, place_ref, near_ref, far_ref, targets, pieces, sems),
        groups,
        [(pltpu.make_async_copy(x_ref, tokens_ref, sems.at[groups, 0]), 0)],
        normalize,
    )
    rows = x_ref.shape[0]
    width = 2 * heads * feature_dim
    queries = project(normed_ref, feat_w_ref, step).astype(BF16)
    keys = pltpu.roll(queries.astype(F32), width - feature_dim, 1).astype(BF16)
    values = (project(normed_ref, value_w_ref, step) + column_ref[...]).astype(BF16)
    q_ref[0] = queries
    lane = lax.broadcasted_iota(jnp.int32, (rows, width), 1)
    causal = lax.broadcasted_iota(jnp.int32, (rows, rows), 1) <= lax.broadcasted_iota(
        jnp.int32, (rows, rows), 0
    )
    key_features = features(keys, first_ref[...], second_ref[...], ones_ref[...]).astype(BF16)
    for h in range(heads):
        at = 2 * h * feature_dim
        own = jnp.where((lane >= at) & (lane < at + feature_dim), queries, jnp.zeros_like(queries))
        scores = dot(own, keys, ((1,), (1,))) * feature_dim**-0.5
        kernel = jnp.where(causal, 1.0 + scores + 0.5 * scores * scores, 0.0).astype(BF16)
        value = values[:, h * SLOT : (h + 1) * SLOT]
        num_ref[0, :, h * SLOT : (h + 1) * SLOT] = dot(kernel, value)
        state = dot(key_features[:, h * FEAT_SLOT : h * FEAT_SLOT + kept], value, ((0,), (0,)))
        head = pl.multiple_of(place_ref[h] * kept, 16)
        state_ref[0, pl.ds(head, kept), :] = state.astype(BF16)


def add_branch(mixed, w_ref, total_ref):
    step = pl.program_id(0)
    total_ref[...] += dot(mixed, group_weights(w_ref, step)).astype(BF16).astype(F32)


def out_one_kernel(
    heads,
    kept,
    place_ref,
    num_ref,
    q_ref,
    first_ref,
    second_ref,
    ones_ref,
    scale_ref,
    prior_ref,
    own_ref,
    near_ref,
    far_ref,
    x_ref,
    gain_ref,
    residual_ref,
    normed_ref,
    tail_ref,
    tokens_ref,
    total_ref,
    mixed_ref,
    w_ref,
    sems,
):
    step = pl.program_id(0)
    groups = w_ref.shape[0]

    @pl.when(step == 0)
    def _():
        total_ref[...] = jnp.zeros_like(total_ref)
        zero_between_heads(w_ref)

    loads = [(pltpu.make_async_copy(x_ref, tokens_ref, sems.at[groups, 0]), groups - 1)]
    run_copies(
        functools.partial(
            weight_copies,
            place_ref,
            near_ref,
            far_ref,
            [(own_ref, 0, w_ref, 0)],
            [(HEAD, w_ref, 0)],
            sems,
        ),
        groups,
        loads,
    )

    query_features = features(q_ref[0], first_ref[...], second_ref[...], ones_ref[...])
    query_features = (query_features * scale_ref[...]).astype(BF16)
    for h in range(heads):
        prior = prior_ref[0, pl.ds(pl.multiple_of(place_ref[h] * kept, 16), kept), :]
        lanes = slice(h * SLOT, (h + 1) * SLOT)
        total = num_ref[0, :, lanes] + dot(
            query_features[:, h * FEAT_SLOT : h * FEAT_SLOT + kept], prior.astype(BF16)
        )
        mixed_ref[:, lanes] = (total * (1.0 / total[:, HEAD : HEAD + 1])).astype(BF16)
    add_branch(mixed_ref[...], w_ref, total_ref)

    @pl.when(step == pl.num_programs(0) - 1)
    def _():
        residual = (tokens_ref[...].astype(F32) + total_ref[...]).astype(BF16)
        residual_ref[...] = residual
        normed = normed_rows(residual.astype(F32), gain_ref[...])
        normed_ref[...] = normed
        tail_ref[...] = normed[normed.shape[0] - HALO :]


def window_kernel(
    heads,
    place_ref,
    first_ref,
    x_ref,
    halo_ref,
    own_ref,
    near_ref,
    far_ref,
    tap_ref,
    _,
    mixed_ref,
    rows_ref,
    w_ref,
    sems,
):
    step = pl.program_id(0)
    targets = [(own_ref, kind, w_ref, kind * SLOT) for kind in range(3)]
    pieces = [(HEAD, w_ref, kind * SLOT) for kind in range(3)]

    groups = w_ref.shape[0]
    loads = [
        (pltpu.make_async_copy(src, rows_ref.at[at : at + src.shape[0], :], sems.at[groups, n]), 0)
        for n, (src, at) in enumerate(((halo_ref, 0), (x_ref, HALO)))
    ]

    @pl.when(step == 0)
    def _():
        zero_between_heads(w_ref)

    run_copies(
        functools.partial(weight_copies, place_ref, near_ref, far_ref, targets, pieces, sems),
        groups,
        loads,
    )
    rows = x_ref.shape[0]
    lead = HALO - WINDOW
    projected = project(rows_ref, w_ref, step)
    taps = tap_ref[0]
    convolved = taps[0:1] * projected
    for offset in range(1, taps.shape[0]):
        convolved = convolved + taps[offset : offset + 1] * pltpu.roll(projected, offset, 0)
    convolved = convolved[lead:].astype(BF16)
    tile = 128
    span = tile + WINDOW
    row = lax.broadcasted_iota(jnp.int32, (tile, span), 0)
    col = lax.broadcasted_iota(jnp.int32, (tile, span), 1)
    band = (col > row) & (col <= row + WINDOW)
    for h in range(heads):
        at = 3 * h * SLOT
        queries = convolved[WINDOW:, at : at + SLOT]
        keys = convolved[:, at + SLOT : at + 2 * SLOT]
        values = convolved[:, at + 2 * SLOT : at + 3 * SLOT]
        for start in range(0, rows, tile):
            logits = dot(queries[start : start + tile], keys[start : start + span], ((1,), (1,)))
            allowed = band
            if start < WINDOW:
                allowed = band & (col >= WINDOW - start - first_ref[0])
            logits = jnp.where(allowed, logits * HEAD**-0.5, -jnp.inf)
            weights = jnp.exp(logits - jnp.max(logits, axis=1, keepdims=True))
            weights = weights * (1.0 / jnp.sum(weights, axis=1, keepdims=True))
            mixed = dot(weights.astype(BF16), values[start : start + span])
            mixed_ref[0, start : start + tile, h * SLOT : (h + 1) * SLOT] = mixed.astype(BF16)


def out_two_kernel(
    place_ref,
    live_ref,
    mixed_ref,
    pair_ref,
    own_ref,
    near_ref,
    far_ref,
    residual_ref,
    out_ref,
    mixed_all_ref,
    rows_ref,
    total_ref,
    w_ref,
    sems,
):
    step = pl.program_id(0)
    groups = w_ref.shape[0]
    loads = [
        (pltpu.make_async_copy(mixed_ref, mixed_all_ref.at[:2], sems.at[groups, 0]), 0),
        (pltpu.make_async_copy(pair_ref, mixed_all_ref.at[2:], sems.at[groups, 1]), 2),
        (pltpu.make_async_copy(residual_ref, rows_ref, sems.at[groups, 2]), groups - 1),
    ]

    @pl.when(step == 0)
    def _():
        total_ref[...] = jnp.zeros_like(total_ref)
        zero_between_heads(w_ref)

    run_copies(
        functools.partial(
            weight_copies,
            place_ref,
            near_ref,
            far_ref,
            [(own_ref, 0, w_ref, 0)],
            [(HEAD, w_ref, 0)],
            sems,
        ),
        groups,
        loads,
    )
    add_branch(mixed_all_ref[step], w_ref, total_ref)

    @pl.when(step == pl.num_programs(0) - 1)
    def _():
        result = (rows_ref[...].astype(F32) + total_ref[...]).astype(BF16)
        row = lax.broadcasted_iota(jnp.int32, result.shape, 0)
        out_ref[...] = jnp.where(row < live_ref[0], result, jnp.zeros_like(result))


def whole(shape):
    return pl.BlockSpec(shape, lambda g: (0,) * len(shape))


def each(shape):
    return pl.BlockSpec((1,) + shape, lambda g: (g,) + (0,) * len(shape))


SMEM = pl.BlockSpec(memory_space=pltpu.SMEM)
HBM = pl.BlockSpec(memory_space=pl.ANY)


def call(kernel, groups, in_specs, out_specs, out_shape, scratch, name):
    return pl.pallas_call(
        kernel,
        grid=(groups,),
        in_specs=in_specs,
        out_specs=out_specs,
        out_shape=out_shape,
        scratch_shapes=scratch,
        compiler_params=pltpu.CompilerParams(
            dimension_semantics=("arbitrary",), vmem_limit_bytes=VMEM
        ),
        cost_estimate=pl.CostEstimate(flops=0, bytes_accessed=0, transcendentals=0),
        name=name,
    )


def own_piece(whole_weights):
    head, part = lax.axis_index("seq") % NEAR, lax.axis_index("dp")
    found = []
    for weights in whole_weights:
        kinds, _, rows, cols = weights.shape
        cols = cols // lax.axis_size("dp")
        piece = lax.dynamic_slice(weights, (0, head, 0, part * cols), (kinds, 1, rows, cols))
        found.append(piece.reshape(kinds * rows, cols))
    return jnp.concatenate(found, axis=0)


def across(array, axis, bit):
    return lax.ppermute(array, axis, [(i, i ^ bit) for i in range(lax.axis_size(axis))])


def after(array, others):
    if not others:
        return array
    first = [lax.slice(other, (0,) * other.ndim, (1,) * other.ndim) for other in others]
    zero = sum(one.reshape(()).astype(F32) * 0.0 for one in first)
    return jnp.where(zero == 0.0, array, jnp.zeros_like(array))


def settled(array, others=()):
    return lax.optimization_barrier(after(array, others))


def from_group(piece, over_z):
    return across(after(piece, over_z), "tensor", 2)[None]


def from_groups(piece, over_z, order=(0, 1, 2)):
    piece = after(piece, over_z)
    beside, beyond = across(piece, "tensor", 1), across(piece, "tensor", 2)
    found = (beside, beyond, across(beyond, "tensor", 1))
    return [found[n] for n in order]


def neighbours(held):
    return across(held, "seq", 1), across(held, "seq", 2)


def from_plane(held, near_by, diagonal, over_cores):
    beside, above = near_by
    if diagonal is None:
        opposite = across(held, "seq", 3)
    else:
        half = -(-held.shape[1] // 32) * 16
        opposite = [
            across(after(above[:, :half], diagonal), "seq", 1),
            across(after(beside[:, half:], diagonal), "seq", 2),
        ]
        opposite = after(jnp.concatenate(opposite, axis=1), over_cores)
    near = after(jnp.stack([held, beside, above, opposite]), over_cores)
    return near, across(near, "dp", 1)


def earlier_blocks(state, axis):
    peers = lax.axis_size(axis)
    if peers <= 4:
        found = [
            lax.ppermute(state, axis, [(i, i + by) for i in range(peers - by)])
            for by in range(1, peers)
        ]
        return sum(one.astype(F32) for one in found)
    everything = lax.all_gather(state, axis).astype(F32)
    reached = jnp.arange(peers) < lax.axis_index(axis)
    return jnp.sum(jnp.where(reached[:, None, None, None], everything, 0.0), axis=0)


def on_device(
    pool,
    page_table,
    reassign,
    lengths,
    gain_one,
    w_featmap,
    w_value,
    w_out_one,
    gain_two,
    w_window,
    conv_window,
    w_out_two,
):
    dp_count, seq_count, group_count = (lax.axis_size(n) for n in ("dp", "seq", "tensor"))
    groups = dp_count * seq_count
    device_place = lax.axis_index(("dp", "seq"))
    dp_place, seq_place, tensor_place = (lax.axis_index(n) for n in ("dp", "seq", "tensor"))
    pages_dev, page_share, width = pool.shape
    slots_total, pages_total = page_table.shape
    req_dev = slots_total // dp_count
    page_span = pages_total // seq_count
    page_rows = page_share * group_count
    rows = page_span * page_rows
    assert req_dev == group_count
    heads = w_value.shape[1] // HEAD
    head_cols = heads * HEAD
    feat_cols = w_featmap.shape[2]
    feature_dim = feat_cols // heads
    tap_count = conv_window.shape[0]

    assert heads == NEAR and dp_count == 2
    values_t = w_value.T.reshape(1, heads, HEAD, width)
    featmap_t = w_featmap.transpose(1, 2, 0).reshape(2, heads, feature_dim, width)
    window_t = w_window.transpose(1, 2, 0).reshape(3, heads, HEAD, width)
    out_one, out_two = (w.reshape(1, heads, HEAD, width) for w in (w_out_one, w_out_two))
    places = jnp.concatenate([(seq_place % NEAR) ^ jnp.arange(NEAR), dp_place[None]])
    places = places.astype(jnp.int32)
    taps = conv_window.reshape(tap_count, 3, heads, HEAD).transpose(0, 2, 1, 3)
    taps = jnp.take(taps, places[:NEAR], axis=1, mode="clip")
    taps = jnp.pad(taps, ((0, 0), (0, 0), (0, 0), (0, SLOT - HEAD)))
    taps = taps.reshape(tap_count, 3 * heads * SLOT)
    taps = settled(jnp.stack([taps, across(taps, "tensor", 2)]))
    held_one = from_groups(own_piece([values_t, featmap_t]), ())
    held_one = settled(jnp.stack(held_one), (taps,))

    placed = reassign[:, None] == jnp.arange(slots_total, dtype=jnp.int32)[None, :]
    table = jnp.sum(jnp.where(placed[:, :, None], page_table[None], 0), axis=1)
    slot_lengths = jnp.sum(jnp.where(placed, lengths[None, :], 0), axis=1)
    source_page = (
        table.reshape(dp_count, req_dev, seq_count, page_span)
        .transpose(0, 2, 1, 3)
        .reshape(groups, req_dev * page_span)
    )
    capacity = (pages_dev + groups - 1) // groups
    page_owner = source_page // pages_dev
    pool_slot = source_page % pages_dev
    before = jnp.arange(pages_dev)[None, :] < jnp.arange(pages_dev)[:, None]
    pair_rank = jnp.sum((page_owner[:, :, None] == page_owner[:, None, :]) & before[None], axis=2)
    send_hit = (page_owner == device_place)[:, None, :] & (
        pair_rank[:, None, :] == jnp.arange(capacity)[None, :, None]
    )
    send_slot = jnp.sum(jnp.where(send_hit, pool_slot[:, None, :], 0), axis=2)
    outgoing = pool.at[send_slot.reshape(-1)].get(mode="promise_in_bounds")
    outgoing = outgoing.reshape(groups, capacity, page_share, width)
    arrived = lax.all_to_all(outgoing, ("dp", "seq"), split_axis=0, concat_axis=0, tiled=True)
    own_row = jnp.arange(groups)[:, None] == device_place
    pick_rows = jnp.sum(jnp.where(own_row, page_owner * capacity + pair_rank, 0), axis=0)
    picked = arrived.reshape(groups * capacity, page_share, width)
    picked = picked.at[pick_rows].get(mode="promise_in_bounds")

    picked = after(picked.reshape(req_dev, page_span, page_share, width), (held_one,))
    swapped = lax.all_to_all(picked, "tensor", split_axis=0, concat_axis=0, tiled=True)
    tokens = swapped.transpose(1, 0, 2, 3).reshape(rows, width)
    slot = dp_place * req_dev + tensor_place
    length = jnp.sum(jnp.where(jnp.arange(slots_total) == slot, slot_lengths, 0))

    held_out_one = settled(jnp.stack(from_groups(own_piece([out_one]), (picked,))))
    near_one = from_plane(held_one, neighbours(held_one), (swapped,), (held_out_one,))
    out_piece = after(own_piece([out_two]), (swapped,))
    beyond = from_group(own_piece([window_t, out_two]), (swapped,))
    first, second, ones, scale, kept = feature_tables(heads, feature_dim)
    first, second = jnp.asarray(first, BF16), jnp.asarray(second, BF16)
    column = np.zeros((1, heads * SLOT), np.float32)
    column[0, HEAD::SLOT] = 1

    def copy_sems(kinds):
        return pltpu.SemaphoreType.DMA((group_count + 1, NEAR * kinds))

    def weights_of(rows_of_head):
        return pltpu.VMEM((group_count, heads, rows_of_head, width), BF16)

    slots = heads * SLOT
    num, queries, state = call(
        functools.partial(linear_kernel, heads, feature_dim, kept),
        group_count,
        [
            SMEM,
            HBM,
            whole((1, width)),
            *[HBM] * 4,
            whole(first.shape),
            whole(second.shape),
            whole(ones.shape),
            whole(column.shape),
        ],
        [each((rows, slots)), each((rows, 2 * feat_cols)), each((heads * kept, SLOT))],
        [
            jax.ShapeDtypeStruct((group_count, rows, slots), F32),
            jax.ShapeDtypeStruct((group_count, rows, 2 * feat_cols), BF16),
            jax.ShapeDtypeStruct((group_count, heads * kept, SLOT), BF16),
        ],
        [
            pltpu.VMEM((rows, width), BF16),
            pltpu.VMEM((rows, width), BF16),
            weights_of(SLOT),
            weights_of(2 * feature_dim),
            copy_sems(3),
        ],
        "linear_rows",
    )(
        places, tokens, gain_one[None], values_t, featmap_t, *near_one, first, second, ones, column
    )
    prior = settled(earlier_blocks(state, "seq"))
    beyond = after(beyond, (state,))
    held_window, out_beyond = beyond[:, : 3 * HEAD], beyond[0, 3 * HEAD :]
    held_out_two = [out_beyond, across(out_piece, "tensor", 1), across(out_beyond, "tensor", 1)]
    held_out_two = settled(jnp.stack(held_out_two), (prior,))
    near_out_one = from_plane(
        held_out_one, neighbours(held_out_one), (state,), (beyond, held_out_two)
    )
    held_window = after(held_window, (prior,))
    near_by_window = neighbours(held_window)
    residual, normed_two, tail = call(
        functools.partial(out_one_kernel, heads, kept),
        group_count,
        [
            SMEM,
            each((rows, slots)),
            each((rows, 2 * feat_cols)),
            whole(first.shape),
            whole(second.shape),
            whole(ones.shape),
            whole(scale.shape),
        ]
        + [each((heads * kept, SLOT))]
        + [HBM] * 4
        + [whole((1, width))],
        [whole((n, width)) for n in (rows, rows, HALO)],
        [jax.ShapeDtypeStruct((n, width), BF16) for n in (rows, rows, HALO)],
        [
            pltpu.VMEM((rows, width), BF16),
            pltpu.VMEM((rows, width), F32),
            pltpu.VMEM((rows, slots), BF16),
            weights_of(SLOT),
            copy_sems(1),
        ],
        "linear_out",
    )(
        places, num, queries, first, second, ones, scale, prior, out_one, *near_out_one, tokens,
        gain_two[None],
    )

    halo = lax.ppermute(tail, "seq", [(i, i + 1) for i in range(seq_count - 1)])
    pair_rows = across(normed_two, "tensor", 1)
    pair_halo = lax.ppermute(
        tail,
        ("seq", "tensor"),
        [
            (i * group_count + j, (i + 1) * group_count + (j ^ 1))
            for i in range(seq_count - 1)
            for j in range(group_count)
        ],
    )
    near_window = from_plane(held_window, near_by_window, (residual,), (pair_rows, pair_halo))
    held_out_two = after(held_out_two, (halo,))
    block_start = (seq_place * rows).astype(jnp.int32)[None]

    def window_rows(slot_rows, slot_halo, earlier):
        return call(
            functools.partial(window_kernel, heads),
            2,
            [
                SMEM,
                SMEM,
                *[HBM] * 5,
                each((tap_count, 3 * slots)),
                HBM,
            ],
            each((rows, slots)),
            jax.ShapeDtypeStruct((2, rows, slots), BF16),
            [
                pltpu.VMEM((HALO + rows, width), BF16),
                pltpu.VMEM((2, heads, 3 * SLOT, width), BF16),
                copy_sems(3),
            ],
            "window_rows",
        )(places, block_start, slot_rows, slot_halo, window_t, *near_window, taps, earlier)

    mixed_pair = window_rows(pair_rows, pair_halo, normed_two)
    near_out_two = from_plane(held_out_two, neighbours(held_out_two), None, (mixed_pair,))
    mixed_own = window_rows(normed_two, halo, mixed_pair)
    mixed_pair = across(mixed_pair, "tensor", 1)
    live = (length - seq_place * rows).astype(jnp.int32)[None]
    result = call(
        out_two_kernel,
        group_count,
        [
            SMEM,
            SMEM,
            *[HBM] * 6,
        ],
        whole((rows, width)),
        jax.ShapeDtypeStruct((rows, width), BF16),
        [
            pltpu.VMEM((group_count, rows, slots), BF16),
            pltpu.VMEM((rows, width), BF16),
            pltpu.VMEM((rows, width), F32),
            weights_of(SLOT),
            copy_sems(1),
        ],
        "window_out",
    )(places, live, mixed_own, mixed_pair, out_two, *near_out_two, residual)

    result = result.reshape(page_span, group_count, page_share, width).transpose(1, 0, 2, 3)
    return lax.all_to_all(result, "tensor", split_axis=0, concat_axis=0, tiled=True)


def solution(mesh):
    return jax.shard_map(
        on_device,
        mesh=mesh,
        in_specs=(
            P(("dp", "seq"), "tensor", None),
            P(),
            P(),
            P(),
            P(),
            P(None, None, "tensor"),
            P(None, "tensor"),
            P("tensor", None),
            P(),
            P(None, None, "tensor"),
            P(None, None, "tensor"),
            P("tensor", None),
        ),
        out_specs=P("dp", "seq", "tensor", None),
        check_vma=False,
    )
```

```python
import functools

import jax
import jax.numpy as jnp
import numpy as np
from jax import lax
from jax.experimental import pallas as pl
from jax.experimental.pallas import tpu as pltpu
from jax.sharding import PartitionSpec as P

HEAD = 112
WINDOW = 64
EPS = 1e-05
SLOT = 128
FEAT_SLOT = 256
HALO = 80
NEAR = 4
VMEM = 60 * 1024 * 1024
F32 = jnp.float32
BF16 = jnp.bfloat16


def dot(a, b, dims=((1,), (0,))):
    return lax.dot_general(a, b, (dims, ((), ())), preferred_element_type=F32)


def normed_rows(rows, gain):
    scale = lax.rsqrt(jnp.mean(rows * rows, axis=-1, keepdims=True) + EPS)
    return (rows * scale * gain).astype(BF16)


def feature_tables(heads, feature_dim):
    pairs = [(i, j) for i in range(feature_dim) for j in range(i, feature_dim)]
    pairs += [(i, -1) for i in range(feature_dim)] + [(-1, -1)]
    first = np.zeros((2 * heads * feature_dim, heads * FEAT_SLOT), np.float32)
    second = np.zeros_like(first)
    ones = np.zeros((2, heads * FEAT_SLOT), np.float32)
    scale = np.zeros((1, heads * FEAT_SLOT), np.float32)
    for h in range(heads):
        for n, (i, j) in enumerate(pairs):
            at = h * FEAT_SLOT + n
            if i >= 0:
                first[2 * h * feature_dim + i, at] = 1
            else:
                ones[0, at] = 1
            if j >= 0:
                second[2 * h * feature_dim + j, at] = 1
            else:
                ones[1, at] = 1
            if i < 0:
                scale[0, at] = 1
            elif j < 0:
                scale[0, at] = feature_dim**-0.5
            else:
                scale[0, at] = (0.5 if i == j else 1.0) / feature_dim
    return first, second, ones, scale, -(-len(pairs) // 16) * 16


def features(rows, first, second, ones):
    return (dot(rows, first) + ones[0:1]) * (dot(rows, second) + ones[1:2])


def run_copies(copies_of, groups, loads, meanwhile=None):
    step = pl.program_id(0)

    @pl.when(step == 0)
    def _():
        for copy, _ in loads:
            copy.start()
        for group in range(groups):
            for copy in copies_of(group):
                copy.start()

    for group in range(groups):

        @pl.when(step == group)
        def _(group=group):
            for copy, at in loads:
                if at == group:
                    copy.wait()
            if meanwhile is not None and group == 0:
                meanwhile()
            for copy in copies_of(group):
                copy.wait()


def weight_copies(place_ref, near_ref, far_ref, targets, pieces, sems, group):
    found = []

    def copy(src, dst):
        found.append(pltpu.make_async_copy(src, dst, sems.at[group, len(found)]))

    if group == 0:
        for own_ref, kind, w_ref, off in targets:
            rows = own_ref.shape[2]
            for n in range(NEAR):
                copy(own_ref.at[kind, place_ref[n]], w_ref.at[0, n, off : off + rows, :])
        return found
    cols = near_ref.shape[3]
    for ref, part in ((near_ref, place_ref[NEAR]), (far_ref, 1 - place_ref[NEAR])):
        at = 0
        lanes = pl.ds(pl.multiple_of(part * cols, SLOT), cols)
        for rows, w_ref, off in pieces:
            copy(ref.at[:, group - 1, at : at + rows, :], w_ref.at[group, :, off : off + rows, lanes])
            at += rows
    return found


def zero_between_heads(w_ref):
    groups, heads, rows, width = w_ref.shape
    for at in range(HEAD, rows, SLOT):
        w_ref[:, :, at : at + SLOT - HEAD, :] = jnp.zeros(
            (groups, heads, SLOT - HEAD, width), BF16
        )


def group_weights(w_ref, step):
    heads, rows, width = w_ref.shape[1:]
    return w_ref[step].reshape(heads * rows, width)


def project(rows_ref, w_ref, step):
    return dot(rows_ref[...], group_weights(w_ref, step), ((1,), (1,)))


def linear_kernel(
    heads,
    feature_dim,
    kept,
    place_ref,
    x_ref,
    gain_ref,
    value_ref,
    featmap_ref,
    near_ref,
    far_ref,
    first_ref,
    second_ref,
    ones_ref,
    column_ref,
    num_ref,
    q_ref,
    state_ref,
    tokens_ref,
    normed_ref,
    value_w_ref,
    feat_w_ref,
    sems,
):
    step = pl.program_id(0)
    targets = [
        (value_ref, 0, value_w_ref, 0),
        (featmap_ref, 0, feat_w_ref, 0),
        (featmap_ref, 1, feat_w_ref, feature_dim),
    ]
    pieces = [(HEAD, value_w_ref, 0), (2 * feature_dim, feat_w_ref, 0)]

    groups = value_w_ref.shape[0]

    @pl.when(step == 0)
    def _():
        zero_between_heads(value_w_ref)

    def normalize():
        normed_ref[...] = normed_rows(tokens_ref[...].astype(F32), gain_ref[...])

    run_copies(
        functools.partial(weight_copies, place_ref, near_ref, far_ref, targets, pieces, sems),
        groups,
        [(pltpu.make_async_copy(x_ref, tokens_ref, sems.at[groups, 0]), 0)],
        normalize,
    )
    rows = x_ref.shape[0]
    width = 2 * heads * feature_dim
    queries = project(normed_ref, feat_w_ref, step).astype(BF16)
    keys = pltpu.roll(queries.astype(F32), width - feature_dim, 1).astype(BF16)
    values = (project(normed_ref, value_w_ref, step) + column_ref[...]).astype(BF16)
    q_ref[0] = queries
    lane = lax.broadcasted_iota(jnp.int32, (rows, width), 1)
    causal = lax.broadcasted_iota(jnp.int32, (rows, rows), 1) <= lax.broadcasted_iota(
        jnp.int32, (rows, rows), 0
    )
    key_features = features(keys, first_ref[...], second_ref[...], ones_ref[...]).astype(BF16)
    for h in range(heads):
        at = 2 * h * feature_dim
        own = jnp.where((lane >= at) & (lane < at + feature_dim), queries, jnp.zeros_like(queries))
        scores = dot(own, keys, ((1,), (1,))) * feature_dim**-0.5
        kernel = jnp.where(causal, 1.0 + scores + 0.5 * scores * scores, 0.0).astype(BF16)
        value = values[:, h * SLOT : (h + 1) * SLOT]
        num_ref[0, :, h * SLOT : (h + 1) * SLOT] = dot(kernel, value)
        state = dot(key_features[:, h * FEAT_SLOT : h * FEAT_SLOT + kept], value, ((0,), (0,)))
        head = pl.multiple_of(place_ref[h] * kept, 16)
        state_ref[0, pl.ds(head, kept), :] = state.astype(BF16)


def add_branch(mixed, w_ref, total_ref):
    step = pl.program_id(0)
    total_ref[...] += dot(mixed, group_weights(w_ref, step)).astype(BF16).astype(F32)


def out_one_kernel(
    heads,
    kept,
    place_ref,
    num_ref,
    q_ref,
    first_ref,
    second_ref,
    ones_ref,
    scale_ref,
    prior_ref,
    own_ref,
    near_ref,
    far_ref,
    x_ref,
    gain_ref,
    residual_ref,
    normed_ref,
    tail_ref,
    tokens_ref,
    total_ref,
    mixed_ref,
    w_ref,
    sems,
):
    step = pl.program_id(0)
    groups = w_ref.shape[0]

    @pl.when(step == 0)
    def _():
        total_ref[...] = jnp.zeros_like(total_ref)
        zero_between_heads(w_ref)

    loads = [(pltpu.make_async_copy(x_ref, tokens_ref, sems.at[groups, 0]), groups - 1)]
    run_copies(
        functools.partial(
            weight_copies,
            place_ref,
            near_ref,
            far_ref,
            [(own_ref, 0, w_ref, 0)],
            [(HEAD, w_ref, 0)],
            sems,
        ),
        groups,
        loads,
    )

    query_features = features(q_ref[0], first_ref[...], second_ref[...], ones_ref[...])
    query_features = (query_features * scale_ref[...]).astype(BF16)
    for h in range(heads):
        prior = prior_ref[0, pl.ds(pl.multiple_of(place_ref[h] * kept, 16), kept), :]
        lanes = slice(h * SLOT, (h + 1) * SLOT)
        total = num_ref[0, :, lanes] + dot(
            query_features[:, h * FEAT_SLOT : h * FEAT_SLOT + kept], prior.astype(BF16)
        )
        mixed_ref[:, lanes] = (total * (1.0 / total[:, HEAD : HEAD + 1])).astype(BF16)
    add_branch(mixed_ref[...], w_ref, total_ref)

    @pl.when(step == pl.num_programs(0) - 1)
    def _():
        residual = (tokens_ref[...].astype(F32) + total_ref[...]).astype(BF16)
        residual_ref[...] = residual
        normed = normed_rows(residual.astype(F32), gain_ref[...])
        normed_ref[...] = normed
        tail_ref[...] = normed[normed.shape[0] - HALO :]


def window_kernel(
    heads,
    place_ref,
    first_ref,
    x_ref,
    halo_ref,
    own_ref,
    near_ref,
    far_ref,
    tap_ref,
    _,
    mixed_ref,
    rows_ref,
    w_ref,
    sems,
):
    step = pl.program_id(0)
    targets = [(own_ref, kind, w_ref, kind * SLOT) for kind in range(3)]
    pieces = [(HEAD, w_ref, kind * SLOT) for kind in range(3)]

    groups = w_ref.shape[0]
    loads = [
        (pltpu.make_async_copy(src, rows_ref.at[at : at + src.shape[0], :], sems.at[groups, n]), 0)
        for n, (src, at) in enumerate(((halo_ref, 0), (x_ref, HALO)))
    ]

    @pl.when(step == 0)
    def _():
        zero_between_heads(w_ref)

    run_copies(
        functools.partial(weight_copies, place_ref, near_ref, far_ref, targets, pieces, sems),
        groups,
        loads,
    )
    rows = x_ref.shape[0]
    lead = HALO - WINDOW
    projected = project(rows_ref, w_ref, step)
    taps = tap_ref[0]
    convolved = taps[0:1] * projected
    for offset in range(1, taps.shape[0]):
        convolved = convolved + taps[offset : offset + 1] * pltpu.roll(projected, offset, 0)
    convolved = convolved[lead:].astype(BF16)
    tile = 128
    span = tile + WINDOW
    row = lax.broadcasted_iota(jnp.int32, (tile, span), 0)
    col = lax.broadcasted_iota(jnp.int32, (tile, span), 1)
    band = (col > row) & (col <= row + WINDOW)
    for h in range(heads):
        at = 3 * h * SLOT
        queries = convolved[WINDOW:, at : at + SLOT]
        keys = convolved[:, at + SLOT : at + 2 * SLOT]
        values = convolved[:, at + 2 * SLOT : at + 3 * SLOT]
        for start in range(0, rows, tile):
            logits = dot(queries[start : start + tile], keys[start : start + span], ((1,), (1,)))
            allowed = band
            if start < WINDOW:
                allowed = band & (col >= WINDOW - start - first_ref[0])
            logits = jnp.where(allowed, logits * HEAD**-0.5, -jnp.inf)
            weights = jnp.exp(logits - jnp.max(logits, axis=1, keepdims=True))
            weights = weights * (1.0 / jnp.sum(weights, axis=1, keepdims=True))
            mixed = dot(weights.astype(BF16), values[start : start + span])
            mixed_ref[0, start : start + tile, h * SLOT : (h + 1) * SLOT] = mixed.astype(BF16)


def out_two_kernel(
    place_ref,
    live_ref,
    mixed_ref,
    pair_ref,
    own_ref,
    near_ref,
    far_ref,
    residual_ref,
    out_ref,
    mixed_all_ref,
    rows_ref,
    total_ref,
    w_ref,
    sems,
):
    step = pl.program_id(0)
    groups = w_ref.shape[0]
    loads = [
        (pltpu.make_async_copy(mixed_ref, mixed_all_ref.at[:2], sems.at[groups, 0]), 0),
        (pltpu.make_async_copy(pair_ref, mixed_all_ref.at[2:], sems.at[groups, 1]), 2),
        (pltpu.make_async_copy(residual_ref, rows_ref, sems.at[groups, 2]), groups - 1),
    ]

    @pl.when(step == 0)
    def _():
        total_ref[...] = jnp.zeros_like(total_ref)
        zero_between_heads(w_ref)

    run_copies(
        functools.partial(
            weight_copies,
            place_ref,
            near_ref,
            far_ref,
            [(own_ref, 0, w_ref, 0)],
            [(HEAD, w_ref, 0)],
            sems,
        ),
        groups,
        loads,
    )
    add_branch(mixed_all_ref[step], w_ref, total_ref)

    @pl.when(step == pl.num_programs(0) - 1)
    def _():
        result = (rows_ref[...].astype(F32) + total_ref[...]).astype(BF16)
        row = lax.broadcasted_iota(jnp.int32, result.shape, 0)
        out_ref[...] = jnp.where(row < live_ref[0], result, jnp.zeros_like(result))


def whole(shape):
    return pl.BlockSpec(shape, lambda g: (0,) * len(shape))


def each(shape):
    return pl.BlockSpec((1,) + shape, lambda g: (g,) + (0,) * len(shape))


SMEM = pl.BlockSpec(memory_space=pltpu.SMEM)
HBM = pl.BlockSpec(memory_space=pl.ANY)


def call(kernel, groups, in_specs, out_specs, out_shape, scratch, name):
    return pl.pallas_call(
        kernel,
        grid=(groups,),
        in_specs=in_specs,
        out_specs=out_specs,
        out_shape=out_shape,
        scratch_shapes=scratch,
        compiler_params=pltpu.CompilerParams(
            dimension_semantics=("arbitrary",), vmem_limit_bytes=VMEM
        ),
        cost_estimate=pl.CostEstimate(flops=0, bytes_accessed=0, transcendentals=0),
        name=name,
    )


def own_piece(whole_weights):
    head, part = lax.axis_index("seq") % NEAR, lax.axis_index("dp")
    found = []
    for weights in whole_weights:
        kinds, _, rows, cols = weights.shape
        cols = cols // lax.axis_size("dp")
        piece = lax.dynamic_slice(weights, (0, head, 0, part * cols), (kinds, 1, rows, cols))
        found.append(piece.reshape(kinds * rows, cols))
    return jnp.concatenate(found, axis=0)


def across(array, axis, bit):
    return lax.ppermute(array, axis, [(i, i ^ bit) for i in range(lax.axis_size(axis))])


def after(array, others):
    if not others:
        return array
    first = [lax.slice(other, (0,) * other.ndim, (1,) * other.ndim) for other in others]
    zero = sum(one.reshape(()).astype(F32) * 0.0 for one in first)
    return jnp.where(zero == 0.0, array, jnp.zeros_like(array))


def settled(array, others=()):
    return lax.optimization_barrier(after(array, others))


def from_group(piece, over_z):
    return across(after(piece, over_z), "tensor", 2)[None]


def from_groups(piece, over_z, order=(0, 1, 2)):
    piece = after(piece, over_z)
    beside, beyond = across(piece, "tensor", 1), across(piece, "tensor", 2)
    found = (beside, beyond, across(beyond, "tensor", 1))
    return [found[n] for n in order]


def neighbours(held):
    return across(held, "seq", 1), across(held, "seq", 2)


def from_plane(held, near_by, diagonal, over_cores, over_across=()):
    beside, above = near_by
    if diagonal is None:
        opposite = across(after(held, over_across), "seq", 3)
    else:
        half = -(-held.shape[1] // 32) * 16
        opposite = [
            across(after(above[:, :half], diagonal), "seq", 1),
            across(after(beside[:, half:], diagonal), "seq", 2),
        ]
        opposite = after(jnp.concatenate(opposite, axis=1), over_cores)
    near = after(jnp.stack([held, beside, above, opposite]), over_cores)
    return near, across(near, "dp", 1)


def earlier_blocks(state, axis):
    peers = lax.axis_size(axis)
    if peers <= 4:
        found = [
            lax.ppermute(state, axis, [(i, i + by) for i in range(peers - by)])
            for by in range(1, peers)
        ]
        return sum(one.astype(F32) for one in found)
    everything = lax.all_gather(state, axis).astype(F32)
    reached = jnp.arange(peers) < lax.axis_index(axis)
    return jnp.sum(jnp.where(reached[:, None, None, None], everything, 0.0), axis=0)


def on_device(
    pool,
    page_table,
    reassign,
    lengths,
    gain_one,
    w_featmap,
    w_value,
    w_out_one,
    gain_two,
    w_window,
    conv_window,
    w_out_two,
):
    dp_count, seq_count, group_count = (lax.axis_size(n) for n in ("dp", "seq", "tensor"))
    groups = dp_count * seq_count
    device_place = lax.axis_index(("dp", "seq"))
    dp_place, seq_place, tensor_place = (lax.axis_index(n) for n in ("dp", "seq", "tensor"))
    pages_dev, page_share, width = pool.shape
    slots_total, pages_total = page_table.shape
    req_dev = slots_total // dp_count
    page_span = pages_total // seq_count
    page_rows = page_share * group_count
    rows = page_span * page_rows
    assert req_dev == group_count
    heads = w_value.shape[1] // HEAD
    head_cols = heads * HEAD
    feat_cols = w_featmap.shape[2]
    feature_dim = feat_cols // heads
    tap_count = conv_window.shape[0]

    assert heads == NEAR and dp_count == 2
    values_t = w_value.T.reshape(1, heads, HEAD, width)
    featmap_t = w_featmap.transpose(1, 2, 0).reshape(2, heads, feature_dim, width)
    window_t = w_window.transpose(1, 2, 0).reshape(3, heads, HEAD, width)
    out_one, out_two = (w.reshape(1, heads, HEAD, width) for w in (w_out_one, w_out_two))
    places = jnp.concatenate([(seq_place % NEAR) ^ jnp.arange(NEAR), dp_place[None]])
    places = places.astype(jnp.int32)
    taps = conv_window.reshape(tap_count, 3, heads, HEAD).transpose(0, 2, 1, 3)
    taps = jnp.take(taps, places[:NEAR], axis=1, mode="clip")
    taps = jnp.pad(taps, ((0, 0), (0, 0), (0, 0), (0, SLOT - HEAD)))
    taps = taps.reshape(tap_count, 3 * heads * SLOT)
    taps = settled(jnp.stack([taps, across(taps, "tensor", 2)]))
    held_one = from_groups(own_piece([values_t, featmap_t]), ())
    held_one = settled(jnp.stack(held_one), (taps,))

    placed = reassign[:, None] == jnp.arange(slots_total, dtype=jnp.int32)[None, :]
    table = jnp.sum(jnp.where(placed[:, :, None], page_table[None], 0), axis=1)
    slot_lengths = jnp.sum(jnp.where(placed, lengths[None, :], 0), axis=1)
    source_page = (
        table.reshape(dp_count, req_dev, seq_count, page_span)
        .transpose(0, 2, 1, 3)
        .reshape(groups, req_dev * page_span)
    )
    capacity = (pages_dev + groups - 1) // groups
    page_owner = source_page // pages_dev
    pool_slot = source_page % pages_dev
    before = jnp.arange(pages_dev)[None, :] < jnp.arange(pages_dev)[:, None]
    pair_rank = jnp.sum((page_owner[:, :, None] == page_owner[:, None, :]) & before[None], axis=2)
    send_hit = (page_owner == device_place)[:, None, :] & (
        pair_rank[:, None, :] == jnp.arange(capacity)[None, :, None]
    )
    send_slot = jnp.sum(jnp.where(send_hit, pool_slot[:, None, :], 0), axis=2)
    outgoing = pool.at[send_slot.reshape(-1)].get(mode="promise_in_bounds")
    outgoing = outgoing.reshape(groups, capacity, page_share, width)
    arrived = lax.all_to_all(outgoing, ("dp", "seq"), split_axis=0, concat_axis=0, tiled=True)
    own_row = jnp.arange(groups)[:, None] == device_place
    pick_rows = jnp.sum(jnp.where(own_row, page_owner * capacity + pair_rank, 0), axis=0)
    picked = arrived.reshape(groups * capacity, page_share, width)
    picked = picked.at[pick_rows].get(mode="promise_in_bounds")

    picked = after(picked.reshape(req_dev, page_span, page_share, width), (held_one,))
    swapped = lax.all_to_all(picked, "tensor", split_axis=0, concat_axis=0, tiled=True)
    tokens = swapped.transpose(1, 0, 2, 3).reshape(rows, width)
    slot = dp_place * req_dev + tensor_place
    length = jnp.sum(jnp.where(jnp.arange(slots_total) == slot, slot_lengths, 0))

    held_out_one = settled(jnp.stack(from_groups(own_piece([out_one]), (picked,))))
    near_one = from_plane(held_one, neighbours(held_one), (swapped,), (held_out_one,))
    out_piece = after(own_piece([out_two]), (swapped,))
    beyond = from_group(own_piece([window_t, out_two]), (swapped,))
    first, second, ones, scale, kept = feature_tables(heads, feature_dim)
    first, second = jnp.asarray(first, BF16), jnp.asarray(second, BF16)
    column = np.zeros((1, heads * SLOT), np.float32)
    column[0, HEAD::SLOT] = 1

    def copy_sems(kinds):
        return pltpu.SemaphoreType.DMA((group_count + 1, NEAR * kinds))

    def weights_of(rows_of_head):
        return pltpu.VMEM((group_count, heads, rows_of_head, width), BF16)

    slots = heads * SLOT
    num, queries, state = call(
        functools.partial(linear_kernel, heads, feature_dim, kept),
        group_count,
        [
            SMEM,
            HBM,
            whole((1, width)),
            *[HBM] * 4,
            whole(first.shape),
            whole(second.shape),
            whole(ones.shape),
            whole(column.shape),
        ],
        [each((rows, slots)), each((rows, 2 * feat_cols)), each((heads * kept, SLOT))],
        [
            jax.ShapeDtypeStruct((group_count, rows, slots), F32),
            jax.ShapeDtypeStruct((group_count, rows, 2 * feat_cols), BF16),
            jax.ShapeDtypeStruct((group_count, heads * kept, SLOT), BF16),
        ],
        [
            pltpu.VMEM((rows, width), BF16),
            pltpu.VMEM((rows, width), BF16),
            weights_of(SLOT),
            weights_of(2 * feature_dim),
            copy_sems(3),
        ],
        "linear_rows",
    )(
        places, tokens, gain_one[None], values_t, featmap_t, *near_one, first, second, ones, column
    )
    prior = settled(earlier_blocks(state, "seq"))
    beyond = after(beyond, (state,))
    held_window, out_beyond = beyond[:, : 3 * HEAD], beyond[0, 3 * HEAD :]
    held_out_two = [out_beyond, across(out_piece, "tensor", 1), across(out_beyond, "tensor", 1)]
    held_out_two = settled(jnp.stack(held_out_two), (prior,))
    near_out_one = from_plane(
        held_out_one, neighbours(held_out_one), (state,), (beyond, held_out_two)
    )
    held_window = after(held_window, (prior,))
    near_by_window = neighbours(held_window)
    residual, normed_two, tail = call(
        functools.partial(out_one_kernel, heads, kept),
        group_count,
        [
            SMEM,
            each((rows, slots)),
            each((rows, 2 * feat_cols)),
            whole(first.shape),
            whole(second.shape),
            whole(ones.shape),
            whole(scale.shape),
        ]
        + [each((heads * kept, SLOT))]
        + [HBM] * 4
        + [whole((1, width))],
        [whole((n, width)) for n in (rows, rows, HALO)],
        [jax.ShapeDtypeStruct((n, width), BF16) for n in (rows, rows, HALO)],
        [
            pltpu.VMEM((rows, width), BF16),
            pltpu.VMEM((rows, width), F32),
            pltpu.VMEM((rows, slots), BF16),
            weights_of(SLOT),
            copy_sems(1),
        ],
        "linear_out",
    )(
        places, num, queries, first, second, ones, scale, prior, out_one, *near_out_one, tokens,
        gain_two[None],
    )

    halo = lax.ppermute(tail, "seq", [(i, i + 1) for i in range(seq_count - 1)])
    pair_rows = across(normed_two, "tensor", 1)
    pair_halo = lax.ppermute(
        tail,
        ("seq", "tensor"),
        [
            (i * group_count + j, (i + 1) * group_count + (j ^ 1))
            for i in range(seq_count - 1)
            for j in range(group_count)
        ],
    )
    held_out_two = after(held_out_two, (residual,))
    near_by_two = neighbours(held_out_two)
    near_window = from_plane(
        held_window, near_by_window, (residual,), (pair_rows, pair_halo, *near_by_two)
    )
    block_start = (seq_place * rows).astype(jnp.int32)[None]

    def window_rows(slot_rows, slot_halo, earlier):
        return call(
            functools.partial(window_kernel, heads),
            2,
            [
                SMEM,
                SMEM,
                *[HBM] * 5,
                each((tap_count, 3 * slots)),
                HBM,
            ],
            each((rows, slots)),
            jax.ShapeDtypeStruct((2, rows, slots), BF16),
            [
                pltpu.VMEM((HALO + rows, width), BF16),
                pltpu.VMEM((2, heads, 3 * SLOT, width), BF16),
                copy_sems(3),
            ],
            "window_rows",
        )(places, block_start, slot_rows, slot_halo, window_t, *near_window, taps, earlier)

    mixed_pair = window_rows(pair_rows, pair_halo, normed_two)
    near_out_two = from_plane(held_out_two, near_by_two, None, (mixed_pair,))
    mixed_own = window_rows(normed_two, halo, mixed_pair)
    mixed_pair = across(mixed_pair, "tensor", 1)
    live = (length - seq_place * rows).astype(jnp.int32)[None]
    result = call(
        out_two_kernel,
        group_count,
        [
            SMEM,
            SMEM,
            *[HBM] * 6,
        ],
        whole((rows, width)),
        jax.ShapeDtypeStruct((rows, width), BF16),
        [
            pltpu.VMEM((group_count, rows, slots), BF16),
            pltpu.VMEM((rows, width), BF16),
            pltpu.VMEM((rows, width), F32),
            weights_of(SLOT),
            copy_sems(1),
        ],
        "window_out",
    )(places, live, mixed_own, mixed_pair, out_two, *near_out_two, residual)

    result = result.reshape(page_span, group_count, page_share, width).transpose(1, 0, 2, 3)
    return lax.all_to_all(result, "tensor", split_axis=0, concat_axis=0, tiled=True)


def solution(mesh):
    return jax.shard_map(
        on_device,
        mesh=mesh,
        in_specs=(
            P(("dp", "seq"), "tensor", None),
            P(),
            P(),
            P(),
            P(),
            P(None, None, "tensor"),
            P(None, "tensor"),
            P("tensor", None),
            P(),
            P(None, None, "tensor"),
            P(None, None, "tensor"),
            P("tensor", None),
        ),
        out_specs=P("dp", "seq", "tensor", None),
        check_vma=False,
    )
```

```python
import functools

import jax
import jax.numpy as jnp
import numpy as np
from jax import lax
from jax.experimental import pallas as pl
from jax.experimental.pallas import tpu as pltpu
from jax.sharding import PartitionSpec as P

HEAD = 112
WINDOW = 64
EPS = 1e-05
SLOT = 128
FEAT_SLOT = 256
HALO = 80
NEAR = 4
VMEM = 60 * 1024 * 1024
F32 = jnp.float32
BF16 = jnp.bfloat16


def dot(a, b, dims=((1,), (0,))):
    return lax.dot_general(a, b, (dims, ((), ())), preferred_element_type=F32)


def normed_rows(rows, gain):
    scale = lax.rsqrt(jnp.mean(rows * rows, axis=-1, keepdims=True) + EPS)
    return (rows * scale * gain).astype(BF16)


def feature_tables(heads, feature_dim):
    pairs = [(i, j) for i in range(feature_dim) for j in range(i, feature_dim)]
    pairs += [(i, -1) for i in range(feature_dim)] + [(-1, -1)]
    first = np.zeros((2 * heads * feature_dim, heads * FEAT_SLOT), np.float32)
    second = np.zeros_like(first)
    ones = np.zeros((2, heads * FEAT_SLOT), np.float32)
    scale = np.zeros((1, heads * FEAT_SLOT), np.float32)
    for h in range(heads):
        for n, (i, j) in enumerate(pairs):
            at = h * FEAT_SLOT + n
            if i >= 0:
                first[2 * h * feature_dim + i, at] = 1
            else:
                ones[0, at] = 1
            if j >= 0:
                second[2 * h * feature_dim + j, at] = 1
            else:
                ones[1, at] = 1
            if i < 0:
                scale[0, at] = 1
            elif j < 0:
                scale[0, at] = feature_dim**-0.5
            else:
                scale[0, at] = (0.5 if i == j else 1.0) / feature_dim
    return first, second, ones, scale, -(-len(pairs) // 16) * 16


def features(rows, first, second, ones):
    return (dot(rows, first) + ones[0:1]) * (dot(rows, second) + ones[1:2])


def run_copies(copies_of, groups, loads, meanwhile=None):
    step = pl.program_id(0)

    @pl.when(step == 0)
    def _():
        for copy, _ in loads:
            copy.start()
        for group in range(groups):
            for copy in copies_of(group):
                copy.start()

    for group in range(groups):

        @pl.when(step == group)
        def _(group=group):
            for copy, at in loads:
                if at == group:
                    copy.wait()
            if meanwhile is not None and group == 0:
                meanwhile()
            for copy in copies_of(group):
                copy.wait()


def weight_copies(place_ref, near_ref, far_ref, targets, pieces, sems, group):
    found = []

    def copy(src, dst):
        found.append(pltpu.make_async_copy(src, dst, sems.at[group, len(found)]))

    if group == 0:
        for own_ref, kind, w_ref, off in targets:
            rows = own_ref.shape[2]
            for n in range(NEAR):
                copy(own_ref.at[kind, place_ref[n]], w_ref.at[0, n, off : off + rows, :])
        return found
    cols = near_ref.shape[3]
    for ref, part in ((near_ref, place_ref[NEAR]), (far_ref, 1 - place_ref[NEAR])):
        at = 0
        lanes = pl.ds(pl.multiple_of(part * cols, SLOT), cols)
        for rows, w_ref, off in pieces:
            copy(ref.at[:, group - 1, at : at + rows, :], w_ref.at[group, :, off : off + rows, lanes])
            at += rows
    return found


def zero_between_heads(w_ref):
    groups, heads, rows, width = w_ref.shape
    for at in range(HEAD, rows, SLOT):
        w_ref[:, :, at : at + SLOT - HEAD, :] = jnp.zeros(
            (groups, heads, SLOT - HEAD, width), BF16
        )


def group_weights(w_ref, step):
    heads, rows, width = w_ref.shape[1:]
    return w_ref[step].reshape(heads * rows, width)


def project(rows_ref, w_ref, step):
    return dot(rows_ref[...], group_weights(w_ref, step), ((1,), (1,)))


def linear_kernel(
    heads,
    feature_dim,
    kept,
    place_ref,
    x_ref,
    gain_ref,
    value_ref,
    featmap_ref,
    near_ref,
    far_ref,
    first_ref,
    second_ref,
    ones_ref,
    column_ref,
    num_ref,
    q_ref,
    state_ref,
    tokens_ref,
    normed_ref,
    value_w_ref,
    feat_w_ref,
    sems,
):
    step = pl.program_id(0)
    targets = [
        (value_ref, 0, value_w_ref, 0),
        (featmap_ref, 0, feat_w_ref, 0),
        (featmap_ref, 1, feat_w_ref, feature_dim),
    ]
    pieces = [(HEAD, value_w_ref, 0), (2 * feature_dim, feat_w_ref, 0)]

    groups = value_w_ref.shape[0]

    @pl.when(step == 0)
    def _():
        zero_between_heads(value_w_ref)

    def normalize():
        normed_ref[...] = normed_rows(tokens_ref[...].astype(F32), gain_ref[...])

    run_copies(
        functools.partial(weight_copies, place_ref, near_ref, far_ref, targets, pieces, sems),
        groups,
        [(pltpu.make_async_copy(x_ref, tokens_ref, sems.at[groups, 0]), 0)],
        normalize,
    )
    rows = x_ref.shape[0]
    width = 2 * heads * feature_dim
    queries = project(normed_ref, feat_w_ref, step).astype(BF16)
    keys = pltpu.roll(queries.astype(F32), width - feature_dim, 1).astype(BF16)
    values = (project(normed_ref, value_w_ref, step) + column_ref[...]).astype(BF16)
    q_ref[0] = queries
    lane = lax.broadcasted_iota(jnp.int32, (rows, width), 1)
    causal = lax.broadcasted_iota(jnp.int32, (rows, rows), 1) <= lax.broadcasted_iota(
        jnp.int32, (rows, rows), 0
    )
    key_features = features(keys, first_ref[...], second_ref[...], ones_ref[...]).astype(BF16)
    for h in range(heads):
        at = 2 * h * feature_dim
        own = jnp.where((lane >= at) & (lane < at + feature_dim), queries, jnp.zeros_like(queries))
        scores = dot(own, keys, ((1,), (1,))) * feature_dim**-0.5
        kernel = jnp.where(causal, 1.0 + scores + 0.5 * scores * scores, 0.0).astype(BF16)
        value = values[:, h * SLOT : (h + 1) * SLOT]
        num_ref[0, :, h * SLOT : (h + 1) * SLOT] = dot(kernel, value)
        state = dot(key_features[:, h * FEAT_SLOT : h * FEAT_SLOT + kept], value, ((0,), (0,)))
        head = pl.multiple_of(place_ref[h] * kept, 16)
        state_ref[0, pl.ds(head, kept), :] = state.astype(BF16)


def add_branch(mixed, w_ref, total_ref):
    step = pl.program_id(0)
    total_ref[...] += dot(mixed, group_weights(w_ref, step)).astype(BF16).astype(F32)


def out_one_kernel(
    heads,
    kept,
    place_ref,
    num_ref,
    q_ref,
    first_ref,
    second_ref,
    ones_ref,
    scale_ref,
    prior_ref,
    own_ref,
    near_ref,
    far_ref,
    x_ref,
    gain_ref,
    residual_ref,
    normed_ref,
    tail_ref,
    tokens_ref,
    total_ref,
    mixed_ref,
    w_ref,
    sems,
):
    step = pl.program_id(0)
    groups = w_ref.shape[0]

    @pl.when(step == 0)
    def _():
        total_ref[...] = jnp.zeros_like(total_ref)
        zero_between_heads(w_ref)

    loads = [(pltpu.make_async_copy(x_ref, tokens_ref, sems.at[groups, 0]), groups - 1)]
    run_copies(
        functools.partial(
            weight_copies,
            place_ref,
            near_ref,
            far_ref,
            [(own_ref, 0, w_ref, 0)],
            [(HEAD, w_ref, 0)],
            sems,
        ),
        groups,
        loads,
    )

    query_features = features(q_ref[0], first_ref[...], second_ref[...], ones_ref[...])
    query_features = (query_features * scale_ref[...]).astype(BF16)
    for h in range(heads):
        prior = prior_ref[0, pl.ds(pl.multiple_of(place_ref[h] * kept, 16), kept), :]
        lanes = slice(h * SLOT, (h + 1) * SLOT)
        total = num_ref[0, :, lanes] + dot(
            query_features[:, h * FEAT_SLOT : h * FEAT_SLOT + kept], prior.astype(BF16)
        )
        mixed_ref[:, lanes] = (total * (1.0 / total[:, HEAD : HEAD + 1])).astype(BF16)
    add_branch(mixed_ref[...], w_ref, total_ref)

    @pl.when(step == pl.num_programs(0) - 1)
    def _():
        residual = (tokens_ref[...].astype(F32) + total_ref[...]).astype(BF16)
        residual_ref[...] = residual
        normed = normed_rows(residual.astype(F32), gain_ref[...])
        normed_ref[...] = normed
        tail_ref[...] = normed[normed.shape[0] - HALO :]


def window_kernel(
    heads,
    place_ref,
    first_ref,
    x_ref,
    halo_ref,
    own_ref,
    near_ref,
    far_ref,
    tap_ref,
    _,
    mixed_ref,
    rows_ref,
    w_ref,
    sems,
):
    step = pl.program_id(0)
    targets = [(own_ref, kind, w_ref, kind * SLOT) for kind in range(3)]
    pieces = [(HEAD, w_ref, kind * SLOT) for kind in range(3)]

    groups = w_ref.shape[0]
    loads = [
        (pltpu.make_async_copy(src, rows_ref.at[at : at + src.shape[0], :], sems.at[groups, n]), 0)
        for n, (src, at) in enumerate(((halo_ref, 0), (x_ref, HALO)))
    ]

    @pl.when(step == 0)
    def _():
        zero_between_heads(w_ref)

    run_copies(
        functools.partial(weight_copies, place_ref, near_ref, far_ref, targets, pieces, sems),
        groups,
        loads,
    )
    rows = x_ref.shape[0]
    lead = HALO - WINDOW
    projected = project(rows_ref, w_ref, step)
    taps = tap_ref[0]
    convolved = taps[0:1] * projected
    for offset in range(1, taps.shape[0]):
        convolved = convolved + taps[offset : offset + 1] * pltpu.roll(projected, offset, 0)
    convolved = convolved[lead:].astype(BF16)
    tile = 128
    span = tile + WINDOW
    row = lax.broadcasted_iota(jnp.int32, (tile, span), 0)
    col = lax.broadcasted_iota(jnp.int32, (tile, span), 1)
    band = (col > row) & (col <= row + WINDOW)
    for h in range(heads):
        at = 3 * h * SLOT
        queries = convolved[WINDOW:, at : at + SLOT]
        keys = convolved[:, at + SLOT : at + 2 * SLOT]
        values = convolved[:, at + 2 * SLOT : at + 3 * SLOT]
        for start in range(0, rows, tile):
            logits = dot(queries[start : start + tile], keys[start : start + span], ((1,), (1,)))
            allowed = band
            if start < WINDOW:
                allowed = band & (col >= WINDOW - start - first_ref[0])
            logits = jnp.where(allowed, logits * HEAD**-0.5, -jnp.inf)
            weights = jnp.exp(logits - jnp.max(logits, axis=1, keepdims=True))
            weights = weights * (1.0 / jnp.sum(weights, axis=1, keepdims=True))
            mixed = dot(weights.astype(BF16), values[start : start + span])
            mixed_ref[0, start : start + tile, h * SLOT : (h + 1) * SLOT] = mixed.astype(BF16)


def out_two_kernel(
    place_ref,
    live_ref,
    mixed_ref,
    pair_ref,
    own_ref,
    near_ref,
    far_ref,
    residual_ref,
    out_ref,
    mixed_all_ref,
    rows_ref,
    total_ref,
    w_ref,
    sems,
):
    step = pl.program_id(0)
    groups = w_ref.shape[0]
    loads = [
        (pltpu.make_async_copy(mixed_ref, mixed_all_ref.at[:2], sems.at[groups, 0]), 0),
        (pltpu.make_async_copy(pair_ref, mixed_all_ref.at[2:], sems.at[groups, 1]), 2),
        (pltpu.make_async_copy(residual_ref, rows_ref, sems.at[groups, 2]), groups - 1),
    ]

    @pl.when(step == 0)
    def _():
        total_ref[...] = jnp.zeros_like(total_ref)
        zero_between_heads(w_ref)

    run_copies(
        functools.partial(
            weight_copies,
            place_ref,
            near_ref,
            far_ref,
            [(own_ref, 0, w_ref, 0)],
            [(HEAD, w_ref, 0)],
            sems,
        ),
        groups,
        loads,
    )
    add_branch(mixed_all_ref[step], w_ref, total_ref)

    @pl.when(step == pl.num_programs(0) - 1)
    def _():
        result = (rows_ref[...].astype(F32) + total_ref[...]).astype(BF16)
        row = lax.broadcasted_iota(jnp.int32, result.shape, 0)
        out_ref[...] = jnp.where(row < live_ref[0], result, jnp.zeros_like(result))


def whole(shape):
    return pl.BlockSpec(shape, lambda g: (0,) * len(shape))


def each(shape):
    return pl.BlockSpec((1,) + shape, lambda g: (g,) + (0,) * len(shape))


SMEM = pl.BlockSpec(memory_space=pltpu.SMEM)
HBM = pl.BlockSpec(memory_space=pl.ANY)


def call(kernel, groups, in_specs, out_specs, out_shape, scratch, name):
    return pl.pallas_call(
        kernel,
        grid=(groups,),
        in_specs=in_specs,
        out_specs=out_specs,
        out_shape=out_shape,
        scratch_shapes=scratch,
        compiler_params=pltpu.CompilerParams(
            dimension_semantics=("arbitrary",), vmem_limit_bytes=VMEM
        ),
        cost_estimate=pl.CostEstimate(flops=0, bytes_accessed=0, transcendentals=0),
        name=name,
    )


def own_piece(whole_weights):
    head, part = lax.axis_index("seq") % NEAR, lax.axis_index("dp")
    found = []
    for weights in whole_weights:
        kinds, _, rows, cols = weights.shape
        cols = cols // lax.axis_size("dp")
        piece = lax.dynamic_slice(weights, (0, head, 0, part * cols), (kinds, 1, rows, cols))
        found.append(piece.reshape(kinds * rows, cols))
    return jnp.concatenate(found, axis=0)


def across(array, axis, bit):
    return lax.ppermute(array, axis, [(i, i ^ bit) for i in range(lax.axis_size(axis))])


def after(array, others):
    if not others:
        return array
    first = [lax.slice(other, (0,) * other.ndim, (1,) * other.ndim) for other in others]
    zero = sum(one.reshape(()).astype(F32) * 0.0 for one in first)
    return jnp.where(zero == 0.0, array, jnp.zeros_like(array))


def settled(array, others=()):
    return lax.optimization_barrier(after(array, others))


def from_group(piece, over_z):
    return across(after(piece, over_z), "tensor", 2)[None]


def from_groups(piece, over_z, order=(0, 1, 2)):
    piece = after(piece, over_z)
    beside, beyond = across(piece, "tensor", 1), across(piece, "tensor", 2)
    found = (beside, beyond, across(beyond, "tensor", 1))
    return [found[n] for n in order]


def neighbours(held):
    return across(held, "seq", 1), across(held, "seq", 2)


def from_plane(held, near_by, diagonal, over_cores, by_one_way=False):
    beside, above = near_by
    if by_one_way:
        beside = settled(beside, diagonal)
        opposite = across(after(above, (beside,)), "seq", 1)
    elif diagonal is None:
        opposite = across(held, "seq", 3)
    else:
        half = -(-held.shape[1] // 32) * 16
        opposite = [
            across(after(above[:, :half], diagonal), "seq", 1),
            across(after(beside[:, half:], diagonal), "seq", 2),
        ]
        opposite = after(jnp.concatenate(opposite, axis=1), over_cores)
    near = after(jnp.stack([held, beside, above, opposite]), over_cores)
    return near, across(near, "dp", 1)


def earlier_blocks(state, axis):
    peers = lax.axis_size(axis)
    if peers <= 4:
        found = [
            lax.ppermute(state, axis, [(i, i + by) for i in range(peers - by)])
            for by in range(1, peers)
        ]
        return sum(one.astype(F32) for one in found)
    everything = lax.all_gather(state, axis).astype(F32)
    reached = jnp.arange(peers) < lax.axis_index(axis)
    return jnp.sum(jnp.where(reached[:, None, None, None], everything, 0.0), axis=0)


def on_device(
    pool,
    page_table,
    reassign,
    lengths,
    gain_one,
    w_featmap,
    w_value,
    w_out_one,
    gain_two,
    w_window,
    conv_window,
    w_out_two,
):
    dp_count, seq_count, group_count = (lax.axis_size(n) for n in ("dp", "seq", "tensor"))
    groups = dp_count * seq_count
    device_place = lax.axis_index(("dp", "seq"))
    dp_place, seq_place, tensor_place = (lax.axis_index(n) for n in ("dp", "seq", "tensor"))
    pages_dev, page_share, width = pool.shape
    slots_total, pages_total = page_table.shape
    req_dev = slots_total // dp_count
    page_span = pages_total // seq_count
    page_rows = page_share * group_count
    rows = page_span * page_rows
    assert req_dev == group_count
    heads = w_value.shape[1] // HEAD
    head_cols = heads * HEAD
    feat_cols = w_featmap.shape[2]
    feature_dim = feat_cols // heads
    tap_count = conv_window.shape[0]

    assert heads == NEAR and dp_count == 2
    values_t = w_value.T.reshape(1, heads, HEAD, width)
    featmap_t = w_featmap.transpose(1, 2, 0).reshape(2, heads, feature_dim, width)
    window_t = w_window.transpose(1, 2, 0).reshape(3, heads, HEAD, width)
    out_one, out_two = (w.reshape(1, heads, HEAD, width) for w in (w_out_one, w_out_two))
    places = jnp.concatenate([(seq_place % NEAR) ^ jnp.arange(NEAR), dp_place[None]])
    places = places.astype(jnp.int32)
    taps = conv_window.reshape(tap_count, 3, heads, HEAD).transpose(0, 2, 1, 3)
    taps = jnp.take(taps, places[:NEAR], axis=1, mode="clip")
    taps = jnp.pad(taps, ((0, 0), (0, 0), (0, 0), (0, SLOT - HEAD)))
    taps = taps.reshape(tap_count, 3 * heads * SLOT)
    taps = settled(jnp.stack([taps, across(taps, "tensor", 2)]))
    held_one = from_groups(own_piece([values_t, featmap_t]), ())
    held_one = settled(jnp.stack(held_one), (taps,))

    placed = reassign[:, None] == jnp.arange(slots_total, dtype=jnp.int32)[None, :]
    table = jnp.sum(jnp.where(placed[:, :, None], page_table[None], 0), axis=1)
    slot_lengths = jnp.sum(jnp.where(placed, lengths[None, :], 0), axis=1)
    source_page = (
        table.reshape(dp_count, req_dev, seq_count, page_span)
        .transpose(0, 2, 1, 3)
        .reshape(groups, req_dev * page_span)
    )
    capacity = (pages_dev + groups - 1) // groups
    page_owner = source_page // pages_dev
    pool_slot = source_page % pages_dev
    before = jnp.arange(pages_dev)[None, :] < jnp.arange(pages_dev)[:, None]
    pair_rank = jnp.sum((page_owner[:, :, None] == page_owner[:, None, :]) & before[None], axis=2)
    send_hit = (page_owner == device_place)[:, None, :] & (
        pair_rank[:, None, :] == jnp.arange(capacity)[None, :, None]
    )
    send_slot = jnp.sum(jnp.where(send_hit, pool_slot[:, None, :], 0), axis=2)
    outgoing = pool.at[send_slot.reshape(-1)].get(mode="promise_in_bounds")
    outgoing = outgoing.reshape(groups, capacity, page_share, width)
    arrived = lax.all_to_all(outgoing, ("dp", "seq"), split_axis=0, concat_axis=0, tiled=True)
    own_row = jnp.arange(groups)[:, None] == device_place
    pick_rows = jnp.sum(jnp.where(own_row, page_owner * capacity + pair_rank, 0), axis=0)
    picked = arrived.reshape(groups * capacity, page_share, width)
    picked = picked.at[pick_rows].get(mode="promise_in_bounds")

    picked = after(picked.reshape(req_dev, page_span, page_share, width), (held_one,))
    swapped = lax.all_to_all(picked, "tensor", split_axis=0, concat_axis=0, tiled=True)
    tokens = swapped.transpose(1, 0, 2, 3).reshape(rows, width)
    slot = dp_place * req_dev + tensor_place
    length = jnp.sum(jnp.where(jnp.arange(slots_total) == slot, slot_lengths, 0))

    held_out_one = settled(jnp.stack(from_groups(own_piece([out_one]), (picked,))))
    beyond_piece = settled(own_piece([window_t, out_two]), (swapped,))
    near_one = from_plane(
        held_one, neighbours(held_one), (swapped,), (held_out_one, tokens, beyond_piece)
    )
    out_piece = after(own_piece([out_two]), (swapped,))
    beyond = from_group(beyond_piece, ())
    first, second, ones, scale, kept = feature_tables(heads, feature_dim)
    first, second = jnp.asarray(first, BF16), jnp.asarray(second, BF16)
    column = np.zeros((1, heads * SLOT), np.float32)
    column[0, HEAD::SLOT] = 1

    def copy_sems(kinds):
        return pltpu.SemaphoreType.DMA((group_count + 1, NEAR * kinds))

    def weights_of(rows_of_head):
        return pltpu.VMEM((group_count, heads, rows_of_head, width), BF16)

    slots = heads * SLOT
    num, queries, state = call(
        functools.partial(linear_kernel, heads, feature_dim, kept),
        group_count,
        [
            SMEM,
            HBM,
            whole((1, width)),
            *[HBM] * 4,
            whole(first.shape),
            whole(second.shape),
            whole(ones.shape),
            whole(column.shape),
        ],
        [each((rows, slots)), each((rows, 2 * feat_cols)), each((heads * kept, SLOT))],
        [
            jax.ShapeDtypeStruct((group_count, rows, slots), F32),
            jax.ShapeDtypeStruct((group_count, rows, 2 * feat_cols), BF16),
            jax.ShapeDtypeStruct((group_count, heads * kept, SLOT), BF16),
        ],
        [
            pltpu.VMEM((rows, width), BF16),
            pltpu.VMEM((rows, width), BF16),
            weights_of(SLOT),
            weights_of(2 * feature_dim),
            copy_sems(3),
        ],
        "linear_rows",
    )(
        places, tokens, gain_one[None], values_t, featmap_t, *near_one, first, second, ones, column
    )
    prior = settled(earlier_blocks(state, "seq"))
    beyond = after(beyond, (state,))
    held_window, out_beyond = beyond[:, : 3 * HEAD], beyond[0, 3 * HEAD :]
    held_out_two = [out_beyond, across(out_piece, "tensor", 1), across(out_beyond, "tensor", 1)]
    held_out_two = settled(jnp.stack(held_out_two), (prior,))
    near_out_one = from_plane(
        held_out_one, neighbours(held_out_one), (state,), (beyond, held_out_two)
    )
    held_window = after(held_window, (prior,))
    near_by_window = neighbours(held_window)
    residual, normed_two, tail = call(
        functools.partial(out_one_kernel, heads, kept),
        group_count,
        [
            SMEM,
            each((rows, slots)),
            each((rows, 2 * feat_cols)),
            whole(first.shape),
            whole(second.shape),
            whole(ones.shape),
            whole(scale.shape),
        ]
        + [each((heads * kept, SLOT))]
        + [HBM] * 4
        + [whole((1, width))],
        [whole((n, width)) for n in (rows, rows, HALO)],
        [jax.ShapeDtypeStruct((n, width), BF16) for n in (rows, rows, HALO)],
        [
            pltpu.VMEM((rows, width), BF16),
            pltpu.VMEM((rows, width), F32),
            pltpu.VMEM((rows, slots), BF16),
            weights_of(SLOT),
            copy_sems(1),
        ],
        "linear_out",
    )(
        places, num, queries, first, second, ones, scale, prior, out_one, *near_out_one, tokens,
        gain_two[None],
    )

    halo = lax.ppermute(tail, "seq", [(i, i + 1) for i in range(seq_count - 1)])
    pair_rows = across(normed_two, "tensor", 1)
    pair_halo = lax.ppermute(
        tail,
        ("seq", "tensor"),
        [
            (i * group_count + j, (i + 1) * group_count + (j ^ 1))
            for i in range(seq_count - 1)
            for j in range(group_count)
        ],
    )
    held_out_two = after(held_out_two, (residual,))
    near_by_two = neighbours(held_out_two)
    near_window = from_plane(
        held_window, near_by_window, (residual,), (pair_rows, pair_halo, *near_by_two)
    )
    block_start = (seq_place * rows).astype(jnp.int32)[None]

    def window_rows(slot_rows, slot_halo, earlier):
        return call(
            functools.partial(window_kernel, heads),
            2,
            [
                SMEM,
                SMEM,
                *[HBM] * 5,
                each((tap_count, 3 * slots)),
                HBM,
            ],
            each((rows, slots)),
            jax.ShapeDtypeStruct((2, rows, slots), BF16),
            [
                pltpu.VMEM((HALO + rows, width), BF16),
                pltpu.VMEM((2, heads, 3 * SLOT, width), BF16),
                copy_sems(3),
            ],
            "window_rows",
        )(places, block_start, slot_rows, slot_halo, window_t, *near_window, taps, earlier)

    mixed_pair = window_rows(pair_rows, pair_halo, normed_two)
    near_out_two = from_plane(held_out_two, near_by_two, None, (mixed_pair,))
    mixed_own = window_rows(normed_two, halo, mixed_pair)
    mixed_pair = across(mixed_pair, "tensor", 1)
    live = (length - seq_place * rows).astype(jnp.int32)[None]
    result = call(
        out_two_kernel,
        group_count,
        [
            SMEM,
            SMEM,
            *[HBM] * 6,
        ],
        whole((rows, width)),
        jax.ShapeDtypeStruct((rows, width), BF16),
        [
            pltpu.VMEM((group_count, rows, slots), BF16),
            pltpu.VMEM((rows, width), BF16),
            pltpu.VMEM((rows, width), F32),
            weights_of(SLOT),
            copy_sems(1),
        ],
        "window_out",
    )(places, live, mixed_own, mixed_pair, out_two, *near_out_two, residual)

    result = result.reshape(page_span, group_count, page_share, width).transpose(1, 0, 2, 3)
    return lax.all_to_all(result, "tensor", split_axis=0, concat_axis=0, tiled=True)


def solution(mesh):
    return jax.shard_map(
        on_device,
        mesh=mesh,
        in_specs=(
            P(("dp", "seq"), "tensor", None),
            P(),
            P(),
            P(),
            P(),
            P(None, None, "tensor"),
            P(None, "tensor"),
            P("tensor", None),
            P(),
            P(None, None, "tensor"),
            P(None, None, "tensor"),
            P("tensor", None),
        ),
        out_specs=P("dp", "seq", "tensor", None),
        check_vma=False,
    )
```

```python
import functools

import jax
import jax.numpy as jnp
import numpy as np
from jax import lax
from jax.experimental import pallas as pl
from jax.experimental.pallas import tpu as pltpu
from jax.sharding import PartitionSpec as P

HEAD = 112
WINDOW = 64
EPS = 1e-05
SLOT = 128
FEAT_SLOT = 256
HALO = 80
NEAR = 4
VMEM = 60 * 1024 * 1024
F32 = jnp.float32
BF16 = jnp.bfloat16


def dot(a, b, dims=((1,), (0,))):
    return lax.dot_general(a, b, (dims, ((), ())), preferred_element_type=F32)


def normed_rows(rows, gain):
    scale = lax.rsqrt(jnp.mean(rows * rows, axis=-1, keepdims=True) + EPS)
    return (rows * scale * gain).astype(BF16)


def feature_tables(heads, feature_dim):
    pairs = [(i, j) for i in range(feature_dim) for j in range(i, feature_dim)]
    pairs += [(i, -1) for i in range(feature_dim)] + [(-1, -1)]
    first = np.zeros((2 * heads * feature_dim, heads * FEAT_SLOT), np.float32)
    second = np.zeros_like(first)
    ones = np.zeros((2, heads * FEAT_SLOT), np.float32)
    scale = np.zeros((1, heads * FEAT_SLOT), np.float32)
    for h in range(heads):
        for n, (i, j) in enumerate(pairs):
            at = h * FEAT_SLOT + n
            if i >= 0:
                first[2 * h * feature_dim + i, at] = 1
            else:
                ones[0, at] = 1
            if j >= 0:
                second[2 * h * feature_dim + j, at] = 1
            else:
                ones[1, at] = 1
            if i < 0:
                scale[0, at] = 1
            elif j < 0:
                scale[0, at] = feature_dim**-0.5
            else:
                scale[0, at] = (0.5 if i == j else 1.0) / feature_dim
    return first, second, ones, scale, -(-len(pairs) // 16) * 16


def features(rows, first, second, ones):
    return (dot(rows, first) + ones[0:1]) * (dot(rows, second) + ones[1:2])


def run_copies(copies_of, groups, loads, meanwhile=None):
    step = pl.program_id(0)

    @pl.when(step == 0)
    def _():
        for copy, _ in loads:
            copy.start()
        for group in range(groups):
            for copy in copies_of(group):
                copy.start()

    for group in range(groups):

        @pl.when(step == group)
        def _(group=group):
            for copy, at in loads:
                if at == group:
                    copy.wait()
            if meanwhile is not None and group == 0:
                meanwhile()
            for copy in copies_of(group):
                copy.wait()


def weight_copies(place_ref, near_ref, far_ref, targets, pieces, sems, group):
    found = []

    def copy(src, dst):
        found.append(pltpu.make_async_copy(src, dst, sems.at[group, len(found)]))

    if group == 0:
        for own_ref, kind, w_ref, off in targets:
            rows = own_ref.shape[2]
            for n in range(NEAR):
                copy(own_ref.at[kind, place_ref[n]], w_ref.at[0, n, off : off + rows, :])
        return found
    cols = near_ref.shape[3]
    for ref, part in ((near_ref, place_ref[NEAR]), (far_ref, 1 - place_ref[NEAR])):
        at = 0
        lanes = pl.ds(pl.multiple_of(part * cols, SLOT), cols)
        for rows, w_ref, off in pieces:
            copy(ref.at[:, group - 1, at : at + rows, :], w_ref.at[group, :, off : off + rows, lanes])
            at += rows
    return found


def zero_between_heads(w_ref):
    groups, heads, rows, width = w_ref.shape
    for at in range(HEAD, rows, SLOT):
        w_ref[:, :, at : at + SLOT - HEAD, :] = jnp.zeros(
            (groups, heads, SLOT - HEAD, width), BF16
        )


def group_weights(w_ref, step):
    heads, rows, width = w_ref.shape[1:]
    return w_ref[step].reshape(heads * rows, width)


def project(rows_ref, w_ref, step):
    return dot(rows_ref[...], group_weights(w_ref, step), ((1,), (1,)))


def linear_kernel(
    heads,
    feature_dim,
    kept,
    place_ref,
    x_ref,
    gain_ref,
    value_ref,
    featmap_ref,
    near_ref,
    far_ref,
    first_ref,
    second_ref,
    ones_ref,
    column_ref,
    num_ref,
    q_ref,
    state_ref,
    tokens_ref,
    normed_ref,
    value_w_ref,
    feat_w_ref,
    sems,
):
    step = pl.program_id(0)
    targets = [
        (value_ref, 0, value_w_ref, 0),
        (featmap_ref, 0, feat_w_ref, 0),
        (featmap_ref, 1, feat_w_ref, feature_dim),
    ]
    pieces = [(HEAD, value_w_ref, 0), (2 * feature_dim, feat_w_ref, 0)]

    groups = value_w_ref.shape[0]

    @pl.when(step == 0)
    def _():
        zero_between_heads(value_w_ref)

    def normalize():
        normed_ref[...] = normed_rows(tokens_ref[...].astype(F32), gain_ref[...])

    run_copies(
        functools.partial(weight_copies, place_ref, near_ref, far_ref, targets, pieces, sems),
        groups,
        [(pltpu.make_async_copy(x_ref, tokens_ref, sems.at[groups, 0]), 0)],
        normalize,
    )
    rows = x_ref.shape[0]
    width = 2 * heads * feature_dim
    queries = project(normed_ref, feat_w_ref, step).astype(BF16)
    keys = pltpu.roll(queries.astype(F32), width - feature_dim, 1).astype(BF16)
    values = (project(normed_ref, value_w_ref, step) + column_ref[...]).astype(BF16)
    q_ref[0] = queries
    lane = lax.broadcasted_iota(jnp.int32, (rows, width), 1)
    causal = lax.broadcasted_iota(jnp.int32, (rows, rows), 1) <= lax.broadcasted_iota(
        jnp.int32, (rows, rows), 0
    )
    key_features = features(keys, first_ref[...], second_ref[...], ones_ref[...]).astype(BF16)
    for h in range(heads):
        at = 2 * h * feature_dim
        own = jnp.where((lane >= at) & (lane < at + feature_dim), queries, jnp.zeros_like(queries))
        scores = dot(own, keys, ((1,), (1,))) * feature_dim**-0.5
        kernel = jnp.where(causal, 1.0 + scores + 0.5 * scores * scores, 0.0).astype(BF16)
        value = values[:, h * SLOT : (h + 1) * SLOT]
        num_ref[0, :, h * SLOT : (h + 1) * SLOT] = dot(kernel, value)
        state = dot(key_features[:, h * FEAT_SLOT : h * FEAT_SLOT + kept], value, ((0,), (0,)))
        head = pl.multiple_of(place_ref[h] * kept, 16)
        state_ref[0, pl.ds(head, kept), :] = state.astype(BF16)


def add_branch(mixed, w_ref, total_ref):
    step = pl.program_id(0)
    total_ref[...] += dot(mixed, group_weights(w_ref, step)).astype(BF16).astype(F32)


def out_one_kernel(
    heads,
    kept,
    place_ref,
    num_ref,
    q_ref,
    first_ref,
    second_ref,
    ones_ref,
    scale_ref,
    prior_ref,
    own_ref,
    near_ref,
    far_ref,
    x_ref,
    gain_ref,
    residual_ref,
    normed_ref,
    tail_ref,
    tokens_ref,
    total_ref,
    mixed_ref,
    w_ref,
    sems,
):
    step = pl.program_id(0)
    groups = w_ref.shape[0]

    @pl.when(step == 0)
    def _():
        total_ref[...] = jnp.zeros_like(total_ref)
        zero_between_heads(w_ref)

    loads = [(pltpu.make_async_copy(x_ref, tokens_ref, sems.at[groups, 0]), groups - 1)]
    run_copies(
        functools.partial(
            weight_copies,
            place_ref,
            near_ref,
            far_ref,
            [(own_ref, 0, w_ref, 0)],
            [(HEAD, w_ref, 0)],
            sems,
        ),
        groups,
        loads,
    )

    query_features = features(q_ref[0], first_ref[...], second_ref[...], ones_ref[...])
    query_features = (query_features * scale_ref[...]).astype(BF16)
    for h in range(heads):
        prior = prior_ref[0, pl.ds(pl.multiple_of(place_ref[h] * kept, 16), kept), :]
        lanes = slice(h * SLOT, (h + 1) * SLOT)
        total = num_ref[0, :, lanes] + dot(
            query_features[:, h * FEAT_SLOT : h * FEAT_SLOT + kept], prior.astype(BF16)
        )
        mixed_ref[:, lanes] = (total * (1.0 / total[:, HEAD : HEAD + 1])).astype(BF16)
    add_branch(mixed_ref[...], w_ref, total_ref)

    @pl.when(step == pl.num_programs(0) - 1)
    def _():
        residual = (tokens_ref[...].astype(F32) + total_ref[...]).astype(BF16)
        residual_ref[...] = residual
        normed = normed_rows(residual.astype(F32), gain_ref[...])
        normed_ref[...] = normed
        tail_ref[...] = normed[normed.shape[0] - HALO :]


def window_kernel(
    heads,
    place_ref,
    first_ref,
    x_ref,
    halo_ref,
    own_ref,
    near_ref,
    far_ref,
    tap_ref,
    _,
    mixed_ref,
    rows_ref,
    w_ref,
    sems,
):
    step = pl.program_id(0)
    targets = [(own_ref, kind, w_ref, kind * SLOT) for kind in range(3)]
    pieces = [(HEAD, w_ref, kind * SLOT) for kind in range(3)]

    groups = w_ref.shape[0]
    loads = [
        (pltpu.make_async_copy(src, rows_ref.at[at : at + src.shape[0], :], sems.at[groups, n]), 0)
        for n, (src, at) in enumerate(((halo_ref, 0), (x_ref, HALO)))
    ]

    @pl.when(step == 0)
    def _():
        zero_between_heads(w_ref)

    run_copies(
        functools.partial(weight_copies, place_ref, near_ref, far_ref, targets, pieces, sems),
        groups,
        loads,
    )
    rows = x_ref.shape[0]
    lead = HALO - WINDOW
    projected = project(rows_ref, w_ref, step)
    taps = tap_ref[0]
    convolved = taps[0:1] * projected
    for offset in range(1, taps.shape[0]):
        convolved = convolved + taps[offset : offset + 1] * pltpu.roll(projected, offset, 0)
    convolved = convolved[lead:].astype(BF16)
    tile = 128
    span = tile + WINDOW
    row = lax.broadcasted_iota(jnp.int32, (tile, span), 0)
    col = lax.broadcasted_iota(jnp.int32, (tile, span), 1)
    band = (col > row) & (col <= row + WINDOW)
    for h in range(heads):
        at = 3 * h * SLOT
        queries = convolved[WINDOW:, at : at + SLOT]
        keys = convolved[:, at + SLOT : at + 2 * SLOT]
        values = convolved[:, at + 2 * SLOT : at + 3 * SLOT]
        for start in range(0, rows, tile):
            logits = dot(queries[start : start + tile], keys[start : start + span], ((1,), (1,)))
            allowed = band
            if start < WINDOW:
                allowed = band & (col >= WINDOW - start - first_ref[0])
            logits = jnp.where(allowed, logits * HEAD**-0.5, -jnp.inf)
            weights = jnp.exp(logits - jnp.max(logits, axis=1, keepdims=True))
            weights = weights * (1.0 / jnp.sum(weights, axis=1, keepdims=True))
            mixed = dot(weights.astype(BF16), values[start : start + span])
            mixed_ref[0, start : start + tile, h * SLOT : (h + 1) * SLOT] = mixed.astype(BF16)


def out_two_kernel(
    place_ref,
    live_ref,
    mixed_ref,
    pair_ref,
    own_ref,
    near_ref,
    far_ref,
    residual_ref,
    out_ref,
    mixed_all_ref,
    rows_ref,
    total_ref,
    w_ref,
    sems,
):
    step = pl.program_id(0)
    groups = w_ref.shape[0]
    loads = [
        (pltpu.make_async_copy(mixed_ref, mixed_all_ref.at[:2], sems.at[groups, 0]), 0),
        (pltpu.make_async_copy(pair_ref, mixed_all_ref.at[2:], sems.at[groups, 1]), 2),
        (pltpu.make_async_copy(residual_ref, rows_ref, sems.at[groups, 2]), groups - 1),
    ]

    @pl.when(step == 0)
    def _():
        total_ref[...] = jnp.zeros_like(total_ref)
        zero_between_heads(w_ref)

    run_copies(
        functools.partial(
            weight_copies,
            place_ref,
            near_ref,
            far_ref,
            [(own_ref, 0, w_ref, 0)],
            [(HEAD, w_ref, 0)],
            sems,
        ),
        groups,
        loads,
    )
    add_branch(mixed_all_ref[step], w_ref, total_ref)

    @pl.when(step == pl.num_programs(0) - 1)
    def _():
        result = (rows_ref[...].astype(F32) + total_ref[...]).astype(BF16)
        row = lax.broadcasted_iota(jnp.int32, result.shape, 0)
        out_ref[...] = jnp.where(row < live_ref[0], result, jnp.zeros_like(result))


def whole(shape):
    return pl.BlockSpec(shape, lambda g: (0,) * len(shape))


def each(shape):
    return pl.BlockSpec((1,) + shape, lambda g: (g,) + (0,) * len(shape))


SMEM = pl.BlockSpec(memory_space=pltpu.SMEM)
HBM = pl.BlockSpec(memory_space=pl.ANY)


def call(kernel, groups, in_specs, out_specs, out_shape, scratch, name):
    return pl.pallas_call(
        kernel,
        grid=(groups,),
        in_specs=in_specs,
        out_specs=out_specs,
        out_shape=out_shape,
        scratch_shapes=scratch,
        compiler_params=pltpu.CompilerParams(
            dimension_semantics=("arbitrary",), vmem_limit_bytes=VMEM
        ),
        cost_estimate=pl.CostEstimate(flops=0, bytes_accessed=0, transcendentals=0),
        name=name,
    )


def own_piece(whole_weights):
    head, part = lax.axis_index("seq") % NEAR, lax.axis_index("dp")
    found = []
    for weights in whole_weights:
        kinds, _, rows, cols = weights.shape
        cols = cols // lax.axis_size("dp")
        piece = lax.dynamic_slice(weights, (0, head, 0, part * cols), (kinds, 1, rows, cols))
        found.append(piece.reshape(kinds * rows, cols))
    return jnp.concatenate(found, axis=0)


def across(array, axis, bit):
    return lax.ppermute(array, axis, [(i, i ^ bit) for i in range(lax.axis_size(axis))])


def after(array, others):
    if not others:
        return array
    first = [lax.slice(other, (0,) * other.ndim, (1,) * other.ndim) for other in others]
    zero = sum(one.reshape(()).astype(F32) * 0.0 for one in first)
    return jnp.where(zero == 0.0, array, jnp.zeros_like(array))


def settled(array, others=()):
    return lax.optimization_barrier(after(array, others))


def from_group(piece, over_z):
    return across(after(piece, over_z), "tensor", 2)[None]


def from_groups(piece, over_z, order=(0, 1, 2)):
    piece = after(piece, over_z)
    beside, beyond = across(piece, "tensor", 1), across(piece, "tensor", 2)
    found = (beside, beyond, across(beyond, "tensor", 1))
    return [found[n] for n in order]


def neighbours(held):
    return across(held, "seq", 1), across(held, "seq", 2)


def from_plane(held, near_by, diagonal, over_cores, over_across=()):
    beside, above = near_by
    if diagonal is None:
        opposite = across(after(held, over_across), "seq", 3)
    else:
        half = -(-held.shape[1] // 32) * 16
        opposite = [
            across(after(above[:, :half], diagonal), "seq", 1),
            across(after(beside[:, half:], diagonal), "seq", 2),
        ]
        if callable(over_cores):
            over_cores = over_cores(opposite)
        opposite = after(jnp.concatenate(opposite, axis=1), over_cores)
    near = after(jnp.stack([held, beside, above, opposite]), over_cores)
    return near, across(near, "dp", 1)


def earlier_blocks(state, axis):
    peers = lax.axis_size(axis)
    if peers <= 4:
        found = [
            lax.ppermute(state, axis, [(i, i + by) for i in range(peers - by)])
            for by in range(1, peers)
        ]
        return sum(one.astype(F32) for one in found)
    everything = lax.all_gather(state, axis).astype(F32)
    reached = jnp.arange(peers) < lax.axis_index(axis)
    return jnp.sum(jnp.where(reached[:, None, None, None], everything, 0.0), axis=0)


def on_device(
    pool,
    page_table,
    reassign,
    lengths,
    gain_one,
    w_featmap,
    w_value,
    w_out_one,
    gain_two,
    w_window,
    conv_window,
    w_out_two,
):
    dp_count, seq_count, group_count = (lax.axis_size(n) for n in ("dp", "seq", "tensor"))
    groups = dp_count * seq_count
    device_place = lax.axis_index(("dp", "seq"))
    dp_place, seq_place, tensor_place = (lax.axis_index(n) for n in ("dp", "seq", "tensor"))
    pages_dev, page_share, width = pool.shape
    slots_total, pages_total = page_table.shape
    req_dev = slots_total // dp_count
    page_span = pages_total // seq_count
    page_rows = page_share * group_count
    rows = page_span * page_rows
    assert req_dev == group_count
    heads = w_value.shape[1] // HEAD
    head_cols = heads * HEAD
    feat_cols = w_featmap.shape[2]
    feature_dim = feat_cols // heads
    tap_count = conv_window.shape[0]

    assert heads == NEAR and dp_count == 2
    values_t = w_value.T.reshape(1, heads, HEAD, width)
    featmap_t = w_featmap.transpose(1, 2, 0).reshape(2, heads, feature_dim, width)
    window_t = w_window.transpose(1, 2, 0).reshape(3, heads, HEAD, width)
    out_one, out_two = (w.reshape(1, heads, HEAD, width) for w in (w_out_one, w_out_two))
    places = jnp.concatenate([(seq_place % NEAR) ^ jnp.arange(NEAR), dp_place[None]])
    places = places.astype(jnp.int32)
    taps = conv_window.reshape(tap_count, 3, heads, HEAD).transpose(0, 2, 1, 3)
    taps = jnp.take(taps, places[:NEAR], axis=1, mode="clip")
    taps = jnp.pad(taps, ((0, 0), (0, 0), (0, 0), (0, SLOT - HEAD)))
    taps = taps.reshape(tap_count, 3 * heads * SLOT)
    taps = settled(jnp.stack([taps, across(taps, "tensor", 2)]))
    held_one = from_groups(own_piece([values_t, featmap_t]), ())
    held_one = settled(jnp.stack(held_one), (taps,))

    placed = reassign[:, None] == jnp.arange(slots_total, dtype=jnp.int32)[None, :]
    table = jnp.sum(jnp.where(placed[:, :, None], page_table[None], 0), axis=1)
    slot_lengths = jnp.sum(jnp.where(placed, lengths[None, :], 0), axis=1)
    source_page = (
        table.reshape(dp_count, req_dev, seq_count, page_span)
        .transpose(0, 2, 1, 3)
        .reshape(groups, req_dev * page_span)
    )
    capacity = (pages_dev + groups - 1) // groups
    page_owner = source_page // pages_dev
    pool_slot = source_page % pages_dev
    before = jnp.arange(pages_dev)[None, :] < jnp.arange(pages_dev)[:, None]
    pair_rank = jnp.sum((page_owner[:, :, None] == page_owner[:, None, :]) & before[None], axis=2)
    send_hit = (page_owner == device_place)[:, None, :] & (
        pair_rank[:, None, :] == jnp.arange(capacity)[None, :, None]
    )
    send_slot = jnp.sum(jnp.where(send_hit, pool_slot[:, None, :], 0), axis=2)
    outgoing = pool.at[send_slot.reshape(-1)].get(mode="promise_in_bounds")
    outgoing = outgoing.reshape(groups, capacity, page_share, width)
    arrived = lax.all_to_all(outgoing, ("dp", "seq"), split_axis=0, concat_axis=0, tiled=True)
    own_row = jnp.arange(groups)[:, None] == device_place
    pick_rows = jnp.sum(jnp.where(own_row, page_owner * capacity + pair_rank, 0), axis=0)
    picked = arrived.reshape(groups * capacity, page_share, width)
    picked = picked.at[pick_rows].get(mode="promise_in_bounds")

    picked = after(picked.reshape(req_dev, page_span, page_share, width), (held_one,))
    swapped = lax.all_to_all(picked, "tensor", split_axis=0, concat_axis=0, tiled=True)
    tokens = swapped.transpose(1, 0, 2, 3).reshape(rows, width)
    slot = dp_place * req_dev + tensor_place
    length = jnp.sum(jnp.where(jnp.arange(slots_total) == slot, slot_lengths, 0))

    held_out_one = settled(jnp.stack(from_groups(own_piece([out_one]), (picked,))))
    near_one = from_plane(held_one, neighbours(held_one), (swapped,), (held_out_one,))
    out_piece = after(own_piece([out_two]), (swapped,))
    beyond = from_group(own_piece([window_t, out_two]), (swapped,))
    first, second, ones, scale, kept = feature_tables(heads, feature_dim)
    first, second = jnp.asarray(first, BF16), jnp.asarray(second, BF16)
    column = np.zeros((1, heads * SLOT), np.float32)
    column[0, HEAD::SLOT] = 1

    def copy_sems(kinds):
        return pltpu.SemaphoreType.DMA((group_count + 1, NEAR * kinds))

    def weights_of(rows_of_head):
        return pltpu.VMEM((group_count, heads, rows_of_head, width), BF16)

    slots = heads * SLOT
    num, queries, state = call(
        functools.partial(linear_kernel, heads, feature_dim, kept),
        group_count,
        [
            SMEM,
            HBM,
            whole((1, width)),
            *[HBM] * 4,
            whole(first.shape),
            whole(second.shape),
            whole(ones.shape),
            whole(column.shape),
        ],
        [each((rows, slots)), each((rows, 2 * feat_cols)), each((heads * kept, SLOT))],
        [
            jax.ShapeDtypeStruct((group_count, rows, slots), F32),
            jax.ShapeDtypeStruct((group_count, rows, 2 * feat_cols), BF16),
            jax.ShapeDtypeStruct((group_count, heads * kept, SLOT), BF16),
        ],
        [
            pltpu.VMEM((rows, width), BF16),
            pltpu.VMEM((rows, width), BF16),
            weights_of(SLOT),
            weights_of(2 * feature_dim),
            copy_sems(3),
        ],
        "linear_rows",
    )(
        places, tokens, gain_one[None], values_t, featmap_t, *near_one, first, second, ones, column
    )
    prior = settled(earlier_blocks(state, "seq"))
    beyond = after(beyond, (state,))
    held_window, out_beyond = beyond[:, : 3 * HEAD], beyond[0, 3 * HEAD :]
    held_out_two = [out_beyond, across(out_piece, "tensor", 1), across(out_beyond, "tensor", 1)]
    held_out_two = settled(jnp.stack(held_out_two), (prior,))
    near_out_one = from_plane(
        held_out_one, neighbours(held_out_one), (state,), (beyond, held_out_two)
    )
    held_window = after(held_window, (prior,))
    near_by_window = neighbours(held_window)
    residual, normed_two, tail = call(
        functools.partial(out_one_kernel, heads, kept),
        group_count,
        [
            SMEM,
            each((rows, slots)),
            each((rows, 2 * feat_cols)),
            whole(first.shape),
            whole(second.shape),
            whole(ones.shape),
            whole(scale.shape),
        ]
        + [each((heads * kept, SLOT))]
        + [HBM] * 4
        + [whole((1, width))],
        [whole((n, width)) for n in (rows, rows, HALO)],
        [jax.ShapeDtypeStruct((n, width), BF16) for n in (rows, rows, HALO)],
        [
            pltpu.VMEM((rows, width), BF16),
            pltpu.VMEM((rows, width), F32),
            pltpu.VMEM((rows, slots), BF16),
            weights_of(SLOT),
            copy_sems(1),
        ],
        "linear_out",
    )(
        places, num, queries, first, second, ones, scale, prior, out_one, *near_out_one, tokens,
        gain_two[None],
    )

    halo = lax.ppermute(tail, "seq", [(i, i + 1) for i in range(seq_count - 1)])
    pair_rows = across(normed_two, "tensor", 1)
    pair_halo = lax.ppermute(
        tail,
        ("seq", "tensor"),
        [
            (i * group_count + j, (i + 1) * group_count + (j ^ 1))
            for i in range(seq_count - 1)
            for j in range(group_count)
        ],
    )
    near_by_two = []

    def before_window(opposite):
        held = after(held_out_two, opposite)
        near_by_two.extend([held, *neighbours(held)])
        return (pair_rows, pair_halo, halo, *near_by_two[1:])

    near_window = from_plane(held_window, near_by_window, (residual,), before_window)
    held_out_two, *near_by_two = near_by_two
    block_start = (seq_place * rows).astype(jnp.int32)[None]

    def window_rows(slot_rows, slot_halo, earlier):
        return call(
            functools.partial(window_kernel, heads),
            2,
            [
                SMEM,
                SMEM,
                *[HBM] * 5,
                each((tap_count, 3 * slots)),
                HBM,
            ],
            each((rows, slots)),
            jax.ShapeDtypeStruct((2, rows, slots), BF16),
            [
                pltpu.VMEM((HALO + rows, width), BF16),
                pltpu.VMEM((2, heads, 3 * SLOT, width), BF16),
                copy_sems(3),
            ],
            "window_rows",
        )(places, block_start, slot_rows, slot_halo, window_t, *near_window, taps, earlier)

    mixed_pair = window_rows(pair_rows, pair_halo, normed_two)
    near_out_two = from_plane(held_out_two, near_by_two, None, (mixed_pair,))
    mixed_own = window_rows(normed_two, halo, mixed_pair)
    mixed_pair = across(mixed_pair, "tensor", 1)
    live = (length - seq_place * rows).astype(jnp.int32)[None]
    result = call(
        out_two_kernel,
        group_count,
        [
            SMEM,
            SMEM,
            *[HBM] * 6,
        ],
        whole((rows, width)),
        jax.ShapeDtypeStruct((rows, width), BF16),
        [
            pltpu.VMEM((group_count, rows, slots), BF16),
            pltpu.VMEM((rows, width), BF16),
            pltpu.VMEM((rows, width), F32),
            weights_of(SLOT),
            copy_sems(1),
        ],
        "window_out",
    )(places, live, mixed_own, mixed_pair, out_two, *near_out_two, residual)

    result = result.reshape(page_span, group_count, page_share, width).transpose(1, 0, 2, 3)
    return lax.all_to_all(result, "tensor", split_axis=0, concat_axis=0, tiled=True)


def solution(mesh):
    return jax.shard_map(
        on_device,
        mesh=mesh,
        in_specs=(
            P(("dp", "seq"), "tensor", None),
            P(),
            P(),
            P(),
            P(),
            P(None, None, "tensor"),
            P(None, "tensor"),
            P("tensor", None),
            P(),
            P(None, None, "tensor"),
            P(None, None, "tensor"),
            P("tensor", None),
        ),
        out_specs=P("dp", "seq", "tensor", None),
        check_vma=False,
    )
```

```python
import functools

import jax
import jax.numpy as jnp
import numpy as np
from jax import lax
from jax.experimental import pallas as pl
from jax.experimental.pallas import tpu as pltpu
from jax.sharding import PartitionSpec as P

HEAD = 112
WINDOW = 64
EPS = 1e-05
SLOT = 128
FEAT_SLOT = 256
HALO = 80
NEAR = 4
VMEM = 60 * 1024 * 1024
F32 = jnp.float32
BF16 = jnp.bfloat16


def dot(a, b, dims=((1,), (0,))):
    return lax.dot_general(a, b, (dims, ((), ())), preferred_element_type=F32)


def normed_rows(rows, gain):
    scale = lax.rsqrt(jnp.mean(rows * rows, axis=-1, keepdims=True) + EPS)
    return (rows * scale * gain).astype(BF16)


def feature_tables(heads, feature_dim):
    pairs = [(i, j) for i in range(feature_dim) for j in range(i, feature_dim)]
    pairs += [(i, -1) for i in range(feature_dim)] + [(-1, -1)]
    first = np.zeros((2 * heads * feature_dim, heads * FEAT_SLOT), np.float32)
    second = np.zeros_like(first)
    ones = np.zeros((2, heads * FEAT_SLOT), np.float32)
    scale = np.zeros((1, heads * FEAT_SLOT), np.float32)
    for h in range(heads):
        for n, (i, j) in enumerate(pairs):
            at = h * FEAT_SLOT + n
            if i >= 0:
                first[2 * h * feature_dim + i, at] = 1
            else:
                ones[0, at] = 1
            if j >= 0:
                second[2 * h * feature_dim + j, at] = 1
            else:
                ones[1, at] = 1
            if i < 0:
                scale[0, at] = 1
            elif j < 0:
                scale[0, at] = feature_dim**-0.5
            else:
                scale[0, at] = (0.5 if i == j else 1.0) / feature_dim
    return first, second, ones, scale, -(-len(pairs) // 16) * 16


def features(rows, first, second, ones):
    return (dot(rows, first) + ones[0:1]) * (dot(rows, second) + ones[1:2])


def run_copies(copies_of, groups, loads, meanwhile=None):
    step = pl.program_id(0)

    @pl.when(step == 0)
    def _():
        for copy, _ in loads:
            copy.start()
        for group in range(groups):
            for copy in copies_of(group):
                copy.start()

    for group in range(groups):

        @pl.when(step == group)
        def _(group=group):
            for copy, at in loads:
                if at == group:
                    copy.wait()
            if meanwhile is not None and group == 0:
                meanwhile()
            for copy in copies_of(group):
                copy.wait()


def weight_copies(place_ref, near_ref, far_ref, targets, pieces, sems, group):
    found = []

    def copy(src, dst):
        found.append(pltpu.make_async_copy(src, dst, sems.at[group, len(found)]))

    if group == 0:
        for own_ref, kind, w_ref, off in targets:
            rows = own_ref.shape[2]
            for n in range(NEAR):
                copy(own_ref.at[kind, place_ref[n]], w_ref.at[0, n, off : off + rows, :])
        return found
    cols = near_ref.shape[3]
    for ref, part in ((near_ref, place_ref[NEAR]), (far_ref, 1 - place_ref[NEAR])):
        at = 0
        lanes = pl.ds(pl.multiple_of(part * cols, SLOT), cols)
        for rows, w_ref, off in pieces:
            copy(ref.at[:, group - 1, at : at + rows, :], w_ref.at[group, :, off : off + rows, lanes])
            at += rows
    return found


def zero_between_heads(w_ref):
    groups, heads, rows, width = w_ref.shape
    for at in range(HEAD, rows, SLOT):
        w_ref[:, :, at : at + SLOT - HEAD, :] = jnp.zeros(
            (groups, heads, SLOT - HEAD, width), BF16
        )


def group_weights(w_ref, step):
    heads, rows, width = w_ref.shape[1:]
    return w_ref[step].reshape(heads * rows, width)


def project(rows_ref, w_ref, step):
    return dot(rows_ref[...], group_weights(w_ref, step), ((1,), (1,)))


def linear_kernel(
    heads,
    feature_dim,
    kept,
    place_ref,
    x_ref,
    gain_ref,
    value_ref,
    featmap_ref,
    near_ref,
    far_ref,
    first_ref,
    second_ref,
    ones_ref,
    column_ref,
    num_ref,
    q_ref,
    state_ref,
    tokens_ref,
    normed_ref,
    value_w_ref,
    feat_w_ref,
    sems,
):
    step = pl.program_id(0)
    targets = [
        (value_ref, 0, value_w_ref, 0),
        (featmap_ref, 0, feat_w_ref, 0),
        (featmap_ref, 1, feat_w_ref, feature_dim),
    ]
    pieces = [(HEAD, value_w_ref, 0), (2 * feature_dim, feat_w_ref, 0)]

    groups = value_w_ref.shape[0]

    @pl.when(step == 0)
    def _():
        zero_between_heads(value_w_ref)

    def normalize():
        normed_ref[...] = normed_rows(tokens_ref[...].astype(F32), gain_ref[...])

    run_copies(
        functools.partial(weight_copies, place_ref, near_ref, far_ref, targets, pieces, sems),
        groups,
        [(pltpu.make_async_copy(x_ref, tokens_ref, sems.at[groups, 0]), 0)],
        normalize,
    )
    rows = x_ref.shape[0]
    width = 2 * heads * feature_dim
    queries = project(normed_ref, feat_w_ref, step).astype(BF16)
    keys = pltpu.roll(queries.astype(F32), width - feature_dim, 1).astype(BF16)
    values = (project(normed_ref, value_w_ref, step) + column_ref[...]).astype(BF16)
    q_ref[0] = queries
    lane = lax.broadcasted_iota(jnp.int32, (rows, width), 1)
    causal = lax.broadcasted_iota(jnp.int32, (rows, rows), 1) <= lax.broadcasted_iota(
        jnp.int32, (rows, rows), 0
    )
    key_features = features(keys, first_ref[...], second_ref[...], ones_ref[...]).astype(BF16)
    for h in range(heads):
        at = 2 * h * feature_dim
        own = jnp.where((lane >= at) & (lane < at + feature_dim), queries, jnp.zeros_like(queries))
        scores = dot(own, keys, ((1,), (1,))) * feature_dim**-0.5
        kernel = jnp.where(causal, 1.0 + scores + 0.5 * scores * scores, 0.0).astype(BF16)
        value = values[:, h * SLOT : (h + 1) * SLOT]
        num_ref[0, :, h * SLOT : (h + 1) * SLOT] = dot(kernel, value)
        state = dot(key_features[:, h * FEAT_SLOT : h * FEAT_SLOT + kept], value, ((0,), (0,)))
        head = pl.multiple_of(place_ref[h] * kept, 16)
        state_ref[0, pl.ds(head, kept), :] = state.astype(BF16)


def add_branch(mixed, w_ref, total_ref):
    step = pl.program_id(0)
    total_ref[...] += dot(mixed, group_weights(w_ref, step)).astype(BF16).astype(F32)


def out_one_kernel(
    heads,
    kept,
    place_ref,
    num_ref,
    q_ref,
    first_ref,
    second_ref,
    ones_ref,
    scale_ref,
    prior_ref,
    own_ref,
    near_ref,
    far_ref,
    x_ref,
    gain_ref,
    residual_ref,
    normed_ref,
    tail_ref,
    tokens_ref,
    total_ref,
    mixed_ref,
    w_ref,
    sems,
):
    step = pl.program_id(0)
    groups = w_ref.shape[0]

    @pl.when(step == 0)
    def _():
        total_ref[...] = jnp.zeros_like(total_ref)
        zero_between_heads(w_ref)

    loads = [(pltpu.make_async_copy(x_ref, tokens_ref, sems.at[groups, 0]), groups - 1)]
    run_copies(
        functools.partial(
            weight_copies,
            place_ref,
            near_ref,
            far_ref,
            [(own_ref, 0, w_ref, 0)],
            [(HEAD, w_ref, 0)],
            sems,
        ),
        groups,
        loads,
    )

    query_features = features(q_ref[0], first_ref[...], second_ref[...], ones_ref[...])
    query_features = (query_features * scale_ref[...]).astype(BF16)
    for h in range(heads):
        prior = prior_ref[0, pl.ds(pl.multiple_of(place_ref[h] * kept, 16), kept), :]
        lanes = slice(h * SLOT, (h + 1) * SLOT)
        total = num_ref[0, :, lanes] + dot(
            query_features[:, h * FEAT_SLOT : h * FEAT_SLOT + kept], prior.astype(BF16)
        )
        mixed_ref[:, lanes] = (total * (1.0 / total[:, HEAD : HEAD + 1])).astype(BF16)
    add_branch(mixed_ref[...], w_ref, total_ref)

    @pl.when(step == pl.num_programs(0) - 1)
    def _():
        residual = (tokens_ref[...].astype(F32) + total_ref[...]).astype(BF16)
        residual_ref[...] = residual
        normed = normed_rows(residual.astype(F32), gain_ref[...])
        normed_ref[...] = normed
        tail_ref[...] = normed[normed.shape[0] - HALO :]


def window_kernel(
    heads,
    place_ref,
    first_ref,
    x_ref,
    halo_ref,
    own_ref,
    near_ref,
    far_ref,
    tap_ref,
    _,
    mixed_ref,
    rows_ref,
    w_ref,
    sems,
):
    step = pl.program_id(0)
    targets = [(own_ref, kind, w_ref, kind * SLOT) for kind in range(3)]
    pieces = [(HEAD, w_ref, kind * SLOT) for kind in range(3)]

    groups = w_ref.shape[0]
    loads = [
        (pltpu.make_async_copy(src, rows_ref.at[at : at + src.shape[0], :], sems.at[groups, n]), 0)
        for n, (src, at) in enumerate(((halo_ref, 0), (x_ref, HALO)))
    ]

    @pl.when(step == 0)
    def _():
        zero_between_heads(w_ref)

    run_copies(
        functools.partial(weight_copies, place_ref, near_ref, far_ref, targets, pieces, sems),
        groups,
        loads,
    )
    rows = x_ref.shape[0]
    lead = HALO - WINDOW
    projected = project(rows_ref, w_ref, step)
    taps = tap_ref[0]
    convolved = taps[0:1] * projected
    for offset in range(1, taps.shape[0]):
        convolved = convolved + taps[offset : offset + 1] * pltpu.roll(projected, offset, 0)
    convolved = convolved[lead:].astype(BF16)
    tile = 128
    span = tile + WINDOW
    row = lax.broadcasted_iota(jnp.int32, (tile, span), 0)
    col = lax.broadcasted_iota(jnp.int32, (tile, span), 1)
    band = (col > row) & (col <= row + WINDOW)
    for h in range(heads):
        at = 3 * h * SLOT
        queries = convolved[WINDOW:, at : at + SLOT]
        keys = convolved[:, at + SLOT : at + 2 * SLOT]
        values = convolved[:, at + 2 * SLOT : at + 3 * SLOT]
        for start in range(0, rows, tile):
            logits = dot(queries[start : start + tile], keys[start : start + span], ((1,), (1,)))
            allowed = band
            if start < WINDOW:
                allowed = band & (col >= WINDOW - start - first_ref[0])
            logits = jnp.where(allowed, logits * HEAD**-0.5, -jnp.inf)
            weights = jnp.exp(logits - jnp.max(logits, axis=1, keepdims=True))
            weights = weights * (1.0 / jnp.sum(weights, axis=1, keepdims=True))
            mixed = dot(weights.astype(BF16), values[start : start + span])
            mixed_ref[0, start : start + tile, h * SLOT : (h + 1) * SLOT] = mixed.astype(BF16)


def out_two_kernel(
    place_ref,
    live_ref,
    mixed_ref,
    pair_ref,
    own_ref,
    near_ref,
    far_ref,
    residual_ref,
    out_ref,
    mixed_all_ref,
    rows_ref,
    total_ref,
    w_ref,
    sems,
):
    step = pl.program_id(0)
    groups = w_ref.shape[0]
    loads = [
        (pltpu.make_async_copy(mixed_ref, mixed_all_ref.at[:2], sems.at[groups, 0]), 0),
        (pltpu.make_async_copy(pair_ref, mixed_all_ref.at[2:], sems.at[groups, 1]), 2),
        (pltpu.make_async_copy(residual_ref, rows_ref, sems.at[groups, 2]), groups - 1),
    ]

    @pl.when(step == 0)
    def _():
        total_ref[...] = jnp.zeros_like(total_ref)
        zero_between_heads(w_ref)

    run_copies(
        functools.partial(
            weight_copies,
            place_ref,
            near_ref,
            far_ref,
            [(own_ref, 0, w_ref, 0)],
            [(HEAD, w_ref, 0)],
            sems,
        ),
        groups,
        loads,
    )
    add_branch(mixed_all_ref[step], w_ref, total_ref)

    @pl.when(step == pl.num_programs(0) - 1)
    def _():
        result = (rows_ref[...].astype(F32) + total_ref[...]).astype(BF16)
        row = lax.broadcasted_iota(jnp.int32, result.shape, 0)
        out_ref[...] = jnp.where(row < live_ref[0], result, jnp.zeros_like(result))


def whole(shape):
    return pl.BlockSpec(shape, lambda g: (0,) * len(shape))


def each(shape):
    return pl.BlockSpec((1,) + shape, lambda g: (g,) + (0,) * len(shape))


SMEM = pl.BlockSpec(memory_space=pltpu.SMEM)
HBM = pl.BlockSpec(memory_space=pl.ANY)


def call(kernel, groups, in_specs, out_specs, out_shape, scratch, name):
    return pl.pallas_call(
        kernel,
        grid=(groups,),
        in_specs=in_specs,
        out_specs=out_specs,
        out_shape=out_shape,
        scratch_shapes=scratch,
        compiler_params=pltpu.CompilerParams(
            dimension_semantics=("arbitrary",), vmem_limit_bytes=VMEM
        ),
        cost_estimate=pl.CostEstimate(flops=0, bytes_accessed=0, transcendentals=0),
        name=name,
    )


def own_piece(whole_weights):
    head, part = lax.axis_index("seq") % NEAR, lax.axis_index("dp")
    found = []
    for weights in whole_weights:
        kinds, _, rows, cols = weights.shape
        cols = cols // lax.axis_size("dp")
        piece = lax.dynamic_slice(weights, (0, head, 0, part * cols), (kinds, 1, rows, cols))
        found.append(piece.reshape(kinds * rows, cols))
    return jnp.concatenate(found, axis=0)


def across(array, axis, bit):
    return lax.ppermute(array, axis, [(i, i ^ bit) for i in range(lax.axis_size(axis))])


def after(array, others):
    if not others:
        return array
    first = [lax.slice(other, (0,) * other.ndim, (1,) * other.ndim) for other in others]
    zero = sum(one.reshape(()).astype(F32) * 0.0 for one in first)
    return jnp.where(zero == 0.0, array, jnp.zeros_like(array))


def settled(array, others=()):
    return lax.optimization_barrier(after(array, others))


def from_group(piece, over_z):
    return across(after(piece, over_z), "tensor", 2)[None]


def from_groups(piece, over_z, order=(0, 1, 2)):
    piece = after(piece, over_z)
    beside, beyond = across(piece, "tensor", 1), across(piece, "tensor", 2)
    found = (beside, beyond, across(beyond, "tensor", 1))
    return [found[n] for n in order]


def neighbours(held):
    return across(held, "seq", 1), across(held, "seq", 2)


def from_plane(held, near_by, diagonal, over_cores, over_across=(), others=()):
    beside, above = near_by
    if diagonal is None:
        opposite = across(after(held, over_across), "seq", 3)
    else:
        half = -(-held.shape[1] // 32) * 16
        opposite = [
            across(after(above[:, :half], diagonal), "seq", 1),
            across(after(beside[:, half:], diagonal), "seq", 2),
        ]
        opposite = after(jnp.concatenate(opposite, axis=1), over_cores)
    near = [held, beside, above, opposite]
    for other in others:
        near[3] = near[3] + other.reshape(near[3].shape) * jnp.zeros((), BF16)
    near = after(jnp.stack(near), over_cores)
    return near, across(near, "dp", 1)


def earlier_blocks(state, axis):
    peers = lax.axis_size(axis)
    if peers <= 4:
        found = [
            lax.ppermute(state, axis, [(i, i + by) for i in range(peers - by)])
            for by in range(1, peers)
        ]
        return sum(one.astype(F32) for one in found)
    everything = lax.all_gather(state, axis).astype(F32)
    reached = jnp.arange(peers) < lax.axis_index(axis)
    return jnp.sum(jnp.where(reached[:, None, None, None], everything, 0.0), axis=0)


def on_device(
    pool,
    page_table,
    reassign,
    lengths,
    gain_one,
    w_featmap,
    w_value,
    w_out_one,
    gain_two,
    w_window,
    conv_window,
    w_out_two,
):
    dp_count, seq_count, group_count = (lax.axis_size(n) for n in ("dp", "seq", "tensor"))
    groups = dp_count * seq_count
    device_place = lax.axis_index(("dp", "seq"))
    dp_place, seq_place, tensor_place = (lax.axis_index(n) for n in ("dp", "seq", "tensor"))
    pages_dev, page_share, width = pool.shape
    slots_total, pages_total = page_table.shape
    req_dev = slots_total // dp_count
    page_span = pages_total // seq_count
    page_rows = page_share * group_count
    rows = page_span * page_rows
    assert req_dev == group_count
    heads = w_value.shape[1] // HEAD
    head_cols = heads * HEAD
    feat_cols = w_featmap.shape[2]
    feature_dim = feat_cols // heads
    tap_count = conv_window.shape[0]

    assert heads == NEAR and dp_count == 2
    values_t = w_value.T.reshape(1, heads, HEAD, width)
    featmap_t = w_featmap.transpose(1, 2, 0).reshape(2, heads, feature_dim, width)
    window_t = w_window.transpose(1, 2, 0).reshape(3, heads, HEAD, width)
    out_one, out_two = (w.reshape(1, heads, HEAD, width) for w in (w_out_one, w_out_two))
    places = jnp.concatenate([(seq_place % NEAR) ^ jnp.arange(NEAR), dp_place[None]])
    places = places.astype(jnp.int32)
    taps = conv_window.reshape(tap_count, 3, heads, HEAD).transpose(0, 2, 1, 3)
    taps = jnp.take(taps, places[:NEAR], axis=1, mode="clip")
    taps = jnp.pad(taps, ((0, 0), (0, 0), (0, 0), (0, SLOT - HEAD)))
    taps = taps.reshape(tap_count, 3 * heads * SLOT)
    taps = settled(jnp.stack([taps, across(taps, "tensor", 2)]))
    held_one = from_groups(own_piece([values_t, featmap_t]), ())
    held_one = settled(jnp.stack(held_one), (taps,))

    placed = reassign[:, None] == jnp.arange(slots_total, dtype=jnp.int32)[None, :]
    table = jnp.sum(jnp.where(placed[:, :, None], page_table[None], 0), axis=1)
    slot_lengths = jnp.sum(jnp.where(placed, lengths[None, :], 0), axis=1)
    source_page = (
        table.reshape(dp_count, req_dev, seq_count, page_span)
        .transpose(0, 2, 1, 3)
        .reshape(groups, req_dev * page_span)
    )
    capacity = (pages_dev + groups - 1) // groups
    page_owner = source_page // pages_dev
    pool_slot = source_page % pages_dev
    before = jnp.arange(pages_dev)[None, :] < jnp.arange(pages_dev)[:, None]
    pair_rank = jnp.sum((page_owner[:, :, None] == page_owner[:, None, :]) & before[None], axis=2)
    send_hit = (page_owner == device_place)[:, None, :] & (
        pair_rank[:, None, :] == jnp.arange(capacity)[None, :, None]
    )
    send_slot = jnp.sum(jnp.where(send_hit, pool_slot[:, None, :], 0), axis=2)
    outgoing = pool.at[send_slot.reshape(-1)].get(mode="promise_in_bounds")
    outgoing = outgoing.reshape(groups, capacity, page_share, width)
    arrived = lax.all_to_all(outgoing, ("dp", "seq"), split_axis=0, concat_axis=0, tiled=True)
    own_row = jnp.arange(groups)[:, None] == device_place
    pick_rows = jnp.sum(jnp.where(own_row, page_owner * capacity + pair_rank, 0), axis=0)
    picked = arrived.reshape(groups * capacity, page_share, width)
    picked = picked.at[pick_rows].get(mode="promise_in_bounds")

    picked = after(picked.reshape(req_dev, page_span, page_share, width), (held_one,))
    swapped = lax.all_to_all(picked, "tensor", split_axis=0, concat_axis=0, tiled=True)
    tokens = swapped.transpose(1, 0, 2, 3).reshape(rows, width)
    slot = dp_place * req_dev + tensor_place
    length = jnp.sum(jnp.where(jnp.arange(slots_total) == slot, slot_lengths, 0))

    held_out_one = settled(jnp.stack(from_groups(own_piece([out_one]), (picked,))))
    near_one = from_plane(held_one, neighbours(held_one), (swapped,), (held_out_one,))
    out_piece = after(own_piece([out_two]), (swapped,))
    beyond = from_group(own_piece([window_t, out_two]), (swapped,))
    first, second, ones, scale, kept = feature_tables(heads, feature_dim)
    first, second = jnp.asarray(first, BF16), jnp.asarray(second, BF16)
    column = np.zeros((1, heads * SLOT), np.float32)
    column[0, HEAD::SLOT] = 1

    def copy_sems(kinds):
        return pltpu.SemaphoreType.DMA((group_count + 1, NEAR * kinds))

    def weights_of(rows_of_head):
        return pltpu.VMEM((group_count, heads, rows_of_head, width), BF16)

    slots = heads * SLOT
    num, queries, state = call(
        functools.partial(linear_kernel, heads, feature_dim, kept),
        group_count,
        [
            SMEM,
            HBM,
            whole((1, width)),
            *[HBM] * 4,
            whole(first.shape),
            whole(second.shape),
            whole(ones.shape),
            whole(column.shape),
        ],
        [each((rows, slots)), each((rows, 2 * feat_cols)), each((heads * kept, SLOT))],
        [
            jax.ShapeDtypeStruct((group_count, rows, slots), F32),
            jax.ShapeDtypeStruct((group_count, rows, 2 * feat_cols), BF16),
            jax.ShapeDtypeStruct((group_count, heads * kept, SLOT), BF16),
        ],
        [
            pltpu.VMEM((rows, width), BF16),
            pltpu.VMEM((rows, width), BF16),
            weights_of(SLOT),
            weights_of(2 * feature_dim),
            copy_sems(3),
        ],
        "linear_rows",
    )(
        places, tokens, gain_one[None], values_t, featmap_t, *near_one, first, second, ones, column
    )
    prior = settled(earlier_blocks(state, "seq"))
    beyond = after(beyond, (state,))
    held_window, out_beyond = beyond[:, : 3 * HEAD], beyond[0, 3 * HEAD :]
    held_out_two = [out_beyond, across(out_piece, "tensor", 1), across(out_beyond, "tensor", 1)]
    held_out_two = settled(jnp.stack(held_out_two), (prior,))
    near_out_one = from_plane(
        held_out_one, neighbours(held_out_one), (state,), (beyond, held_out_two)
    )
    held_window = after(held_window, (prior,))
    near_by_window = neighbours(held_window)
    residual, normed_two, tail = call(
        functools.partial(out_one_kernel, heads, kept),
        group_count,
        [
            SMEM,
            each((rows, slots)),
            each((rows, 2 * feat_cols)),
            whole(first.shape),
            whole(second.shape),
            whole(ones.shape),
            whole(scale.shape),
        ]
        + [each((heads * kept, SLOT))]
        + [HBM] * 4
        + [whole((1, width))],
        [whole((n, width)) for n in (rows, rows, HALO)],
        [jax.ShapeDtypeStruct((n, width), BF16) for n in (rows, rows, HALO)],
        [
            pltpu.VMEM((rows, width), BF16),
            pltpu.VMEM((rows, width), F32),
            pltpu.VMEM((rows, slots), BF16),
            weights_of(SLOT),
            copy_sems(1),
        ],
        "linear_out",
    )(
        places, num, queries, first, second, ones, scale, prior, out_one, *near_out_one, tokens,
        gain_two[None],
    )

    halo = lax.ppermute(tail, "seq", [(i, i + 1) for i in range(seq_count - 1)])
    pair_rows = across(normed_two, "tensor", 1)
    pair_halo = lax.ppermute(
        tail,
        ("seq", "tensor"),
        [
            (i * group_count + j, (i + 1) * group_count + (j ^ 1))
            for i in range(seq_count - 1)
            for j in range(group_count)
        ],
    )
    held_out_two = after(held_out_two, (residual,))
    near_by_two = neighbours(held_out_two)
    near_window = from_plane(
        held_window, near_by_window, (residual,), (pair_rows, pair_halo), (), near_by_two
    )
    block_start = (seq_place * rows).astype(jnp.int32)[None]

    def window_rows(slot_rows, slot_halo, earlier):
        return call(
            functools.partial(window_kernel, heads),
            2,
            [
                SMEM,
                SMEM,
                *[HBM] * 5,
                each((tap_count, 3 * slots)),
                HBM,
            ],
            each((rows, slots)),
            jax.ShapeDtypeStruct((2, rows, slots), BF16),
            [
                pltpu.VMEM((HALO + rows, width), BF16),
                pltpu.VMEM((2, heads, 3 * SLOT, width), BF16),
                copy_sems(3),
            ],
            "window_rows",
        )(places, block_start, slot_rows, slot_halo, window_t, *near_window, taps, earlier)

    mixed_pair = window_rows(pair_rows, pair_halo, normed_two)
    near_out_two = from_plane(held_out_two, near_by_two, None, (mixed_pair,))
    mixed_own = window_rows(normed_two, halo, mixed_pair)
    mixed_pair = across(mixed_pair, "tensor", 1)
    live = (length - seq_place * rows).astype(jnp.int32)[None]
    result = call(
        out_two_kernel,
        group_count,
        [
            SMEM,
            SMEM,
            *[HBM] * 6,
        ],
        whole((rows, width)),
        jax.ShapeDtypeStruct((rows, width), BF16),
        [
            pltpu.VMEM((group_count, rows, slots), BF16),
            pltpu.VMEM((rows, width), BF16),
            pltpu.VMEM((rows, width), F32),
            weights_of(SLOT),
            copy_sems(1),
        ],
        "window_out",
    )(places, live, mixed_own, mixed_pair, out_two, *near_out_two, residual)

    result = result.reshape(page_span, group_count, page_share, width).transpose(1, 0, 2, 3)
    return lax.all_to_all(result, "tensor", split_axis=0, concat_axis=0, tiled=True)


def solution(mesh):
    return jax.shard_map(
        on_device,
        mesh=mesh,
        in_specs=(
            P(("dp", "seq"), "tensor", None),
            P(),
            P(),
            P(),
            P(),
            P(None, None, "tensor"),
            P(None, "tensor"),
            P("tensor", None),
            P(),
            P(None, None, "tensor"),
            P(None, None, "tensor"),
            P("tensor", None),
        ),
        out_specs=P("dp", "seq", "tensor", None),
        check_vma=False,
    )
```

```python
import functools

import jax
import jax.numpy as jnp
import numpy as np
from jax import lax
from jax.experimental import pallas as pl
from jax.experimental.pallas import tpu as pltpu
from jax.sharding import PartitionSpec as P

HEAD = 112
WINDOW = 64
EPS = 1e-05
SLOT = 128
FEAT_SLOT = 256
HALO = 80
NEAR = 4
VMEM = 60 * 1024 * 1024
F32 = jnp.float32
BF16 = jnp.bfloat16


def dot(a, b, dims=((1,), (0,))):
    return lax.dot_general(a, b, (dims, ((), ())), preferred_element_type=F32)


def normed_rows(rows, gain):
    scale = lax.rsqrt(jnp.mean(rows * rows, axis=-1, keepdims=True) + EPS)
    return (rows * scale * gain).astype(BF16)


def feature_tables(heads, feature_dim):
    pairs = [(i, j) for i in range(feature_dim) for j in range(i, feature_dim)]
    pairs += [(i, -1) for i in range(feature_dim)] + [(-1, -1)]
    first = np.zeros((2 * heads * feature_dim, heads * FEAT_SLOT), np.float32)
    second = np.zeros_like(first)
    ones = np.zeros((2, heads * FEAT_SLOT), np.float32)
    scale = np.zeros((1, heads * FEAT_SLOT), np.float32)
    for h in range(heads):
        for n, (i, j) in enumerate(pairs):
            at = h * FEAT_SLOT + n
            if i >= 0:
                first[2 * h * feature_dim + i, at] = 1
            else:
                ones[0, at] = 1
            if j >= 0:
                second[2 * h * feature_dim + j, at] = 1
            else:
                ones[1, at] = 1
            if i < 0:
                scale[0, at] = 1
            elif j < 0:
                scale[0, at] = feature_dim**-0.5
            else:
                scale[0, at] = (0.5 if i == j else 1.0) / feature_dim
    return first, second, ones, scale, -(-len(pairs) // 16) * 16


def features(rows, first, second, ones):
    return (dot(rows, first) + ones[0:1]) * (dot(rows, second) + ones[1:2])


def run_copies(copies_of, groups, loads, meanwhile=None):
    step = pl.program_id(0)

    @pl.when(step == 0)
    def _():
        for copy, _ in loads:
            copy.start()
        for group in range(groups):
            for copy in copies_of(group):
                copy.start()

    for group in range(groups):

        @pl.when(step == group)
        def _(group=group):
            for copy, at in loads:
                if at == group:
                    copy.wait()
            if meanwhile is not None and group == 0:
                meanwhile()
            for copy in copies_of(group):
                copy.wait()


def weight_copies(place_ref, near_ref, far_ref, targets, pieces, sems, group):
    found = []

    def copy(src, dst):
        found.append(pltpu.make_async_copy(src, dst, sems.at[group, len(found)]))

    if group == 0:
        for own_ref, kind, w_ref, off in targets:
            rows = own_ref.shape[2]
            for n in range(NEAR):
                copy(own_ref.at[kind, place_ref[n]], w_ref.at[0, n, off : off + rows, :])
        return found
    cols = near_ref.shape[3]
    for ref, part in ((near_ref, place_ref[NEAR]), (far_ref, 1 - place_ref[NEAR])):
        at = 0
        lanes = pl.ds(pl.multiple_of(part * cols, SLOT), cols)
        for rows, w_ref, off in pieces:
            copy(ref.at[:, group - 1, at : at + rows, :], w_ref.at[group, :, off : off + rows, lanes])
            at += rows
    return found


def zero_between_heads(w_ref):
    groups, heads, rows, width = w_ref.shape
    for at in range(HEAD, rows, SLOT):
        w_ref[:, :, at : at + SLOT - HEAD, :] = jnp.zeros(
            (groups, heads, SLOT - HEAD, width), BF16
        )


def group_weights(w_ref, step):
    heads, rows, width = w_ref.shape[1:]
    return w_ref[step].reshape(heads * rows, width)


def project(rows_ref, w_ref, step):
    return dot(rows_ref[...], group_weights(w_ref, step), ((1,), (1,)))


def linear_kernel(
    heads,
    feature_dim,
    kept,
    place_ref,
    x_ref,
    gain_ref,
    value_ref,
    featmap_ref,
    near_ref,
    far_ref,
    first_ref,
    second_ref,
    ones_ref,
    column_ref,
    num_ref,
    q_ref,
    state_ref,
    tokens_ref,
    normed_ref,
    value_w_ref,
    feat_w_ref,
    sems,
):
    step = pl.program_id(0)
    targets = [
        (value_ref, 0, value_w_ref, 0),
        (featmap_ref, 0, feat_w_ref, 0),
        (featmap_ref, 1, feat_w_ref, feature_dim),
    ]
    pieces = [(HEAD, value_w_ref, 0), (2 * feature_dim, feat_w_ref, 0)]

    groups = value_w_ref.shape[0]

    @pl.when(step == 0)
    def _():
        zero_between_heads(value_w_ref)

    def normalize():
        normed_ref[...] = normed_rows(tokens_ref[...].astype(F32), gain_ref[...])

    run_copies(
        functools.partial(weight_copies, place_ref, near_ref, far_ref, targets, pieces, sems),
        groups,
        [(pltpu.make_async_copy(x_ref, tokens_ref, sems.at[groups, 0]), 0)],
        normalize,
    )
    rows = x_ref.shape[0]
    width = 2 * heads * feature_dim
    queries = project(normed_ref, feat_w_ref, step).astype(BF16)
    keys = pltpu.roll(queries.astype(F32), width - feature_dim, 1).astype(BF16)
    values = (project(normed_ref, value_w_ref, step) + column_ref[...]).astype(BF16)
    q_ref[0] = queries
    lane = lax.broadcasted_iota(jnp.int32, (rows, width), 1)
    causal = lax.broadcasted_iota(jnp.int32, (rows, rows), 1) <= lax.broadcasted_iota(
        jnp.int32, (rows, rows), 0
    )
    key_features = features(keys, first_ref[...], second_ref[...], ones_ref[...]).astype(BF16)
    for h in range(heads):
        at = 2 * h * feature_dim
        own = jnp.where((lane >= at) & (lane < at + feature_dim), queries, jnp.zeros_like(queries))
        scores = dot(own, keys, ((1,), (1,))) * feature_dim**-0.5
        kernel = jnp.where(causal, 1.0 + scores + 0.5 * scores * scores, 0.0).astype(BF16)
        value = values[:, h * SLOT : (h + 1) * SLOT]
        num_ref[0, :, h * SLOT : (h + 1) * SLOT] = dot(kernel, value)
        state = dot(key_features[:, h * FEAT_SLOT : h * FEAT_SLOT + kept], value, ((0,), (0,)))
        head = pl.multiple_of(place_ref[h] * kept, 16)
        state_ref[0, pl.ds(head, kept), :] = state.astype(BF16)


def add_branch(mixed, w_ref, total_ref):
    step = pl.program_id(0)
    total_ref[...] += dot(mixed, group_weights(w_ref, step)).astype(BF16).astype(F32)


def out_one_kernel(
    heads,
    kept,
    place_ref,
    num_ref,
    q_ref,
    first_ref,
    second_ref,
    ones_ref,
    scale_ref,
    prior_ref,
    own_ref,
    near_ref,
    far_ref,
    x_ref,
    gain_ref,
    residual_ref,
    normed_ref,
    tail_ref,
    tokens_ref,
    total_ref,
    mixed_ref,
    w_ref,
    sems,
):
    step = pl.program_id(0)
    groups = w_ref.shape[0]

    @pl.when(step == 0)
    def _():
        total_ref[...] = jnp.zeros_like(total_ref)
        zero_between_heads(w_ref)

    loads = [(pltpu.make_async_copy(x_ref, tokens_ref, sems.at[groups, 0]), groups - 1)]
    run_copies(
        functools.partial(
            weight_copies,
            place_ref,
            near_ref,
            far_ref,
            [(own_ref, 0, w_ref, 0)],
            [(HEAD, w_ref, 0)],
            sems,
        ),
        groups,
        loads,
    )

    query_features = features(q_ref[0], first_ref[...], second_ref[...], ones_ref[...])
    query_features = (query_features * scale_ref[...]).astype(BF16)
    for h in range(heads):
        prior = prior_ref[0, pl.ds(pl.multiple_of(place_ref[h] * kept, 16), kept), :]
        lanes = slice(h * SLOT, (h + 1) * SLOT)
        total = num_ref[0, :, lanes] + dot(
            query_features[:, h * FEAT_SLOT : h * FEAT_SLOT + kept], prior.astype(BF16)
        )
        mixed_ref[:, lanes] = (total * (1.0 / total[:, HEAD : HEAD + 1])).astype(BF16)
    add_branch(mixed_ref[...], w_ref, total_ref)

    @pl.when(step == pl.num_programs(0) - 1)
    def _():
        residual = (tokens_ref[...].astype(F32) + total_ref[...]).astype(BF16)
        residual_ref[...] = residual
        normed = normed_rows(residual.astype(F32), gain_ref[...])
        normed_ref[...] = normed
        tail_ref[...] = normed[normed.shape[0] - HALO :]


def window_kernel(
    heads,
    place_ref,
    first_ref,
    x_ref,
    halo_ref,
    own_ref,
    near_ref,
    far_ref,
    tap_ref,
    _,
    mixed_ref,
    rows_ref,
    w_ref,
    sems,
):
    step = pl.program_id(0)
    targets = [(own_ref, kind, w_ref, kind * SLOT) for kind in range(3)]
    pieces = [(HEAD, w_ref, kind * SLOT) for kind in range(3)]

    groups = w_ref.shape[0]
    loads = [
        (pltpu.make_async_copy(src, rows_ref.at[at : at + src.shape[0], :], sems.at[groups, n]), 0)
        for n, (src, at) in enumerate(((halo_ref, 0), (x_ref, HALO)))
    ]

    @pl.when(step == 0)
    def _():
        zero_between_heads(w_ref)

    run_copies(
        functools.partial(weight_copies, place_ref, near_ref, far_ref, targets, pieces, sems),
        groups,
        loads,
    )
    rows = x_ref.shape[0]
    lead = HALO - WINDOW
    projected = project(rows_ref, w_ref, step)
    taps = tap_ref[0]
    convolved = taps[0:1] * projected
    for offset in range(1, taps.shape[0]):
        convolved = convolved + taps[offset : offset + 1] * pltpu.roll(projected, offset, 0)
    convolved = convolved[lead:].astype(BF16)
    tile = 128
    span = tile + WINDOW
    row = lax.broadcasted_iota(jnp.int32, (tile, span), 0)
    col = lax.broadcasted_iota(jnp.int32, (tile, span), 1)
    band = (col > row) & (col <= row + WINDOW)
    for h in range(heads):
        at = 3 * h * SLOT
        queries = convolved[WINDOW:, at : at + SLOT]
        keys = convolved[:, at + SLOT : at + 2 * SLOT]
        values = convolved[:, at + 2 * SLOT : at + 3 * SLOT]
        for start in range(0, rows, tile):
            logits = dot(queries[start : start + tile], keys[start : start + span], ((1,), (1,)))
            allowed = band
            if start < WINDOW:
                allowed = band & (col >= WINDOW - start - first_ref[0])
            logits = jnp.where(allowed, logits * HEAD**-0.5, -jnp.inf)
            weights = jnp.exp(logits - jnp.max(logits, axis=1, keepdims=True))
            weights = weights * (1.0 / jnp.sum(weights, axis=1, keepdims=True))
            mixed = dot(weights.astype(BF16), values[start : start + span])
            mixed_ref[0, start : start + tile, h * SLOT : (h + 1) * SLOT] = mixed.astype(BF16)


def out_two_kernel(
    place_ref,
    live_ref,
    mixed_ref,
    pair_ref,
    own_ref,
    near_ref,
    far_ref,
    residual_ref,
    out_ref,
    mixed_all_ref,
    rows_ref,
    total_ref,
    w_ref,
    sems,
):
    step = pl.program_id(0)
    groups = w_ref.shape[0]
    loads = [
        (pltpu.make_async_copy(mixed_ref, mixed_all_ref.at[:2], sems.at[groups, 0]), 0),
        (pltpu.make_async_copy(pair_ref, mixed_all_ref.at[2:], sems.at[groups, 1]), 2),
        (pltpu.make_async_copy(residual_ref, rows_ref, sems.at[groups, 2]), groups - 1),
    ]

    @pl.when(step == 0)
    def _():
        total_ref[...] = jnp.zeros_like(total_ref)
        zero_between_heads(w_ref)

    run_copies(
        functools.partial(
            weight_copies,
            place_ref,
            near_ref,
            far_ref,
            [(own_ref, 0, w_ref, 0)],
            [(HEAD, w_ref, 0)],
            sems,
        ),
        groups,
        loads,
    )
    add_branch(mixed_all_ref[step], w_ref, total_ref)

    @pl.when(step == pl.num_programs(0) - 1)
    def _():
        result = (rows_ref[...].astype(F32) + total_ref[...]).astype(BF16)
        row = lax.broadcasted_iota(jnp.int32, result.shape, 0)
        out_ref[...] = jnp.where(row < live_ref[0], result, jnp.zeros_like(result))


def whole(shape):
    return pl.BlockSpec(shape, lambda g: (0,) * len(shape))


def each(shape):
    return pl.BlockSpec((1,) + shape, lambda g: (g,) + (0,) * len(shape))


SMEM = pl.BlockSpec(memory_space=pltpu.SMEM)
HBM = pl.BlockSpec(memory_space=pl.ANY)


def call(kernel, groups, in_specs, out_specs, out_shape, scratch, name):
    return pl.pallas_call(
        kernel,
        grid=(groups,),
        in_specs=in_specs,
        out_specs=out_specs,
        out_shape=out_shape,
        scratch_shapes=scratch,
        compiler_params=pltpu.CompilerParams(
            dimension_semantics=("arbitrary",), vmem_limit_bytes=VMEM
        ),
        cost_estimate=pl.CostEstimate(flops=0, bytes_accessed=0, transcendentals=0),
        name=name,
    )


def own_piece(whole_weights):
    head, part = lax.axis_index("seq") % NEAR, lax.axis_index("dp")
    found = []
    for weights in whole_weights:
        kinds, _, rows, cols = weights.shape
        cols = cols // lax.axis_size("dp")
        piece = lax.dynamic_slice(weights, (0, head, 0, part * cols), (kinds, 1, rows, cols))
        found.append(piece.reshape(kinds * rows, cols))
    return jnp.concatenate(found, axis=0)


def across(array, axis, bit):
    return lax.ppermute(array, axis, [(i, i ^ bit) for i in range(lax.axis_size(axis))])


def after(array, others):
    if not others:
        return array
    first = [lax.slice(other, (0,) * other.ndim, (1,) * other.ndim) for other in others]
    zero = sum(one.reshape(()).astype(F32) * 0.0 for one in first)
    return jnp.where(zero == 0.0, array, jnp.zeros_like(array))


def settled(array, others=()):
    return lax.optimization_barrier(after(array, others))


def from_group(piece, over_z):
    return across(after(piece, over_z), "tensor", 2)[None]


def from_groups(piece, over_z, order=(0, 1, 2)):
    piece = after(piece, over_z)
    beside, beyond = across(piece, "tensor", 1), across(piece, "tensor", 2)
    found = (beside, beyond, across(beyond, "tensor", 1))
    return [found[n] for n in order]


def neighbours(held):
    return across(held, "seq", 1), across(held, "seq", 2)


def from_plane(held, near_by, diagonal, over_cores, over_across=(), by_one_way=False):
    beside, above = near_by
    if by_one_way:
        beside = settled(beside, diagonal)
        opposite = across(after(above, (beside,)), "seq", 1)
    elif diagonal is None:
        opposite = across(after(held, over_across), "seq", 3)
    else:
        half = -(-held.shape[1] // 32) * 16
        opposite = [
            across(after(above[:, :half], diagonal), "seq", 1),
            across(after(beside[:, half:], diagonal), "seq", 2),
        ]
        opposite = after(jnp.concatenate(opposite, axis=1), over_cores)
    near = after(jnp.stack([held, beside, above, opposite]), over_cores)
    return near, across(near, "dp", 1)


def earlier_blocks(state, axis):
    peers = lax.axis_size(axis)
    if peers <= 4:
        found = [
            lax.ppermute(state, axis, [(i, i + by) for i in range(peers - by)])
            for by in range(1, peers)
        ]
        return sum(one.astype(F32) for one in found)
    everything = lax.all_gather(state, axis).astype(F32)
    reached = jnp.arange(peers) < lax.axis_index(axis)
    return jnp.sum(jnp.where(reached[:, None, None, None], everything, 0.0), axis=0)


def on_device(
    pool,
    page_table,
    reassign,
    lengths,
    gain_one,
    w_featmap,
    w_value,
    w_out_one,
    gain_two,
    w_window,
    conv_window,
    w_out_two,
):
    dp_count, seq_count, group_count = (lax.axis_size(n) for n in ("dp", "seq", "tensor"))
    groups = dp_count * seq_count
    device_place = lax.axis_index(("dp", "seq"))
    dp_place, seq_place, tensor_place = (lax.axis_index(n) for n in ("dp", "seq", "tensor"))
    pages_dev, page_share, width = pool.shape
    slots_total, pages_total = page_table.shape
    req_dev = slots_total // dp_count
    page_span = pages_total // seq_count
    page_rows = page_share * group_count
    rows = page_span * page_rows
    assert req_dev == group_count
    heads = w_value.shape[1] // HEAD
    head_cols = heads * HEAD
    feat_cols = w_featmap.shape[2]
    feature_dim = feat_cols // heads
    tap_count = conv_window.shape[0]

    assert heads == NEAR and dp_count == 2
    values_t = w_value.T.reshape(1, heads, HEAD, width)
    featmap_t = w_featmap.transpose(1, 2, 0).reshape(2, heads, feature_dim, width)
    window_t = w_window.transpose(1, 2, 0).reshape(3, heads, HEAD, width)
    out_one, out_two = (w.reshape(1, heads, HEAD, width) for w in (w_out_one, w_out_two))
    places = jnp.concatenate([(seq_place % NEAR) ^ jnp.arange(NEAR), dp_place[None]])
    places = places.astype(jnp.int32)
    taps = conv_window.reshape(tap_count, 3, heads, HEAD).transpose(0, 2, 1, 3)
    taps = jnp.take(taps, places[:NEAR], axis=1, mode="clip")
    taps = jnp.pad(taps, ((0, 0), (0, 0), (0, 0), (0, SLOT - HEAD)))
    taps = taps.reshape(tap_count, 3 * heads * SLOT)
    taps = settled(jnp.stack([taps, across(taps, "tensor", 2)]))
    held_one = from_groups(own_piece([values_t, featmap_t]), ())
    held_one = settled(jnp.stack(held_one), (taps,))

    placed = reassign[:, None] == jnp.arange(slots_total, dtype=jnp.int32)[None, :]
    table = jnp.sum(jnp.where(placed[:, :, None], page_table[None], 0), axis=1)
    slot_lengths = jnp.sum(jnp.where(placed, lengths[None, :], 0), axis=1)
    source_page = (
        table.reshape(dp_count, req_dev, seq_count, page_span)
        .transpose(0, 2, 1, 3)
        .reshape(groups, req_dev * page_span)
    )
    capacity = (pages_dev + groups - 1) // groups
    page_owner = source_page // pages_dev
    pool_slot = source_page % pages_dev
    before = jnp.arange(pages_dev)[None, :] < jnp.arange(pages_dev)[:, None]
    pair_rank = jnp.sum((page_owner[:, :, None] == page_owner[:, None, :]) & before[None], axis=2)
    send_hit = (page_owner == device_place)[:, None, :] & (
        pair_rank[:, None, :] == jnp.arange(capacity)[None, :, None]
    )
    send_slot = jnp.sum(jnp.where(send_hit, pool_slot[:, None, :], 0), axis=2)
    outgoing = pool.at[send_slot.reshape(-1)].get(mode="promise_in_bounds")
    outgoing = outgoing.reshape(groups, capacity, page_share, width)
    arrived = lax.all_to_all(outgoing, ("dp", "seq"), split_axis=0, concat_axis=0, tiled=True)
    own_row = jnp.arange(groups)[:, None] == device_place
    pick_rows = jnp.sum(jnp.where(own_row, page_owner * capacity + pair_rank, 0), axis=0)
    picked = arrived.reshape(groups * capacity, page_share, width)
    picked = picked.at[pick_rows].get(mode="promise_in_bounds")

    picked = after(picked.reshape(req_dev, page_span, page_share, width), (held_one,))
    swapped = lax.all_to_all(picked, "tensor", split_axis=0, concat_axis=0, tiled=True)
    tokens = swapped.transpose(1, 0, 2, 3).reshape(rows, width)
    slot = dp_place * req_dev + tensor_place
    length = jnp.sum(jnp.where(jnp.arange(slots_total) == slot, slot_lengths, 0))

    held_out_one = settled(jnp.stack(from_groups(own_piece([out_one]), (picked,))))
    near_one = from_plane(held_one, neighbours(held_one), (swapped,), (held_out_one,))
    out_piece = after(own_piece([out_two]), (swapped,))
    beyond = from_group(own_piece([window_t, out_two]), (swapped,))
    first, second, ones, scale, kept = feature_tables(heads, feature_dim)
    first, second = jnp.asarray(first, BF16), jnp.asarray(second, BF16)
    column = np.zeros((1, heads * SLOT), np.float32)
    column[0, HEAD::SLOT] = 1

    def copy_sems(kinds):
        return pltpu.SemaphoreType.DMA((group_count + 1, NEAR * kinds))

    def weights_of(rows_of_head):
        return pltpu.VMEM((group_count, heads, rows_of_head, width), BF16)

    slots = heads * SLOT
    num, queries, state = call(
        functools.partial(linear_kernel, heads, feature_dim, kept),
        group_count,
        [
            SMEM,
            HBM,
            whole((1, width)),
            *[HBM] * 4,
            whole(first.shape),
            whole(second.shape),
            whole(ones.shape),
            whole(column.shape),
        ],
        [each((rows, slots)), each((rows, 2 * feat_cols)), each((heads * kept, SLOT))],
        [
            jax.ShapeDtypeStruct((group_count, rows, slots), F32),
            jax.ShapeDtypeStruct((group_count, rows, 2 * feat_cols), BF16),
            jax.ShapeDtypeStruct((group_count, heads * kept, SLOT), BF16),
        ],
        [
            pltpu.VMEM((rows, width), BF16),
            pltpu.VMEM((rows, width), BF16),
            weights_of(SLOT),
            weights_of(2 * feature_dim),
            copy_sems(3),
        ],
        "linear_rows",
    )(
        places, tokens, gain_one[None], values_t, featmap_t, *near_one, first, second, ones, column
    )
    prior = settled(earlier_blocks(state, "seq"))
    beyond = after(beyond, (state,))
    held_window, out_beyond = beyond[:, : 3 * HEAD], beyond[0, 3 * HEAD :]
    held_out_two = [out_beyond, across(out_piece, "tensor", 1), across(out_beyond, "tensor", 1)]
    held_out_two = settled(jnp.stack(held_out_two), (prior,))
    near_out_one = from_plane(
        held_out_one, neighbours(held_out_one), (state,), (beyond, held_out_two)
    )
    held_window = after(held_window, (prior,))
    near_by_window = neighbours(held_window)
    residual, normed_two, tail = call(
        functools.partial(out_one_kernel, heads, kept),
        group_count,
        [
            SMEM,
            each((rows, slots)),
            each((rows, 2 * feat_cols)),
            whole(first.shape),
            whole(second.shape),
            whole(ones.shape),
            whole(scale.shape),
        ]
        + [each((heads * kept, SLOT))]
        + [HBM] * 4
        + [whole((1, width))],
        [whole((n, width)) for n in (rows, rows, HALO)],
        [jax.ShapeDtypeStruct((n, width), BF16) for n in (rows, rows, HALO)],
        [
            pltpu.VMEM((rows, width), BF16),
            pltpu.VMEM((rows, width), F32),
            pltpu.VMEM((rows, slots), BF16),
            weights_of(SLOT),
            copy_sems(1),
        ],
        "linear_out",
    )(
        places, num, queries, first, second, ones, scale, prior, out_one, *near_out_one, tokens,
        gain_two[None],
    )

    halo = lax.ppermute(tail, "seq", [(i, i + 1) for i in range(seq_count - 1)])
    pair_rows = across(normed_two, "tensor", 1)
    pair_halo = lax.ppermute(
        tail,
        ("seq", "tensor"),
        [
            (i * group_count + j, (i + 1) * group_count + (j ^ 1))
            for i in range(seq_count - 1)
            for j in range(group_count)
        ],
    )
    held_out_two = after(held_out_two, (residual,))
    near_by_two = neighbours(held_out_two)
    near_window = from_plane(
        held_window, near_by_window, (residual,), (pair_rows, pair_halo, *near_by_two), (), True
    )
    block_start = (seq_place * rows).astype(jnp.int32)[None]

    def window_rows(slot_rows, slot_halo, earlier):
        return call(
            functools.partial(window_kernel, heads),
            2,
            [
                SMEM,
                SMEM,
                *[HBM] * 5,
                each((tap_count, 3 * slots)),
                HBM,
            ],
            each((rows, slots)),
            jax.ShapeDtypeStruct((2, rows, slots), BF16),
            [
                pltpu.VMEM((HALO + rows, width), BF16),
                pltpu.VMEM((2, heads, 3 * SLOT, width), BF16),
                copy_sems(3),
            ],
            "window_rows",
        )(places, block_start, slot_rows, slot_halo, window_t, *near_window, taps, earlier)

    mixed_pair = window_rows(pair_rows, pair_halo, normed_two)
    near_out_two = from_plane(held_out_two, near_by_two, None, (mixed_pair,))
    mixed_own = window_rows(normed_two, halo, mixed_pair)
    mixed_pair = across(mixed_pair, "tensor", 1)
    live = (length - seq_place * rows).astype(jnp.int32)[None]
    result = call(
        out_two_kernel,
        group_count,
        [
            SMEM,
            SMEM,
            *[HBM] * 6,
        ],
        whole((rows, width)),
        jax.ShapeDtypeStruct((rows, width), BF16),
        [
            pltpu.VMEM((group_count, rows, slots), BF16),
            pltpu.VMEM((rows, width), BF16),
            pltpu.VMEM((rows, width), F32),
            weights_of(SLOT),
            copy_sems(1),
        ],
        "window_out",
    )(places, live, mixed_own, mixed_pair, out_two, *near_out_two, residual)

    result = result.reshape(page_span, group_count, page_share, width).transpose(1, 0, 2, 3)
    return lax.all_to_all(result, "tensor", split_axis=0, concat_axis=0, tiled=True)


def solution(mesh):
    return jax.shard_map(
        on_device,
        mesh=mesh,
        in_specs=(
            P(("dp", "seq"), "tensor", None),
            P(),
            P(),
            P(),
            P(),
            P(None, None, "tensor"),
            P(None, "tensor"),
            P("tensor", None),
            P(),
            P(None, None, "tensor"),
            P(None, None, "tensor"),
            P("tensor", None),
        ),
        out_specs=P("dp", "seq", "tensor", None),
        check_vma=False,
    )
```
